32 devices in a mesh: fsdp: 16 (over z, y, core), tensor: 2 (over x).
Axes of the slice: x: 2, y: 2, z: 4, core: 2. Of those that a mesh axis runs over, the one named last changes fastest.
Arguments:
- tokens: bfloat16 [2048, 8192], P('fsdp'), may hold values from -6 to 6
- cotangent: bfloat16 [2048, 8192], P('fsdp'), may hold values from -1.5 to 1.5
- gate_blocks: bfloat16 [2, 32, 128, 128], P('tensor', 'fsdp'), may hold values from -0.75 to 0.75
- up_blocks: bfloat16 [2, 32, 128, 128], P('tensor', 'fsdp'), may hold values from -0.75 to 0.75
- down_blocks: bfloat16 [2, 32, 128, 128], P('tensor', 'fsdp'), may hold values from -0.75 to 0.75
- gate_where: int32 [2, 32], P('tensor'), may hold values from 0 to 3583, as said below
- up_where: int32 [2, 32], P('tensor'), may hold values from 0 to 3583, as said below
- down_where: int32 [2, 32], P('tensor'), may hold values from 0 to 3583, as said below
- block_counts: int32 [3, 2], P(None, 'tensor'), may hold values from 16 to 32, as said below
Outputs:
- outputs: bfloat16 [2048, 8192], P('fsdp', 'tensor')
- input_grads: bfloat16 [2048, 8192], P('fsdp', 'tensor')
- gate_grads: bfloat16 [2, 32, 128, 128], P('tensor', 'fsdp')
- up_grads: bfloat16 [2, 32, 128, 128], P('tensor', 'fsdp')
- down_grads: bfloat16 [2, 32, 128, 128], P('tensor', 'fsdp')
The draws below stay inside these ranges and needn't reach their ends.
Inputs may be any that keep to these rules, and one draw needn't show every extreme that they name: Within one group of hidden units the 32 positions of gate_where are distinct. Within one group of hidden units the 32 positions of up_where are distinct. Within one group of hidden units the 32 positions of down_where are distinct. `block_counts`: for each matrix some group has all 32 slots live.
All inputs are finite; a program needn't handle non-finite values.
Results may differ from the reference program's by a relative error of at most 0.015.
Values may be sent and summed in bfloat16 or wider, within the bound.
No kernel may reach another device: no remote copies, remote signals or barrier semaphores. Data moves between devices by JAX's collectives and lax.ppermute only.
A program may use at most 128 MiB of HBM per device.

```python
import jax
import jax.numpy as jnp
from jax import lax

D = 8192
FF = 14336
TOK_DEV = 128
NB_DEV = 2
TOKENS = 2048
SLOTS = 32
N_FSDP = 16
N_TENSOR = 2


def where_draw(key, salt):
    cells = D // 128 * (FF // (128 * N_TENSOR))
    keys = jax.random.split(jax.random.fold_in(key, salt), N_TENSOR)
    picked = jax.vmap(lambda single: jax.random.permutation(single, cells)[:NB_DEV * N_FSDP])(keys)
    return picked.astype(jnp.int32)


def draw_gate_where(key, part):
    return where_draw(key, 11)


def draw_up_where(key, part):
    return where_draw(key, 23)


def draw_down_where(key, part):
    return where_draw(key, 37)


def draw_block_counts(key, part):
    slot_count = NB_DEV * N_FSDP
    first, second = jax.random.split(jax.random.fold_in(key, 41))
    drawn = jax.random.randint(first, (3, N_TENSOR), slot_count // 2, slot_count + 1)
    full_shard = jax.random.randint(second, (3, 1), 0, N_TENSOR)
    column = lax.broadcasted_iota(jnp.int32, (3, N_TENSOR), 1)
    return jnp.where(column == full_shard, slot_count, drawn).astype(jnp.int32)


def levels(rng, dims, shards, smallest, high):
    loudness = 1.0
    for axis_at, shards_of in shards:
        heights = jax.random.uniform(jax.random.fold_in(jax.random.fold_in(rng, 6), axis_at), (shards_of,), jnp.float32, smallest / len(shards), high / len(shards))
        loudness = loudness * jnp.repeat(jnp.exp(heights), dims[axis_at] // shards_of).reshape((-1,) + (1,) * (len(dims) - 1 - axis_at))
    return loudness


def scatter_about(own_key, extent, width, reach, pieces=(), held_as=jnp.bfloat16):
    values = width * jax.random.normal(own_key, extent, jnp.float32)
    if pieces:
        values = values * levels(own_key, extent, pieces, -0.22, 0.18)
    return jnp.clip(values, -reach, reach).astype(held_as)


def setup_inputs(seed: int = 0) -> dict:
    key_of = jax.random.split(jax.random.key(seed), 10)
    return {
        "tokens": scatter_about(key_of[0], (TOKENS, D), 1.0, 6.0, ((0, 16),)),
        "cotangent": scatter_about(key_of[1], (TOKENS, D), 0.25, 1.5, ((0, 16),)),
        "gate_blocks": scatter_about(key_of[2], (N_TENSOR, SLOTS, 128, 128), (SLOTS * 16384 * N_TENSOR // FF) ** -0.5, 0.75, ((0, 2), (1, 16))),
        "up_blocks": scatter_about(key_of[3], (N_TENSOR, SLOTS, 128, 128), (SLOTS * 16384 * N_TENSOR // FF) ** -0.5, 0.75, ((0, 2), (1, 16))),
        "down_blocks": scatter_about(key_of[4], (N_TENSOR, SLOTS, 128, 128), (SLOTS * 16384 * N_TENSOR // FF) ** -0.5, 0.75, ((0, 2), (1, 16))),
        "gate_where": draw_gate_where(jax.random.fold_in(key_of[9], 71), 0),
        "up_where": draw_up_where(jax.random.fold_in(key_of[9], 71), 0),
        "down_where": draw_down_where(jax.random.fold_in(key_of[9], 71), 0),
        "block_counts": draw_block_counts(jax.random.fold_in(key_of[9], 71), 0),
    }


def blockwise(pattern, left_side, right_side):
    return jnp.einsum(pattern, left_side.astype(jnp.float32), right_side.astype(jnp.float32), precision=lax.Precision.HIGHEST)


def collect(block_terms, segment_ids, segments):
    return jax.ops.segment_sum(block_terms, segment_ids, num_segments=segments)


def rounded(values):
    return lax.optimization_barrier(values.astype(jnp.bfloat16)).astype(jnp.float32)


def shard_pass(rows_x, rows_g, gate_eff, up_eff, down_eff, gate_where, up_where, down_where, live_parts, row_blocks, col_blocks):
    tok_rows = rows_x.shape[0]
    rows_blocked = rows_x.reshape(tok_rows, row_blocks, 128).transpose(1, 0, 2)
    grad_blocked = rows_g.reshape(tok_rows, row_blocks, 128).transpose(1, 0, 2)
    gate_row = gate_where // col_blocks
    gate_col = gate_where % col_blocks
    up_row = up_where // col_blocks
    up_col = up_where % col_blocks
    down_ff = down_where // row_blocks
    down_d = down_where % row_blocks
    rows_gate = jnp.take(rows_blocked, gate_row, axis=0)
    rows_up = jnp.take(rows_blocked, up_row, axis=0)
    gate_val = collect(blockwise("ntk,nkj->ntj", rows_gate, gate_eff), gate_col, col_blocks)
    up_val = collect(blockwise("ntk,nkj->ntj", rows_up, up_eff), up_col, col_blocks)
    gate_sig = jax.nn.sigmoid(gate_val)
    silu_gate = gate_val * gate_sig
    hidden = (silu_gate * up_val).astype(jnp.bfloat16)
    hidden_sel = jnp.take(hidden, down_ff, axis=0)
    grad_sel = jnp.take(grad_blocked, down_d, axis=0)
    output_term = collect(blockwise("ntk,nkj->ntj", hidden_sel, down_eff), down_d, row_blocks)
    hidden_grad = collect(blockwise("ntj,nkj->ntk", grad_sel, down_eff), down_ff, col_blocks)
    down_part = blockwise("ntk,ntj->nkj", hidden_sel, grad_sel) * live_parts[2]
    gate_delta = (hidden_grad * up_val * gate_sig * (1.0 + gate_val * (1.0 - gate_sig))).astype(jnp.bfloat16)
    up_delta = (hidden_grad * silu_gate).astype(jnp.bfloat16)
    delta_gate = jnp.take(gate_delta, gate_col, axis=0)
    delta_up = jnp.take(up_delta, up_col, axis=0)
    input_term = collect(blockwise("ntj,nkj->ntk", delta_gate, gate_eff), gate_row, row_blocks)
    input_term = input_term + collect(blockwise("ntj,nkj->ntk", delta_up, up_eff), up_row, row_blocks)
    gate_part = blockwise("ntk,ntj->nkj", rows_gate, delta_gate) * live_parts[0]
    up_part = blockwise("ntk,ntj->nkj", rows_up, delta_up) * live_parts[1]
    return output_term, input_term, gate_part, up_part, down_part


def reference(tokens, cotangent, gate_blocks, up_blocks, down_blocks, gate_where, up_where, down_where, block_counts):
    row_blocks = D // 128
    col_blocks = FF // (128 * N_TENSOR)
    slot_count = NB_DEV * N_FSDP
    member_x = tokens.reshape(N_FSDP, TOK_DEV, D)
    member_g = cotangent.reshape(N_FSDP, TOK_DEV, D)
    output_acc = jnp.zeros((N_FSDP, row_blocks, TOK_DEV, 128), jnp.float32)
    input_acc = jnp.zeros((N_FSDP, row_blocks, TOK_DEV, 128), jnp.float32)
    gate_list = []
    up_list = []
    down_list = []
    for tensor_shard in range(N_TENSOR):
        live_slots = lax.broadcasted_iota(jnp.int32, (3, slot_count), 1) < block_counts[:, tensor_shard:tensor_shard + 1]
        live_blocks = live_slots.astype(jnp.bfloat16)[:, :, None, None]
        live_parts = live_slots.astype(jnp.float32)[:, :, None, None]
        gate_eff = gate_blocks[tensor_shard] * live_blocks[0]
        up_eff = up_blocks[tensor_shard] * live_blocks[1]
        down_eff = down_blocks[tensor_shard] * live_blocks[2]

        def per_member(member_rows):
            return shard_pass(member_rows[0], member_rows[1], gate_eff, up_eff, down_eff,
                              gate_where[tensor_shard], up_where[tensor_shard], down_where[tensor_shard],
                              live_parts, row_blocks, col_blocks)

        output_terms, input_terms, gate_parts, up_parts, down_parts = lax.map(per_member, (member_x, member_g))
        output_acc = output_acc + rounded(output_terms)
        input_acc = input_acc + rounded(input_terms)
        gate_list.append(jnp.sum(rounded(gate_parts), axis=0).astype(jnp.bfloat16))
        up_list.append(jnp.sum(rounded(up_parts), axis=0).astype(jnp.bfloat16))
        down_list.append(jnp.sum(rounded(down_parts), axis=0).astype(jnp.bfloat16))
    outputs = output_acc.astype(jnp.bfloat16).transpose(0, 2, 1, 3).reshape(TOKENS, D)
    input_grads = input_acc.astype(jnp.bfloat16).transpose(0, 2, 1, 3).reshape(TOKENS, D)
    return outputs, input_grads, jnp.stack(gate_list), jnp.stack(up_list), jnp.stack(down_list)
```

```python
import functools

import jax
import jax.numpy as jnp
import numpy as np
from jax import lax
from jax.experimental import pallas as pl
from jax.experimental.pallas import tpu as pltpu
from jax.sharding import PartitionSpec as P

FF = 14336
BLK = 128
GROUP = 4
FIRST_SEND = 20
HEAD = 8
VMEM_LIMIT = 52 * 1024 * 1024


class Sizes:
    def __init__(self, tokens, gate_blocks, slots, n_fsdp, n_tensor):
        self.tok, self.width = tokens.shape
        self.n_fsdp, self.n_tensor = n_fsdp, n_tensor
        self.rb = self.width // BLK
        self.cb = FF // (BLK * n_tensor)
        self.slots = slots
        self.nb = gate_blocks.shape[1]
        self.half = self.nb // 2
        self.ring = n_fsdp // 2
        self.rbt = self.rb // n_tensor
        self.per = 3 * self.half
        self.blocks = 2 * self.ring * 2 * self.per
        top = self.ring // 2
        order = [top]
        for d in range(top - 1, 0, -1):
            order += [d, self.ring - d]
        self.order = order + [0]
        self.far = min(3, self.ring - 1)
        self.send_all = 2 * self.rbt
        self.first = min(FIRST_SEND, self.send_all)
        self.rest = self.send_all - self.first
        self.room = slots + GROUP
        self.at_send = HEAD
        self.at_recv = self.at_send + n_tensor
        self.at_slots = self.at_recv + n_tensor
        self.at_cols = self.at_slots + 3 * 5 * self.room
        self.at_out = self.at_cols + self.cb + 1
        self.at_acc = self.at_out + n_tensor * self.send_all
        self.at_in = self.at_acc + n_tensor * self.send_all
        self.plan = -(-(self.at_in + n_tensor * self.send_all) // 128) * 128

    def slot_at(self, kind, field):
        return self.at_slots + (kind * 5 + field) * self.room


def ring_pairs(ring):
    return list(range(0, ring, 2)) + list(range(ring - 1, 0, -2))


def permutations(sz):
    seq = ring_pairs(sz.ring)
    fwd, back, swap = [], [], []
    for i, q in enumerate(seq):
        for c in range(2):
            fwd.append((q * 2 + c, seq[(i + 1) % sz.ring] * 2 + c))
            back.append((q * 2 + c, seq[i - 1] * 2 + c))
            swap.append((q * 2 + c, q * 2 + 1 - c))
    return fwd, back, swap


def base_table(sz):
    seq = ring_pairs(sz.ring)
    pos = {q: i for i, q in enumerate(seq)}
    table = np.zeros((sz.n_fsdp, sz.n_fsdp), np.int32)
    for f in range(sz.n_fsdp):
        for g in range(sz.n_fsdp):
            rel = (pos[g // 2] - pos[f // 2]) % sz.ring
            table[f, g] = (0 if f % 2 == g % 2 else 1) * sz.ring + sz.order.index(rel)
    return table


def plan_kernel(sz, rows, cols, counts, base, rank, plan, mark, seen, outm):
    S, CB, RB, T, RBT = sz.slots, sz.cb, sz.rb, sz.n_tensor, sz.rbt
    me = rank[0]

    def clear(ref, n):
        def step(i, _):
            ref[i] = 0
            return 0

        lax.fori_loop(0, n, step, 0)

    over = jnp.int32(0)
    for g in range(T):
        own = g == 0
        clear(mark, 3 * CB)
        clear(outm, 2 * RB)
        if own:
            clear(seen, 3 * CB)
        for k in range(3):
            def put(n, _, k=k, g=g):
                mark[k * CB + cols[(g * 3 + k) * S + n]] = 1
                return 0

            lax.fori_loop(0, counts[g * 3 + k], put, 0)
        for k in range(3):
            o = 0 if k == 2 else 1

            def slot(n, carry, k=k, g=g, o=o, own=own):
                i, m = carry
                c = cols[(g * 3 + k) * S + n]
                r = rows[(g * 3 + k) * S + n]
                act = mark[c] * mark[CB + c] * mark[2 * CB + c]
                was_out = outm[o * RB + r]
                outm[o * RB + r] = jnp.maximum(was_out, act)
                if own:
                    was = seen[k * CB + c]
                    seen[k * CB + c] = jnp.maximum(was, act)
                    f = n // sz.nb
                    a = n % sz.nb
                    place = ((base[f] * 2 + a // sz.half) * 3 + k) * sz.half + a % sz.half
                    plan[sz.slot_at(k, 0) + i] = place
                    plan[sz.slot_at(k, 1) + i] = r
                    plan[sz.slot_at(k, 2) + i] = c
                    plan[sz.slot_at(k, 3) + i] = was
                    plan[sz.slot_at(k, 4) + i] = was_out
                    if k == 0:
                        plan[sz.at_cols + m] = c
                        m = m + act * (1 - was)
                return i + act, m

            n_k, m = lax.fori_loop(0, counts[g * 3 + k], slot, (jnp.int32(0), jnp.int32(0)))
            if own:
                plan[k] = n_k
                if k == 0:
                    plan[3] = m
                for p in range(GROUP):
                    plan[sz.slot_at(k, 0) + n_k + p] = sz.blocks
                    plan[sz.slot_at(k, 1) + n_k + p] = 0
                    plan[sz.slot_at(k, 2) + n_k + p] = CB
                    plan[sz.slot_at(k, 3) + n_k + p] = 0
                    plan[sz.slot_at(k, 4) + n_k + p] = 0

        def listed(first, put, n0):
            for o in range(2):
                def step(w, n, o=o):
                    put(n, o, w)
                    return n + outm[o * RB + first + w]

                n0 = lax.fori_loop(0, RBT, step, n0)
            return n0

        if own:
            for s in range(T):
                first = lax.rem(me + s, T) * RBT

                def put(n, o, w, s=s, first=first):
                    at = s * sz.send_all + jnp.minimum(n, sz.send_all - 1)
                    plan[sz.at_out + at] = o * RBT + w
                    plan[sz.at_acc + at] = o * RB + first + w

                n = listed(first, put, jnp.int32(0))
                plan[sz.at_send + s] = n
                if s > 0:
                    over = jnp.maximum(over, n)
        else:
            def put(n, o, w, g=g):
                plan[sz.at_in + g * sz.send_all + jnp.minimum(n, sz.send_all - 1)] = o * RBT + w

            n = listed(me * RBT, put, jnp.int32(0))
            plan[sz.at_recv + g] = n
            over = jnp.maximum(over, n)
            if sz.rest > 0 and T > 2:
                for d in range(T):
                    n = listed(d * RBT, lambda *_: None, jnp.int32(0))
                    same = lax.rem(me - g + T, T) == d
                    over = jnp.maximum(over, jnp.where(same, 0, n))
    plan[4] = over


def dot(a, b, ca, cb):
    return lax.dot_general(a, b, (((ca,), (cb,)), ((), ())), preferred_element_type=jnp.float32)


def compute_kernel(sz, n_chunks, *refs):
    plan, tokens, cot = refs[:3]
    chunks = refs[3:3 + n_chunks]
    refs = refs[3 + n_chunks:]
    n_send = sz.n_tensor - 1
    out_own, in_own, same, far, near = refs[:5]
    sends = refs[5:5 + 2 * n_send]
    (x_buf, g_buf, wbuf, parts, gate_acc, up_acc, hg_acc, hid, gate_d, up_d, out_acc, stage, sems, rest_sems) = refs[5 + 2 * n_send:]
    CB, RB = sz.cb, sz.rb

    copies = [
        pltpu.make_async_copy(tokens, x_buf, sems.at[0]),
        pltpu.make_async_copy(cot, g_buf, sems.at[1]),
    ]
    for i, chunk in enumerate(chunks):
        copies.append(pltpu.make_async_copy(chunk, wbuf.at[pl.ds(i * sz.per, sz.per)], sems.at[2 + i]))
    for c in copies:
        c.start()
    parts[...] = jnp.zeros_like(parts)
    out_own[...] = jnp.zeros_like(out_own)
    in_own[...] = jnp.zeros_like(in_own)
    for c in copies:
        c.wait()

    def field(k, j, e):
        return plan[sz.slot_at(k, j) + e]

    def strip(buf, r):
        return buf[:, pl.ds(pl.multiple_of(r * BLK, BLK), BLK)]

    def steps(k, body):
        lax.fori_loop(0, (plan[k] + (GROUP - 1)) // GROUP, lambda p, _: body(p * GROUP), None)

    def forward(k, buf, acc, w_dim):
        def body(e0):
            prods = []
            for u in range(GROUP):
                prods.append(dot(strip(buf, field(k, 1, e0 + u)), wbuf[field(k, 0, e0 + u)], 1, w_dim))
            for u in range(GROUP):
                c = field(k, 2, e0 + u)
                acc[c] = prods[u] + jnp.where(field(k, 3, e0 + u) == 0, 0.0, acc[c])

        steps(k, body)

    forward(0, x_buf, gate_acc, 0)
    forward(1, x_buf, up_acc, 0)
    forward(2, g_buf, hg_acc, 1)

    def column(m, _):
        c = plan[sz.at_cols + m]
        g, u, h = gate_acc[c], up_acc[c], hg_acc[c]
        s = lax.logistic(g)
        silu = g * s
        hid[c] = (silu * u).astype(jnp.bfloat16)
        gate_d[c] = (h * u * s * (1.0 + g * (1.0 - s))).astype(jnp.bfloat16)
        up_d[c] = (h * silu).astype(jnp.bfloat16)

    lax.fori_loop(0, plan[3], column, None)

    def backward(k, buf, act, o, w_dim):
        def body(e0):
            terms, grads = [], []
            for u in range(GROUP):
                place = field(k, 0, e0 + u)
                a = act[field(k, 2, e0 + u)]
                x = strip(buf, field(k, 1, e0 + u))
                terms.append(dot(a, wbuf[place], 1, w_dim))
                grads.append(dot(a, x, 0, 0) if k == 2 else dot(x, a, 0, 0))
            for u in range(GROUP):
                parts[field(k, 0, e0 + u)] = grads[u].astype(jnp.bfloat16)
            for u in range(GROUP):
                dummy = field(k, 2, e0 + u) == CB
                at = jnp.where(dummy, 2 * RB, o * RB + field(k, 1, e0 + u))
                out_acc[at] = terms[u] + jnp.where(field(k, 4, e0 + u) == 0, 0.0, out_acc[at])

        steps(k, body)

    backward(2, g_buf, hid, 0, 0)
    backward(0, x_buf, gate_d, 1, 1)
    backward(1, x_buf, up_d, 1, 1)

    split = sz.ring * 2 * sz.per
    cut = split + sz.far * 2 * sz.per
    outs = [
        pltpu.make_async_copy(parts.at[pl.ds(0, split)], same, sems.at[0]),
        pltpu.make_async_copy(parts.at[pl.ds(split, cut - split)], far, sems.at[1]),
        pltpu.make_async_copy(parts.at[pl.ds(cut, sz.blocks - cut)], near, sems.at[2]),
    ]
    for c in outs:
        c.start()

    for s in range(1, sz.n_tensor):
        def staged(n, _, s=s):
            at = s * sz.send_all + n
            stage[(s - 1) * sz.send_all + n] = out_acc[plan[sz.at_acc + at]].astype(jnp.bfloat16)

        n = plan[sz.at_send + s]
        lax.fori_loop(0, n, staged, None)
        first = pltpu.make_async_copy(stage.at[pl.ds((s - 1) * sz.send_all, sz.first)], sends[s - 1], sems.at[2 + s])
        first.start()
        outs.append(first)

    def keep(n, _):
        at = plan[sz.at_out + n]
        value = out_acc[plan[sz.at_acc + n]].astype(jnp.bfloat16)

        @pl.when(at < sz.rbt)
        def _():
            out_own[:, pl.ds(pl.multiple_of(at * BLK, BLK), BLK)] = value

        @pl.when(at >= sz.rbt)
        def _():
            in_own[:, pl.ds(pl.multiple_of((at - sz.rbt) * BLK, BLK), BLK)] = value

    lax.fori_loop(0, plan[sz.at_send], keep, None)

    if sz.rest > 0:
        @pl.when(plan[4] > sz.first)
        def _():
            for s in range(1, sz.n_tensor):
                more = pltpu.make_async_copy(
                    stage.at[pl.ds((s - 1) * sz.send_all + sz.first, sz.rest)],
                    sends[n_send + s - 1], rest_sems.at[s - 1])
                more.start()
                more.wait()
    for c in outs:
        c.wait()


def join_kernel(sz, *refs):
    n_send = sz.n_tensor - 1
    plan, out_own, in_own = refs[:3]
    firsts = refs[3:3 + n_send]
    rests = refs[3 + n_send:-4]
    outputs, input_grads, spare, sem = refs[-4:]
    outputs[...] = out_own[...]
    input_grads[...] = in_own[...]

    def add(at, value):
        def into(ref, w):
            cols = pl.ds(pl.multiple_of(w * BLK, BLK), BLK)
            ref[:, cols] = (ref[:, cols].astype(jnp.float32) + value.astype(jnp.float32)).astype(jnp.bfloat16)

        @pl.when(at < sz.rbt)
        def _():
            into(outputs, at)

        @pl.when(at >= sz.rbt)
        def _():
            into(input_grads, at - sz.rbt)

    for s in range(1, sz.n_tensor):
        n = plan[sz.at_recv + s]

        def early(i, _, s=s):
            add(plan[sz.at_in + s * sz.send_all + i], firsts[s - 1][i])

        lax.fori_loop(0, jnp.minimum(n, sz.first), early, None)
        if sz.rest > 0:
            def late(i, _, s=s):
                copy = pltpu.make_async_copy(rests[s - 1].at[i - sz.first], spare, sem)
                copy.start()
                copy.wait()
                add(plan[sz.at_in + s * sz.send_all + i], spare[...])

            lax.fori_loop(jnp.minimum(n, sz.first), n, late, None)


def any_spec():
    return pl.BlockSpec(memory_space=pl.ANY)


def vmem_spec():
    return pl.BlockSpec(memory_space=pltpu.VMEM)


def smem_spec():
    return pl.BlockSpec(memory_space=pltpu.SMEM)


def call_plan(sz, rows, cols, counts, base, rank):
    return pl.pallas_call(
        functools.partial(plan_kernel, sz),
        out_shape=jax.ShapeDtypeStruct((sz.plan,), jnp.int32),
        in_specs=[smem_spec()] * 5,
        out_specs=smem_spec(),
        scratch_shapes=[
            pltpu.SMEM((3 * sz.cb,), jnp.int32),
            pltpu.SMEM((3 * sz.cb,), jnp.int32),
            pltpu.SMEM((2 * sz.rb,), jnp.int32),
        ],
        cost_estimate=pl.CostEstimate(flops=10_000_000, bytes_accessed=20_000_000, transcendentals=0),
        name="plan",
    )(rows, cols, counts, base, rank)


def call_compute(sz, plan, tokens, cot, chunks):
    half_width = sz.width // sz.n_tensor
    n_send = sz.n_tensor - 1
    bf, f32 = jnp.bfloat16, jnp.float32

    def blocks(n, dtype=bf):
        return jax.ShapeDtypeStruct((n, BLK, BLK), dtype)

    out_shape = [
        jax.ShapeDtypeStruct((sz.tok, half_width), bf),
        jax.ShapeDtypeStruct((sz.tok, half_width), bf),
        blocks(sz.ring * 2 * sz.per),
        blocks(sz.far * 2 * sz.per),
        blocks((sz.ring - sz.far) * 2 * sz.per),
    ]
    out_specs = [vmem_spec(), vmem_spec(), any_spec(), any_spec(), any_spec()]
    out_shape += [blocks(sz.first)] * n_send
    out_specs += [any_spec()] * n_send
    out_shape += [blocks(max(sz.rest, 1))] * n_send
    out_specs += [any_spec()] * n_send
    return pl.pallas_call(
        functools.partial(compute_kernel, sz, len(chunks)),
        out_shape=out_shape,
        in_specs=[smem_spec()] + [any_spec()] * (2 + len(chunks)),
        out_specs=out_specs,
        scratch_shapes=[
            pltpu.VMEM((sz.tok, sz.width), bf),
            pltpu.VMEM((sz.tok, sz.width), bf),
            pltpu.VMEM((sz.blocks + 1, BLK, BLK), bf),
            pltpu.VMEM((sz.blocks + 1, BLK, BLK), bf),
            pltpu.VMEM((sz.cb + 1, sz.tok, BLK), f32),
            pltpu.VMEM((sz.cb + 1, sz.tok, BLK), f32),
            pltpu.VMEM((sz.cb + 1, sz.tok, BLK), f32),
            pltpu.VMEM((sz.cb + 1, sz.tok, BLK), bf),
            pltpu.VMEM((sz.cb + 1, sz.tok, BLK), bf),
            pltpu.VMEM((sz.cb + 1, sz.tok, BLK), bf),
            pltpu.VMEM((2 * sz.rb + 1, sz.tok, BLK), f32),
            pltpu.VMEM((n_send * sz.send_all, sz.tok, BLK), bf),
            pltpu.SemaphoreType.DMA((2 + max(len(chunks), sz.n_tensor),)),
            pltpu.SemaphoreType.DMA((max(n_send, 1),)),
        ],
        compiler_params=pltpu.CompilerParams(vmem_limit_bytes=VMEM_LIMIT),
        cost_estimate=pl.CostEstimate(flops=1_000_000_000, bytes_accessed=20_000_000, transcendentals=0),
        name="compute",
    )(plan, tokens, cot, *chunks)


def call_join(sz, plan, out_own, in_own, firsts, rests):
    whole = jax.ShapeDtypeStruct(out_own.shape, out_own.dtype)
    return pl.pallas_call(
        functools.partial(join_kernel, sz),
        out_shape=[whole, whole],
        in_specs=[smem_spec(), vmem_spec(), vmem_spec()] + [vmem_spec()] * len(firsts) + [any_spec()] * len(rests),
        out_specs=[vmem_spec(), vmem_spec()],
        scratch_shapes=[pltpu.VMEM((sz.tok, BLK), jnp.bfloat16), pltpu.SemaphoreType.DMA],
        compiler_params=pltpu.CompilerParams(vmem_limit_bytes=VMEM_LIMIT),
        cost_estimate=pl.CostEstimate(flops=1_000_000, bytes_accessed=6_000_000, transcendentals=0),
        name="join",
    )(plan, out_own, in_own, *firsts, *rests)


def gather_chunks(sz, halves):
    fwd, back, swap = permutations(sz)

    def send(arrays, perm):
        return [lax.ppermute(a, "fsdp", perm) for a in arrays]

    top = sz.ring // 2
    same = {0: halves}
    right = left = halves
    for d in range(1, top):
        right, left = send(right, fwd), send(left, back)
        same[sz.ring - d], same[d] = right, left
    same[top] = send(right[:1], fwd) + send(left[1:], back)
    other = {d: send(same[d], swap) for d in same}
    return [part for side in (same, other) for d in sz.order for part in side[d]]


def reduce_parts(sz, same, far, near):
    fwd, back, swap = permutations(sz)
    far, near = lax.ppermute(far, "fsdp", swap), lax.ppermute(near, "fsdp", swap)
    top = sz.ring // 2

    def term(d, h, *more):
        j = sz.order.index(d)
        at = (j * 2 + h) * sz.per
        mine = same[at:at + sz.per]
        pair = far[at:at + sz.per] if j < sz.far else near[at - sz.far * 2 * sz.per:][:sz.per]
        total = mine.astype(jnp.float32) + pair.astype(jnp.float32)
        for m in more:
            if m is not None:
                total = total + m.astype(jnp.float32)
        return total.astype(jnp.bfloat16)

    right = [lax.ppermute(term(top, 0), "fsdp", fwd), None]
    left = [None, lax.ppermute(term(top, 1), "fsdp", back)]
    for d in range(top - 1, 0, -1):
        right = [lax.ppermute(term(d, h, right[h]), "fsdp", fwd) for h in range(2)]
        left = [lax.ppermute(term(sz.ring - d, h, left[h]), "fsdp", back) for h in range(2)]
    final = jnp.stack([term(0, h, right[h], left[h]) for h in range(2)])
    final = final.reshape(2, 3, sz.half, BLK, BLK).transpose(1, 0, 2, 3, 4)
    return final.reshape(3, 1, sz.nb, BLK, BLK)


def shards(
    tokens,
    cotangent,
    gate_blocks,
    up_blocks,
    down_blocks,
    gate_where,
    up_where,
    down_where,
    block_counts,
):
    n_fsdp, n_tensor = lax.axis_size("fsdp"), lax.axis_size("tensor")
    sz = Sizes(tokens, gate_blocks, gate_where.shape[1], n_fsdp, n_tensor)
    S = sz.slots

    halves = [
        jnp.concatenate([b[0, h * sz.half:(h + 1) * sz.half] for b in (gate_blocks, up_blocks, down_blocks)])
        for h in range(2)
    ]
    chunks = gather_chunks(sz, halves)

    table = jnp.concatenate([gate_where[0], up_where[0], down_where[0], block_counts[:, 0]])
    tables = [table]
    for s in range(1, n_tensor):
        tables.append(lax.ppermute(table, "tensor", [(i, (i + s) % n_tensor) for i in range(n_tensor)]))
    tables = jnp.stack(tables)
    where = tables[:, :3 * S].reshape(n_tensor, 3, S)
    is_down = (jnp.arange(3) == 2)[None, :, None]
    rows = jnp.where(is_down, where % sz.rb, where // sz.cb).reshape(-1)
    cols = jnp.where(is_down, where // sz.rb, where % sz.cb).reshape(-1)
    counts = tables[:, 3 * S:].reshape(-1)
    base = lax.dynamic_index_in_dim(jnp.asarray(base_table(sz)), lax.axis_index("fsdp"), 0, keepdims=False)
    rank = lax.axis_index("tensor").astype(jnp.int32).reshape(1)
    plan = call_plan(sz, rows, cols, counts, base, rank)

    outs = call_compute(sz, plan, tokens, cotangent, chunks)
    out_own, in_own, same, far, near = outs[:5]
    firsts, rests = outs[5:5 + n_tensor - 1], outs[5 + n_tensor - 1:]

    def exchange(arrays):
        return tuple(
            lax.ppermute(a, "tensor", [(i, (i + s + 1) % n_tensor) for i in range(n_tensor)])
            for s, a in enumerate(arrays)
        )

    firsts = exchange(firsts)
    if sz.rest > 0:
        rests = lax.cond(plan[4] > sz.first, exchange, lambda arrays: tuple(arrays), tuple(rests))
    else:
        rests = ()
    grads = reduce_parts(sz, same, far, near)
    outputs, input_grads = call_join(sz, plan, out_own, in_own, firsts, rests)
    return outputs, input_grads, grads[0], grads[1], grads[2]


def solution(mesh):
    placed = (
        P("fsdp", None),
        P("fsdp", None),
        P("tensor", "fsdp", None, None),
        P("tensor", "fsdp", None, None),
        P("tensor", "fsdp", None, None),
        P("tensor", None),
        P("tensor", None),
        P("tensor", None),
        P(None, "tensor"),
    )
    return jax.shard_map(
        shards,
        mesh=mesh,
        in_specs=placed,
        out_specs=(
            P("fsdp", "tensor"),
            P("fsdp", "tensor"),
            P("tensor", "fsdp", None, None),
            P("tensor", "fsdp", None, None),
            P("tensor", "fsdp", None, None),
        ),
        check_vma=False,
    )
```

```python
import functools

import jax
import jax.numpy as jnp
from jax import lax
from jax.experimental import pallas as pl
from jax.experimental.pallas import tpu as pltpu
from jax.sharding import PartitionSpec as P

FF = 14336
BLK = 128
GROUP = 4
FIRST_SEND = 20
FIRST_GRADS = 4
COL, ROW, LIVE, OWNER, BASE, SHIFT, LOCAL, MINE, WAT = range(9)
TABLE_ROWS = 16
PLACE, PART, STRIP, CIDX, CWAS, OIDX, OWAS = range(7)
FIELDS = 7
COLS_ROW = 3 * FIELDS
HEAD_ROW = COLS_ROW + 1
MINE_ROW = COLS_ROW + 2
LISTS_ROW = COLS_ROW + 3
HEAD_COLS, HEAD_OVER, HEAD_LISTS = 3, 4, 8


class Sizes:
    def __init__(self, tokens, gate_blocks, slots, n_fsdp, n_tensor):
        self.tok, self.width = tokens.shape
        self.n_fsdp, self.n_tensor = n_fsdp, n_tensor
        self.rb = self.width // BLK
        self.cb = FF // (BLK * n_tensor)
        self.slots = slots
        self.all = 3 * slots
        self.lanes = -(-(self.all + GROUP) // 128) * 128
        self.nb = gate_blocks.shape[1]
        self.chunk = 3 * self.nb
        self.ring = n_fsdp // 2
        self.top = self.ring // 2
        self.rbt = self.rb // n_tensor
        self.order = [self.top]
        for d in range(1, self.top):
            self.order += [self.top + d, self.top - d]
        self.order.append(0)
        self.far = min(4, self.ring - 1)
        sparse = slots < self.cb
        self.keep = min(FIRST_GRADS, self.chunk) if sparse else self.chunk
        self.more = self.chunk - self.keep
        self.send_all = 2 * self.rbt
        self.first = min(FIRST_SEND, self.send_all) if sparse else self.send_all
        self.rest = self.send_all - self.first
        self.blocks = 2 * self.ring * self.chunk
        self.main = 2 * self.ring * self.keep
        self.plan_rows = -(-(LISTS_ROW + 2 * n_tensor) // 8) * 8
        self.recv_rows = -(-n_tensor // 8) * 8
        self.room = slots + GROUP


def permutations(sz):
    seq = list(range(0, sz.ring, 2)) + list(range(sz.ring - 1, 0, -2))
    ahead, behind, swap = [], [], []
    for i, q in enumerate(seq):
        up, down = seq[(i + 1) % sz.ring], seq[i - 1]
        ahead += [(q * 2, up * 2), (q * 2 + 1, down * 2 + 1)]
        behind += [(q * 2, down * 2), (q * 2 + 1, up * 2 + 1)]
        swap += [(q * 2, q * 2 + 1), (q * 2 + 1, q * 2)]
    return ahead, behind, swap


def group_table(sz, where, counts, f, rank):
    S, R, top = sz.slots, sz.ring, sz.top
    lane = lax.iota(jnp.int32, sz.lanes)
    kind = (lane >= S).astype(jnp.int32) + (lane >= 2 * S).astype(jnp.int32)
    n = lane - kind * S
    pad = sz.lanes - sz.all
    w = jnp.pad(where, (0, pad))
    limit = jnp.pad(jnp.repeat(counts, S, total_repeat_length=sz.all), (0, pad))
    live = (n < limit) & (lane < sz.all)
    down = kind == 2
    row = jnp.where(down, w % sz.rb, w // sz.cb)
    col = jnp.where(down, w // sz.rb, w % sz.cb)
    owner = n // sz.nb

    def position(chip):
        return jnp.where(chip % 2 == 0, chip // 2, R - 1 - chip // 2)

    away = position(owner // 2) - position(f // 2)
    away = jnp.where(owner % 2 == 0, away, -away)
    rel = (away + R) % R
    j = jnp.where(rel > top, 2 * (rel - top) - 1, 2 * (top - rel))
    j = jnp.where(rel == 0, R - 1, j)
    base = jnp.where(owner % 2 == f % 2, 0, R) + j
    shift = (row // sz.rbt - rank + sz.n_tensor) % sz.n_tensor
    local = jnp.where(down, 0, sz.rbt) + row % sz.rbt
    mine = (lane // sz.nb) * S + f * sz.nb + lane % sz.nb
    at = kind * sz.nb + n % sz.nb
    rows = [col, row, live.astype(jnp.int32), owner, base, shift, local, mine, at]
    table = jnp.stack([r.astype(jnp.float32) for r in rows])
    return jnp.pad(table, ((0, TABLE_ROWS - len(rows)), (0, 0)))


class Marks:
    def __init__(self, sz, table):
        N, L, S = sz.all, sz.lanes, sz.slots
        f32 = jnp.float32
        self.sub = lax.broadcasted_iota(jnp.int32, (N, L), 0)
        self.lane = lax.broadcasted_iota(jnp.int32, (N, L), 1)
        same = self.sub == self.lane
        self.row = lambda i: table[i:i + 1, :]
        self.col = lambda i: jnp.sum(jnp.where(same, table[i:i + 1, :], 0.0), axis=1, keepdims=True)
        sub_c = self.sub[:, :1]
        lane_r = self.lane[:1, :]

        def kind(x):
            return (x >= S).astype(f32) + (x >= 2 * S).astype(f32)

        self.kind_c, self.kind_r = kind(sub_c), kind(lane_r)
        live_c, live_r = self.col(LIVE), self.row(LIVE)
        self.same_col = (self.col(COL) == self.row(COL)).astype(f32)
        act_c, act_r = live_c, live_r
        for k in range(3):
            lanes = self.same_col * (live_r * (self.kind_r == k).astype(f32))
            act_c = act_c * jnp.max(lanes, axis=1, keepdims=True)
            subs = self.same_col * (live_c * (self.kind_c == k).astype(f32))
            act_r = act_r * jnp.max(subs, axis=0, keepdims=True)
        self.act_c, self.act_r = act_c, act_r
        out_c = jnp.where(self.kind_c == 2, 0.0, f32(sz.rb)) + self.col(ROW)
        out_r = jnp.where(self.kind_r == 2, 0.0, f32(sz.rb)) + self.row(ROW)
        self.same_out = (out_c == out_r).astype(f32)
        self.before = (self.lane < self.sub).astype(f32)
        self.after = (self.sub < self.lane).astype(f32)
        self.owas_c = jnp.max(self.same_out * self.before * act_r, axis=1, keepdims=True)
        self.owas_r = jnp.max(self.same_out * self.after * act_c, axis=0, keepdims=True)
        self.lead_c = act_c * (1.0 - self.owas_c)
        self.lead_r = act_r * (1.0 - self.owas_r)

    def ranks(self, chosen_r):
        return jnp.sum(self.before * chosen_r, axis=1, keepdims=True)

    def listed(self, chosen_c, rank_c, value_c, lo=0, hi=None):
        at = rank_c[lo:hi] == self.lane[lo:hi].astype(jnp.float32)
        return jnp.sum(jnp.where(at, chosen_c[lo:hi] * value_c[lo:hi], 0.0), axis=0, keepdims=True)

    def most_owned(self):
        owned = (self.col(OWNER) == self.row(OWNER)).astype(jnp.float32)
        return jnp.max(jnp.sum(owned * self.act_r, axis=1, keepdims=True), axis=0, keepdims=True)


def total(x):
    return jnp.sum(x, axis=0, keepdims=True)


def head_row(sz, entries):
    lane = lax.broadcasted_iota(jnp.int32, (1, sz.lanes), 1)
    row = jnp.zeros((1, sz.lanes), jnp.float32)
    for i, value in entries:
        row = jnp.where(lane == i, value, row)
    return row


def plan_kernel(sz, table_ref, plan):
    S, N = sz.slots, sz.all
    m = Marks(sz, table_ref)
    f32 = jnp.float32
    lane_r = m.lane[:1, :].astype(f32)
    same_kind = (m.kind_c == m.kind_r).astype(f32)
    rank_c = jnp.sum(m.before * same_kind * m.act_r, axis=1, keepdims=True)
    cwas_c = jnp.max(m.before * same_kind * m.same_col * m.act_r, axis=1, keepdims=True)
    cwas_r = jnp.max(m.after * same_kind * m.same_col * m.act_c, axis=0, keepdims=True)
    big = f32(4 * N)
    lanes_f = m.lane.astype(f32)
    gates_r = m.act_r * (m.kind_r == 0).astype(f32)
    cidx_c = jnp.min(jnp.where(m.same_col * gates_r > 0, lanes_f, big), axis=1, keepdims=True)
    oidx_c = jnp.min(jnp.where(m.same_out * m.act_r > 0, lanes_f, big), axis=1, keepdims=True)
    owned = (m.col(OWNER) == m.row(OWNER)).astype(f32)
    pos_c = jnp.sum(m.before * owned * m.act_r, axis=1, keepdims=True)
    base_c = m.col(BASE)
    place_c = base_c * sz.chunk + m.col(WAT)
    part_c = jnp.where(
        pos_c < sz.keep, base_c * sz.keep + pos_c, sz.main + base_c * sz.more + pos_c - sz.keep)
    fields = [
        (place_c, sz.blocks), (part_c, sz.blocks), (m.col(ROW), 0), (cidx_c, S), (cwas_c, 0), (oidx_c, N), (m.owas_c, 0)]
    rows = []
    head = []
    for k in range(3):
        lo, hi = k * S, (k + 1) * S
        n_k = total(m.act_c[lo:hi])
        head.append((k, n_k))
        for value, spare in fields:
            row = m.listed(m.act_c, rank_c, value, lo, hi)
            rows.append(jnp.where(lane_r < n_k, row, f32(spare)))
    sub_c = m.sub[:, :1].astype(f32)
    leader_c = m.act_c * (1.0 - cwas_c) * (m.kind_c == 0).astype(f32)
    leader_r = m.act_r * (1.0 - cwas_r) * (m.kind_r == 0).astype(f32)
    rows.append(m.listed(leader_c, m.ranks(leader_r), sub_c, 0, S))
    head.append((HEAD_COLS, total(leader_c)))
    over = (m.most_owned() > sz.keep).astype(f32)
    lists = []
    shift_c, shift_r = m.col(SHIFT), m.row(SHIFT)
    for s in range(sz.n_tensor):
        chosen_c = m.lead_c * (shift_c == s).astype(f32)
        chosen_r = m.lead_r * (shift_r == s).astype(f32)
        rank = m.ranks(chosen_r)
        lists.append(m.listed(chosen_c, rank, sub_c))
        lists.append(m.listed(chosen_c, rank, m.col(LOCAL)))
        n = total(chosen_c)
        head.append((HEAD_LISTS + s, n))
        over = jnp.maximum(over, (n > sz.first).astype(f32))
    head.append((HEAD_OVER, over))
    rows.append(head_row(sz, head))
    mine = m.sub.astype(f32) == m.row(MINE)
    rows.append(jnp.sum(jnp.where(mine, m.act_c * (pos_c + 1.0), 0.0), axis=0, keepdims=True))
    rows += lists
    for i, row in enumerate(rows):
        plan[i:i + 1, :] = row.astype(jnp.int32)


def recv_kernel(sz, *refs):
    tables, recv = refs[:-1], refs[-1]
    f32 = jnp.float32
    head = []
    over = jnp.zeros((1, 1), f32)
    for s, table in enumerate(tables, 1):
        m = Marks(sz, table)
        shift_c, shift_r = m.col(SHIFT), m.row(SHIFT)
        chosen_c = m.lead_c * (shift_c == 0).astype(f32)
        chosen_r = m.lead_r * (shift_r == 0).astype(f32)
        recv[s:s + 1, :] = m.listed(chosen_c, m.ranks(chosen_r), m.col(LOCAL)).astype(jnp.int32)
        head.append((HEAD_LISTS + s, total(chosen_c)))
        over = jnp.maximum(over, (m.most_owned() > sz.keep).astype(f32))
        for d in range(sz.n_tensor):
            n = total(m.lead_c * (shift_c == d).astype(f32))
            over = jnp.maximum(over, (n > sz.first).astype(f32))
    head.append((HEAD_OVER, over))
    recv[0:1, :] = head_row(sz, head).astype(jnp.int32)


def dot(a, b, ca, cb):
    return lax.dot_general(a, b, (((ca,), (cb,)), ((), ())), preferred_element_type=jnp.float32)


def compute_kernel(sz, *refs):
    plan, tokens, cot = refs[:3]
    n_chunks = 2 * sz.ring
    chunks = refs[3:3 + n_chunks]
    refs = refs[3 + n_chunks:]
    T = sz.n_tensor
    same, far, near, extra = refs[:4]
    firsts, rests = refs[4:4 + T], refs[4 + T:4 + 2 * T]
    (xs, wbuf, parts, gate_acc, up_acc, hg_acc, hid, gate_d, up_d, out_acc, stage, strip_sems, sems, rest_sems) = refs[4 + 2 * T:]

    def field(k, j, e):
        return plan[k * FIELDS + j, e]

    def steps(k):
        return (plan[HEAD_ROW, k] + (GROUP - 1)) // GROUP

    def strip_copy(k, e):
        src = cot if k == 2 else tokens
        cols = pl.ds(pl.multiple_of(field(k, STRIP, e) * BLK, BLK), BLK)
        return pltpu.make_async_copy(src.at[:, cols], xs.at[k * sz.room + e], strip_sems.at[k * sz.room + e])

    for k in range(3):
        lax.fori_loop(0, steps(k) * GROUP, lambda e, _, k=k: strip_copy(k, e).start(), None)
    loads = [
        pltpu.make_async_copy(chunk, wbuf.at[pl.ds(i * sz.chunk, sz.chunk)], sems.at[i])
        for i, chunk in enumerate(chunks)
    ]
    for c in loads:
        c.start()
    for k in range(3):
        lax.fori_loop(0, steps(k) * GROUP, lambda e, _, k=k: strip_copy(k, e).wait(), None)
    for c in loads:
        c.wait()

    def walk(k, body):
        lax.fori_loop(0, steps(k), lambda p, _: body(p * GROUP), None)

    def forward(k, acc, w_dim):
        def body(e0):
            prods = [
                dot(xs[k * sz.room + e0 + u], wbuf[field(k, PLACE, e0 + u)], 1, w_dim) for u in range(GROUP)]
            for u in range(GROUP):
                c = field(k, CIDX, e0 + u)
                acc[c] = prods[u] + jnp.where(field(k, CWAS, e0 + u) == 0, 0.0, acc[c])

        walk(k, body)

    forward(0, gate_acc, 0)
    forward(1, up_acc, 0)
    forward(2, hg_acc, 1)

    def column(i, _):
        c = plan[COLS_ROW, i]
        g, u, h = gate_acc[c], up_acc[c], hg_acc[c]
        s = lax.logistic(g)
        silu = g * s
        hid[c] = (silu * u).astype(jnp.bfloat16)
        gate_d[c] = (h * u * s * (1.0 + g * (1.0 - s))).astype(jnp.bfloat16)
        up_d[c] = (h * silu).astype(jnp.bfloat16)

    lax.fori_loop(0, plan[HEAD_ROW, HEAD_COLS], column, None)

    def backward(k, act, w_dim):
        def body(e0):
            terms, grads = [], []
            for u in range(GROUP):
                a = act[field(k, CIDX, e0 + u)]
                x = xs[k * sz.room + e0 + u]
                terms.append(dot(a, wbuf[field(k, PLACE, e0 + u)], 1, w_dim))
                grads.append(dot(a, x, 0, 0) if k == 2 else dot(x, a, 0, 0))
            for u in range(GROUP):
                parts[field(k, PART, e0 + u)] = grads[u].astype(jnp.bfloat16)
            for u in range(GROUP):
                at = field(k, OIDX, e0 + u)
                out_acc[at] = terms[u] + jnp.where(field(k, OWAS, e0 + u) == 0, 0.0, out_acc[at])

        walk(k, body)

    backward(2, hid, 0)
    backward(0, gate_d, 1)
    backward(1, up_d, 1)

    split = sz.ring * sz.keep
    cut = split + sz.far * sz.keep
    outs = [
        pltpu.make_async_copy(parts.at[pl.ds(split, cut - split)], far, sems.at[0]),
        pltpu.make_async_copy(parts.at[pl.ds(0, split)], same, sems.at[1]),
        pltpu.make_async_copy(parts.at[pl.ds(cut, sz.main - cut)], near, sems.at[2]),
    ]
    for c in outs:
        c.start()

    for s in range(T):
        def staged(i, _, s=s):
            stage[s * sz.send_all + i] = out_acc[plan[LISTS_ROW + 2 * s, i]].astype(jnp.bfloat16)

        lax.fori_loop(0, plan[HEAD_ROW, HEAD_LISTS + s], staged, None)
        first = pltpu.make_async_copy(stage.at[pl.ds(s * sz.send_all, sz.first)], firsts[s], sems.at[3 + s])
        first.start()
        outs.append(first)

    if sz.rest + sz.more > 0:
        @pl.when(plan[HEAD_ROW, HEAD_OVER] > 0)
        def _():
            copies = []
            if sz.rest > 0:
                copies += [
                    pltpu.make_async_copy(
                        stage.at[pl.ds(s * sz.send_all + sz.first, sz.rest)], rests[s], rest_sems.at[s])
                    for s in range(T)
                ]
            if sz.more > 0:
                copies.append(pltpu.make_async_copy(
                    parts.at[pl.ds(sz.main, sz.blocks - sz.main)], extra, rest_sems.at[T]))
            for c in copies:
                c.start()
            for c in copies:
                c.wait()
    for c in outs:
        c.wait()


def join_kernel(sz, *refs):
    T = sz.n_tensor
    plan, recv = refs[:2]
    firsts, rests = refs[2:2 + T], refs[2 + T:2 + 2 * T]
    outputs, input_grads, spare, sem = refs[-4:]
    outputs[...] = jnp.zeros_like(outputs)
    input_grads[...] = jnp.zeros_like(input_grads)

    def add(at, value):
        def into(ref, w):
            cols = pl.ds(pl.multiple_of(w * BLK, BLK), BLK)
            ref[:, cols] = (ref[:, cols].astype(jnp.float32) + value.astype(jnp.float32)).astype(jnp.bfloat16)

        @pl.when(at < sz.rbt)
        def _():
            into(outputs, at)

        @pl.when(at >= sz.rbt)
        def _():
            into(input_grads, at - sz.rbt)

    for s in range(T):
        n = (recv[0, HEAD_LISTS + s] if s else plan[HEAD_ROW, HEAD_LISTS])

        def where_to(i, s=s):
            return recv[s, i] if s else plan[LISTS_ROW + 1, i]

        def early(i, _, s=s):
            add(where_to(i), firsts[s][i])

        lax.fori_loop(0, jnp.minimum(n, sz.first), early, None)
        if sz.rest > 0:
            def late(i, _, s=s):
                copy = pltpu.make_async_copy(rests[s].at[i - sz.first], spare, sem)
                copy.start()
                copy.wait()
                add(where_to(i), spare[...])

            lax.fori_loop(jnp.minimum(n, sz.first), n, late, None)


def spec(space):
    return pl.BlockSpec(memory_space=space)


ANY, VMEM, SMEM = pl.ANY, pltpu.VMEM, pltpu.SMEM


def cost(flops, moved):
    return pl.CostEstimate(flops=flops, bytes_accessed=moved, transcendentals=0)


def call_plan(sz, table):
    return pl.pallas_call(
        functools.partial(plan_kernel, sz),
        out_shape=jax.ShapeDtypeStruct((sz.plan_rows, sz.lanes), jnp.int32),
        in_specs=[spec(VMEM)],
        out_specs=spec(VMEM),
        cost_estimate=cost(1_000_000, 4_000_000),
        name="plan",
    )(table)


def call_recv(sz, tables):
    return pl.pallas_call(
        functools.partial(recv_kernel, sz),
        out_shape=jax.ShapeDtypeStruct((sz.recv_rows, sz.lanes), jnp.int32),
        in_specs=[spec(VMEM)] * len(tables),
        out_specs=spec(VMEM),
        cost_estimate=cost(1_000_000, 4_000_000),
        name="recv",
    )(*tables)


def call_compute(sz, plan, tokens, cot, chunks):
    T = sz.n_tensor
    bf, f32 = jnp.bfloat16, jnp.float32

    def blocks(n):
        return jax.ShapeDtypeStruct((max(n, 1), BLK, BLK), bf)

    out_shape = [
        blocks(sz.ring * sz.keep),
        blocks(sz.far * sz.keep),
        blocks((sz.ring - sz.far) * sz.keep),
        blocks(sz.blocks - sz.main),
    ]
    out_shape += [blocks(sz.first)] * T + [blocks(sz.rest)] * T
    scratch = [
        ((3 * sz.room, sz.tok, BLK), bf),
        ((sz.blocks + 1, BLK, BLK), bf),
        ((sz.blocks + 1, BLK, BLK), bf),
        ((sz.slots + 1, sz.tok, BLK), f32),
        ((sz.slots + 1, sz.tok, BLK), f32),
        ((sz.slots + 1, sz.tok, BLK), f32),
        ((sz.slots + 1, sz.tok, BLK), bf),
        ((sz.slots + 1, sz.tok, BLK), bf),
        ((sz.slots + 1, sz.tok, BLK), bf),
        ((sz.all + 1, sz.tok, BLK), f32),
        ((T * sz.send_all, sz.tok, BLK), bf),
    ]
    held = sum(s[0] * s[1] * s[2] * jnp.dtype(t).itemsize for s, t in scratch)
    return pl.pallas_call(
        functools.partial(compute_kernel, sz),
        out_shape=out_shape,
        in_specs=[spec(SMEM)] + [spec(ANY)] * (2 + len(chunks)),
        out_specs=[spec(ANY)] * len(out_shape),
        scratch_shapes=[pltpu.VMEM(s, t) for s, t in scratch] + [
            pltpu.SemaphoreType.DMA((3 * sz.room,)),
            pltpu.SemaphoreType.DMA((max(len(chunks), 3 + T),)),
            pltpu.SemaphoreType.DMA((T + 1,)),
        ],
        compiler_params=pltpu.CompilerParams(vmem_limit_bytes=held + 2 * 1024 * 1024),
        cost_estimate=cost(1_000_000_000, 20_000_000),
        name="compute",
    )(plan, tokens, cot, *chunks)


def call_join(sz, plan, recv, firsts, rests):
    half = jax.ShapeDtypeStruct((sz.tok, sz.width // sz.n_tensor), jnp.bfloat16)
    return pl.pallas_call(
        functools.partial(join_kernel, sz),
        out_shape=[half, half],
        in_specs=[spec(SMEM)] * 2 + [spec(VMEM)] * len(firsts) + [spec(ANY)] * len(rests),
        out_specs=[spec(VMEM), spec(VMEM)],
        scratch_shapes=[pltpu.VMEM((sz.tok, BLK), jnp.bfloat16), pltpu.SemaphoreType.DMA],
        compiler_params=pltpu.CompilerParams(vmem_limit_bytes=16 * 1024 * 1024),
        cost_estimate=cost(1_000_000, 6_000_000),
        name="join",
    )(plan, recv, *firsts, *rests)


def gather_chunks(sz, chunk, plan_of):
    ahead, behind, swap = permutations(sz)
    same = {0: chunk}
    a = b = chunk
    for s in range(1, sz.top + 1):
        if s == 2:
            (a, b), plan = lax.optimization_barrier(((a, b), plan_of()))
        a = lax.ppermute(a, "fsdp", ahead)
        same[sz.ring - s] = a
        if s < sz.top:
            b = lax.ppermute(b, "fsdp", behind)
            same[s] = b
    other = {d: lax.ppermute(same[d], "fsdp", swap) for d in same}
    return [side[d] for side in (same, other) for d in sz.order], plan


def reduce_parts(sz, per, same, pair):
    ahead, behind, _ = permutations(sz)

    def term(d, *more):
        j = sz.order.index(d)
        out = same[j * per:(j + 1) * per].astype(jnp.float32) + pair(j).astype(jnp.float32)
        for m in more:
            out = out + m.astype(jnp.float32)
        return out.astype(jnp.bfloat16)

    a, b = term(sz.top), term(sz.top + 1) if sz.top > 1 else None
    for s in range(1, sz.top + 1):
        if b is not None and s < sz.top:
            a, b = lax.optimization_barrier((a, b))
        a = lax.ppermute(a, "fsdp", ahead)
        if s < sz.top:
            b = lax.ppermute(b, "fsdp", behind)
            a = term(sz.top - s, a)
            if s + 1 < sz.top:
                b = term(sz.top + 1 + s, b)
    return term(0, a, b) if b is not None else term(0, a)


def shards(
    tokens,
    cotangent,
    gate_blocks,
    up_blocks,
    down_blocks,
    gate_where,
    up_where,
    down_where,
    block_counts,
):
    n_fsdp, T = lax.axis_size("fsdp"), lax.axis_size("tensor")
    sz = Sizes(tokens, gate_blocks, gate_where.shape[1], n_fsdp, T)
    f, rank = lax.axis_index("fsdp"), lax.axis_index("tensor")
    _, _, swap = permutations(sz)

    chunk = jnp.concatenate([gate_blocks[0], up_blocks[0], down_blocks[0]])
    where = jnp.concatenate([gate_where[0], up_where[0], down_where[0], block_counts[:, 0]])

    def table_of(raw):
        return group_table(sz, raw[:sz.all], raw[sz.all:], f, rank)

    chunks, plan = gather_chunks(sz, chunk, lambda: call_plan(sz, table_of(where)))
    theirs = [
        lax.ppermute(where, "tensor", [(i, (i + s) % T) for i in range(T)]) for s in range(1, T)]
    recv = call_recv(sz, [table_of(raw) for raw in theirs])

    outs = call_compute(sz, plan, tokens, cotangent, chunks)
    same, far, near, extra = outs[:4]
    firsts, rests = outs[4:4 + T], outs[4 + T:]

    def exchange(arrays):
        return [arrays[0]] + [
            lax.ppermute(arrays[s], "tensor", [(i, (i + s) % T) for i in range(T)]) for s in range(1, T)]

    far, near = lax.ppermute(far, "fsdp", swap), lax.ppermute(near, "fsdp", swap)
    firsts = exchange(firsts)

    def pair(j):
        at = j * sz.keep
        return far[at:at + sz.keep] if j < sz.far else near[at - sz.far * sz.keep:][:sz.keep]

    grads = reduce_parts(sz, sz.keep, same, pair)

    if sz.rest + sz.more > 0:
        def spill(rests, extra):
            moved = exchange(rests)
            if sz.more == 0:
                return moved, extra
            n = sz.ring * sz.more
            other = lax.ppermute(extra[n:], "fsdp", swap)
            late = reduce_parts(sz, sz.more, extra[:n], lambda j: other[j * sz.more:(j + 1) * sz.more])
            return moved, late

        def none(rests, extra):
            return list(rests), extra[:max(sz.more, 1)]

        over = plan[HEAD_ROW, HEAD_OVER] + recv[0, HEAD_OVER]
        rests, late = lax.cond(over > 0, spill, none, list(rests), extra)
        if sz.more > 0:
            grads = jnp.concatenate([grads, late])
    outputs, input_grads = call_join(sz, plan, recv, firsts, rests)

    def owned(i):
        at = plan[MINE_ROW, i]
        out = jnp.zeros((BLK, BLK), jnp.bfloat16)
        for p in range(sz.chunk):
            out = jnp.where(at == p + 1, grads[p], out)
        return out

    mine = [
        jnp.stack([owned(k * sz.nb + a) for a in range(sz.nb)])[None] for k in range(3)]
    return outputs, input_grads, *mine


def solution(mesh):
    placed = (
        P("fsdp", None),
        P("fsdp", None),
        P("tensor", "fsdp", None, None),
        P("tensor", "fsdp", None, None),
        P("tensor", "fsdp", None, None),
        P("tensor", None),
        P("tensor", None),
        P("tensor", None),
        P(None, "tensor"),
    )
    return jax.shard_map(
        shards,
        mesh=mesh,
        in_specs=placed,
        out_specs=(
            P("fsdp", "tensor"),
            P("fsdp", "tensor"),
            P("tensor", "fsdp", None, None),
            P("tensor", "fsdp", None, None),
            P("tensor", "fsdp", None, None),
        ),
        check_vma=False,
    )
```

```python
import functools

import jax
import jax.numpy as jnp
from jax import lax
from jax.experimental import pallas as pl
from jax.experimental.pallas import tpu as pltpu
from jax.sharding import PartitionSpec as P

FF = 14336
BLK = 128
GROUP = 4
FIRST_SEND = 20
FIRST_GRADS = 4
SMALL = 4 * 1024 * 1024
PLACE, PART, STRIP, CIDX, CWAS, OIDX, OWAS = range(7)
FIELDS = 7
COLS_ROW = 3 * FIELDS
HEAD_ROW = COLS_ROW + 1
MINE_ROW = COLS_ROW + 2
LISTS_ROW = COLS_ROW + 3
HEAD_COLS, HEAD_OVER, HEAD_LISTS = 3, 4, 8


class Sizes:
    def __init__(self, tokens, gate_blocks, slots, n_fsdp, n_tensor):
        self.tok, self.width = tokens.shape
        self.n_fsdp, self.n_tensor = n_fsdp, n_tensor
        self.rb = self.width // BLK
        self.cb = FF // (BLK * n_tensor)
        self.slots = slots
        self.all = 3 * slots
        self.lanes = -(-(self.all + GROUP) // 128) * 128
        self.nb = gate_blocks.shape[1]
        self.chunk = 3 * self.nb
        self.ring = n_fsdp // 2
        self.top = self.ring // 2
        self.rbt = self.rb // n_tensor
        self.order = [self.top]
        for d in range(1, self.top):
            self.order += [self.top + d, self.top - d]
        self.order.append(0)
        self.far = min(4, self.ring - 1)
        sparse = slots < self.cb
        self.keep = min(FIRST_GRADS, self.chunk) if sparse else self.chunk
        self.more = self.chunk - self.keep
        self.send_all = 2 * self.rbt
        self.first = min(FIRST_SEND, self.send_all) if sparse else self.send_all
        self.rest = self.send_all - self.first
        self.blocks = 2 * self.ring * self.chunk
        self.main = 2 * self.ring * self.keep
        self.plan_rows = -(-(LISTS_ROW + 2 * n_tensor) // 8) * 8
        self.recv_rows = -(-n_tensor // 8) * 8
        self.room = slots + GROUP


def permutations(sz):
    seq = list(range(0, sz.ring, 2)) + list(range(sz.ring - 1, 0, -2))
    ahead, behind, swap = [], [], []
    for i, q in enumerate(seq):
        up, down = seq[(i + 1) % sz.ring], seq[i - 1]
        ahead += [(q * 2, up * 2), (q * 2 + 1, down * 2 + 1)]
        behind += [(q * 2, down * 2), (q * 2 + 1, up * 2 + 1)]
        swap += [(q * 2, q * 2 + 1), (q * 2 + 1, q * 2)]
    return ahead, behind, swap


def ratio(x, d):
    return jnp.floor((x + 0.5) * (1.0 / d))


def rest_of(x, d):
    return x - d * ratio(x, d)


def ring_position(sz, chip):
    return jnp.where(rest_of(chip, 2) == 0, ratio(chip, 2), sz.ring - 1 - ratio(chip, 2))


class Marks:
    def __init__(self, sz, own, raw):
        N, L, S = sz.all, sz.lanes, sz.slots
        f32 = jnp.float32
        self.sz = sz
        self.sub = lax.broadcasted_iota(jnp.int32, (N, L), 0)
        self.lane = lax.broadcasted_iota(jnp.int32, (N, L), 1)
        self.same = self.sub == self.lane
        sub_c = self.sub[:, :1].astype(f32)
        lane_r = lax.broadcasted_iota(jnp.int32, (1, L), 1).astype(f32)
        self.sub_c, self.lane_r = sub_c, lane_r
        raw_r = raw[...].astype(f32)
        own_r = own[...].astype(f32)

        def single(row, at):
            return jnp.sum(jnp.where(lane_r == at, row, 0.0), axis=1, keepdims=True)

        self.f, self.rank = single(own_r, N + 3), single(own_r, N + 4)

        def kind(x):
            return (x >= S).astype(f32) + (x >= 2 * S).astype(f32)

        self.kind_c, self.kind_r = kind(sub_c), kind(lane_r)
        self.n_r = lane_r - S * self.kind_r
        self.n_c = sub_c - S * self.kind_c
        limit = jnp.zeros((1, L), f32)
        for k in range(3):
            limit = limit + jnp.where(self.kind_r == k, single(raw_r, N + k), 0.0)
        live_r = jnp.where((lane_r < N) & (self.n_r < limit), 1.0, 0.0)
        w_c = self.col(raw_r)
        live_c = self.col(live_r)

        def place(w, k):
            gate, down = ratio(w, sz.cb), ratio(w, sz.rb)
            is_down = k == 2
            return jnp.where(is_down, w - down * sz.rb, gate), jnp.where(is_down, down, w - gate * sz.cb)

        self.row_c, col_c = place(w_c, self.kind_c)
        self.row_r, col_r = place(raw_r, self.kind_r)
        self.owner_c, self.owner_r = ratio(self.n_c, sz.nb), ratio(self.n_r, sz.nb)
        self.same_col = (col_c == col_r).astype(f32)
        act_c, act_r = live_c, live_r
        for k in range(3):
            lanes = self.same_col * (live_r * (self.kind_r == k).astype(f32))
            act_c = act_c * jnp.max(lanes, axis=1, keepdims=True)
            subs = self.same_col * (live_c * (self.kind_c == k).astype(f32))
            act_r = act_r * jnp.max(subs, axis=0, keepdims=True)
        self.act_c, self.act_r = act_c, act_r
        out_c = jnp.where(self.kind_c == 2, 0.0, f32(sz.rb)) + self.row_c
        out_r = jnp.where(self.kind_r == 2, 0.0, f32(sz.rb)) + self.row_r
        self.same_out = (out_c == out_r).astype(f32)
        self.before = (self.lane < self.sub).astype(f32)
        self.after = (self.sub < self.lane).astype(f32)
        self.owas_c = jnp.max(self.same_out * self.before * act_r, axis=1, keepdims=True)
        self.owas_r = jnp.max(self.same_out * self.after * act_c, axis=0, keepdims=True)
        self.lead_c = act_c * (1.0 - self.owas_c)
        self.lead_r = act_r * (1.0 - self.owas_r)
        self.owned = (self.owner_c == self.owner_r).astype(f32)

        def shift(row):
            away = ratio(row, sz.rbt) - self.rank
            return jnp.where(away < 0, away + sz.n_tensor, away)

        self.shift_c, self.shift_r = shift(self.row_c), shift(self.row_r)
        self.local_c = jnp.where(self.kind_c == 2, 0.0, f32(sz.rbt)) + rest_of(self.row_c, sz.rbt)

    def col(self, row):
        return jnp.sum(jnp.where(self.same, row, 0.0), axis=1, keepdims=True)

    def base_c(self):
        sz = self.sz
        away = ring_position(sz, ratio(self.owner_c, 2)) - ring_position(sz, ratio(self.f, 2))
        away = jnp.where(rest_of(self.owner_c, 2) == 0, away, -away)
        rel = jnp.where(away < 0, away + sz.ring, away)
        j = jnp.where(rel > sz.top, 2 * (rel - sz.top) - 1, 2 * (sz.top - rel))
        j = jnp.where(rel == 0, sz.ring - 1.0, j)
        return j + jnp.where(rest_of(self.owner_c, 2) == rest_of(self.f, 2), 0.0, float(sz.ring))

    def ranks(self, chosen_r):
        return jnp.sum(self.before * chosen_r, axis=1, keepdims=True)

    def listed(self, chosen_c, rank_c, value_c, lo=0, hi=None):
        at = rank_c[lo:hi] == self.lane[lo:hi].astype(jnp.float32)
        return jnp.sum(jnp.where(at, chosen_c[lo:hi] * value_c[lo:hi], 0.0), axis=0, keepdims=True)

    def most_owned(self):
        return jnp.max(jnp.sum(self.owned * self.act_r, axis=1, keepdims=True), axis=0, keepdims=True)


def total(x):
    return jnp.sum(x, axis=0, keepdims=True)


def head_row(sz, entries):
    lane = lax.broadcasted_iota(jnp.int32, (1, sz.lanes), 1)
    row = jnp.zeros((1, sz.lanes), jnp.float32)
    for i, value in entries:
        row = jnp.where(lane == i, value, row)
    return row


def plan_kernel(sz, own, plan):
    S, N = sz.slots, sz.all
    m = Marks(sz, own, own)
    f32 = jnp.float32
    lane_r, sub_c = m.lane_r, m.sub_c
    same_kind = (m.kind_c == m.kind_r).astype(f32)
    rank_c = jnp.sum(m.before * same_kind * m.act_r, axis=1, keepdims=True)
    cwas_c = jnp.max(m.before * same_kind * m.same_col * m.act_r, axis=1, keepdims=True)
    cwas_r = jnp.max(m.after * same_kind * m.same_col * m.act_c, axis=0, keepdims=True)
    big = f32(4 * N)
    lanes_f = m.lane.astype(f32)
    gates_r = m.act_r * (m.kind_r == 0).astype(f32)
    cidx_c = jnp.min(jnp.where(m.same_col * gates_r > 0, lanes_f, big), axis=1, keepdims=True)
    oidx_c = jnp.min(jnp.where(m.same_out * m.act_r > 0, lanes_f, big), axis=1, keepdims=True)
    pos_c = jnp.sum(m.before * m.owned * m.act_r, axis=1, keepdims=True)
    base_c = m.base_c()
    place_c = base_c * sz.chunk + m.kind_c * sz.nb + rest_of(m.n_c, sz.nb)
    part_c = jnp.where(
        pos_c < sz.keep, base_c * sz.keep + pos_c, sz.main + base_c * sz.more + pos_c - sz.keep)
    fields = [
        (place_c, sz.blocks), (part_c, sz.blocks), (m.row_c, 0), (cidx_c, S), (cwas_c, 0), (oidx_c, N), (m.owas_c, 0)]
    rows = []
    head = []
    for k in range(3):
        lo, hi = k * S, (k + 1) * S
        n_k = total(m.act_c[lo:hi])
        head.append((k, n_k))
        for value, spare in fields:
            row = m.listed(m.act_c, rank_c, value, lo, hi)
            rows.append(jnp.where(lane_r < n_k, row, f32(spare)))
    leader_c = m.act_c * (1.0 - cwas_c) * (m.kind_c == 0).astype(f32)
    leader_r = m.act_r * (1.0 - cwas_r) * (m.kind_r == 0).astype(f32)
    rows.append(m.listed(leader_c, m.ranks(leader_r), sub_c, 0, S))
    head.append((HEAD_COLS, total(leader_c)))
    over = (m.most_owned() > sz.keep).astype(f32)
    lists = []
    for s in range(sz.n_tensor):
        chosen_c = m.lead_c * (m.shift_c == s).astype(f32)
        chosen_r = m.lead_r * (m.shift_r == s).astype(f32)
        rank = m.ranks(chosen_r)
        lists.append(m.listed(chosen_c, rank, sub_c))
        lists.append(m.listed(chosen_c, rank, m.local_c))
        n = total(chosen_c)
        head.append((HEAD_LISTS + s, n))
        over = jnp.maximum(over, (n > sz.first).astype(f32))
    head.append((HEAD_OVER, over))
    rows.append(head_row(sz, head))
    mine = sub_c == ratio(lane_r, sz.nb) * S + m.f * sz.nb + rest_of(lane_r, sz.nb)
    rows.append(jnp.sum(jnp.where(mine, m.act_c * (pos_c + 1.0), 0.0), axis=0, keepdims=True))
    rows += lists
    for i, row in enumerate(rows):
        plan[i:i + 1, :] = row.astype(jnp.int32)


def recv_kernel(sz, *refs):
    own, raws, recv = refs[0], refs[1:-1], refs[-1]
    f32 = jnp.float32
    head = []
    over = jnp.zeros((1, 1), f32)
    for s, raw in enumerate(raws, 1):
        m = Marks(sz, own, raw)
        chosen_c = m.lead_c * (m.shift_c == 0).astype(f32)
        chosen_r = m.lead_r * (m.shift_r == 0).astype(f32)
        recv[s:s + 1, :] = m.listed(chosen_c, m.ranks(chosen_r), m.local_c).astype(jnp.int32)
        head.append((HEAD_LISTS + s, total(chosen_c)))
        over = jnp.maximum(over, (m.most_owned() > sz.keep).astype(f32))
        for d in range(sz.n_tensor):
            n = total(m.lead_c * (m.shift_c == d).astype(f32))
            over = jnp.maximum(over, (n > sz.first).astype(f32))
    head.append((HEAD_OVER, over))
    recv[0:1, :] = head_row(sz, head).astype(jnp.int32)


def dot(a, b, ca, cb):
    return lax.dot_general(a, b, (((ca,), (cb,)), ((), ())), preferred_element_type=jnp.float32)


def compute_kernel(sz, *refs):
    plan, tokens, cot = refs[:3]
    n_chunks = 2 * sz.ring
    chunks = refs[3:3 + n_chunks]
    refs = refs[3 + n_chunks:]
    T = sz.n_tensor
    same, far, near, extra, _ = refs[:5]
    firsts, rests = refs[5:5 + T], refs[5 + T:5 + 2 * T]
    (xs, wbuf, parts, gate_acc, up_acc, hg_acc, hid, gate_d, up_d, out_acc, stage, strip_sems, sems, rest_sems) = refs[5 + 2 * T:]

    def field(k, j, e):
        return plan[k * FIELDS + j, e]

    def steps(k):
        return (plan[HEAD_ROW, k] + (GROUP - 1)) // GROUP

    def strip_copy(k, e):
        src = cot if k == 2 else tokens
        cols = pl.ds(pl.multiple_of(field(k, STRIP, e) * BLK, BLK), BLK)
        return pltpu.make_async_copy(src.at[:, cols], xs.at[k * sz.room + e], strip_sems.at[k * sz.room + e])

    for k in range(3):
        lax.fori_loop(0, steps(k) * GROUP, lambda e, _, k=k: strip_copy(k, e).start(), None)
    loads = [
        pltpu.make_async_copy(chunk, wbuf.at[pl.ds(i * sz.chunk, sz.chunk)], sems.at[i])
        for i, chunk in enumerate(chunks)
    ]
    for c in loads:
        c.start()
    for k in range(3):
        lax.fori_loop(0, steps(k) * GROUP, lambda e, _, k=k: strip_copy(k, e).wait(), None)
    for c in loads:
        c.wait()

    def walk(k, body):
        lax.fori_loop(0, steps(k), lambda p, _: body(p * GROUP), None)

    def forward(k, acc, w_dim):
        def body(e0):
            prods = [
                dot(xs[k * sz.room + e0 + u], wbuf[field(k, PLACE, e0 + u)], 1, w_dim) for u in range(GROUP)]
            for u in range(GROUP):
                c = field(k, CIDX, e0 + u)
                acc[c] = prods[u] + jnp.where(field(k, CWAS, e0 + u) == 0, 0.0, acc[c])

        walk(k, body)

    forward(0, gate_acc, 0)
    forward(1, up_acc, 0)
    forward(2, hg_acc, 1)

    def column(i, _):
        c = plan[COLS_ROW, i]
        g, u, h = gate_acc[c], up_acc[c], hg_acc[c]
        s = lax.logistic(g)
        silu = g * s
        hid[c] = (silu * u).astype(jnp.bfloat16)
        gate_d[c] = (h * u * s * (1.0 + g * (1.0 - s))).astype(jnp.bfloat16)
        up_d[c] = (h * silu).astype(jnp.bfloat16)

    lax.fori_loop(0, plan[HEAD_ROW, HEAD_COLS], column, None)

    def backward(k, act, w_dim):
        def body(e0):
            terms, grads = [], []
            for u in range(GROUP):
                a = act[field(k, CIDX, e0 + u)]
                x = xs[k * sz.room + e0 + u]
                terms.append(dot(a, wbuf[field(k, PLACE, e0 + u)], 1, w_dim))
                grads.append(dot(a, x, 0, 0) if k == 2 else dot(x, a, 0, 0))
            for u in range(GROUP):
                parts[field(k, PART, e0 + u)] = grads[u].astype(jnp.bfloat16)
            for u in range(GROUP):
                at = field(k, OIDX, e0 + u)
                out_acc[at] = terms[u] + jnp.where(field(k, OWAS, e0 + u) == 0, 0.0, out_acc[at])

        walk(k, body)

    backward(2, hid, 0)
    backward(0, gate_d, 1)
    backward(1, up_d, 1)

    split = sz.ring * sz.keep
    cut = split + sz.far * sz.keep
    outs = [
        pltpu.make_async_copy(parts.at[pl.ds(split, cut - split)], far, sems.at[0]),
        pltpu.make_async_copy(parts.at[pl.ds(0, split)], same, sems.at[1]),
        pltpu.make_async_copy(parts.at[pl.ds(cut, sz.main - cut)], near, sems.at[2]),
    ]
    for c in outs:
        c.start()

    for s in range(T):
        def staged(i, _, s=s):
            stage[s * sz.send_all + i] = out_acc[plan[LISTS_ROW + 2 * s, i]].astype(jnp.bfloat16)

        lax.fori_loop(0, plan[HEAD_ROW, HEAD_LISTS + s], staged, None)
        first = pltpu.make_async_copy(stage.at[pl.ds(s * sz.send_all, sz.first)], firsts[s], sems.at[3 + s])
        first.start()
        outs.append(first)

    if sz.rest + sz.more > 0:
        @pl.when(plan[HEAD_ROW, HEAD_OVER] > 0)
        def _():
            copies = []
            if sz.rest > 0:
                copies += [
                    pltpu.make_async_copy(
                        stage.at[pl.ds(s * sz.send_all + sz.first, sz.rest)], rests[s], rest_sems.at[s])
                    for s in range(T)
                ]
            if sz.more > 0:
                copies.append(pltpu.make_async_copy(
                    parts.at[pl.ds(sz.main, sz.blocks - sz.main)], extra, rest_sems.at[T]))
            for c in copies:
                c.start()
            for c in copies:
                c.wait()
    for c in outs:
        c.wait()


def join_kernel(sz, *refs):
    T = sz.n_tensor
    plan, recv = refs[:2]
    firsts, rests = refs[2:2 + T], refs[2 + T:2 + 2 * T]
    outputs, input_grads, spare, sem = refs[-4:]
    outputs[...] = jnp.zeros_like(outputs)
    input_grads[...] = jnp.zeros_like(input_grads)

    def add(at, value):
        def into(ref, w):
            cols = pl.ds(pl.multiple_of(w * BLK, BLK), BLK)
            ref[:, cols] = (ref[:, cols].astype(jnp.float32) + value.astype(jnp.float32)).astype(jnp.bfloat16)

        @pl.when(at < sz.rbt)
        def _():
            into(outputs, at)

        @pl.when(at >= sz.rbt)
        def _():
            into(input_grads, at - sz.rbt)

    for s in range(T):
        n = (recv[0, HEAD_LISTS + s] if s else plan[HEAD_ROW, HEAD_LISTS])

        def where_to(i, s=s):
            return recv[s, i] if s else plan[LISTS_ROW + 1, i]

        def early(i, _, s=s):
            add(where_to(i), firsts[s][i])

        lax.fori_loop(0, jnp.minimum(n, sz.first), early, None)
        if sz.rest > 0:
            def late(i, _, s=s):
                copy = pltpu.make_async_copy(rests[s].at[i - sz.first], spare, sem)
                copy.start()
                copy.wait()
                add(where_to(i), spare[...])

            lax.fori_loop(jnp.minimum(n, sz.first), n, late, None)


def finish_kernel(sz, plan, here, ahead, behind, late, *outs):
    for k in range(3):
        for a in range(sz.nb):
            at = plan[MINE_ROW, k * sz.nb + a]
            p = jnp.minimum(jnp.maximum(at - 1, 0), sz.keep - 1)
            value = here[p] + ahead[p].astype(jnp.float32) + behind[p].astype(jnp.float32)
            if sz.more > 0:
                q = jnp.minimum(jnp.maximum(at - 1 - sz.keep, 0), sz.more - 1)
                value = jnp.where(at > sz.keep, late[q].astype(jnp.float32), value)
            outs[k][0, a] = jnp.where(at > 0, value, 0.0).astype(jnp.bfloat16)


def spec(space):
    return pl.BlockSpec(memory_space=space)


ANY, HBM, VMEM, SMEM = pl.ANY, pltpu.HBM, pltpu.VMEM, pltpu.SMEM


def cost(flops, moved):
    return pl.CostEstimate(flops=flops, bytes_accessed=moved, transcendentals=0)


def call_plan(sz, own):
    return pl.pallas_call(
        functools.partial(plan_kernel, sz),
        out_shape=jax.ShapeDtypeStruct((sz.plan_rows, sz.lanes), jnp.int32),
        in_specs=[spec(VMEM)],
        out_specs=spec(VMEM),
        compiler_params=pltpu.CompilerParams(vmem_limit_bytes=SMALL),
        cost_estimate=cost(1_000_000, 4_000_000),
        name="plan",
    )(own)


def call_recv(sz, own, raws):
    return pl.pallas_call(
        functools.partial(recv_kernel, sz),
        out_shape=jax.ShapeDtypeStruct((sz.recv_rows, sz.lanes), jnp.int32),
        in_specs=[spec(VMEM)] * (1 + len(raws)),
        out_specs=spec(VMEM),
        compiler_params=pltpu.CompilerParams(vmem_limit_bytes=SMALL),
        cost_estimate=cost(1_000_000, 4_000_000),
        name="recv",
    )(own, *raws)


def call_compute(sz, plan, tokens, cot, chunks):
    T = sz.n_tensor
    bf, f32 = jnp.bfloat16, jnp.float32

    def blocks(n):
        return jax.ShapeDtypeStruct((max(n, 1), BLK, BLK), bf)

    out_shape = [
        blocks(sz.ring * sz.keep),
        blocks(sz.far * sz.keep),
        blocks((sz.ring - sz.far) * sz.keep),
        blocks(sz.blocks - sz.main),
        blocks(sz.more),
    ]
    out_shape += [blocks(sz.first)] * T + [blocks(sz.rest)] * T
    scratch = [
        ((3 * sz.room, sz.tok, BLK), bf),
        ((sz.blocks + 1, BLK, BLK), bf),
        ((sz.blocks + 1, BLK, BLK), bf),
        ((sz.slots + 1, sz.tok, BLK), f32),
        ((sz.slots + 1, sz.tok, BLK), f32),
        ((sz.slots + 1, sz.tok, BLK), f32),
        ((sz.slots + 1, sz.tok, BLK), bf),
        ((sz.slots + 1, sz.tok, BLK), bf),
        ((sz.slots + 1, sz.tok, BLK), bf),
        ((sz.all + 1, sz.tok, BLK), f32),
        ((T * sz.send_all, sz.tok, BLK), bf),
    ]
    held = sum(s[0] * s[1] * s[2] * jnp.dtype(t).itemsize for s, t in scratch)
    return pl.pallas_call(
        functools.partial(compute_kernel, sz),
        out_shape=out_shape,
        in_specs=[spec(SMEM)] + [spec(HBM)] * 2 + [spec(ANY)] * len(chunks),
        out_specs=[spec(ANY)] * len(out_shape),
        scratch_shapes=[pltpu.VMEM(s, t) for s, t in scratch] + [
            pltpu.SemaphoreType.DMA((3 * sz.room,)),
            pltpu.SemaphoreType.DMA((max(len(chunks), 3 + T),)),
            pltpu.SemaphoreType.DMA((T + 1,)),
        ],
        compiler_params=pltpu.CompilerParams(vmem_limit_bytes=held + 2 * 1024 * 1024),
        cost_estimate=cost(1_000_000_000, 20_000_000),
        name="compute",
    )(plan, pltpu.with_memory_space_constraint(tokens, HBM), pltpu.with_memory_space_constraint(cot, HBM), *chunks)


def call_join(sz, plan, recv, firsts, rests):
    half = jax.ShapeDtypeStruct((sz.tok, sz.width // sz.n_tensor), jnp.bfloat16)
    return pl.pallas_call(
        functools.partial(join_kernel, sz),
        out_shape=[half, half],
        in_specs=[spec(SMEM)] * 2 + [spec(VMEM)] * len(firsts) + [spec(ANY)] * len(rests),
        out_specs=[spec(VMEM), spec(VMEM)],
        scratch_shapes=[pltpu.VMEM((sz.tok, BLK), jnp.bfloat16), pltpu.SemaphoreType.DMA],
        compiler_params=pltpu.CompilerParams(vmem_limit_bytes=10 * 1024 * 1024),
        cost_estimate=cost(1_000_000, 6_000_000),
        name="join",
    )(plan, recv, *firsts, *rests)


def call_finish(sz, plan, here, ahead, behind, late):
    out = jax.ShapeDtypeStruct((1, sz.nb, BLK, BLK), jnp.bfloat16)
    return pl.pallas_call(
        functools.partial(finish_kernel, sz),
        out_shape=[out] * 3,
        in_specs=[spec(SMEM)] + [spec(VMEM)] * 4,
        out_specs=[spec(VMEM)] * 3,
        compiler_params=pltpu.CompilerParams(vmem_limit_bytes=SMALL),
        cost_estimate=cost(1_000_000, 1_000_000),
        name="finish",
    )(plan, here, ahead, behind, late)


def gather_chunks(sz, chunk, plan_of, recv_of):
    ahead, behind, swap = permutations(sz)
    same = {0: chunk}
    a = b = chunk
    for s in range(1, sz.top + 1):
        if s == 2:
            (a, b), plan = lax.optimization_barrier(((a, b), plan_of()))
        if s == 3 or s == sz.top < 3:
            (a, b), recv = lax.optimization_barrier(((a, b), recv_of()))
        a = lax.ppermute(a, "fsdp", ahead)
        same[sz.ring - s] = a
        if s < sz.top:
            b = lax.ppermute(b, "fsdp", behind)
            same[s] = b
    other = {d: lax.ppermute(same[d], "fsdp", swap) for d in same}
    return [side[d] for side in (same, other) for d in sz.order], plan, recv


def reduce_parts(sz, per, same, pair, beside=lambda a: a):
    ahead, behind, _ = permutations(sz)

    def wide(d, *more):
        j = sz.order.index(d)
        out = same[j * per:(j + 1) * per].astype(jnp.float32) + pair(j).astype(jnp.float32)
        for m in more:
            out = out + m.astype(jnp.float32)
        return out

    def term(d, *more):
        return wide(d, *more).astype(jnp.bfloat16)

    a, b = term(sz.top), term(sz.top + 1)
    for s in range(1, sz.top + 1):
        if s < sz.top:
            a, b = lax.optimization_barrier((a, b))
        else:
            a = beside(a)
        a = lax.ppermute(a, "fsdp", ahead)
        if s < sz.top:
            b = lax.ppermute(b, "fsdp", behind)
            a = term(sz.top - s, a)
            if s + 1 < sz.top:
                b = term(sz.top + 1 + s, b)
    return wide(0), a, b


def shards(
    tokens,
    cotangent,
    gate_blocks,
    up_blocks,
    down_blocks,
    gate_where,
    up_where,
    down_where,
    block_counts,
):
    n_fsdp, T = lax.axis_size("fsdp"), lax.axis_size("tensor")
    sz = Sizes(tokens, gate_blocks, gate_where.shape[1], n_fsdp, T)
    f, rank = lax.axis_index("fsdp"), lax.axis_index("tensor")
    _, _, swap = permutations(sz)

    chunk = jnp.concatenate([gate_blocks[0], up_blocks[0], down_blocks[0]])
    own = jnp.concatenate([
        gate_where[0], up_where[0], down_where[0], block_counts[:, 0],
        f.astype(jnp.int32)[None], rank.astype(jnp.int32)[None]])
    own = jnp.pad(own, (0, sz.lanes - own.shape[0]))[None]

    def recv_of():
        raws = [
            lax.ppermute(own, "tensor", [(i, (i + s) % T) for i in range(T)]) for s in range(1, T)]
        return call_recv(sz, own, raws)

    chunks, plan, recv = gather_chunks(sz, chunk, lambda: call_plan(sz, own), recv_of)

    outs = call_compute(sz, plan, tokens, cotangent, chunks)
    same, far, near, extra, idle = outs[:5]
    firsts, rests = outs[5:5 + T], list(outs[5 + T:])

    def exchange(arrays):
        return [arrays[0]] + [
            lax.ppermute(arrays[s], "tensor", [(i, (i + s) % T) for i in range(T)]) for s in range(1, T)]

    far, near = lax.ppermute(far, "fsdp", swap), lax.ppermute(near, "fsdp", swap)
    firsts = exchange(firsts)

    def pair(j):
        at = j * sz.keep
        return far[at:at + sz.keep] if j < sz.far else near[at - sz.far * sz.keep:][:sz.keep]

    late = idle

    def beside(a):
        nonlocal rests, late
        if sz.rest + sz.more == 0:
            return a

        def spill(rests, extra, idle):
            moved = exchange(rests)
            if sz.more == 0:
                return moved, idle
            n = sz.ring * sz.more
            other = lax.ppermute(extra[n:], "fsdp", swap)
            terms = reduce_parts(sz, sz.more, extra[:n], lambda j: other[j * sz.more:(j + 1) * sz.more])
            return moved, sum(t.astype(jnp.float32) for t in terms).astype(jnp.bfloat16)

        over = plan[HEAD_ROW, HEAD_OVER] + recv[0, HEAD_OVER]
        a, over, rests, more = lax.optimization_barrier((a, over, rests, extra))
        rests, late = lax.cond(over > 0, spill, lambda r, e, i: (r, i), rests, more, idle)
        return a

    here, ahead, behind = reduce_parts(sz, sz.keep, same, pair, beside)
    outputs, input_grads = call_join(sz, plan, recv, firsts, rests)
    grads = call_finish(sz, plan, here, ahead, behind, late)
    return (outputs, input_grads, *grads)


def solution(mesh):
    placed = (
        P("fsdp", None),
        P("fsdp", None),
        P("tensor", "fsdp", None, None),
        P("tensor", "fsdp", None, None),
        P("tensor", "fsdp", None, None),
        P("tensor", None),
        P("tensor", None),
        P("tensor", None),
        P(None, "tensor"),
    )
    return jax.shard_map(
        shards,
        mesh=mesh,
        in_specs=placed,
        out_specs=(
            P("fsdp", "tensor"),
            P("fsdp", "tensor"),
            P("tensor", "fsdp", None, None),
            P("tensor", "fsdp", None, None),
            P("tensor", "fsdp", None, None),
        ),
        check_vma=False,
    )
```

```python
import functools

import jax
import jax.numpy as jnp
from jax import lax
from jax.experimental import pallas as pl
from jax.experimental.pallas import tpu as pltpu
from jax.sharding import PartitionSpec as P

FF = 14336
BLK = 128
GROUP = 4
FIRST_SEND = 18
FIRST_GRADS = 4
SMALL = 4 * 1024 * 1024
PART, STRIP, CIDX, CWAS, OIDX, OWAS = range(6)
FIELDS = 6
COLS_ROW = 3 * FIELDS
HEAD_ROW = COLS_ROW + 1
MINE_ROW = COLS_ROW + 2
LISTS_ROW = COLS_ROW + 3
HEAD_COLS, HEAD_OVER, HEAD_LISTS = 3, 4, 8


class Sizes:
    def __init__(self, tokens, gate_blocks, slots, n_fsdp, n_tensor):
        self.tok, self.width = tokens.shape
        self.n_fsdp, self.n_tensor = n_fsdp, n_tensor
        self.rb = self.width // BLK
        self.cb = FF // (BLK * n_tensor)
        self.slots = slots
        self.all = 3 * slots
        self.lanes = -(-(self.all + GROUP) // 128) * 128
        self.nb = gate_blocks.shape[1]
        self.chunk = 3 * self.nb
        self.ring = n_fsdp // 2
        self.top = self.ring // 2
        self.rbt = self.rb // n_tensor
        self.order = [self.top]
        for d in range(1, self.top):
            self.order += [self.top + d, self.top - d]
        self.order.append(0)
        self.far = min(4, self.ring - 1)
        sparse = slots < self.cb
        self.keep = min(FIRST_GRADS, self.chunk) if sparse else self.chunk
        self.more = self.chunk - self.keep
        self.send_all = 2 * self.rbt
        self.first = min(FIRST_SEND, self.send_all) if sparse else self.send_all
        self.rest = self.send_all - self.first
        step = -(-self.first // min(3, self.top - 1))
        self.parts = [(lo, min(step, self.first - lo)) for lo in range(0, self.first, step)]
        self.blocks = 2 * self.ring * self.chunk
        self.main = 2 * self.ring * self.keep
        self.plan_rows = -(-(LISTS_ROW + 2 * n_tensor) // 8) * 8
        self.recv_rows = -(-n_tensor // 8) * 8
        self.room = slots + GROUP


def permutations(sz):
    seq = list(range(0, sz.ring, 2)) + list(range(sz.ring - 1, 0, -2))
    ahead, behind, swap = [], [], []
    for i, q in enumerate(seq):
        up, down = seq[(i + 1) % sz.ring], seq[i - 1]
        ahead += [(q * 2, up * 2), (q * 2 + 1, down * 2 + 1)]
        behind += [(q * 2, down * 2), (q * 2 + 1, up * 2 + 1)]
        swap += [(q * 2, q * 2 + 1), (q * 2 + 1, q * 2)]
    return ahead, behind, swap


def ratio(x, d):
    return jnp.floor((x + 0.5) * (1.0 / d))


def rest_of(x, d):
    return x - d * ratio(x, d)


def ring_position(sz, chip):
    return jnp.where(rest_of(chip, 2) == 0, ratio(chip, 2), sz.ring - 1 - ratio(chip, 2))


class Marks:
    def __init__(self, sz, own, raw):
        N, L, S = sz.all, sz.lanes, sz.slots
        f32 = jnp.float32
        self.sz = sz
        self.sub = lax.broadcasted_iota(jnp.int32, (N, L), 0)
        self.lane = lax.broadcasted_iota(jnp.int32, (N, L), 1)
        self.same = self.sub == self.lane
        sub_c = self.sub[:, :1].astype(f32)
        lane_r = lax.broadcasted_iota(jnp.int32, (1, L), 1).astype(f32)
        self.sub_c, self.lane_r = sub_c, lane_r
        raw_r = raw[...].astype(f32)
        own_r = own[...].astype(f32)

        def single(row, at):
            return jnp.sum(jnp.where(lane_r == at, row, 0.0), axis=1, keepdims=True)

        self.f, self.rank = single(own_r, N + 3), single(own_r, N + 4)

        def kind(x):
            return (x >= S).astype(f32) + (x >= 2 * S).astype(f32)

        self.kind_c, self.kind_r = kind(sub_c), kind(lane_r)
        self.n_r = lane_r - S * self.kind_r
        self.n_c = sub_c - S * self.kind_c
        limit = jnp.zeros((1, L), f32)
        for k in range(3):
            limit = limit + jnp.where(self.kind_r == k, single(raw_r, N + k), 0.0)
        live_r = jnp.where((lane_r < N) & (self.n_r < limit), 1.0, 0.0)
        w_c = self.col(raw_r)
        live_c = self.col(live_r)

        def place(w, k):
            gate, down = ratio(w, sz.cb), ratio(w, sz.rb)
            is_down = k == 2
            return jnp.where(is_down, w - down * sz.rb, gate), jnp.where(is_down, down, w - gate * sz.cb)

        self.row_c, col_c = place(w_c, self.kind_c)
        self.row_r, col_r = place(raw_r, self.kind_r)
        self.owner_c, self.owner_r = ratio(self.n_c, sz.nb), ratio(self.n_r, sz.nb)
        self.same_col = (col_c == col_r).astype(f32)
        act_c, act_r = live_c, live_r
        for k in range(3):
            lanes = self.same_col * (live_r * (self.kind_r == k).astype(f32))
            act_c = act_c * jnp.max(lanes, axis=1, keepdims=True)
            subs = self.same_col * (live_c * (self.kind_c == k).astype(f32))
            act_r = act_r * jnp.max(subs, axis=0, keepdims=True)
        self.act_c, self.act_r = act_c, act_r
        out_c = jnp.where(self.kind_c == 2, 0.0, f32(sz.rb)) + self.row_c
        out_r = jnp.where(self.kind_r == 2, 0.0, f32(sz.rb)) + self.row_r
        self.same_out = (out_c == out_r).astype(f32)
        self.before = (self.lane < self.sub).astype(f32)
        self.after = (self.sub < self.lane).astype(f32)
        self.owas_c = jnp.max(self.same_out * self.before * act_r, axis=1, keepdims=True)
        self.owas_r = jnp.max(self.same_out * self.after * act_c, axis=0, keepdims=True)
        self.lead_c = act_c * (1.0 - self.owas_c)
        self.lead_r = act_r * (1.0 - self.owas_r)
        self.owned = (self.owner_c == self.owner_r).astype(f32)

        def shift(row):
            away = ratio(row, sz.rbt) - self.rank
            return jnp.where(away < 0, away + sz.n_tensor, away)

        self.shift_c, self.shift_r = shift(self.row_c), shift(self.row_r)
        self.local_c = jnp.where(self.kind_c == 2, 0.0, f32(sz.rbt)) + rest_of(self.row_c, sz.rbt)

    def col(self, row):
        return jnp.sum(jnp.where(self.same, row, 0.0), axis=1, keepdims=True)

    def base_c(self):
        sz = self.sz
        away = ring_position(sz, ratio(self.owner_c, 2)) - ring_position(sz, ratio(self.f, 2))
        away = jnp.where(rest_of(self.owner_c, 2) == 0, away, -away)
        rel = jnp.where(away < 0, away + sz.ring, away)
        j = jnp.where(rel > sz.top, 2 * (rel - sz.top) - 1, 2 * (sz.top - rel))
        j = jnp.where(rel == 0, sz.ring - 1.0, j)
        return j + jnp.where(rest_of(self.owner_c, 2) == rest_of(self.f, 2), 0.0, float(sz.ring))

    def ranks(self, chosen_r):
        return jnp.sum(self.before * chosen_r, axis=1, keepdims=True)

    def listed(self, chosen_c, rank_c, value_c, lo=0, hi=None):
        at = rank_c[lo:hi] == self.lane[lo:hi].astype(jnp.float32)
        return jnp.sum(jnp.where(at, chosen_c[lo:hi] * value_c[lo:hi], 0.0), axis=0, keepdims=True)

    def most_owned(self):
        return jnp.max(jnp.sum(self.owned * self.act_r, axis=1, keepdims=True), axis=0, keepdims=True)


def total(x):
    return jnp.sum(x, axis=0, keepdims=True)


def head_row(sz, entries):
    lane = lax.broadcasted_iota(jnp.int32, (1, sz.lanes), 1)
    row = jnp.zeros((1, sz.lanes), jnp.float32)
    for i, value in entries:
        row = jnp.where(lane == i, value, row)
    return row


def plan_kernel(sz, gate_where, up_where, down_where, counts, f, rank, gate, up, down, own, plan, chunk, extra, _):
    S, N = sz.slots, sz.all
    own[...] = jnp.zeros_like(own)
    for k, where in enumerate((gate_where, up_where, down_where)):
        own[:, k * S:(k + 1) * S] = where[...]
    lane = lax.broadcasted_iota(jnp.int32, (1, sz.lanes), 1)
    row = own[...]
    for k in range(3):
        row = jnp.where(lane == N + k, counts[k], row)
    row = jnp.where(lane == N + 3, f[0], row)
    own[...] = jnp.where(lane == N + 4, rank[0], row)
    m = Marks(sz, own, own)
    f32 = jnp.float32
    lane_r, sub_c = m.lane_r, m.sub_c
    same_kind = (m.kind_c == m.kind_r).astype(f32)
    rank_c = jnp.sum(m.before * same_kind * m.act_r, axis=1, keepdims=True)
    cwas_c = jnp.max(m.before * same_kind * m.same_col * m.act_r, axis=1, keepdims=True)
    cwas_r = jnp.max(m.after * same_kind * m.same_col * m.act_c, axis=0, keepdims=True)
    big = f32(4 * N)
    lanes_f = m.lane.astype(f32)
    gates_r = m.act_r * (m.kind_r == 0).astype(f32)
    cidx_c = jnp.min(jnp.where(m.same_col * gates_r > 0, lanes_f, big), axis=1, keepdims=True)
    oidx_c = jnp.min(jnp.where(m.same_out * m.act_r > 0, lanes_f, big), axis=1, keepdims=True)
    pos_c = jnp.sum(m.before * m.owned * m.act_r, axis=1, keepdims=True)
    base_c = m.base_c()
    part_c = jnp.where(
        pos_c < sz.keep, base_c * sz.keep + pos_c, sz.main + base_c * sz.more + pos_c - sz.keep)
    fields = [
        (part_c, sz.blocks), (m.row_c, 0), (cidx_c, S), (cwas_c, 0), (oidx_c, N), (m.owas_c, 0)]
    rows = []
    head = []
    for k in range(3):
        lo, hi = k * S, (k + 1) * S
        n_k = total(m.act_c[lo:hi])
        head.append((k, n_k))
        for value, spare in fields:
            row = m.listed(m.act_c, rank_c, value, lo, hi)
            rows.append(jnp.where(lane_r < n_k, row, f32(spare)))
    leader_c = m.act_c * (1.0 - cwas_c) * (m.kind_c == 0).astype(f32)
    leader_r = m.act_r * (1.0 - cwas_r) * (m.kind_r == 0).astype(f32)
    rows.append(m.listed(leader_c, m.ranks(leader_r), sub_c, 0, S))
    head.append((HEAD_COLS, total(leader_c)))
    over = (m.most_owned() > sz.keep).astype(f32)
    lists = []
    for s in range(sz.n_tensor):
        chosen_c = m.lead_c * (m.shift_c == s).astype(f32)
        chosen_r = m.lead_r * (m.shift_r == s).astype(f32)
        rank = m.ranks(chosen_r)
        lists.append(m.listed(chosen_c, rank, sub_c))
        lists.append(m.listed(chosen_c, rank, m.local_c))
        n = total(chosen_c)
        head.append((HEAD_LISTS + s, n))
        over = jnp.maximum(over, (n > sz.first).astype(f32))
    head.append((HEAD_OVER, over))
    rows.append(head_row(sz, head))
    mine = sub_c == ratio(lane_r, sz.nb) * S + m.f * sz.nb + rest_of(lane_r, sz.nb)
    mine = jnp.sum(jnp.where(mine, m.act_c * (pos_c + 1.0), 0.0), axis=0, keepdims=True)
    for k, blocks in enumerate((gate, up, down)):
        for a in range(sz.nb):
            at = jnp.max(jnp.where(lane_r == k * sz.nb + a, mine, 0.0)).astype(jnp.int32)

            @pl.when((at > 0) & (at <= sz.keep))
            def _(at=at, blocks=blocks, a=a):
                chunk[at - 1] = blocks[0, a]

            if sz.more > 0:
                @pl.when(at > sz.keep)
                def _(at=at, blocks=blocks, a=a):
                    extra[at - 1 - sz.keep] = blocks[0, a]

    rows.append(mine)
    rows += lists
    for i, row in enumerate(rows):
        plan[i:i + 1, :] = row.astype(jnp.int32)


def recv_kernel(sz, *refs):
    own, plan, raws, recv, flag = refs[0], refs[1], refs[2:1 + sz.n_tensor], refs[-2], refs[-1]
    f32 = jnp.float32
    head = []
    over = jnp.zeros((1, 1), f32)
    for s, raw in enumerate(raws, 1):
        m = Marks(sz, own, raw)
        chosen_c = m.lead_c * (m.shift_c == 0).astype(f32)
        chosen_r = m.lead_r * (m.shift_r == 0).astype(f32)
        recv[s:s + 1, :] = m.listed(chosen_c, m.ranks(chosen_r), m.local_c).astype(jnp.int32)
        head.append((HEAD_LISTS + s, total(chosen_c)))
        over = jnp.maximum(over, (m.most_owned() > sz.keep).astype(f32))
        for d in range(sz.n_tensor):
            n = total(m.lead_c * (m.shift_c == d).astype(f32))
            over = jnp.maximum(over, (n > sz.first).astype(f32))
    known = plan[HEAD_ROW:HEAD_ROW + 1, HEAD_OVER:HEAD_OVER + 1]
    flag[...] = jnp.maximum(known, over.astype(jnp.int32))
    recv[0:1, :] = head_row(sz, head).astype(jnp.int32)


def dot(a, b, ca, cb):
    return lax.dot_general(a, b, (((ca,), (cb,)), ((), ())), preferred_element_type=jnp.float32)


def compute_kernel(sz, *refs):
    plan, tokens, cot, spilled = refs[:4]
    n_chunks = 2 * sz.ring
    chunks = refs[4:4 + n_chunks]
    refs = refs[4 + n_chunks:]
    T = sz.n_tensor
    same, far, near, extra, _ = refs[:5]
    n_first = T * len(sz.parts)
    firsts, rests = refs[5:5 + n_first], refs[5 + n_first:5 + n_first + T]
    (xs, wbuf, parts, gate_acc, up_acc, hg_acc, hid, gate_d, up_d, out_acc, stage, strip_sems, sems, rest_sems) = refs[5 + n_first + T:]

    def field(k, j, e):
        return plan[k * FIELDS + j, e]

    def steps(k):
        return (plan[HEAD_ROW, k] + (GROUP - 1)) // GROUP

    def strip_copy(k, e):
        src = cot if k == 2 else tokens
        cols = pl.ds(pl.multiple_of(field(k, STRIP, e) * BLK, BLK), BLK)
        return pltpu.make_async_copy(src.at[:, cols], xs.at[k * sz.room + e], strip_sems.at[k * sz.room + e])

    for k in range(3):
        lax.fori_loop(0, steps(k) * GROUP, lambda e, _, k=k: strip_copy(k, e).start(), None)
    loads = [
        pltpu.make_async_copy(chunk, wbuf.at[pl.ds(i * sz.keep, sz.keep)], sems.at[i])
        for i, chunk in enumerate(chunks)
    ]
    for c in loads:
        c.start()
    if sz.more > 0:
        @pl.when(plan[HEAD_ROW, HEAD_OVER] > 0)
        def _():
            copy = pltpu.make_async_copy(spilled, wbuf.at[pl.ds(sz.main, sz.blocks - sz.main)], rest_sems.at[0])
            copy.start()
            copy.wait()

    for k in range(3):
        lax.fori_loop(0, steps(k) * GROUP, lambda e, _, k=k: strip_copy(k, e).wait(), None)
    for c in loads:
        c.wait()

    def walk(k, body):
        lax.fori_loop(0, steps(k), lambda p, _: body(p * GROUP), None)

    def forward(k, acc, w_dim):
        def body(e0):
            prods = [
                dot(xs[k * sz.room + e0 + u], wbuf[field(k, PART, e0 + u)], 1, w_dim) for u in range(GROUP)]
            for u in range(GROUP):
                c = field(k, CIDX, e0 + u)
                acc[c] = prods[u] + jnp.where(field(k, CWAS, e0 + u) == 0, 0.0, acc[c])

        walk(k, body)

    forward(0, gate_acc, 0)
    forward(1, up_acc, 0)
    forward(2, hg_acc, 1)

    def column(i, _):
        c = plan[COLS_ROW, i]
        g, u, h = gate_acc[c], up_acc[c], hg_acc[c]
        s = lax.logistic(g)
        silu = g * s
        hid[c] = (silu * u).astype(jnp.bfloat16)
        gate_d[c] = (h * u * s * (1.0 + g * (1.0 - s))).astype(jnp.bfloat16)
        up_d[c] = (h * silu).astype(jnp.bfloat16)

    lax.fori_loop(0, plan[HEAD_ROW, HEAD_COLS], column, None)

    def backward(k, act, w_dim):
        def body(e0):
            terms, grads = [], []
            for u in range(GROUP):
                a = act[field(k, CIDX, e0 + u)]
                x = xs[k * sz.room + e0 + u]
                terms.append(dot(a, wbuf[field(k, PART, e0 + u)], 1, w_dim))
                grads.append(dot(a, x, 0, 0) if k == 2 else dot(x, a, 0, 0))
            for u in range(GROUP):
                parts[field(k, PART, e0 + u)] = grads[u].astype(jnp.bfloat16)
            for u in range(GROUP):
                at = field(k, OIDX, e0 + u)
                out_acc[at] = terms[u] + jnp.where(field(k, OWAS, e0 + u) == 0, 0.0, out_acc[at])

        walk(k, body)

    backward(2, hid, 0)
    backward(0, gate_d, 1)
    backward(1, up_d, 1)

    split = sz.ring * sz.keep
    cut = split + sz.far * sz.keep
    outs = [
        pltpu.make_async_copy(parts.at[pl.ds(split, cut - split)], far, sems.at[0]),
        pltpu.make_async_copy(parts.at[pl.ds(0, split)], same, sems.at[1]),
        pltpu.make_async_copy(parts.at[pl.ds(cut, sz.main - cut)], near, sems.at[2]),
    ]
    for c in outs:
        c.start()

    for s in range(T):
        def staged(i, _, s=s):
            stage[s * sz.send_all + i] = out_acc[plan[LISTS_ROW + 2 * s, i]].astype(jnp.bfloat16)

        lax.fori_loop(0, plan[HEAD_ROW, HEAD_LISTS + s], staged, None)
        at = s * sz.send_all
        for j, (lo, n) in enumerate(sz.parts):
            copy = pltpu.make_async_copy(stage.at[pl.ds(at + lo, n)], firsts[j * T + s], sems.at[3 + j * T + s])
            copy.start()
            outs.append(copy)

    if sz.rest + sz.more > 0:
        @pl.when(plan[HEAD_ROW, HEAD_OVER] > 0)
        def _():
            copies = []
            if sz.rest > 0:
                copies += [
                    pltpu.make_async_copy(
                        stage.at[pl.ds(s * sz.send_all + sz.first, sz.rest)], rests[s], rest_sems.at[s])
                    for s in range(T)
                ]
            if sz.more > 0:
                copies.append(pltpu.make_async_copy(
                    parts.at[pl.ds(sz.main, sz.blocks - sz.main)], extra, rest_sems.at[T]))
            for c in copies:
                c.start()
            for c in copies:
                c.wait()
    for c in outs:
        c.wait()


def join_kernel(sz, *refs):
    T = sz.n_tensor
    plan, recv = refs[:2]
    n_first = T * len(sz.parts)
    firsts, rests = refs[2:2 + n_first], refs[2 + n_first:2 + n_first + T]
    outputs, input_grads, spare, sem = refs[-4:]
    outputs[...] = jnp.zeros_like(outputs)
    input_grads[...] = jnp.zeros_like(input_grads)

    def add(at, value):
        def into(ref, w):
            cols = pl.ds(pl.multiple_of(w * BLK, BLK), BLK)
            ref[:, cols] = (ref[:, cols].astype(jnp.float32) + value.astype(jnp.float32)).astype(jnp.bfloat16)

        @pl.when(at < sz.rbt)
        def _():
            into(outputs, at)

        @pl.when(at >= sz.rbt)
        def _():
            into(input_grads, at - sz.rbt)

    for s in range(T):
        n = (recv[0, HEAD_LISTS + s] if s else plan[HEAD_ROW, HEAD_LISTS])

        def where_to(i, s=s):
            return recv[s, i] if s else plan[LISTS_ROW + 1, i]

        for j, (lo, size) in enumerate(sz.parts):
            def early(i, _, ref=firsts[j * T + s], lo=lo):
                add(where_to(i), ref[i - lo])

            lax.fori_loop(lo, jnp.minimum(n, lo + size), early, None)
        if sz.rest > 0:
            def late(i, _, s=s):
                copy = pltpu.make_async_copy(rests[s].at[i - sz.first], spare, sem)
                copy.start()
                copy.wait()
                add(where_to(i), spare[...])

            lax.fori_loop(sz.first, n, late, None)


def finish_kernel(sz, plan, here, ahead, behind, late, *outs):
    for k in range(3):
        for a in range(sz.nb):
            at = plan[MINE_ROW, k * sz.nb + a]
            p = jnp.minimum(jnp.maximum(at - 1, 0), sz.keep - 1)
            value = here[p] + ahead[p].astype(jnp.float32) + behind[p].astype(jnp.float32)
            if sz.more > 0:
                q = jnp.minimum(jnp.maximum(at - 1 - sz.keep, 0), sz.more - 1)
                value = jnp.where(at > sz.keep, late[q].astype(jnp.float32), value)
            outs[k][0, a] = jnp.where(at > 0, value, 0.0).astype(jnp.bfloat16)


def spec(space):
    return pl.BlockSpec(memory_space=space)


ANY, HBM, VMEM, SMEM = pl.ANY, pltpu.HBM, pltpu.VMEM, pltpu.SMEM


def cost(flops, moved):
    return pl.CostEstimate(flops=flops, bytes_accessed=moved, transcendentals=0)


def call_plan(sz, where, counts, f, rank, blocks):
    bf = jnp.bfloat16
    return pl.pallas_call(
        functools.partial(plan_kernel, sz),
        out_shape=[
            jax.ShapeDtypeStruct((1, sz.lanes), jnp.int32),
            jax.ShapeDtypeStruct((sz.plan_rows, sz.lanes), jnp.int32),
            jax.ShapeDtypeStruct((sz.keep, BLK, BLK), bf),
            jax.ShapeDtypeStruct((max(sz.more, 1), BLK, BLK), bf),
            jax.ShapeDtypeStruct((max(sz.blocks - sz.main, 1), BLK, BLK), bf),
        ],
        in_specs=[spec(VMEM)] * 3 + [spec(SMEM)] * 3 + [spec(VMEM)] * 3,
        out_specs=[spec(VMEM)] * 4 + [spec(ANY)],
        compiler_params=pltpu.CompilerParams(vmem_limit_bytes=SMALL),
        cost_estimate=cost(1_000_000, 4_000_000),
        name="plan",
    )(*where, counts, f, rank, *blocks)


def call_recv(sz, own, plan, raws, after):
    return pl.pallas_call(
        functools.partial(recv_kernel, sz),
        out_shape=[
            jax.ShapeDtypeStruct((sz.recv_rows, sz.lanes), jnp.int32),
            jax.ShapeDtypeStruct((1, 1), jnp.int32),
        ],
        in_specs=[spec(VMEM)] * (2 + len(raws)) + [spec(ANY)] * len(after),
        out_specs=[spec(VMEM)] * 2,
        compiler_params=pltpu.CompilerParams(vmem_limit_bytes=SMALL),
        cost_estimate=cost(1_000_000, 4_000_000),
        name="recv",
    )(own, plan, *raws, *after)


def turn_kernel(flag, *refs):
    refs[-1][...] = flag[...]


def call_turn(flag, sent, arrived):
    return pl.pallas_call(
        turn_kernel,
        out_shape=[jax.ShapeDtypeStruct(sent.shape, sent.dtype), jax.ShapeDtypeStruct(flag.shape, flag.dtype)],
        in_specs=[spec(VMEM)] + [spec(ANY)] * (1 + len(arrived)),
        out_specs=[spec(ANY), spec(VMEM)],
        input_output_aliases={1: 0},
        compiler_params=pltpu.CompilerParams(vmem_limit_bytes=SMALL),
        cost_estimate=cost(1000, 1000),
        name="turn",
    )(flag, sent, *arrived)


def call_compute(sz, plan, tokens, cot, spilled, chunks):
    T = sz.n_tensor
    bf, f32 = jnp.bfloat16, jnp.float32

    def blocks(n):
        return jax.ShapeDtypeStruct((max(n, 1), BLK, BLK), bf)

    out_shape = [
        blocks(sz.ring * sz.keep),
        blocks(sz.far * sz.keep),
        blocks((sz.ring - sz.far) * sz.keep),
        blocks(sz.blocks - sz.main),
        blocks(sz.more),
    ]
    for _, n in sz.parts:
        out_shape += [blocks(n)] * T
    out_shape += [blocks(sz.rest)] * T
    scratch = [
        ((3 * sz.room, sz.tok, BLK), bf),
        ((sz.blocks + 1, BLK, BLK), bf),
        ((sz.blocks + 1, BLK, BLK), bf),
        ((sz.slots + 1, sz.tok, BLK), f32),
        ((sz.slots + 1, sz.tok, BLK), f32),
        ((sz.slots + 1, sz.tok, BLK), f32),
        ((sz.slots + 1, sz.tok, BLK), bf),
        ((sz.slots + 1, sz.tok, BLK), bf),
        ((sz.slots + 1, sz.tok, BLK), bf),
        ((sz.all + 1, sz.tok, BLK), f32),
        ((T * sz.send_all, sz.tok, BLK), bf),
    ]
    held = sum(s[0] * s[1] * s[2] * jnp.dtype(t).itemsize for s, t in scratch)
    return pl.pallas_call(
        functools.partial(compute_kernel, sz),
        out_shape=out_shape,
        in_specs=[spec(SMEM)] + [spec(HBM)] * 2 + [spec(ANY)] * (1 + len(chunks)),
        out_specs=[spec(ANY)] * len(out_shape),
        scratch_shapes=[pltpu.VMEM(s, t) for s, t in scratch] + [
            pltpu.SemaphoreType.DMA((3 * sz.room,)),
            pltpu.SemaphoreType.DMA((max(len(chunks), 3 + T * len(sz.parts)),)),
            pltpu.SemaphoreType.DMA((T + 1,)),
        ],
        compiler_params=pltpu.CompilerParams(vmem_limit_bytes=held + 2 * 1024 * 1024),
        cost_estimate=cost(1_000_000_000, 20_000_000),
        name="compute",
    )(plan, pltpu.with_memory_space_constraint(tokens, HBM), pltpu.with_memory_space_constraint(cot, HBM), spilled, *chunks)


def call_join(sz, plan, recv, firsts, rests):
    half = jax.ShapeDtypeStruct((sz.tok, sz.width // sz.n_tensor), jnp.bfloat16)
    return pl.pallas_call(
        functools.partial(join_kernel, sz),
        out_shape=[half, half],
        in_specs=[spec(SMEM)] * 2 + [spec(VMEM)] * len(firsts) + [spec(ANY)] * len(rests),
        out_specs=[spec(VMEM), spec(VMEM)],
        scratch_shapes=[pltpu.VMEM((sz.tok, BLK), jnp.bfloat16), pltpu.SemaphoreType.DMA],
        compiler_params=pltpu.CompilerParams(vmem_limit_bytes=10 * 1024 * 1024),
        cost_estimate=cost(1_000_000, 6_000_000),
        name="join",
    )(plan, recv, *firsts, *rests)


def call_finish(sz, plan, here, ahead, behind, late):
    out = jax.ShapeDtypeStruct((1, sz.nb, BLK, BLK), jnp.bfloat16)
    return pl.pallas_call(
        functools.partial(finish_kernel, sz),
        out_shape=[out] * 3,
        in_specs=[spec(SMEM)] + [spec(VMEM)] * 4,
        out_specs=[spec(VMEM)] * 3,
        compiler_params=pltpu.CompilerParams(vmem_limit_bytes=SMALL),
        cost_estimate=cost(1_000_000, 1_000_000),
        name="finish",
    )(plan, here, ahead, behind, late)


def gather_chunks(sz, chunk):
    ahead, behind, swap = permutations(sz)
    same = {0: chunk}
    a = b = chunk
    for s in range(1, sz.top):
        a, b = lax.ppermute(a, "fsdp", ahead), lax.ppermute(b, "fsdp", behind)
        same[sz.ring - s], same[s] = a, b
    other = {d: lax.ppermute(same[d], "fsdp", swap) for d in same}
    same[sz.top] = lax.ppermute(a, "fsdp", ahead)
    other[sz.top] = lax.ppermute(a, "fsdp", [(i, j ^ 1) for i, j in ahead])
    return [side[d] for side in (same, other) for d in sz.order]


def reduce_parts(sz, per, same, pair, beside=lambda s, a: a):
    ahead, behind, _ = permutations(sz)

    def wide(d, *more):
        j = sz.order.index(d)
        out = same[j * per:(j + 1) * per].astype(jnp.float32) + pair(j).astype(jnp.float32)
        for m in more:
            out = out + m.astype(jnp.float32)
        return out

    def term(d, *more):
        return wide(d, *more).astype(jnp.bfloat16)

    a, b = term(sz.top), term(sz.top + 1)
    for s in range(1, sz.top + 1):
        if s < sz.top:
            a, b = lax.optimization_barrier((a, b))
        a = beside(s, a)
        a = lax.ppermute(a, "fsdp", ahead)
        if s < sz.top:
            b = lax.ppermute(b, "fsdp", behind)
            a = term(sz.top - s, a)
            if s + 1 < sz.top:
                b = term(sz.top + 1 + s, b)
    return wide(0), a, b


def shards(
    tokens,
    cotangent,
    gate_blocks,
    up_blocks,
    down_blocks,
    gate_where,
    up_where,
    down_where,
    block_counts,
):
    n_fsdp, T = lax.axis_size("fsdp"), lax.axis_size("tensor")
    sz = Sizes(tokens, gate_blocks, gate_where.shape[1], n_fsdp, T)
    f, rank = lax.axis_index("fsdp"), lax.axis_index("tensor")
    _, _, swap = permutations(sz)

    own, plan, chunk, spill_own, spilled = call_plan(
        sz, (gate_where, up_where, down_where), block_counts.reshape(3), f.astype(jnp.int32).reshape(1),
        rank.astype(jnp.int32).reshape(1), (gate_blocks, up_blocks, down_blocks))
    raws = [lax.ppermute(own, "tensor", [(i, (i + s) % T) for i in range(T)]) for s in range(1, T)]
    chunks = gather_chunks(sz, chunk)
    recv, flag = call_recv(sz, own, plan, raws, [chunks[0]] + chunks[sz.ring:])
    if sz.more > 0:
        spilled = lax.cond(
            flag[0, 0] > 0, lambda x, _: jnp.concatenate(gather_chunks(sz, x)), lambda _, y: y, spill_own, spilled)

    outs = call_compute(sz, plan, tokens, cotangent, spilled, chunks)
    same, far, near, extra, idle = outs[:5]
    n_first = T * len(sz.parts)
    firsts, rests = outs[5:5 + n_first], list(outs[5 + n_first:])

    def exchange(arrays):
        return [arrays[0]] + [
            lax.ppermute(arrays[s], "tensor", [(i, (i + s) % T) for i in range(T)]) for s in range(1, T)]

    far, near = lax.ppermute(far, "fsdp", swap), lax.ppermute(near, "fsdp", swap)
    firsts = [exchange(firsts[j * T:(j + 1) * T]) for j in range(len(sz.parts))]

    def pair(j):
        at = j * sz.keep
        return far[at:at + sz.keep] if j < sz.far else near[at - sz.far * sz.keep:][:sz.keep]

    late = idle

    def beside(s, a):
        nonlocal rests, late
        over = flag
        part = s - 1 - sz.top + len(sz.parts)
        if part >= 0:
            a, over = call_turn(flag, a, firsts[part][1:])
        if s < sz.top or sz.rest + sz.more == 0:
            return a

        def spill(rests, extra, idle):
            moved = exchange(rests)
            if sz.more == 0:
                return moved, idle
            n = sz.ring * sz.more
            other = lax.ppermute(extra[n:], "fsdp", swap)
            terms = reduce_parts(sz, sz.more, extra[:n], lambda j: other[j * sz.more:(j + 1) * sz.more])
            return moved, sum(t.astype(jnp.float32) for t in terms).astype(jnp.bfloat16)

        rests, late = lax.cond(over[0, 0] > 0, spill, lambda r, e, i: (r, i), rests, extra, idle)
        return a

    here, ahead, behind = reduce_parts(sz, sz.keep, same, pair, beside)
    outputs, input_grads = call_join(sz, plan, recv, sum(firsts, []), rests)
    grads = call_finish(sz, plan, here, ahead, behind, late)
    return (outputs, input_grads, *grads)


def solution(mesh):
    placed = (
        P("fsdp", None),
        P("fsdp", None),
        P("tensor", "fsdp", None, None),
        P("tensor", "fsdp", None, None),
        P("tensor", "fsdp", None, None),
        P("tensor", None),
        P("tensor", None),
        P("tensor", None),
        P(None, "tensor"),
    )
    return jax.shard_map(
        shards,
        mesh=mesh,
        in_specs=placed,
        out_specs=(
            P("fsdp", "tensor"),
            P("fsdp", "tensor"),
            P("tensor", "fsdp", None, None),
            P("tensor", "fsdp", None, None),
            P("tensor", "fsdp", None, None),
        ),
        check_vma=False,
    )
```

```python
import functools

import jax
import jax.numpy as jnp
from jax import lax
from jax.experimental import pallas as pl
from jax.experimental.pallas import tpu as pltpu
from jax.sharding import PartitionSpec as P

FF = 14336
BLK = 128
GROUP = 4
FIRST_SEND = 16
FIRST_GRADS = 4
SMALL = 4 * 1024 * 1024
PLACE, PART, STRIP, CIDX, CWAS, OIDX, OWAS = range(7)
FIELDS = 7
COLS_ROW = 3 * FIELDS
HEAD_ROW = COLS_ROW + 1
MINE_ROW = COLS_ROW + 2
LISTS_ROW = COLS_ROW + 3
HEAD_COLS, HEAD_OVER, HEAD_LISTS = 3, 4, 8


class Sizes:
    def __init__(self, tokens, gate_blocks, slots, n_fsdp, n_tensor):
        self.tok, self.width = tokens.shape
        self.n_fsdp, self.n_tensor = n_fsdp, n_tensor
        self.rb = self.width // BLK
        self.cb = FF // (BLK * n_tensor)
        self.slots = slots
        self.all = 3 * slots
        self.lanes = -(-(self.all + GROUP) // 128) * 128
        self.nb = gate_blocks.shape[1]
        self.chunk = 3 * self.nb
        self.ring = n_fsdp // 2
        self.top = self.ring // 2
        self.rbt = self.rb // n_tensor
        self.order = [self.top]
        for d in range(1, self.top):
            self.order += [self.top + d, self.top - d]
        self.order.append(0)
        self.far = min(4, self.ring - 1)
        sparse = slots < self.cb
        self.keep = min(FIRST_GRADS, self.chunk) if sparse else self.chunk
        self.more = self.chunk - self.keep
        self.send_all = 2 * self.rbt
        self.first = min(FIRST_SEND, self.send_all) if sparse else self.send_all
        self.rest = self.send_all - self.first
        self.blocks = 2 * self.ring * self.chunk
        self.main = 2 * self.ring * self.keep
        self.plan_rows = -(-(LISTS_ROW + 2 * n_tensor) // 8) * 8
        self.recv_rows = -(-n_tensor // 8) * 8
        self.room = slots + GROUP


def permutations(sz):
    seq = list(range(0, sz.ring, 2)) + list(range(sz.ring - 1, 0, -2))
    ahead, behind, far, swap = [], [], [], []
    for i, q in enumerate(seq):
        up, down = seq[(i + 1) % sz.ring], seq[i - 1]
        far += [(q * 2, seq[(i + 2) % sz.ring] * 2), (q * 2 + 1, seq[i - 2] * 2 + 1)]
        ahead += [(q * 2, up * 2), (q * 2 + 1, down * 2 + 1)]
        behind += [(q * 2, down * 2), (q * 2 + 1, up * 2 + 1)]
        swap += [(q * 2, q * 2 + 1), (q * 2 + 1, q * 2)]
    return ahead, behind, far, swap


def ratio(x, d):
    return jnp.floor((x + 0.5) * (1.0 / d))


def rest_of(x, d):
    return x - d * ratio(x, d)


def ring_position(sz, chip):
    return jnp.where(rest_of(chip, 2) == 0, ratio(chip, 2), sz.ring - 1 - ratio(chip, 2))


class Marks:
    def __init__(self, sz, own, raw):
        N, L, S = sz.all, sz.lanes, sz.slots
        f32 = jnp.float32
        self.sz = sz
        self.sub = lax.broadcasted_iota(jnp.int32, (N, L), 0)
        self.lane = lax.broadcasted_iota(jnp.int32, (N, L), 1)
        self.same = self.sub == self.lane
        sub_c = self.sub[:, :1].astype(f32)
        lane_r = lax.broadcasted_iota(jnp.int32, (1, L), 1).astype(f32)
        self.sub_c, self.lane_r = sub_c, lane_r
        raw_r = raw[...].astype(f32)
        own_r = own[...].astype(f32)

        def single(row, at):
            return jnp.sum(jnp.where(lane_r == at, row, 0.0), axis=1, keepdims=True)

        self.f, self.rank = single(own_r, N + 3), single(own_r, N + 4)

        def kind(x):
            return (x >= S).astype(f32) + (x >= 2 * S).astype(f32)

        self.kind_c, self.kind_r = kind(sub_c), kind(lane_r)
        self.n_r = lane_r - S * self.kind_r
        self.n_c = sub_c - S * self.kind_c
        limit = jnp.zeros((1, L), f32)
        for k in range(3):
            limit = limit + jnp.where(self.kind_r == k, single(raw_r, N + k), 0.0)
        live_r = jnp.where((lane_r < N) & (self.n_r < limit), 1.0, 0.0)
        w_c = self.col(raw_r)
        live_c = self.col(live_r)

        def place(w, k):
            gate, down = ratio(w, sz.cb), ratio(w, sz.rb)
            is_down = k == 2
            return jnp.where(is_down, w - down * sz.rb, gate), jnp.where(is_down, down, w - gate * sz.cb)

        self.row_c, col_c = place(w_c, self.kind_c)
        self.row_r, col_r = place(raw_r, self.kind_r)
        self.owner_c, self.owner_r = ratio(self.n_c, sz.nb), ratio(self.n_r, sz.nb)
        self.same_col = (col_c == col_r).astype(f32)
        act_c, act_r = live_c, live_r
        for k in range(3):
            lanes = self.same_col * (live_r * (self.kind_r == k).astype(f32))
            act_c = act_c * jnp.max(lanes, axis=1, keepdims=True)
            subs = self.same_col * (live_c * (self.kind_c == k).astype(f32))
            act_r = act_r * jnp.max(subs, axis=0, keepdims=True)
        self.act_c, self.act_r = act_c, act_r
        out_c = jnp.where(self.kind_c == 2, 0.0, f32(sz.rb)) + self.row_c
        out_r = jnp.where(self.kind_r == 2, 0.0, f32(sz.rb)) + self.row_r
        self.same_out = (out_c == out_r).astype(f32)
        self.before = (self.lane < self.sub).astype(f32)
        self.after = (self.sub < self.lane).astype(f32)
        self.owas_c = jnp.max(self.same_out * self.before * act_r, axis=1, keepdims=True)
        self.owas_r = jnp.max(self.same_out * self.after * act_c, axis=0, keepdims=True)
        self.lead_c = act_c * (1.0 - self.owas_c)
        self.lead_r = act_r * (1.0 - self.owas_r)
        self.owned = (self.owner_c == self.owner_r).astype(f32)

        def shift(row):
            away = ratio(row, sz.rbt) - self.rank
            return jnp.where(away < 0, away + sz.n_tensor, away)

        self.shift_c, self.shift_r = shift(self.row_c), shift(self.row_r)
        self.local_c = jnp.where(self.kind_c == 2, 0.0, f32(sz.rbt)) + rest_of(self.row_c, sz.rbt)

    def col(self, row):
        return jnp.sum(jnp.where(self.same, row, 0.0), axis=1, keepdims=True)

    def base_c(self):
        sz = self.sz
        away = ring_position(sz, ratio(self.owner_c, 2)) - ring_position(sz, ratio(self.f, 2))
        away = jnp.where(rest_of(self.owner_c, 2) == 0, away, -away)
        rel = jnp.where(away < 0, away + sz.ring, away)
        j = jnp.where(rel > sz.top, 2 * (rel - sz.top) - 1, 2 * (sz.top - rel))
        j = jnp.where(rel == 0, sz.ring - 1.0, j)
        return j + jnp.where(rest_of(self.owner_c, 2) == rest_of(self.f, 2), 0.0, float(sz.ring))

    def ranks(self, chosen_r):
        return jnp.sum(self.before * chosen_r, axis=1, keepdims=True)

    def listed(self, chosen_c, rank_c, value_c, lo=0, hi=None):
        at = rank_c[lo:hi] == self.lane[lo:hi].astype(jnp.float32)
        return jnp.sum(jnp.where(at, chosen_c[lo:hi] * value_c[lo:hi], 0.0), axis=0, keepdims=True)

    def most_owned(self):
        return jnp.max(jnp.sum(self.owned * self.act_r, axis=1, keepdims=True), axis=0, keepdims=True)


def total(x):
    return jnp.sum(x, axis=0, keepdims=True)


def head_row(sz, entries):
    lane = lax.broadcasted_iota(jnp.int32, (1, sz.lanes), 1)
    row = jnp.zeros((1, sz.lanes), jnp.float32)
    for i, value in entries:
        row = jnp.where(lane == i, value, row)
    return row


def plan_kernel(sz, own, plan):
    S, N = sz.slots, sz.all
    m = Marks(sz, own, own)
    f32 = jnp.float32
    lane_r, sub_c = m.lane_r, m.sub_c
    same_kind = (m.kind_c == m.kind_r).astype(f32)
    rank_c = jnp.sum(m.before * same_kind * m.act_r, axis=1, keepdims=True)
    cwas_c = jnp.max(m.before * same_kind * m.same_col * m.act_r, axis=1, keepdims=True)
    cwas_r = jnp.max(m.after * same_kind * m.same_col * m.act_c, axis=0, keepdims=True)
    big = f32(4 * N)
    lanes_f = m.lane.astype(f32)
    gates_r = m.act_r * (m.kind_r == 0).astype(f32)
    cidx_c = jnp.min(jnp.where(m.same_col * gates_r > 0, lanes_f, big), axis=1, keepdims=True)
    oidx_c = jnp.min(jnp.where(m.same_out * m.act_r > 0, lanes_f, big), axis=1, keepdims=True)
    pos_c = jnp.sum(m.before * m.owned * m.act_r, axis=1, keepdims=True)
    base_c = m.base_c()
    place_c = base_c * sz.chunk + m.kind_c * sz.nb + rest_of(m.n_c, sz.nb)
    part_c = jnp.where(
        pos_c < sz.keep, base_c * sz.keep + pos_c, sz.main + base_c * sz.more + pos_c - sz.keep)
    fields = [
        (place_c, sz.blocks), (part_c, sz.blocks), (m.row_c, 0), (cidx_c, S), (cwas_c, 0), (oidx_c, N), (m.owas_c, 0)]
    rows = []
    head = []
    for k in range(3):
        lo, hi = k * S, (k + 1) * S
        n_k = total(m.act_c[lo:hi])
        head.append((k, n_k))
        for value, spare in fields:
            row = m.listed(m.act_c, rank_c, value, lo, hi)
            rows.append(jnp.where(lane_r < n_k, row, f32(spare)))
    leader_c = m.act_c * (1.0 - cwas_c) * (m.kind_c == 0).astype(f32)
    leader_r = m.act_r * (1.0 - cwas_r) * (m.kind_r == 0).astype(f32)
    rows.append(m.listed(leader_c, m.ranks(leader_r), sub_c, 0, S))
    head.append((HEAD_COLS, total(leader_c)))
    over = (m.most_owned() > sz.keep).astype(f32)
    lists = []
    for s in range(sz.n_tensor):
        chosen_c = m.lead_c * (m.shift_c == s).astype(f32)
        chosen_r = m.lead_r * (m.shift_r == s).astype(f32)
        rank = m.ranks(chosen_r)
        lists.append(m.listed(chosen_c, rank, sub_c))
        lists.append(m.listed(chosen_c, rank, m.local_c))
        n = total(chosen_c)
        head.append((HEAD_LISTS + s, n))
        over = jnp.maximum(over, (n > sz.first).astype(f32))
    head.append((HEAD_OVER, over))
    rows.append(head_row(sz, head))
    mine = sub_c == ratio(lane_r, sz.nb) * S + m.f * sz.nb + rest_of(lane_r, sz.nb)
    rows.append(jnp.sum(jnp.where(mine, m.act_c * (pos_c + 1.0), 0.0), axis=0, keepdims=True))
    rows += lists
    for i, row in enumerate(rows):
        plan[i:i + 1, :] = row.astype(jnp.int32)


def recv_kernel(sz, *refs):
    own, plan, raws, recv, flag = refs[0], refs[1], refs[2:-2], refs[-2], refs[-1]
    f32 = jnp.float32
    head = []
    over = jnp.zeros((1, 1), f32)
    for s, raw in enumerate(raws, 1):
        m = Marks(sz, own, raw)
        chosen_c = m.lead_c * (m.shift_c == 0).astype(f32)
        chosen_r = m.lead_r * (m.shift_r == 0).astype(f32)
        recv[s:s + 1, :] = m.listed(chosen_c, m.ranks(chosen_r), m.local_c).astype(jnp.int32)
        head.append((HEAD_LISTS + s, total(chosen_c)))
        over = jnp.maximum(over, (m.most_owned() > sz.keep).astype(f32))
        for d in range(sz.n_tensor):
            n = total(m.lead_c * (m.shift_c == d).astype(f32))
            over = jnp.maximum(over, (n > sz.first).astype(f32))
    known = plan[HEAD_ROW:HEAD_ROW + 1, HEAD_OVER:HEAD_OVER + 1]
    flag[...] = jnp.maximum(known, over.astype(jnp.int32))
    recv[0:1, :] = head_row(sz, head).astype(jnp.int32)


def dot(a, b, ca, cb):
    return lax.dot_general(a, b, (((ca,), (cb,)), ((), ())), preferred_element_type=jnp.float32)


def compute_kernel(sz, *refs):
    plan, tokens, cot = refs[:3]
    n_chunks = 2 * sz.ring
    chunks = refs[3:3 + n_chunks]
    refs = refs[3 + n_chunks:]
    T = sz.n_tensor
    same, far, near, extra, _ = refs[:5]
    firsts, rests = refs[5:5 + T], refs[5 + T:5 + 2 * T]
    (xs, wbuf, parts, gate_acc, up_acc, hg_acc, hid, gate_d, up_d, out_acc, stage, strip_sems, sems, rest_sems) = refs[5 + 2 * T:]

    def field(k, j, e):
        return plan[k * FIELDS + j, e]

    def steps(k):
        return (plan[HEAD_ROW, k] + (GROUP - 1)) // GROUP

    def strip_copy(k, e):
        src = cot if k == 2 else tokens
        cols = pl.ds(pl.multiple_of(field(k, STRIP, e) * BLK, BLK), BLK)
        return pltpu.make_async_copy(src.at[:, cols], xs.at[k * sz.room + e], strip_sems.at[k * sz.room + e])

    for k in range(3):
        lax.fori_loop(0, steps(k) * GROUP, lambda e, _, k=k: strip_copy(k, e).start(), None)
    loads = [
        pltpu.make_async_copy(chunk, wbuf.at[pl.ds(i * sz.chunk, sz.chunk)], sems.at[i])
        for i, chunk in enumerate(chunks)
    ]
    for c in loads:
        c.start()
    for k in range(3):
        lax.fori_loop(0, steps(k) * GROUP, lambda e, _, k=k: strip_copy(k, e).wait(), None)
    for c in loads:
        c.wait()

    def walk(k, body):
        lax.fori_loop(0, steps(k), lambda p, _: body(p * GROUP), None)

    def forward(k, acc, w_dim):
        def body(e0):
            prods = [
                dot(xs[k * sz.room + e0 + u], wbuf[field(k, PLACE, e0 + u)], 1, w_dim) for u in range(GROUP)]
            for u in range(GROUP):
                c = field(k, CIDX, e0 + u)
                acc[c] = prods[u] + jnp.where(field(k, CWAS, e0 + u) == 0, 0.0, acc[c])

        walk(k, body)

    forward(0, gate_acc, 0)
    forward(1, up_acc, 0)
    forward(2, hg_acc, 1)

    def column(i, _):
        c = plan[COLS_ROW, i]
        g, u, h = gate_acc[c], up_acc[c], hg_acc[c]
        s = lax.logistic(g)
        silu = g * s
        hid[c] = (silu * u).astype(jnp.bfloat16)
        gate_d[c] = (h * u * s * (1.0 + g * (1.0 - s))).astype(jnp.bfloat16)
        up_d[c] = (h * silu).astype(jnp.bfloat16)

    lax.fori_loop(0, plan[HEAD_ROW, HEAD_COLS], column, None)

    def backward(k, act, w_dim):
        def body(e0):
            terms, grads = [], []
            for u in range(GROUP):
                a = act[field(k, CIDX, e0 + u)]
                x = xs[k * sz.room + e0 + u]
                terms.append(dot(a, wbuf[field(k, PLACE, e0 + u)], 1, w_dim))
                grads.append(dot(a, x, 0, 0) if k == 2 else dot(x, a, 0, 0))
            for u in range(GROUP):
                parts[field(k, PART, e0 + u)] = grads[u].astype(jnp.bfloat16)
            for u in range(GROUP):
                at = field(k, OIDX, e0 + u)
                out_acc[at] = terms[u] + jnp.where(field(k, OWAS, e0 + u) == 0, 0.0, out_acc[at])

        walk(k, body)

    backward(2, hid, 0)
    backward(0, gate_d, 1)
    backward(1, up_d, 1)

    split = sz.ring * sz.keep
    cut = split + sz.far * sz.keep
    outs = [
        pltpu.make_async_copy(parts.at[pl.ds(split, cut - split)], far, sems.at[0]),
        pltpu.make_async_copy(parts.at[pl.ds(0, split)], same, sems.at[1]),
        pltpu.make_async_copy(parts.at[pl.ds(cut, sz.main - cut)], near, sems.at[2]),
    ]
    for c in outs:
        c.start()

    for s in range(T):
        def staged(i, _, s=s):
            stage[s * sz.send_all + i] = out_acc[plan[LISTS_ROW + 2 * s, i]].astype(jnp.bfloat16)

        lax.fori_loop(0, plan[HEAD_ROW, HEAD_LISTS + s], staged, None)
        first = pltpu.make_async_copy(stage.at[pl.ds(s * sz.send_all, sz.first)], firsts[s], sems.at[3 + s])
        first.start()
        outs.append(first)

    if sz.rest + sz.more > 0:
        @pl.when(plan[HEAD_ROW, HEAD_OVER] > 0)
        def _():
            copies = []
            if sz.rest > 0:
                copies += [
                    pltpu.make_async_copy(
                        stage.at[pl.ds(s * sz.send_all + sz.first, sz.rest)], rests[s], rest_sems.at[s])
                    for s in range(T)
                ]
            if sz.more > 0:
                copies.append(pltpu.make_async_copy(
                    parts.at[pl.ds(sz.main, sz.blocks - sz.main)], extra, rest_sems.at[T]))
            for c in copies:
                c.start()
            for c in copies:
                c.wait()
    for c in outs:
        c.wait()


def join_kernel(sz, *refs):
    T = sz.n_tensor
    plan, recv = refs[:2]
    firsts, rests = refs[2:2 + T], refs[2 + T:2 + 2 * T]
    outputs, input_grads, spare, sem = refs[-4:]
    outputs[...] = jnp.zeros_like(outputs)
    input_grads[...] = jnp.zeros_like(input_grads)

    def add(at, value):
        def into(ref, w):
            cols = pl.ds(pl.multiple_of(w * BLK, BLK), BLK)
            ref[:, cols] = (ref[:, cols].astype(jnp.float32) + value.astype(jnp.float32)).astype(jnp.bfloat16)

        @pl.when(at < sz.rbt)
        def _():
            into(outputs, at)

        @pl.when(at >= sz.rbt)
        def _():
            into(input_grads, at - sz.rbt)

    for s in range(T):
        n = (recv[0, HEAD_LISTS + s] if s else plan[HEAD_ROW, HEAD_LISTS])

        def where_to(i, s=s):
            return recv[s, i] if s else plan[LISTS_ROW + 1, i]

        def early(i, _, s=s):
            add(where_to(i), firsts[s][i])

        lax.fori_loop(0, jnp.minimum(n, sz.first), early, None)
        if sz.rest > 0:
            def late(i, _, s=s):
                copy = pltpu.make_async_copy(rests[s].at[i - sz.first], spare, sem)
                copy.start()
                copy.wait()
                add(where_to(i), spare[...])

            lax.fori_loop(jnp.minimum(n, sz.first), n, late, None)


def finish_kernel(sz, plan, here, ahead, behind, late, *outs):
    for k in range(3):
        for a in range(sz.nb):
            at = plan[MINE_ROW, k * sz.nb + a]
            p = jnp.minimum(jnp.maximum(at - 1, 0), sz.keep - 1)
            value = here[p] + ahead[p].astype(jnp.float32) + behind[p].astype(jnp.float32)
            if sz.more > 0:
                q = jnp.minimum(jnp.maximum(at - 1 - sz.keep, 0), sz.more - 1)
                value = jnp.where(at > sz.keep, late[q].astype(jnp.float32), value)
            outs[k][0, a] = jnp.where(at > 0, value, 0.0).astype(jnp.bfloat16)


def spec(space):
    return pl.BlockSpec(memory_space=space)


ANY, HBM, VMEM, SMEM = pl.ANY, pltpu.HBM, pltpu.VMEM, pltpu.SMEM


def cost(flops, moved):
    return pl.CostEstimate(flops=flops, bytes_accessed=moved, transcendentals=0)


def call_plan(sz, own):
    return pl.pallas_call(
        functools.partial(plan_kernel, sz),
        out_shape=jax.ShapeDtypeStruct((sz.plan_rows, sz.lanes), jnp.int32),
        in_specs=[spec(VMEM)],
        out_specs=spec(VMEM),
        compiler_params=pltpu.CompilerParams(vmem_limit_bytes=SMALL),
        cost_estimate=cost(1_000_000, 4_000_000),
        name="plan",
    )(own)


def call_recv(sz, own, plan, raws):
    return pl.pallas_call(
        functools.partial(recv_kernel, sz),
        out_shape=[
            jax.ShapeDtypeStruct((sz.recv_rows, sz.lanes), jnp.int32),
            jax.ShapeDtypeStruct((1, 1), jnp.int32),
        ],
        in_specs=[spec(VMEM)] * (2 + len(raws)),
        out_specs=[spec(VMEM)] * 2,
        compiler_params=pltpu.CompilerParams(vmem_limit_bytes=SMALL),
        cost_estimate=cost(1_000_000, 4_000_000),
        name="recv",
    )(own, plan, *raws)


def call_turn(handed, arrived):
    return pl.pallas_call(
        lambda *_: None,
        out_shape=[jax.ShapeDtypeStruct(x.shape, x.dtype) for x in handed],
        in_specs=[spec(ANY)] * (len(handed) + len(arrived)),
        out_specs=[spec(ANY)] * len(handed),
        input_output_aliases={i: i for i in range(len(handed))},
        compiler_params=pltpu.CompilerParams(vmem_limit_bytes=SMALL),
        cost_estimate=cost(1000, 1000),
        name="turn",
    )(*handed, *arrived)


def call_compute(sz, plan, tokens, cot, chunks):
    T = sz.n_tensor
    bf, f32 = jnp.bfloat16, jnp.float32

    def blocks(n):
        return jax.ShapeDtypeStruct((max(n, 1), BLK, BLK), bf)

    out_shape = [
        blocks(sz.ring * sz.keep),
        blocks(sz.far * sz.keep),
        blocks((sz.ring - sz.far) * sz.keep),
        blocks(sz.blocks - sz.main),
        blocks(sz.more),
    ]
    out_shape += [blocks(sz.first)] * T + [blocks(sz.rest)] * T
    scratch = [
        ((3 * sz.room, sz.tok, BLK), bf),
        ((sz.blocks + 1, BLK, BLK), bf),
        ((sz.blocks + 1, BLK, BLK), bf),
        ((sz.slots + 1, sz.tok, BLK), f32),
        ((sz.slots + 1, sz.tok, BLK), f32),
        ((sz.slots + 1, sz.tok, BLK), f32),
        ((sz.slots + 1, sz.tok, BLK), bf),
        ((sz.slots + 1, sz.tok, BLK), bf),
        ((sz.slots + 1, sz.tok, BLK), bf),
        ((sz.all + 1, sz.tok, BLK), f32),
        ((T * sz.send_all, sz.tok, BLK), bf),
    ]
    held = sum(s[0] * s[1] * s[2] * jnp.dtype(t).itemsize for s, t in scratch)
    return pl.pallas_call(
        functools.partial(compute_kernel, sz),
        out_shape=out_shape,
        in_specs=[spec(SMEM)] + [spec(HBM)] * 2 + [spec(ANY)] * len(chunks),
        out_specs=[spec(ANY)] * len(out_shape),
        scratch_shapes=[pltpu.VMEM(s, t) for s, t in scratch] + [
            pltpu.SemaphoreType.DMA((3 * sz.room,)),
            pltpu.SemaphoreType.DMA((max(len(chunks), 3 + T),)),
            pltpu.SemaphoreType.DMA((T + 1,)),
        ],
        compiler_params=pltpu.CompilerParams(vmem_limit_bytes=held + 2 * 1024 * 1024),
        cost_estimate=cost(1_000_000_000, 20_000_000),
        name="compute",
    )(plan, pltpu.with_memory_space_constraint(tokens, HBM), pltpu.with_memory_space_constraint(cot, HBM), *chunks)


def call_join(sz, plan, recv, firsts, rests):
    half = jax.ShapeDtypeStruct((sz.tok, sz.width // sz.n_tensor), jnp.bfloat16)
    return pl.pallas_call(
        functools.partial(join_kernel, sz),
        out_shape=[half, half],
        in_specs=[spec(SMEM)] * 2 + [spec(VMEM)] * len(firsts) + [spec(ANY)] * len(rests),
        out_specs=[spec(VMEM), spec(VMEM)],
        scratch_shapes=[pltpu.VMEM((sz.tok, BLK), jnp.bfloat16), pltpu.SemaphoreType.DMA],
        compiler_params=pltpu.CompilerParams(vmem_limit_bytes=10 * 1024 * 1024),
        cost_estimate=cost(1_000_000, 6_000_000),
        name="join",
    )(plan, recv, *firsts, *rests)


def call_finish(sz, plan, here, ahead, behind, late):
    out = jax.ShapeDtypeStruct((1, sz.nb, BLK, BLK), jnp.bfloat16)
    return pl.pallas_call(
        functools.partial(finish_kernel, sz),
        out_shape=[out] * 3,
        in_specs=[spec(SMEM)] + [spec(VMEM)] * 4,
        out_specs=[spec(VMEM)] * 3,
        compiler_params=pltpu.CompilerParams(vmem_limit_bytes=SMALL),
        cost_estimate=cost(1_000_000, 1_000_000),
        name="finish",
    )(plan, here, ahead, behind, late)


def gather_chunks(sz, chunk):
    ahead, behind, far, swap = permutations(sz)
    same, other = {0: chunk}, {}
    a = b = chunk
    for s in range(1, sz.top):
        if s == sz.top - 1:
            same[sz.top] = lax.ppermute(a, "fsdp", far)
            other[sz.top] = lax.ppermute(a, "fsdp", [(i, j ^ 1) for i, j in far])
        a, b = lax.ppermute(a, "fsdp", ahead), lax.ppermute(b, "fsdp", behind)
        same[sz.ring - s], same[s] = a, b
    for d in same:
        if d != sz.top:
            other[d] = lax.ppermute(same[d], "fsdp", swap)
    return [side[d] for side in (same, other) for d in sz.order]


def reduce_parts(sz, per, same, pair, beside=lambda s, a, b: (a, b)):
    ahead, behind, far, _ = permutations(sz)

    def wide(d, *more):
        j = sz.order.index(d)
        out = same[j * per:(j + 1) * per].astype(jnp.float32) + pair(j).astype(jnp.float32)
        for m in more:
            out = out + m.astype(jnp.float32)
        return out

    def term(d, *more):
        return wide(d, *more).astype(jnp.bfloat16)

    c, a, b = lax.optimization_barrier((term(sz.top), term(sz.top - 1), term(sz.top + 1)))
    c = lax.ppermute(c, "fsdp", far)
    for s in range(1, sz.top):
        if s > 1:
            a = term(sz.top - s, a, c) if s == 2 else term(sz.top - s, a)
            b = term(sz.top + s, b)
            a, b = beside(s, *lax.optimization_barrier((a, b)))
        a, b = lax.ppermute(a, "fsdp", ahead), lax.ppermute(b, "fsdp", behind)
    return wide(0), a, b


def shards(
    tokens,
    cotangent,
    gate_blocks,
    up_blocks,
    down_blocks,
    gate_where,
    up_where,
    down_where,
    block_counts,
):
    n_fsdp, T = lax.axis_size("fsdp"), lax.axis_size("tensor")
    sz = Sizes(tokens, gate_blocks, gate_where.shape[1], n_fsdp, T)
    f, rank = lax.axis_index("fsdp"), lax.axis_index("tensor")
    swap = permutations(sz)[-1]

    chunk = jnp.concatenate([gate_blocks[0], up_blocks[0], down_blocks[0]])
    own = jnp.concatenate([
        gate_where[0], up_where[0], down_where[0], block_counts[:, 0],
        f.astype(jnp.int32)[None], rank.astype(jnp.int32)[None]])
    own = jnp.pad(own, (0, sz.lanes - own.shape[0]))[None]

    plan = call_plan(sz, own)
    raws = [lax.ppermute(own, "tensor", [(i, (i + s) % T) for i in range(T)]) for s in range(1, T)]
    recv, flag = call_recv(sz, own, plan, raws)
    chunks = gather_chunks(sz, chunk)

    outs = call_compute(sz, plan, tokens, cotangent, chunks)
    same, far, near, extra, idle = outs[:5]
    firsts, rests = outs[5:5 + T], list(outs[5 + T:])

    def exchange(arrays):
        return [arrays[0]] + [
            lax.ppermute(arrays[s], "tensor", [(i, (i + s) % T) for i in range(T)]) for s in range(1, T)]

    far, near = lax.ppermute(far, "fsdp", swap), lax.ppermute(near, "fsdp", swap)
    firsts = exchange(firsts)

    def pair(j):
        at = j * sz.keep
        return far[at:at + sz.keep] if j < sz.far else near[at - sz.far * sz.keep:][:sz.keep]

    late = idle

    def beside(s, a, b):
        nonlocal rests, late
        if s != sz.top - 1:
            return a, b
        a, more = call_turn([a, extra], firsts[1:])
        if sz.rest + sz.more == 0:
            return a, b

        def spill(rests, extra, idle):
            moved = exchange(rests)
            if sz.more == 0:
                return moved, idle
            n = sz.ring * sz.more
            other = lax.ppermute(extra[n:], "fsdp", swap)
            terms = reduce_parts(sz, sz.more, extra[:n], lambda j: other[j * sz.more:(j + 1) * sz.more])
            return moved, sum(t.astype(jnp.float32) for t in terms).astype(jnp.bfloat16)

        rests, late = lax.cond(flag[0, 0] > 0, spill, lambda r, e, i: (r, i), rests, more, idle)
        return a, b

    here, ahead, behind = reduce_parts(sz, sz.keep, same, pair, beside)
    outputs, input_grads = call_join(sz, plan, recv, firsts, rests)
    grads = call_finish(sz, plan, here, ahead, behind, late)
    return (outputs, input_grads, *grads)


def solution(mesh):
    placed = (
        P("fsdp", None),
        P("fsdp", None),
        P("tensor", "fsdp", None, None),
        P("tensor", "fsdp", None, None),
        P("tensor", "fsdp", None, None),
        P("tensor", None),
        P("tensor", None),
        P("tensor", None),
        P(None, "tensor"),
    )
    return jax.shard_map(
        shards,
        mesh=mesh,
        in_specs=placed,
        out_specs=(
            P("fsdp", "tensor"),
            P("fsdp", "tensor"),
            P("tensor", "fsdp", None, None),
            P("tensor", "fsdp", None, None),
            P("tensor", "fsdp", None, None),
        ),
        check_vma=False,
    )
```

```python
import functools

import jax
import jax.numpy as jnp
from jax import lax
from jax.experimental import pallas as pl
from jax.experimental.pallas import tpu as pltpu
from jax.sharding import PartitionSpec as P

FF = 14336
BLK = 128
GROUP = 4
FIRST_SEND = 16
FIRST_GRADS = 4
SMALL = 4 * 1024 * 1024
PLACE, PART, STRIP, CIDX, CWAS, OIDX, OWAS = range(7)
FIELDS = 7
COLS_ROW = 3 * FIELDS
HEAD_ROW = COLS_ROW + 1
MINE_ROW = COLS_ROW + 2
LISTS_ROW = COLS_ROW + 3
HEAD_COLS, HEAD_OVER, HEAD_LISTS = 3, 4, 8


class Sizes:
    def __init__(self, tokens, gate_blocks, slots, n_fsdp, n_tensor):
        self.tok, self.width = tokens.shape
        self.n_fsdp, self.n_tensor = n_fsdp, n_tensor
        self.rb = self.width // BLK
        self.cb = FF // (BLK * n_tensor)
        self.slots = slots
        self.all = 3 * slots
        self.lanes = -(-(self.all + GROUP) // 128) * 128
        self.nb = gate_blocks.shape[1]
        self.chunk = 3 * self.nb
        self.ring = n_fsdp // 2
        self.top = self.ring // 2
        self.rbt = self.rb // n_tensor
        self.order = [self.top]
        for d in range(1, self.top):
            self.order += [self.top + d, self.top - d]
        self.order.append(0)
        self.far = min(4, self.ring - 1)
        sparse = slots < self.cb
        self.keep = min(FIRST_GRADS, self.chunk) if sparse else self.chunk
        self.more = self.chunk - self.keep
        self.send_all = 2 * self.rbt
        self.first = min(FIRST_SEND, self.send_all) if sparse else self.send_all
        self.rest = self.send_all - self.first
        self.blocks = 2 * self.ring * self.chunk
        self.main = 2 * self.ring * self.keep
        self.plan_rows = -(-(LISTS_ROW + 2 * n_tensor) // 8) * 8
        self.recv_rows = -(-n_tensor // 8) * 8
        self.room = slots + GROUP


def permutations(sz):
    seq = list(range(0, sz.ring, 2)) + list(range(sz.ring - 1, 0, -2))
    ahead, behind, far, swap = [], [], [], []
    for i, q in enumerate(seq):
        up, down = seq[(i + 1) % sz.ring], seq[i - 1]
        far += [(q * 2, seq[(i + 2) % sz.ring] * 2), (q * 2 + 1, seq[i - 2] * 2 + 1)]
        ahead += [(q * 2, up * 2), (q * 2 + 1, down * 2 + 1)]
        behind += [(q * 2, down * 2), (q * 2 + 1, up * 2 + 1)]
        swap += [(q * 2, q * 2 + 1), (q * 2 + 1, q * 2)]
    return ahead, behind, far, swap


def ratio(x, d):
    return jnp.floor((x + 0.5) * (1.0 / d))


def rest_of(x, d):
    return x - d * ratio(x, d)


def ring_position(sz, chip):
    return jnp.where(rest_of(chip, 2) == 0, ratio(chip, 2), sz.ring - 1 - ratio(chip, 2))


class Marks:
    def __init__(self, sz, own, raw):
        N, L, S = sz.all, sz.lanes, sz.slots
        f32 = jnp.float32
        self.sz = sz
        self.sub = lax.broadcasted_iota(jnp.int32, (N, L), 0)
        self.lane = lax.broadcasted_iota(jnp.int32, (N, L), 1)
        self.same = self.sub == self.lane
        sub_c = self.sub[:, :1].astype(f32)
        lane_r = lax.broadcasted_iota(jnp.int32, (1, L), 1).astype(f32)
        self.sub_c, self.lane_r = sub_c, lane_r
        raw_r = raw[...].astype(f32)
        own_r = own[...].astype(f32)

        def single(row, at):
            return jnp.sum(jnp.where(lane_r == at, row, 0.0), axis=1, keepdims=True)

        self.f, self.rank = single(own_r, N + 3), single(own_r, N + 4)

        def kind(x):
            return (x >= S).astype(f32) + (x >= 2 * S).astype(f32)

        self.kind_c, self.kind_r = kind(sub_c), kind(lane_r)
        self.n_r = lane_r - S * self.kind_r
        self.n_c = sub_c - S * self.kind_c
        limit = jnp.zeros((1, L), f32)
        for k in range(3):
            limit = limit + jnp.where(self.kind_r == k, single(raw_r, N + k), 0.0)
        live_r = jnp.where((lane_r < N) & (self.n_r < limit), 1.0, 0.0)
        w_c = self.col(raw_r)
        live_c = self.col(live_r)

        def place(w, k):
            gate, down = ratio(w, sz.cb), ratio(w, sz.rb)
            is_down = k == 2
            return jnp.where(is_down, w - down * sz.rb, gate), jnp.where(is_down, down, w - gate * sz.cb)

        self.row_c, col_c = place(w_c, self.kind_c)
        self.row_r, col_r = place(raw_r, self.kind_r)
        self.owner_c, self.owner_r = ratio(self.n_c, sz.nb), ratio(self.n_r, sz.nb)
        self.same_col = (col_c == col_r).astype(f32)
        act_c, act_r = live_c, live_r
        for k in range(3):
            lanes = self.same_col * (live_r * (self.kind_r == k).astype(f32))
            act_c = act_c * jnp.max(lanes, axis=1, keepdims=True)
            subs = self.same_col * (live_c * (self.kind_c == k).astype(f32))
            act_r = act_r * jnp.max(subs, axis=0, keepdims=True)
        self.act_c, self.act_r = act_c, act_r
        out_c = jnp.where(self.kind_c == 2, 0.0, f32(sz.rb)) + self.row_c
        out_r = jnp.where(self.kind_r == 2, 0.0, f32(sz.rb)) + self.row_r
        self.same_out = (out_c == out_r).astype(f32)
        self.before = (self.lane < self.sub).astype(f32)
        self.after = (self.sub < self.lane).astype(f32)
        self.owas_c = jnp.max(self.same_out * self.before * act_r, axis=1, keepdims=True)
        self.owas_r = jnp.max(self.same_out * self.after * act_c, axis=0, keepdims=True)
        self.lead_c = act_c * (1.0 - self.owas_c)
        self.lead_r = act_r * (1.0 - self.owas_r)
        self.owned = (self.owner_c == self.owner_r).astype(f32)

        def shift(row):
            away = ratio(row, sz.rbt) - self.rank
            return jnp.where(away < 0, away + sz.n_tensor, away)

        self.shift_c, self.shift_r = shift(self.row_c), shift(self.row_r)
        self.local_c = jnp.where(self.kind_c == 2, 0.0, f32(sz.rbt)) + rest_of(self.row_c, sz.rbt)

    def col(self, row):
        return jnp.sum(jnp.where(self.same, row, 0.0), axis=1, keepdims=True)

    def base_c(self):
        sz = self.sz
        away = ring_position(sz, ratio(self.owner_c, 2)) - ring_position(sz, ratio(self.f, 2))
        away = jnp.where(rest_of(self.owner_c, 2) == 0, away, -away)
        rel = jnp.where(away < 0, away + sz.ring, away)
        j = jnp.where(rel > sz.top, 2 * (rel - sz.top) - 1, 2 * (sz.top - rel))
        j = jnp.where(rel == 0, sz.ring - 1.0, j)
        return j + jnp.where(rest_of(self.owner_c, 2) == rest_of(self.f, 2), 0.0, float(sz.ring))

    def ranks(self, chosen_r):
        return jnp.sum(self.before * chosen_r, axis=1, keepdims=True)

    def listed(self, chosen_c, rank_c, value_c, lo=0, hi=None):
        at = rank_c[lo:hi] == self.lane[lo:hi].astype(jnp.float32)
        return jnp.sum(jnp.where(at, chosen_c[lo:hi] * value_c[lo:hi], 0.0), axis=0, keepdims=True)

    def most_owned(self):
        return jnp.max(jnp.sum(self.owned * self.act_r, axis=1, keepdims=True), axis=0, keepdims=True)


def total(x):
    return jnp.sum(x, axis=0, keepdims=True)


def head_row(sz, entries):
    lane = lax.broadcasted_iota(jnp.int32, (1, sz.lanes), 1)
    row = jnp.zeros((1, sz.lanes), jnp.float32)
    for i, value in entries:
        row = jnp.where(lane == i, value, row)
    return row


def plan_kernel(sz, own, plan):
    S, N = sz.slots, sz.all
    m = Marks(sz, own, own)
    f32 = jnp.float32
    lane_r, sub_c = m.lane_r, m.sub_c
    same_kind = (m.kind_c == m.kind_r).astype(f32)
    rank_c = jnp.sum(m.before * same_kind * m.act_r, axis=1, keepdims=True)
    cwas_c = jnp.max(m.before * same_kind * m.same_col * m.act_r, axis=1, keepdims=True)
    cwas_r = jnp.max(m.after * same_kind * m.same_col * m.act_c, axis=0, keepdims=True)
    big = f32(4 * N)
    lanes_f = m.lane.astype(f32)
    gates_r = m.act_r * (m.kind_r == 0).astype(f32)
    cidx_c = jnp.min(jnp.where(m.same_col * gates_r > 0, lanes_f, big), axis=1, keepdims=True)
    oidx_c = jnp.min(jnp.where(m.same_out * m.act_r > 0, lanes_f, big), axis=1, keepdims=True)
    pos_c = jnp.sum(m.before * m.owned * m.act_r, axis=1, keepdims=True)
    base_c = m.base_c()
    place_c = base_c * sz.chunk + m.kind_c * sz.nb + rest_of(m.n_c, sz.nb)
    part_c = jnp.where(
        pos_c < sz.keep, base_c * sz.keep + pos_c, sz.main + base_c * sz.more + pos_c - sz.keep)
    fields = [
        (place_c, sz.blocks), (part_c, sz.blocks), (m.row_c, 0), (cidx_c, S), (cwas_c, 0), (oidx_c, N), (m.owas_c, 0)]
    rows = []
    head = []
    for k in range(3):
        lo, hi = k * S, (k + 1) * S
        n_k = total(m.act_c[lo:hi])
        head.append((k, n_k))
        for value, spare in fields:
            row = m.listed(m.act_c, rank_c, value, lo, hi)
            rows.append(jnp.where(lane_r < n_k, row, f32(spare)))
    leader_c = m.act_c * (1.0 - cwas_c) * (m.kind_c == 0).astype(f32)
    leader_r = m.act_r * (1.0 - cwas_r) * (m.kind_r == 0).astype(f32)
    rows.append(m.listed(leader_c, m.ranks(leader_r), sub_c, 0, S))
    head.append((HEAD_COLS, total(leader_c)))
    over = (m.most_owned() > sz.keep).astype(f32)
    lists = []
    for s in range(sz.n_tensor):
        chosen_c = m.lead_c * (m.shift_c == s).astype(f32)
        chosen_r = m.lead_r * (m.shift_r == s).astype(f32)
        rank = m.ranks(chosen_r)
        lists.append(m.listed(chosen_c, rank, sub_c))
        lists.append(m.listed(chosen_c, rank, m.local_c))
        n = total(chosen_c)
        head.append((HEAD_LISTS + s, n))
        over = jnp.maximum(over, (n > sz.first).astype(f32))
    head.append((HEAD_OVER, over))
    rows.append(head_row(sz, head))
    mine = sub_c == ratio(lane_r, sz.nb) * S + m.f * sz.nb + rest_of(lane_r, sz.nb)
    rows.append(jnp.sum(jnp.where(mine, m.act_c * (pos_c + 1.0), 0.0), axis=0, keepdims=True))
    rows += lists
    for i, row in enumerate(rows):
        plan[i:i + 1, :] = row.astype(jnp.int32)


def recv_kernel(sz, *refs):
    own, plan, raws, recv, flag = refs[0], refs[1], refs[2:-2], refs[-2], refs[-1]
    f32 = jnp.float32
    head = []
    over = jnp.zeros((1, 1), f32)
    for s, raw in enumerate(raws, 1):
        m = Marks(sz, own, raw)
        chosen_c = m.lead_c * (m.shift_c == 0).astype(f32)
        chosen_r = m.lead_r * (m.shift_r == 0).astype(f32)
        recv[s:s + 1, :] = m.listed(chosen_c, m.ranks(chosen_r), m.local_c).astype(jnp.int32)
        head.append((HEAD_LISTS + s, total(chosen_c)))
        over = jnp.maximum(over, (m.most_owned() > sz.keep).astype(f32))
        for d in range(sz.n_tensor):
            n = total(m.lead_c * (m.shift_c == d).astype(f32))
            over = jnp.maximum(over, (n > sz.first).astype(f32))
    known = plan[HEAD_ROW:HEAD_ROW + 1, HEAD_OVER:HEAD_OVER + 1]
    flag[...] = jnp.maximum(known, over.astype(jnp.int32))
    recv[0:1, :] = head_row(sz, head).astype(jnp.int32)


def dot(a, b, ca, cb):
    return lax.dot_general(a, b, (((ca,), (cb,)), ((), ())), preferred_element_type=jnp.float32)


def compute_kernel(sz, *refs):
    plan, tokens, cot = refs[:3]
    n_chunks = 2 * sz.ring
    chunks = refs[3:3 + n_chunks]
    refs = refs[3 + n_chunks:]
    T = sz.n_tensor
    same, far, near, extra, _ = refs[:5]
    firsts, rests = refs[5:5 + T], refs[5 + T:5 + 2 * T]
    (xs, wbuf, parts, gate_acc, up_acc, hg_acc, hid, gate_d, up_d, out_acc, stage, strip_sems, sems, rest_sems) = refs[5 + 2 * T:]

    def field(k, j, e):
        return plan[k * FIELDS + j, e]

    def steps(k):
        return (plan[HEAD_ROW, k] + (GROUP - 1)) // GROUP

    def strip_copy(k, e):
        src = cot if k == 2 else tokens
        cols = pl.ds(pl.multiple_of(field(k, STRIP, e) * BLK, BLK), BLK)
        return pltpu.make_async_copy(src.at[:, cols], xs.at[k * sz.room + e], strip_sems.at[k * sz.room + e])

    for k in range(3):
        lax.fori_loop(0, steps(k) * GROUP, lambda e, _, k=k: strip_copy(k, e).start(), None)
    loads = [
        pltpu.make_async_copy(chunk, wbuf.at[pl.ds(i * sz.chunk, sz.chunk)], sems.at[i])
        for i, chunk in enumerate(chunks)
    ]
    for c in loads:
        c.start()
    for k in range(3):
        lax.fori_loop(0, steps(k) * GROUP, lambda e, _, k=k: strip_copy(k, e).wait(), None)
    for c in loads:
        c.wait()

    def walk(k, body):
        lax.fori_loop(0, steps(k), lambda p, _: body(p * GROUP), None)

    def forward(k, acc, w_dim):
        def body(e0):
            prods = [
                dot(xs[k * sz.room + e0 + u], wbuf[field(k, PLACE, e0 + u)], 1, w_dim) for u in range(GROUP)]
            for u in range(GROUP):
                c = field(k, CIDX, e0 + u)
                acc[c] = prods[u] + jnp.where(field(k, CWAS, e0 + u) == 0, 0.0, acc[c])

        walk(k, body)

    forward(0, gate_acc, 0)
    forward(1, up_acc, 0)
    forward(2, hg_acc, 1)

    def column(i, _):
        c = plan[COLS_ROW, i]
        g, u, h = gate_acc[c], up_acc[c], hg_acc[c]
        s = lax.logistic(g)
        silu = g * s
        hid[c] = (silu * u).astype(jnp.bfloat16)
        gate_d[c] = (h * u * s * (1.0 + g * (1.0 - s))).astype(jnp.bfloat16)
        up_d[c] = (h * silu).astype(jnp.bfloat16)

    lax.fori_loop(0, plan[HEAD_ROW, HEAD_COLS], column, None)

    def backward(k, act, w_dim):
        def body(e0):
            terms, grads = [], []
            for u in range(GROUP):
                a = act[field(k, CIDX, e0 + u)]
                x = xs[k * sz.room + e0 + u]
                terms.append(dot(a, wbuf[field(k, PLACE, e0 + u)], 1, w_dim))
                grads.append(dot(a, x, 0, 0) if k == 2 else dot(x, a, 0, 0))
            for u in range(GROUP):
                parts[field(k, PART, e0 + u)] = grads[u].astype(jnp.bfloat16)
            for u in range(GROUP):
                at = field(k, OIDX, e0 + u)
                out_acc[at] = terms[u] + jnp.where(field(k, OWAS, e0 + u) == 0, 0.0, out_acc[at])

        walk(k, body)

    backward(2, hid, 0)
    backward(0, gate_d, 1)
    backward(1, up_d, 1)

    split = sz.ring * sz.keep
    cut = split + sz.far * sz.keep
    outs = [
        pltpu.make_async_copy(parts.at[pl.ds(split, cut - split)], far, sems.at[0]),
        pltpu.make_async_copy(parts.at[pl.ds(0, split)], same, sems.at[1]),
        pltpu.make_async_copy(parts.at[pl.ds(cut, sz.main - cut)], near, sems.at[2]),
    ]
    for c in outs:
        c.start()

    for s in range(T):
        def staged(i, _, s=s):
            stage[s * sz.send_all + i] = out_acc[plan[LISTS_ROW + 2 * s, i]].astype(jnp.bfloat16)

        lax.fori_loop(0, plan[HEAD_ROW, HEAD_LISTS + s], staged, None)
        first = pltpu.make_async_copy(stage.at[pl.ds(s * sz.send_all, sz.first)], firsts[s], sems.at[3 + s])
        first.start()
        outs.append(first)

    if sz.rest + sz.more > 0:
        @pl.when(plan[HEAD_ROW, HEAD_OVER] > 0)
        def _():
            copies = []
            if sz.rest > 0:
                copies += [
                    pltpu.make_async_copy(
                        stage.at[pl.ds(s * sz.send_all + sz.first, sz.rest)], rests[s], rest_sems.at[s])
                    for s in range(T)
                ]
            if sz.more > 0:
                copies.append(pltpu.make_async_copy(
                    parts.at[pl.ds(sz.main, sz.blocks - sz.main)], extra, rest_sems.at[T]))
            for c in copies:
                c.start()
            for c in copies:
                c.wait()
    for c in outs:
        c.wait()


def join_kernel(sz, *refs):
    T = sz.n_tensor
    plan, recv = refs[:2]
    firsts, rests = refs[2:2 + T], refs[2 + T:2 + 2 * T]
    outputs, input_grads, spare, sem = refs[-4:]
    outputs[...] = jnp.zeros_like(outputs)
    input_grads[...] = jnp.zeros_like(input_grads)

    def add(at, value):
        def into(ref, w):
            cols = pl.ds(pl.multiple_of(w * BLK, BLK), BLK)
            ref[:, cols] = (ref[:, cols].astype(jnp.float32) + value.astype(jnp.float32)).astype(jnp.bfloat16)

        @pl.when(at < sz.rbt)
        def _():
            into(outputs, at)

        @pl.when(at >= sz.rbt)
        def _():
            into(input_grads, at - sz.rbt)

    for s in range(T):
        n = (recv[0, HEAD_LISTS + s] if s else plan[HEAD_ROW, HEAD_LISTS])

        def where_to(i, s=s):
            return recv[s, i] if s else plan[LISTS_ROW + 1, i]

        def early(i, _, s=s):
            add(where_to(i), firsts[s][i])

        lax.fori_loop(0, jnp.minimum(n, sz.first), early, None)
        if sz.rest > 0:
            def late(i, _, s=s):
                copy = pltpu.make_async_copy(rests[s].at[i - sz.first], spare, sem)
                copy.start()
                copy.wait()
                add(where_to(i), spare[...])

            lax.fori_loop(jnp.minimum(n, sz.first), n, late, None)


def finish_kernel(sz, plan, here, ahead, behind, late, *outs):
    for k in range(3):
        for a in range(sz.nb):
            at = plan[MINE_ROW, k * sz.nb + a]
            p = jnp.minimum(jnp.maximum(at - 1, 0), sz.keep - 1)
            value = here[p] + ahead[p].astype(jnp.float32) + behind[p].astype(jnp.float32)
            if sz.more > 0:
                q = jnp.minimum(jnp.maximum(at - 1 - sz.keep, 0), sz.more - 1)
                value = jnp.where(at > sz.keep, late[q].astype(jnp.float32), value)
            outs[k][0, a] = jnp.where(at > 0, value, 0.0).astype(jnp.bfloat16)


def spec(space):
    return pl.BlockSpec(memory_space=space)


ANY, HBM, VMEM, SMEM = pl.ANY, pltpu.HBM, pltpu.VMEM, pltpu.SMEM


def cost(flops, moved):
    return pl.CostEstimate(flops=flops, bytes_accessed=moved, transcendentals=0)


def call_plan(sz, own):
    return pl.pallas_call(
        functools.partial(plan_kernel, sz),
        out_shape=jax.ShapeDtypeStruct((sz.plan_rows, sz.lanes), jnp.int32),
        in_specs=[spec(VMEM)],
        out_specs=spec(VMEM),
        compiler_params=pltpu.CompilerParams(vmem_limit_bytes=SMALL),
        cost_estimate=cost(1_000_000, 4_000_000),
        name="plan",
    )(own)


def call_recv(sz, own, plan, raws):
    return pl.pallas_call(
        functools.partial(recv_kernel, sz),
        out_shape=[
            jax.ShapeDtypeStruct((sz.recv_rows, sz.lanes), jnp.int32),
            jax.ShapeDtypeStruct((1, 1), jnp.int32),
        ],
        in_specs=[spec(VMEM)] * (2 + len(raws)),
        out_specs=[spec(VMEM)] * 2,
        compiler_params=pltpu.CompilerParams(vmem_limit_bytes=SMALL),
        cost_estimate=cost(1_000_000, 4_000_000),
        name="recv",
    )(own, plan, *raws)


def call_turn(handed, arrived):
    return pl.pallas_call(
        lambda *_: None,
        out_shape=[jax.ShapeDtypeStruct(x.shape, x.dtype) for x in handed],
        in_specs=[spec(ANY)] * (len(handed) + len(arrived)),
        out_specs=[spec(ANY)] * len(handed),
        input_output_aliases={i: i for i in range(len(handed))},
        compiler_params=pltpu.CompilerParams(vmem_limit_bytes=SMALL),
        cost_estimate=cost(1000, 1000),
        name="turn",
    )(*handed, *arrived)


def call_compute(sz, plan, tokens, cot, chunks):
    T = sz.n_tensor
    bf, f32 = jnp.bfloat16, jnp.float32

    def blocks(n):
        return jax.ShapeDtypeStruct((max(n, 1), BLK, BLK), bf)

    out_shape = [
        blocks(sz.ring * sz.keep),
        blocks(sz.far * sz.keep),
        blocks((sz.ring - sz.far) * sz.keep),
        blocks(sz.blocks - sz.main),
        blocks(sz.more),
    ]
    out_shape += [blocks(sz.first)] * T + [blocks(sz.rest)] * T
    scratch = [
        ((3 * sz.room, sz.tok, BLK), bf),
        ((sz.blocks + 1, BLK, BLK), bf),
        ((sz.blocks + 1, BLK, BLK), bf),
        ((sz.slots + 1, sz.tok, BLK), f32),
        ((sz.slots + 1, sz.tok, BLK), f32),
        ((sz.slots + 1, sz.tok, BLK), f32),
        ((sz.slots + 1, sz.tok, BLK), bf),
        ((sz.slots + 1, sz.tok, BLK), bf),
        ((sz.slots + 1, sz.tok, BLK), bf),
        ((sz.all + 1, sz.tok, BLK), f32),
        ((T * sz.send_all, sz.tok, BLK), bf),
    ]
    held = sum(s[0] * s[1] * s[2] * jnp.dtype(t).itemsize for s, t in scratch)
    return pl.pallas_call(
        functools.partial(compute_kernel, sz),
        out_shape=out_shape,
        in_specs=[spec(SMEM)] + [spec(HBM)] * 2 + [spec(ANY)] * len(chunks),
        out_specs=[spec(ANY)] * len(out_shape),
        scratch_shapes=[pltpu.VMEM(s, t) for s, t in scratch] + [
            pltpu.SemaphoreType.DMA((3 * sz.room,)),
            pltpu.SemaphoreType.DMA((max(len(chunks), 3 + T),)),
            pltpu.SemaphoreType.DMA((T + 1,)),
        ],
        compiler_params=pltpu.CompilerParams(vmem_limit_bytes=held + 2 * 1024 * 1024),
        cost_estimate=cost(1_000_000_000, 20_000_000),
        name="compute",
    )(plan, pltpu.with_memory_space_constraint(tokens, HBM), pltpu.with_memory_space_constraint(cot, HBM), *chunks)


def call_join(sz, plan, recv, firsts, rests):
    half = jax.ShapeDtypeStruct((sz.tok, sz.width // sz.n_tensor), jnp.bfloat16)
    return pl.pallas_call(
        functools.partial(join_kernel, sz),
        out_shape=[half, half],
        in_specs=[spec(SMEM)] * 2 + [spec(VMEM)] * len(firsts) + [spec(ANY)] * len(rests),
        out_specs=[spec(VMEM), spec(VMEM)],
        scratch_shapes=[pltpu.VMEM((sz.tok, BLK), jnp.bfloat16), pltpu.SemaphoreType.DMA],
        compiler_params=pltpu.CompilerParams(vmem_limit_bytes=10 * 1024 * 1024),
        cost_estimate=cost(1_000_000, 6_000_000),
        name="join",
    )(plan, recv, *firsts, *rests)


def call_finish(sz, plan, here, ahead, behind, late):
    out = jax.ShapeDtypeStruct((1, sz.nb, BLK, BLK), jnp.bfloat16)
    return pl.pallas_call(
        functools.partial(finish_kernel, sz),
        out_shape=[out] * 3,
        in_specs=[spec(SMEM)] + [spec(VMEM)] * 4,
        out_specs=[spec(VMEM)] * 3,
        compiler_params=pltpu.CompilerParams(vmem_limit_bytes=SMALL),
        cost_estimate=cost(1_000_000, 1_000_000),
        name="finish",
    )(plan, here, ahead, behind, late)


def gather_chunks(sz, chunk, beside=()):
    ahead, behind, far, swap = permutations(sz)
    same, other = {0: chunk}, {}
    a = b = chunk
    for s in range(1, sz.top):
        if s == sz.top - 1:
            same[sz.top] = lax.ppermute(a, "fsdp", far)
            other[sz.top] = lax.ppermute(a, "fsdp", [(i, j ^ 1) for i, j in far])
        a, b = lax.ppermute(a, "fsdp", ahead), lax.ppermute(b, "fsdp", behind)
        if s <= len(beside):
            a, b = call_turn([a, b], [beside[s - 1]])
        same[sz.ring - s], same[s] = a, b
    for d in same:
        if d != sz.top:
            other[d] = lax.ppermute(same[d], "fsdp", swap)
    return [side[d] for side in (same, other) for d in sz.order]


def reduce_parts(sz, per, same, pair, beside=lambda s, a, b: (a, b)):
    ahead, behind, far, _ = permutations(sz)

    def wide(d, *more):
        j = sz.order.index(d)
        out = same[j * per:(j + 1) * per].astype(jnp.float32) + pair(j).astype(jnp.float32)
        for m in more:
            out = out + m.astype(jnp.float32)
        return out

    def term(d, *more):
        return wide(d, *more).astype(jnp.bfloat16)

    c, a, b = lax.optimization_barrier((term(sz.top), term(sz.top - 1), term(sz.top + 1)))
    c = lax.ppermute(c, "fsdp", far)
    for s in range(1, sz.top):
        if s > 1:
            a = term(sz.top - s, a, c) if s == 2 else term(sz.top - s, a)
            b = term(sz.top + s, b)
            a, b = beside(s, *lax.optimization_barrier((a, b)))
        a, b = lax.ppermute(a, "fsdp", ahead), lax.ppermute(b, "fsdp", behind)
    return wide(0), a, b


def shards(
    tokens,
    cotangent,
    gate_blocks,
    up_blocks,
    down_blocks,
    gate_where,
    up_where,
    down_where,
    block_counts,
):
    n_fsdp, T = lax.axis_size("fsdp"), lax.axis_size("tensor")
    sz = Sizes(tokens, gate_blocks, gate_where.shape[1], n_fsdp, T)
    f, rank = lax.axis_index("fsdp"), lax.axis_index("tensor")
    swap = permutations(sz)[-1]

    chunk = jnp.concatenate([gate_blocks[0], up_blocks[0], down_blocks[0]])
    own = jnp.concatenate([
        gate_where[0], up_where[0], down_where[0], block_counts[:, 0],
        f.astype(jnp.int32)[None], rank.astype(jnp.int32)[None]])
    own = jnp.pad(own, (0, sz.lanes - own.shape[0]))[None]

    plan = call_plan(sz, own)
    raws = [lax.ppermute(own, "tensor", [(i, (i + s) % T) for i in range(T)]) for s in range(1, T)]
    recv, flag = call_recv(sz, own, plan, raws)
    chunks = gather_chunks(sz, chunk, (plan, recv))

    outs = call_compute(sz, plan, tokens, cotangent, chunks)
    same, far, near, extra, idle = outs[:5]
    firsts, rests = outs[5:5 + T], list(outs[5 + T:])

    def exchange(arrays):
        return [arrays[0]] + [
            lax.ppermute(arrays[s], "tensor", [(i, (i + s) % T) for i in range(T)]) for s in range(1, T)]

    far, near = lax.ppermute(far, "fsdp", swap), lax.ppermute(near, "fsdp", swap)
    firsts = exchange(firsts)

    def pair(j):
        at = j * sz.keep
        return far[at:at + sz.keep] if j < sz.far else near[at - sz.far * sz.keep:][:sz.keep]

    late = idle

    def beside(s, a, b):
        nonlocal rests, late
        if s != sz.top - 1:
            return a, b
        a, more = call_turn([a, extra], firsts[1:])
        if sz.rest + sz.more == 0:
            return a, b

        def spill(rests, extra, idle):
            moved = exchange(rests)
            if sz.more == 0:
                return moved, idle
            n = sz.ring * sz.more
            other = lax.ppermute(extra[n:], "fsdp", swap)
            terms = reduce_parts(sz, sz.more, extra[:n], lambda j: other[j * sz.more:(j + 1) * sz.more])
            return moved, sum(t.astype(jnp.float32) for t in terms).astype(jnp.bfloat16)

        rests, late = lax.cond(flag[0, 0] > 0, spill, lambda r, e, i: (r, i), rests, more, idle)
        return a, b

    here, ahead, behind = reduce_parts(sz, sz.keep, same, pair, beside)
    outputs, input_grads = call_join(sz, plan, recv, firsts, rests)
    grads = call_finish(sz, plan, here, ahead, behind, late)
    return (outputs, input_grads, *grads)


def solution(mesh):
    placed = (
        P("fsdp", None),
        P("fsdp", None),
        P("tensor", "fsdp", None, None),
        P("tensor", "fsdp", None, None),
        P("tensor", "fsdp", None, None),
        P("tensor", None),
        P("tensor", None),
        P("tensor", None),
        P(None, "tensor"),
    )
    return jax.shard_map(
        shards,
        mesh=mesh,
        in_specs=placed,
        out_specs=(
            P("fsdp", "tensor"),
            P("fsdp", "tensor"),
            P("tensor", "fsdp", None, None),
            P("tensor", "fsdp", None, None),
            P("tensor", "fsdp", None, None),
        ),
        check_vma=False,
    )
```

```python
import functools

import jax
import jax.numpy as jnp
from jax import lax
from jax.experimental import pallas as pl
from jax.experimental.pallas import tpu as pltpu
from jax.sharding import PartitionSpec as P

FF = 14336
BLK = 128
GROUP = 4
FIRST_SEND = 16
FIRST_GRADS = 4
SMALL = 4 * 1024 * 1024
PLACE, PART, STRIP, CIDX, CWAS, OIDX, OWAS = range(7)
FIELDS = 7
COLS_ROW = 3 * FIELDS
HEAD_ROW = COLS_ROW + 1
MINE_ROW = COLS_ROW + 2
LISTS_ROW = COLS_ROW + 3
HEAD_COLS, HEAD_OVER, HEAD_LISTS = 3, 4, 8


class Sizes:
    def __init__(self, tokens, gate_blocks, slots, n_fsdp, n_tensor):
        self.tok, self.width = tokens.shape
        self.n_fsdp, self.n_tensor = n_fsdp, n_tensor
        self.rb = self.width // BLK
        self.cb = FF // (BLK * n_tensor)
        self.slots = slots
        self.all = 3 * slots
        self.lanes = -(-(self.all + GROUP) // 128) * 128
        self.nb = gate_blocks.shape[1]
        self.chunk = 3 * self.nb
        self.ring = n_fsdp // 2
        self.top = self.ring // 2
        self.rbt = self.rb // n_tensor
        self.order = [self.top]
        for d in range(1, self.top):
            self.order += [self.top + d, self.top - d]
        self.order.append(0)
        self.far = min(4, self.ring - 1)
        sparse = slots < self.cb
        self.keep = min(FIRST_GRADS, self.chunk) if sparse else self.chunk
        self.more = self.chunk - self.keep
        self.send_all = 2 * self.rbt
        self.first = min(FIRST_SEND, self.send_all) if sparse else self.send_all
        self.rest = self.send_all - self.first
        self.blocks = 2 * self.ring * self.chunk
        self.main = 2 * self.ring * self.keep
        self.plan_rows = -(-(LISTS_ROW + 2 * n_tensor) // 8) * 8
        self.recv_rows = -(-n_tensor // 8) * 8
        self.room = slots + GROUP


def permutations(sz):
    seq = list(range(0, sz.ring, 2)) + list(range(sz.ring - 1, 0, -2))
    ahead, behind, swap = [], [], []
    for i, q in enumerate(seq):
        up, down = seq[(i + 1) % sz.ring], seq[i - 1]
        ahead += [(q * 2, up * 2), (q * 2 + 1, down * 2 + 1)]
        behind += [(q * 2, down * 2), (q * 2 + 1, up * 2 + 1)]
        swap += [(q * 2, q * 2 + 1), (q * 2 + 1, q * 2)]
    return ahead, behind, swap


def ratio(x, d):
    return jnp.floor((x + 0.5) * (1.0 / d))


def rest_of(x, d):
    return x - d * ratio(x, d)


def ring_position(sz, chip):
    return jnp.where(rest_of(chip, 2) == 0, ratio(chip, 2), sz.ring - 1 - ratio(chip, 2))


class Marks:
    def __init__(self, sz, own, raw):
        N, L, S = sz.all, sz.lanes, sz.slots
        f32 = jnp.float32
        self.sz = sz
        self.sub = lax.broadcasted_iota(jnp.int32, (N, L), 0)
        self.lane = lax.broadcasted_iota(jnp.int32, (N, L), 1)
        self.same = self.sub == self.lane
        sub_c = self.sub[:, :1].astype(f32)
        lane_r = lax.broadcasted_iota(jnp.int32, (1, L), 1).astype(f32)
        self.sub_c, self.lane_r = sub_c, lane_r
        raw_r = raw[...].astype(f32)
        own_r = own[...].astype(f32)

        def single(row, at):
            return jnp.sum(jnp.where(lane_r == at, row, 0.0), axis=1, keepdims=True)

        self.f, self.rank = single(own_r, N + 3), single(own_r, N + 4)

        def kind(x):
            return (x >= S).astype(f32) + (x >= 2 * S).astype(f32)

        self.kind_c, self.kind_r = kind(sub_c), kind(lane_r)
        self.n_r = lane_r - S * self.kind_r
        self.n_c = sub_c - S * self.kind_c
        limit = jnp.zeros((1, L), f32)
        for k in range(3):
            limit = limit + jnp.where(self.kind_r == k, single(raw_r, N + k), 0.0)
        live_r = jnp.where((lane_r < N) & (self.n_r < limit), 1.0, 0.0)
        w_c = self.col(raw_r)
        live_c = self.col(live_r)

        def place(w, k):
            gate, down = ratio(w, sz.cb), ratio(w, sz.rb)
            is_down = k == 2
            return jnp.where(is_down, w - down * sz.rb, gate), jnp.where(is_down, down, w - gate * sz.cb)

        self.row_c, col_c = place(w_c, self.kind_c)
        self.row_r, col_r = place(raw_r, self.kind_r)
        self.owner_c, self.owner_r = ratio(self.n_c, sz.nb), ratio(self.n_r, sz.nb)
        self.same_col = (col_c == col_r).astype(f32)
        act_c, act_r = live_c, live_r
        for k in range(3):
            lanes = self.same_col * (live_r * (self.kind_r == k).astype(f32))
            act_c = act_c * jnp.max(lanes, axis=1, keepdims=True)
            subs = self.same_col * (live_c * (self.kind_c == k).astype(f32))
            act_r = act_r * jnp.max(subs, axis=0, keepdims=True)
        self.act_c, self.act_r = act_c, act_r
        out_c = jnp.where(self.kind_c == 2, 0.0, f32(sz.rb)) + self.row_c
        out_r = jnp.where(self.kind_r == 2, 0.0, f32(sz.rb)) + self.row_r
        self.same_out = (out_c == out_r).astype(f32)
        self.before = (self.lane < self.sub).astype(f32)
        self.after = (self.sub < self.lane).astype(f32)
        self.owas_c = jnp.max(self.same_out * self.before * act_r, axis=1, keepdims=True)
        self.owas_r = jnp.max(self.same_out * self.after * act_c, axis=0, keepdims=True)
        self.lead_c = act_c * (1.0 - self.owas_c)
        self.lead_r = act_r * (1.0 - self.owas_r)
        self.owned = (self.owner_c == self.owner_r).astype(f32)

        def shift(row):
            away = ratio(row, sz.rbt) - self.rank
            return jnp.where(away < 0, away + sz.n_tensor, away)

        self.shift_c, self.shift_r = shift(self.row_c), shift(self.row_r)
        self.local_c = jnp.where(self.kind_c == 2, 0.0, f32(sz.rbt)) + rest_of(self.row_c, sz.rbt)

    def col(self, row):
        return jnp.sum(jnp.where(self.same, row, 0.0), axis=1, keepdims=True)

    def base_c(self):
        sz = self.sz
        away = ring_position(sz, ratio(self.owner_c, 2)) - ring_position(sz, ratio(self.f, 2))
        away = jnp.where(rest_of(self.owner_c, 2) == 0, away, -away)
        rel = jnp.where(away < 0, away + sz.ring, away)
        j = jnp.where(rel > sz.top, 2 * (rel - sz.top) - 1, 2 * (sz.top - rel))
        j = jnp.where(rel == 0, sz.ring - 1.0, j)
        return j + jnp.where(rest_of(self.owner_c, 2) == rest_of(self.f, 2), 0.0, float(sz.ring))

    def ranks(self, chosen_r):
        return jnp.sum(self.before * chosen_r, axis=1, keepdims=True)

    def listed(self, chosen_c, rank_c, value_c, lo=0, hi=None):
        at = rank_c[lo:hi] == self.lane[lo:hi].astype(jnp.float32)
        return jnp.sum(jnp.where(at, chosen_c[lo:hi] * value_c[lo:hi], 0.0), axis=0, keepdims=True)

    def most_owned(self):
        return jnp.max(jnp.sum(self.owned * self.act_r, axis=1, keepdims=True), axis=0, keepdims=True)


def total(x):
    return jnp.sum(x, axis=0, keepdims=True)


def head_row(sz, entries):
    lane = lax.broadcasted_iota(jnp.int32, (1, sz.lanes), 1)
    row = jnp.zeros((1, sz.lanes), jnp.float32)
    for i, value in entries:
        row = jnp.where(lane == i, value, row)
    return row


def plan_kernel(sz, own, plan):
    S, N = sz.slots, sz.all
    m = Marks(sz, own, own)
    f32 = jnp.float32
    lane_r, sub_c = m.lane_r, m.sub_c
    same_kind = (m.kind_c == m.kind_r).astype(f32)
    rank_c = jnp.sum(m.before * same_kind * m.act_r, axis=1, keepdims=True)
    cwas_c = jnp.max(m.before * same_kind * m.same_col * m.act_r, axis=1, keepdims=True)
    cwas_r = jnp.max(m.after * same_kind * m.same_col * m.act_c, axis=0, keepdims=True)
    big = f32(4 * N)
    lanes_f = m.lane.astype(f32)
    gates_r = m.act_r * (m.kind_r == 0).astype(f32)
    cidx_c = jnp.min(jnp.where(m.same_col * gates_r > 0, lanes_f, big), axis=1, keepdims=True)
    oidx_c = jnp.min(jnp.where(m.same_out * m.act_r > 0, lanes_f, big), axis=1, keepdims=True)
    pos_c = jnp.sum(m.before * m.owned * m.act_r, axis=1, keepdims=True)
    base_c = m.base_c()
    place_c = base_c * sz.chunk + m.kind_c * sz.nb + rest_of(m.n_c, sz.nb)
    part_c = jnp.where(
        pos_c < sz.keep, base_c * sz.keep + pos_c, sz.main + base_c * sz.more + pos_c - sz.keep)
    fields = [
        (place_c, sz.blocks), (part_c, sz.blocks), (m.row_c, 0), (cidx_c, S), (cwas_c, 0), (oidx_c, N), (m.owas_c, 0)]
    rows = []
    head = []
    for k in range(3):
        lo, hi = k * S, (k + 1) * S
        n_k = total(m.act_c[lo:hi])
        head.append((k, n_k))
        for value, spare in fields:
            row = m.listed(m.act_c, rank_c, value, lo, hi)
            rows.append(jnp.where(lane_r < n_k, row, f32(spare)))
    leader_c = m.act_c * (1.0 - cwas_c) * (m.kind_c == 0).astype(f32)
    leader_r = m.act_r * (1.0 - cwas_r) * (m.kind_r == 0).astype(f32)
    rows.append(m.listed(leader_c, m.ranks(leader_r), sub_c, 0, S))
    head.append((HEAD_COLS, total(leader_c)))
    over = (m.most_owned() > sz.keep).astype(f32)
    lists = []
    for s in range(sz.n_tensor):
        chosen_c = m.lead_c * (m.shift_c == s).astype(f32)
        chosen_r = m.lead_r * (m.shift_r == s).astype(f32)
        rank = m.ranks(chosen_r)
        lists.append(m.listed(chosen_c, rank, sub_c))
        lists.append(m.listed(chosen_c, rank, m.local_c))
        n = total(chosen_c)
        head.append((HEAD_LISTS + s, n))
        over = jnp.maximum(over, (n > sz.first).astype(f32))
    head.append((HEAD_OVER, over))
    rows.append(head_row(sz, head))
    mine = sub_c == ratio(lane_r, sz.nb) * S + m.f * sz.nb + rest_of(lane_r, sz.nb)
    rows.append(jnp.sum(jnp.where(mine, m.act_c * (pos_c + 1.0), 0.0), axis=0, keepdims=True))
    rows += lists
    for i, row in enumerate(rows):
        plan[i:i + 1, :] = row.astype(jnp.int32)


def recv_kernel(sz, *refs):
    own, plan, raws, recv, flag = refs[0], refs[1], refs[2:-2], refs[-2], refs[-1]
    f32 = jnp.float32
    head = []
    over = jnp.zeros((1, 1), f32)
    for s, raw in enumerate(raws, 1):
        m = Marks(sz, own, raw)
        chosen_c = m.lead_c * (m.shift_c == 0).astype(f32)
        chosen_r = m.lead_r * (m.shift_r == 0).astype(f32)
        recv[s:s + 1, :] = m.listed(chosen_c, m.ranks(chosen_r), m.local_c).astype(jnp.int32)
        head.append((HEAD_LISTS + s, total(chosen_c)))
        over = jnp.maximum(over, (m.most_owned() > sz.keep).astype(f32))
        for d in range(sz.n_tensor):
            n = total(m.lead_c * (m.shift_c == d).astype(f32))
            over = jnp.maximum(over, (n > sz.first).astype(f32))
    known = plan[HEAD_ROW:HEAD_ROW + 1, HEAD_OVER:HEAD_OVER + 1]
    flag[...] = jnp.maximum(known, over.astype(jnp.int32))
    recv[0:1, :] = head_row(sz, head).astype(jnp.int32)


def dot(a, b, ca, cb):
    return lax.dot_general(a, b, (((ca,), (cb,)), ((), ())), preferred_element_type=jnp.float32)


def compute_kernel(sz, *refs):
    plan, tokens, cot = refs[:3]
    n_chunks = 2 * sz.ring
    chunks = refs[3:3 + n_chunks]
    refs = refs[3 + n_chunks:]
    T = sz.n_tensor
    same, far, near, extra, _ = refs[:5]
    firsts, rests = refs[5:5 + T], refs[5 + T:5 + 2 * T]
    (xs, wbuf, parts, gate_acc, up_acc, hg_acc, hid, gate_d, up_d, out_acc, stage, strip_sems, sems, rest_sems) = refs[5 + 2 * T:]

    def field(k, j, e):
        return plan[k * FIELDS + j, e]

    def steps(k):
        return (plan[HEAD_ROW, k] + (GROUP - 1)) // GROUP

    def strip_copy(k, e):
        src = cot if k == 2 else tokens
        cols = pl.ds(pl.multiple_of(field(k, STRIP, e) * BLK, BLK), BLK)
        return pltpu.make_async_copy(src.at[:, cols], xs.at[k * sz.room + e], strip_sems.at[k * sz.room + e])

    for k in range(3):
        lax.fori_loop(0, steps(k) * GROUP, lambda e, _, k=k: strip_copy(k, e).start(), None)
    loads = [
        pltpu.make_async_copy(chunk, wbuf.at[pl.ds(i * sz.chunk, sz.chunk)], sems.at[i])
        for i, chunk in enumerate(chunks)
    ]
    for c in loads:
        c.start()
    for k in range(3):
        lax.fori_loop(0, steps(k) * GROUP, lambda e, _, k=k: strip_copy(k, e).wait(), None)
    for c in loads:
        c.wait()

    def walk(k, body):
        lax.fori_loop(0, steps(k), lambda p, _: body(p * GROUP), None)

    def forward(k, acc, w_dim):
        def body(e0):
            prods = [
                dot(xs[k * sz.room + e0 + u], wbuf[field(k, PLACE, e0 + u)], 1, w_dim) for u in range(GROUP)]
            for u in range(GROUP):
                c = field(k, CIDX, e0 + u)
                acc[c] = prods[u] + jnp.where(field(k, CWAS, e0 + u) == 0, 0.0, acc[c])

        walk(k, body)

    forward(0, gate_acc, 0)
    forward(1, up_acc, 0)
    forward(2, hg_acc, 1)

    def column(i, _):
        c = plan[COLS_ROW, i]
        g, u, h = gate_acc[c], up_acc[c], hg_acc[c]
        s = lax.logistic(g)
        silu = g * s
        hid[c] = (silu * u).astype(jnp.bfloat16)
        gate_d[c] = (h * u * s * (1.0 + g * (1.0 - s))).astype(jnp.bfloat16)
        up_d[c] = (h * silu).astype(jnp.bfloat16)

    lax.fori_loop(0, plan[HEAD_ROW, HEAD_COLS], column, None)

    def backward(k, act, w_dim):
        def body(e0):
            terms, grads = [], []
            for u in range(GROUP):
                a = act[field(k, CIDX, e0 + u)]
                x = xs[k * sz.room + e0 + u]
                terms.append(dot(a, wbuf[field(k, PLACE, e0 + u)], 1, w_dim))
                grads.append(dot(a, x, 0, 0) if k == 2 else dot(x, a, 0, 0))
            for u in range(GROUP):
                parts[field(k, PART, e0 + u)] = grads[u].astype(jnp.bfloat16)
            for u in range(GROUP):
                at = field(k, OIDX, e0 + u)
                out_acc[at] = terms[u] + jnp.where(field(k, OWAS, e0 + u) == 0, 0.0, out_acc[at])

        walk(k, body)

    backward(2, hid, 0)
    backward(0, gate_d, 1)
    backward(1, up_d, 1)

    split = sz.ring * sz.keep
    cut = split + sz.far * sz.keep
    outs = [
        pltpu.make_async_copy(parts.at[pl.ds(split, cut - split)], far, sems.at[0]),
        pltpu.make_async_copy(parts.at[pl.ds(0, split)], same, sems.at[1]),
        pltpu.make_async_copy(parts.at[pl.ds(cut, sz.main - cut)], near, sems.at[2]),
    ]
    for c in outs:
        c.start()

    for s in range(T):
        def staged(i, _, s=s):
            stage[s * sz.send_all + i] = out_acc[plan[LISTS_ROW + 2 * s, i]].astype(jnp.bfloat16)

        lax.fori_loop(0, plan[HEAD_ROW, HEAD_LISTS + s], staged, None)
        first = pltpu.make_async_copy(stage.at[pl.ds(s * sz.send_all, sz.first)], firsts[s], sems.at[3 + s])
        first.start()
        outs.append(first)

    if sz.rest + sz.more > 0:
        @pl.when(plan[HEAD_ROW, HEAD_OVER] > 0)
        def _():
            copies = []
            if sz.rest > 0:
                copies += [
                    pltpu.make_async_copy(
                        stage.at[pl.ds(s * sz.send_all + sz.first, sz.rest)], rests[s], rest_sems.at[s])
                    for s in range(T)
                ]
            if sz.more > 0:
                copies.append(pltpu.make_async_copy(
                    parts.at[pl.ds(sz.main, sz.blocks - sz.main)], extra, rest_sems.at[T]))
            for c in copies:
                c.start()
            for c in copies:
                c.wait()
    for c in outs:
        c.wait()


def join_kernel(sz, *refs):
    T = sz.n_tensor
    plan, recv = refs[:2]
    firsts, rests = refs[2:2 + T], refs[2 + T:2 + 2 * T]
    outputs, input_grads, spare, sem = refs[-4:]
    outputs[...] = jnp.zeros_like(outputs)
    input_grads[...] = jnp.zeros_like(input_grads)

    def add(at, value):
        def into(ref, w):
            cols = pl.ds(pl.multiple_of(w * BLK, BLK), BLK)
            ref[:, cols] = (ref[:, cols].astype(jnp.float32) + value.astype(jnp.float32)).astype(jnp.bfloat16)

        @pl.when(at < sz.rbt)
        def _():
            into(outputs, at)

        @pl.when(at >= sz.rbt)
        def _():
            into(input_grads, at - sz.rbt)

    for s in range(T):
        n = (recv[0, HEAD_LISTS + s] if s else plan[HEAD_ROW, HEAD_LISTS])

        def where_to(i, s=s):
            return recv[s, i] if s else plan[LISTS_ROW + 1, i]

        def early(i, _, s=s):
            add(where_to(i), firsts[s][i])

        lax.fori_loop(0, jnp.minimum(n, sz.first), early, None)
        if sz.rest > 0:
            def late(i, _, s=s):
                copy = pltpu.make_async_copy(rests[s].at[i - sz.first], spare, sem)
                copy.start()
                copy.wait()
                add(where_to(i), spare[...])

            lax.fori_loop(jnp.minimum(n, sz.first), n, late, None)


def finish_kernel(sz, plan, here, ahead, behind, late, *outs):
    for k in range(3):
        for a in range(sz.nb):
            at = plan[MINE_ROW, k * sz.nb + a]
            p = jnp.minimum(jnp.maximum(at - 1, 0), sz.keep - 1)
            value = here[p] + ahead[p].astype(jnp.float32) + behind[p].astype(jnp.float32)
            if sz.more > 0:
                q = jnp.minimum(jnp.maximum(at - 1 - sz.keep, 0), sz.more - 1)
                value = jnp.where(at > sz.keep, late[q].astype(jnp.float32), value)
            outs[k][0, a] = jnp.where(at > 0, value, 0.0).astype(jnp.bfloat16)


def spec(space):
    return pl.BlockSpec(memory_space=space)


ANY, HBM, VMEM, SMEM = pl.ANY, pltpu.HBM, pltpu.VMEM, pltpu.SMEM


def cost(flops, moved):
    return pl.CostEstimate(flops=flops, bytes_accessed=moved, transcendentals=0)


def call_plan(sz, own):
    return pl.pallas_call(
        functools.partial(plan_kernel, sz),
        out_shape=jax.ShapeDtypeStruct((sz.plan_rows, sz.lanes), jnp.int32),
        in_specs=[spec(VMEM)],
        out_specs=spec(VMEM),
        compiler_params=pltpu.CompilerParams(vmem_limit_bytes=SMALL),
        cost_estimate=cost(1_000_000, 4_000_000),
        name="plan",
    )(own)


def call_recv(sz, own, plan, raws):
    return pl.pallas_call(
        functools.partial(recv_kernel, sz),
        out_shape=[
            jax.ShapeDtypeStruct((sz.recv_rows, sz.lanes), jnp.int32),
            jax.ShapeDtypeStruct((1, 1), jnp.int32),
        ],
        in_specs=[spec(VMEM)] * (2 + len(raws)),
        out_specs=[spec(VMEM)] * 2,
        compiler_params=pltpu.CompilerParams(vmem_limit_bytes=SMALL),
        cost_estimate=cost(1_000_000, 4_000_000),
        name="recv",
    )(own, plan, *raws)


def call_turn(handed, arrived):
    return pl.pallas_call(
        lambda *_: None,
        out_shape=[jax.ShapeDtypeStruct(x.shape, x.dtype) for x in handed],
        in_specs=[spec(ANY)] * (len(handed) + len(arrived)),
        out_specs=[spec(ANY)] * len(handed),
        input_output_aliases={i: i for i in range(len(handed))},
        compiler_params=pltpu.CompilerParams(vmem_limit_bytes=SMALL),
        cost_estimate=cost(1000, 1000),
        name="turn",
    )(*handed, *arrived)


def call_compute(sz, plan, tokens, cot, chunks):
    T = sz.n_tensor
    bf, f32 = jnp.bfloat16, jnp.float32

    def blocks(n):
        return jax.ShapeDtypeStruct((max(n, 1), BLK, BLK), bf)

    out_shape = [
        blocks(sz.ring * sz.keep),
        blocks(sz.far * sz.keep),
        blocks((sz.ring - sz.far) * sz.keep),
        blocks(sz.blocks - sz.main),
        blocks(sz.more),
    ]
    out_shape += [blocks(sz.first)] * T + [blocks(sz.rest)] * T
    scratch = [
        ((3 * sz.room, sz.tok, BLK), bf),
        ((sz.blocks + 1, BLK, BLK), bf),
        ((sz.blocks + 1, BLK, BLK), bf),
        ((sz.slots + 1, sz.tok, BLK), f32),
        ((sz.slots + 1, sz.tok, BLK), f32),
        ((sz.slots + 1, sz.tok, BLK), f32),
        ((sz.slots + 1, sz.tok, BLK), bf),
        ((sz.slots + 1, sz.tok, BLK), bf),
        ((sz.slots + 1, sz.tok, BLK), bf),
        ((sz.all + 1, sz.tok, BLK), f32),
        ((T * sz.send_all, sz.tok, BLK), bf),
    ]
    held = sum(s[0] * s[1] * s[2] * jnp.dtype(t).itemsize for s, t in scratch)
    return pl.pallas_call(
        functools.partial(compute_kernel, sz),
        out_shape=out_shape,
        in_specs=[spec(SMEM)] + [spec(HBM)] * 2 + [spec(ANY)] * len(chunks),
        out_specs=[spec(ANY)] * len(out_shape),
        scratch_shapes=[pltpu.VMEM(s, t) for s, t in scratch] + [
            pltpu.SemaphoreType.DMA((3 * sz.room,)),
            pltpu.SemaphoreType.DMA((max(len(chunks), 3 + T),)),
            pltpu.SemaphoreType.DMA((T + 1,)),
        ],
        compiler_params=pltpu.CompilerParams(vmem_limit_bytes=held + 2 * 1024 * 1024),
        cost_estimate=cost(1_000_000_000, 20_000_000),
        name="compute",
    )(plan, pltpu.with_memory_space_constraint(tokens, HBM), pltpu.with_memory_space_constraint(cot, HBM), *chunks)


def call_join(sz, plan, recv, firsts, rests):
    half = jax.ShapeDtypeStruct((sz.tok, sz.width // sz.n_tensor), jnp.bfloat16)
    return pl.pallas_call(
        functools.partial(join_kernel, sz),
        out_shape=[half, half],
        in_specs=[spec(SMEM)] * 2 + [spec(VMEM)] * len(firsts) + [spec(ANY)] * len(rests),
        out_specs=[spec(VMEM), spec(VMEM)],
        scratch_shapes=[pltpu.VMEM((sz.tok, BLK), jnp.bfloat16), pltpu.SemaphoreType.DMA],
        compiler_params=pltpu.CompilerParams(vmem_limit_bytes=10 * 1024 * 1024),
        cost_estimate=cost(1_000_000, 6_000_000),
        name="join",
    )(plan, recv, *firsts, *rests)


def call_finish(sz, plan, here, ahead, behind, late):
    out = jax.ShapeDtypeStruct((1, sz.nb, BLK, BLK), jnp.bfloat16)
    return pl.pallas_call(
        functools.partial(finish_kernel, sz),
        out_shape=[out] * 3,
        in_specs=[spec(SMEM)] + [spec(VMEM)] * 4,
        out_specs=[spec(VMEM)] * 3,
        compiler_params=pltpu.CompilerParams(vmem_limit_bytes=SMALL),
        cost_estimate=cost(1_000_000, 1_000_000),
        name="finish",
    )(plan, here, ahead, behind, late)


def gather_chunks(sz, chunk, beside=()):
    ahead, behind, swap = permutations(sz)
    same = {0: chunk}
    a = b = chunk
    for s in range(1, sz.top):
        a, b = lax.ppermute(a, "fsdp", ahead), lax.ppermute(b, "fsdp", behind)
        if s <= len(beside):
            a, b = call_turn([a, b], [beside[s - 1]])
        same[sz.ring - s], same[s] = a, b
    other = {d: lax.ppermute(same[d], "fsdp", swap) for d in same}
    same[sz.top] = lax.ppermute(a, "fsdp", ahead)
    other[sz.top] = lax.ppermute(a, "fsdp", [(i, j ^ 1) for i, j in ahead])
    return [side[d] for side in (same, other) for d in sz.order]


def reduce_parts(sz, per, same, pair, beside=lambda a: a):
    ahead, behind, _ = permutations(sz)

    def wide(d, *more):
        j = sz.order.index(d)
        out = same[j * per:(j + 1) * per].astype(jnp.float32) + pair(j).astype(jnp.float32)
        for m in more:
            out = out + m.astype(jnp.float32)
        return out

    def term(d, *more):
        return wide(d, *more).astype(jnp.bfloat16)

    a, b = lax.optimization_barrier((term(sz.top), term(sz.top + 1)))
    for s in range(1, sz.top):
        a, b = lax.ppermute(a, "fsdp", ahead), lax.ppermute(b, "fsdp", behind)
        a = term(sz.top - s, a)
        if s + 1 < sz.top:
            a, b = lax.optimization_barrier((a, term(sz.top + 1 + s, b)))
    a = lax.ppermute(beside(a), "fsdp", ahead)
    return wide(0), a, b


def shards(
    tokens,
    cotangent,
    gate_blocks,
    up_blocks,
    down_blocks,
    gate_where,
    up_where,
    down_where,
    block_counts,
):
    n_fsdp, T = lax.axis_size("fsdp"), lax.axis_size("tensor")
    sz = Sizes(tokens, gate_blocks, gate_where.shape[1], n_fsdp, T)
    f, rank = lax.axis_index("fsdp"), lax.axis_index("tensor")
    swap = permutations(sz)[-1]

    chunk = jnp.concatenate([gate_blocks[0], up_blocks[0], down_blocks[0]])
    own = jnp.concatenate([
        gate_where[0], up_where[0], down_where[0], block_counts[:, 0],
        f.astype(jnp.int32)[None], rank.astype(jnp.int32)[None]])
    own = jnp.pad(own, (0, sz.lanes - own.shape[0]))[None]

    plan = call_plan(sz, own)
    raws = [lax.ppermute(own, "tensor", [(i, (i + s) % T) for i in range(T)]) for s in range(1, T)]
    recv, flag = call_recv(sz, own, plan, raws)
    chunks = gather_chunks(sz, chunk, (plan, recv))

    outs = call_compute(sz, plan, tokens, cotangent, chunks)
    same, far, near, extra, idle = outs[:5]
    firsts, rests = outs[5:5 + T], list(outs[5 + T:])

    def exchange(arrays):
        return [arrays[0]] + [
            lax.ppermute(arrays[s], "tensor", [(i, (i + s) % T) for i in range(T)]) for s in range(1, T)]

    far, near = lax.ppermute(far, "fsdp", swap), lax.ppermute(near, "fsdp", swap)
    firsts = exchange(firsts)

    def pair(j):
        at = j * sz.keep
        return far[at:at + sz.keep] if j < sz.far else near[at - sz.far * sz.keep:][:sz.keep]

    late = idle

    def beside(a):
        nonlocal rests, late
        a, more = call_turn([a, extra], [])
        if sz.rest + sz.more == 0:
            return a

        def spill(rests, extra, idle):
            moved = exchange(rests)
            if sz.more == 0:
                return moved, idle
            n = sz.ring * sz.more
            other = lax.ppermute(extra[n:], "fsdp", swap)
            terms = reduce_parts(sz, sz.more, extra[:n], lambda j: other[j * sz.more:(j + 1) * sz.more])
            return moved, sum(t.astype(jnp.float32) for t in terms).astype(jnp.bfloat16)

        rests, late = lax.cond(flag[0, 0] > 0, spill, lambda r, e, i: (r, i), rests, more, idle)
        return a

    here, ahead, behind = reduce_parts(sz, sz.keep, same, pair, beside)
    outputs, input_grads = call_join(sz, plan, recv, firsts, rests)
    grads = call_finish(sz, plan, here, ahead, behind, late)
    return (outputs, input_grads, *grads)


def solution(mesh):
    placed = (
        P("fsdp", None),
        P("fsdp", None),
        P("tensor", "fsdp", None, None),
        P("tensor", "fsdp", None, None),
        P("tensor", "fsdp", None, None),
        P("tensor", None),
        P("tensor", None),
        P("tensor", None),
        P(None, "tensor"),
    )
    return jax.shard_map(
        shards,
        mesh=mesh,
        in_specs=placed,
        out_specs=(
            P("fsdp", "tensor"),
            P("fsdp", "tensor"),
            P("tensor", "fsdp", None, None),
            P("tensor", "fsdp", None, None),
            P("tensor", "fsdp", None, None),
        ),
        check_vma=False,
    )
```

```python
import functools

import jax
import jax.numpy as jnp
from jax import lax
from jax.experimental import pallas as pl
from jax.experimental.pallas import tpu as pltpu
from jax.sharding import PartitionSpec as P

FF = 14336
BLK = 128
GROUP = 4
FIRST_SEND = 18
LEAN_SLOTS = 4
SMALL = 4 * 1024 * 1024
PART, STRIP, CIDX, CWAS, OIDX, OWAS = range(6)
FIELDS = 6
COLS_ROW = 3 * FIELDS
HEAD_ROW = COLS_ROW + 1
MINE_ROW = COLS_ROW + 2
LISTS_ROW = COLS_ROW + 3
HEAD_COLS, HEAD_LISTS = 3, 8


class Sizes:
    def __init__(self, tokens, gate_blocks, slots, n_fsdp, n_tensor, lean):
        self.tok, self.width = tokens.shape
        self.n_fsdp, self.n_tensor = n_fsdp, n_tensor
        self.rb = self.width // BLK
        self.cb = FF // (BLK * n_tensor)
        self.slots = slots
        self.all = 3 * slots
        self.lanes = -(-(self.all + GROUP) // 128) * 128
        self.nb = gate_blocks.shape[1]
        self.owned = 3 * self.nb
        self.ring = n_fsdp // 2
        self.top = self.ring // 2
        self.rbt = self.rb // n_tensor
        self.order = [self.top]
        for d in range(1, self.top):
            self.order += [self.top + d, self.top - d]
        self.order.append(0)
        self.far = min(4, self.ring - 1)
        self.keep = min(LEAN_SLOTS, self.owned) if lean else self.owned
        self.send_all = 2 * self.rbt
        self.first = min(FIRST_SEND, self.send_all) if lean else self.send_all
        self.blocks = 2 * self.ring * self.keep
        self.plan_rows = -(-(LISTS_ROW + 2 * n_tensor) // 8) * 8
        self.recv_rows = -(-n_tensor // 8) * 8
        self.room = slots + GROUP


def permutations(sz):
    seq = list(range(0, sz.ring, 2)) + list(range(sz.ring - 1, 0, -2))
    ahead, behind, swap = [], [], []
    for i, q in enumerate(seq):
        up, down = seq[(i + 1) % sz.ring], seq[i - 1]
        ahead += [(q * 2, up * 2), (q * 2 + 1, down * 2 + 1)]
        behind += [(q * 2, down * 2), (q * 2 + 1, up * 2 + 1)]
        swap += [(q * 2, q * 2 + 1), (q * 2 + 1, q * 2)]
    return ahead, behind, swap


def ratio(x, d):
    return jnp.floor((x + 0.5) * (1.0 / d))


def rest_of(x, d):
    return x - d * ratio(x, d)


def ring_position(sz, chip):
    return jnp.where(rest_of(chip, 2) == 0, ratio(chip, 2), sz.ring - 1 - ratio(chip, 2))


class Marks:
    def __init__(self, sz, own, raw):
        N, L, S = sz.all, sz.lanes, sz.slots
        f32 = jnp.float32
        self.sz = sz
        self.sub = lax.broadcasted_iota(jnp.int32, (N, L), 0)
        self.lane = lax.broadcasted_iota(jnp.int32, (N, L), 1)
        self.same = self.sub == self.lane
        sub_c = self.sub[:, :1].astype(f32)
        lane_r = lax.broadcasted_iota(jnp.int32, (1, L), 1).astype(f32)
        self.sub_c, self.lane_r = sub_c, lane_r
        raw_r = raw[...].astype(f32)
        own_r = own[...].astype(f32)

        def single(row, at):
            return jnp.sum(jnp.where(lane_r == at, row, 0.0), axis=1, keepdims=True)

        self.f, self.rank = single(own_r, N + 3), single(own_r, N + 4)

        def kind(x):
            return (x >= S).astype(f32) + (x >= 2 * S).astype(f32)

        self.kind_c, self.kind_r = kind(sub_c), kind(lane_r)
        self.n_r = lane_r - S * self.kind_r
        self.n_c = sub_c - S * self.kind_c
        limit = jnp.zeros((1, L), f32)
        for k in range(3):
            limit = limit + jnp.where(self.kind_r == k, single(raw_r, N + k), 0.0)
        live_r = jnp.where((lane_r < N) & (self.n_r < limit), 1.0, 0.0)
        w_c = self.col(raw_r)
        live_c = self.col(live_r)

        def place(w, k):
            gate, down = ratio(w, sz.cb), ratio(w, sz.rb)
            is_down = k == 2
            return jnp.where(is_down, w - down * sz.rb, gate), jnp.where(is_down, down, w - gate * sz.cb)

        self.row_c, col_c = place(w_c, self.kind_c)
        self.row_r, col_r = place(raw_r, self.kind_r)
        self.chip_c, chip_r = ratio(self.n_c, 2 * sz.nb), ratio(self.n_r, 2 * sz.nb)
        self.same_chip = (self.chip_c == chip_r).astype(f32)
        self.same_col = (col_c == col_r).astype(f32)
        act_c, act_r = live_c, live_r
        for k in range(3):
            lanes = self.same_col * (live_r * (self.kind_r == k).astype(f32))
            act_c = act_c * jnp.max(lanes, axis=1, keepdims=True)
            subs = self.same_col * (live_c * (self.kind_c == k).astype(f32))
            act_r = act_r * jnp.max(subs, axis=0, keepdims=True)
        self.act_c, self.act_r = act_c, act_r
        out_c = jnp.where(self.kind_c == 2, 0.0, f32(sz.rb)) + self.row_c
        out_r = jnp.where(self.kind_r == 2, 0.0, f32(sz.rb)) + self.row_r
        self.same_out = (out_c == out_r).astype(f32)
        self.before = (self.lane < self.sub).astype(f32)
        self.after = (self.sub < self.lane).astype(f32)
        self.owas_c = jnp.max(self.same_out * self.before * act_r, axis=1, keepdims=True)
        self.owas_r = jnp.max(self.same_out * self.after * act_c, axis=0, keepdims=True)
        self.lead_c = act_c * (1.0 - self.owas_c)
        self.lead_r = act_r * (1.0 - self.owas_r)

        def shift(row):
            away = ratio(row, sz.rbt) - self.rank
            return jnp.where(away < 0, away + sz.n_tensor, away)

        self.shift_c, self.shift_r = shift(self.row_c), shift(self.row_r)
        self.local_c = jnp.where(self.kind_c == 2, 0.0, f32(sz.rbt)) + rest_of(self.row_c, sz.rbt)

    def col(self, row):
        return jnp.sum(jnp.where(self.same, row, 0.0), axis=1, keepdims=True)

    def carried(self):
        sz = self.sz
        rank = jnp.sum(self.before * self.same_chip * self.act_r, axis=1, keepdims=True)
        core = rest_of(rank, 2)
        away = ring_position(sz, self.chip_c) - ring_position(sz, ratio(self.f, 2))
        away = jnp.where(core == 0, away, -away)
        rel = jnp.where(away < 0, away + sz.ring, away)
        j = jnp.where(rel > sz.top, 2 * (rel - sz.top) - 1, 2 * (sz.top - rel))
        j = jnp.where(rel == 0, sz.ring - 1.0, j)
        return core, ratio(rank, 2), j + jnp.where(core == rest_of(self.f, 2), 0.0, float(sz.ring))

    def ranks(self, chosen_r):
        return jnp.sum(self.before * chosen_r, axis=1, keepdims=True)

    def listed(self, chosen_c, rank_c, value_c, lo=0, hi=None):
        at = rank_c[lo:hi] == self.lane[lo:hi].astype(jnp.float32)
        return jnp.sum(jnp.where(at, chosen_c[lo:hi] * value_c[lo:hi], 0.0), axis=0, keepdims=True)

    def most_on_chip(self):
        return jnp.max(jnp.sum(self.same_chip * self.act_r, axis=1, keepdims=True), axis=0, keepdims=True)


def total(x):
    return jnp.sum(x, axis=0, keepdims=True)


def head_row(sz, entries):
    lane = lax.broadcasted_iota(jnp.int32, (1, sz.lanes), 1)
    row = jnp.zeros((1, sz.lanes), jnp.float32)
    for i, value in entries:
        row = jnp.where(lane == i, value, row)
    return row


def plan_kernel(sz, own, *refs):
    mine, theirs, plan, chunk, sems = refs[:3], refs[3:6], *refs[6:]
    S, N = sz.slots, sz.all
    m = Marks(sz, own, own)
    f32 = jnp.float32
    lane_r, sub_c = m.lane_r, m.sub_c
    core_c, pos_c, base_c = m.carried()
    own_core = core_c == rest_of(m.f, 2)

    pair = jnp.where(rest_of(m.f, 2) == 0, m.f + 1, m.f - 1)
    i_r = rest_of(lane_r, sz.owned)
    owner_r = jnp.where(lane_r < sz.owned, m.f, pair)
    slot_r = ratio(i_r, sz.nb) * S + owner_r * sz.nb + rest_of(i_r, sz.nb)
    at_r = jnp.sum(
        jnp.where((sub_c == slot_r) & own_core, m.act_c * (pos_c + 1.0), 0.0), axis=0, keepdims=True)
    copies = []
    for i in range(2 * sz.owned):
        side, k, a = i // sz.owned, i % sz.owned // sz.nb, i % sz.nb
        at = jnp.max(jnp.where(lane_r == i, at_r, 0.0)).astype(jnp.int32)
        fits = (at > 0) & (at <= sz.keep)
        place = jnp.minimum(jnp.maximum(at - 1, 0), sz.keep - 1)
        copy = pltpu.make_async_copy((mine, theirs)[side][k].at[0, a], chunk.at[place], sems.at[i])
        copies.append((fits, copy))
    for fits, copy in copies:
        pl.when(fits)(copy.start)

    same_kind = (m.kind_c == m.kind_r).astype(f32)
    rank_c = jnp.sum(m.before * same_kind * m.act_r, axis=1, keepdims=True)
    cwas_c = jnp.max(m.before * same_kind * m.same_col * m.act_r, axis=1, keepdims=True)
    cwas_r = jnp.max(m.after * same_kind * m.same_col * m.act_c, axis=0, keepdims=True)
    big = f32(4 * N)
    lanes_f = m.lane.astype(f32)
    gates_r = m.act_r * (m.kind_r == 0).astype(f32)
    cidx_c = jnp.min(jnp.where(m.same_col * gates_r > 0, lanes_f, big), axis=1, keepdims=True)
    oidx_c = jnp.min(jnp.where(m.same_out * m.act_r > 0, lanes_f, big), axis=1, keepdims=True)
    part_c = jnp.where(pos_c < sz.keep, base_c * sz.keep + pos_c, f32(sz.blocks))
    fields = [(part_c, sz.blocks), (m.row_c, 0), (cidx_c, S), (cwas_c, 0), (oidx_c, N), (m.owas_c, 0)]
    rows = []
    head = []
    for k in range(3):
        lo, hi = k * S, (k + 1) * S
        n_k = total(m.act_c[lo:hi])
        head.append((k, n_k))
        for value, spare in fields:
            row = m.listed(m.act_c, rank_c, value, lo, hi)
            rows.append(jnp.where(lane_r < n_k, row, f32(spare)))
    leader_c = m.act_c * (1.0 - cwas_c) * (m.kind_c == 0).astype(f32)
    leader_r = m.act_r * (1.0 - cwas_r) * (m.kind_r == 0).astype(f32)
    rows.append(m.listed(leader_c, m.ranks(leader_r), sub_c, 0, S))
    head.append((HEAD_COLS, total(leader_c)))
    lists = []
    for s in range(sz.n_tensor):
        chosen_c = m.lead_c * (m.shift_c == s).astype(f32)
        chosen_r = m.lead_r * (m.shift_r == s).astype(f32)
        rank = m.ranks(chosen_r)
        lists.append(m.listed(chosen_c, rank, sub_c))
        lists.append(m.listed(chosen_c, rank, m.local_c))
        head.append((HEAD_LISTS + s, total(chosen_c)))
    rows.append(head_row(sz, head))
    held_c = pos_c + 1.0 + jnp.where(own_core, 0.0, float(sz.keep))
    rows.append(jnp.sum(
        jnp.where((sub_c == slot_r) & (lane_r < sz.owned), m.act_c * held_c, 0.0), axis=0, keepdims=True))
    rows += lists
    for i, row in enumerate(rows):
        plan[i:i + 1, :] = row.astype(jnp.int32)
    for fits, copy in copies:
        pl.when(fits)(copy.wait)


def recv_kernel(sz, *refs):
    own, raws, recv, flag = refs[0], refs[1:sz.n_tensor], refs[-2], refs[-1]
    f32 = jnp.float32
    head = []
    over = jnp.zeros((1, 1), f32)
    for s, raw in enumerate((own, *raws)):
        m = Marks(sz, own, raw)
        if s:
            chosen_c = m.lead_c * (m.shift_c == 0).astype(f32)
            chosen_r = m.lead_r * (m.shift_r == 0).astype(f32)
            recv[s:s + 1, :] = m.listed(chosen_c, m.ranks(chosen_r), m.local_c).astype(jnp.int32)
            head.append((HEAD_LISTS + s, total(chosen_c)))
        over = jnp.maximum(over, (m.most_on_chip() > 2 * sz.keep).astype(f32))
        for d in range(sz.n_tensor):
            n = total(m.lead_c * (m.shift_c == d).astype(f32))
            over = jnp.maximum(over, (n > sz.first).astype(f32))
    flag[...] = over.astype(jnp.int32)
    recv[0:1, :] = head_row(sz, head).astype(jnp.int32)


def dot(a, b, ca, cb):
    return lax.dot_general(a, b, (((ca,), (cb,)), ((), ())), preferred_element_type=jnp.float32)


def field(sz, plan, k, j, e):
    return plan[k * FIELDS + j, e]


def walk(plan, k, body):
    steps = (plan[HEAD_ROW, k] + (GROUP - 1)) // GROUP
    lax.fori_loop(0, steps, lambda p, _: body(p * GROUP), None)


def each(plan, k, body):
    lax.fori_loop(0, plan[HEAD_ROW, k], lambda e, _: body(e), None)


def load_chunks(sz, chunks, wbuf, sems):
    return [
        pltpu.make_async_copy(chunk, wbuf.at[pl.ds(i * sz.keep, sz.keep)], sems.at[i])
        for i, chunk in enumerate(chunks)
    ]


def grads_kernel(sz, plan, tokens, cot, *refs):
    n_chunks = 2 * sz.ring
    chunks, refs = refs[:n_chunks], refs[n_chunks:]
    same, far, near, acts = refs[:4]
    (xs, wbuf, parts, gate_acc, up_acc, hg_acc, act_buf, strip_sems, sems, part_sems, act_sems) = refs[4:]
    get = functools.partial(field, sz, plan)

    def strip_copy(k, e):
        src = cot if k == 2 else tokens
        cols = pl.ds(pl.multiple_of(get(k, STRIP, e) * BLK, BLK), BLK)
        return pltpu.make_async_copy(src.at[:, cols], xs.at[k * sz.room + e], strip_sems.at[k * sz.room + e])

    for k in range(3):
        each(plan, k, lambda e, k=k: strip_copy(k, e).start())
    loads = load_chunks(sz, chunks, wbuf, sems)
    for c in loads:
        c.start()
    for c in loads:
        c.wait()
    for k in range(3):
        each(plan, k, lambda e, k=k: strip_copy(k, e).wait())

    def forward(k, acc, w_dim):
        def body(e0):
            prods = [
                dot(xs[k * sz.room + e0 + u], wbuf[get(k, PART, e0 + u)], 1, w_dim) for u in range(GROUP)]
            for u in range(GROUP):
                c = get(k, CIDX, e0 + u)
                acc[c] = prods[u] + jnp.where(get(k, CWAS, e0 + u) == 0, 0.0, acc[c])

        walk(plan, k, body)

    forward(0, gate_acc, 0)
    forward(1, up_acc, 0)
    forward(2, hg_acc, 1)
    A = sz.slots + 1

    def act_copy(i, j):
        at = j * A + plan[COLS_ROW, i]
        return pltpu.make_async_copy(act_buf.at[at], acts.at[at], act_sems.at[j * A + i])

    def column(i, _):
        c = plan[COLS_ROW, i]
        g, u, h = gate_acc[c], up_acc[c], hg_acc[c]
        s = lax.logistic(g)
        silu = g * s
        act_buf[c] = (h * u * s * (1.0 + g * (1.0 - s))).astype(jnp.bfloat16)
        act_buf[A + c] = (h * silu).astype(jnp.bfloat16)
        act_buf[2 * A + c] = (silu * u).astype(jnp.bfloat16)
        for j in range(3):
            act_copy(i, j).start()

    lax.fori_loop(0, plan[HEAD_ROW, HEAD_COLS], column, None)
    split = sz.ring * sz.keep
    cut = split + sz.far * sz.keep

    def part_copy(k, e, act):
        p = get(k, PART, e)
        sem = part_sems.at[k * sz.room + e]
        for ref, lo, hi in ((same, 0, split), (far, split, cut), (near, cut, sz.blocks)):
            @pl.when((p >= lo) & (p < hi))
            def _(ref=ref, lo=lo, hi=hi):
                at = jnp.minimum(jnp.maximum(p - lo, 0), hi - lo - 1)
                act(pltpu.make_async_copy(parts.at[p], ref.at[at], sem))

    for k in (2, 0, 1):
        def body(e0, k=k):
            grads = []
            for u in range(GROUP):
                a = act_buf[k * A + get(k, CIDX, e0 + u)]
                x = xs[k * sz.room + e0 + u]
                grads.append(dot(a, x, 0, 0) if k == 2 else dot(x, a, 0, 0))
            for u in range(GROUP):
                parts[get(k, PART, e0 + u)] = grads[u].astype(jnp.bfloat16)

        walk(plan, k, body)
        each(plan, k, lambda e, k=k: part_copy(k, e, lambda c: c.start()))

    for k in range(3):
        each(plan, k, lambda e, k=k: part_copy(k, e, lambda c: c.wait()))

    def act_wait(i, _):
        for j in range(3):
            act_copy(i, j).wait()

    lax.fori_loop(0, plan[HEAD_ROW, HEAD_COLS], act_wait, None)


def terms_kernel(sz, plan, acts, *refs):
    T = sz.n_tensor
    n_chunks = 2 * sz.ring
    chunks, firsts = refs[:n_chunks], refs[n_chunks:n_chunks + T]
    wbuf, act_buf, out_acc, stage, sems, act_sems = refs[n_chunks + T:]
    get = functools.partial(field, sz, plan)
    A = sz.slots + 1

    def act_copy(i, j):
        at = j * A + plan[COLS_ROW, i]
        return pltpu.make_async_copy(acts.at[at], act_buf.at[at], act_sems.at[j * A + i])

    def columns(act):
        def step(i, _):
            for j in range(3):
                act(act_copy(i, j))

        lax.fori_loop(0, plan[HEAD_ROW, HEAD_COLS], step, None)

    columns(lambda c: c.start())
    loads = load_chunks(sz, chunks, wbuf, sems)
    for c in loads:
        c.start()
    for c in loads:
        c.wait()
    columns(lambda c: c.wait())

    for k in (2, 0, 1):
        def body(e0, k=k):
            terms = [
                dot(act_buf[k * A + get(k, CIDX, e0 + u)], wbuf[get(k, PART, e0 + u)], 1, 0 if k == 2 else 1)
                for u in range(GROUP)]
            for u in range(GROUP):
                at = get(k, OIDX, e0 + u)
                out_acc[at] = terms[u] + jnp.where(get(k, OWAS, e0 + u) == 0, 0.0, out_acc[at])

        walk(plan, k, body)

    outs = []
    for s in range(T):
        def staged(i, _, s=s):
            stage[s * sz.first + i] = out_acc[plan[LISTS_ROW + 2 * s, i]].astype(jnp.bfloat16)

        lax.fori_loop(0, jnp.minimum(plan[HEAD_ROW, HEAD_LISTS + s], sz.first), staged, None)
        copy = pltpu.make_async_copy(stage.at[pl.ds(s * sz.first, sz.first)], firsts[s], sems.at[s])
        copy.start()
        outs.append(copy)
    for c in outs:
        c.wait()


def join_kernel(sz, plan, recv, *refs):
    T = sz.n_tensor
    firsts, (outputs, input_grads) = refs[:T], refs[T:]
    outputs[...] = jnp.zeros_like(outputs)
    input_grads[...] = jnp.zeros_like(input_grads)

    def add(at, value):
        def into(ref, w):
            cols = pl.ds(pl.multiple_of(w * BLK, BLK), BLK)
            ref[:, cols] = (ref[:, cols].astype(jnp.float32) + value.astype(jnp.float32)).astype(jnp.bfloat16)

        @pl.when(at < sz.rbt)
        def _():
            into(outputs, at)

        @pl.when(at >= sz.rbt)
        def _():
            into(input_grads, at - sz.rbt)

    for s in range(T):
        n = (recv[0, HEAD_LISTS + s] if s else plan[HEAD_ROW, HEAD_LISTS])

        def step(i, _, s=s):
            add(recv[s, i] if s else plan[LISTS_ROW + 1, i], firsts[s][i])

        lax.fori_loop(0, jnp.minimum(n, sz.first), step, None)


def finish_kernel(sz, plan, *refs):
    mine, theirs, outs = refs[:3], refs[3:6], refs[6:]
    for k in range(3):
        for a in range(sz.nb):
            at = plan[MINE_ROW, k * sz.nb + a]

            def value(terms, p):
                p = jnp.minimum(jnp.maximum(p, 0), sz.keep - 1)
                return sum(t[p].astype(jnp.float32) for t in terms)

            out = jnp.where(at > sz.keep, value(theirs, at - 1 - sz.keep), value(mine, at - 1))
            outs[k][0, a] = jnp.where(at > 0, out, 0.0).astype(jnp.bfloat16)


def spec(space):
    return pl.BlockSpec(memory_space=space)


ANY, HBM, VMEM, SMEM = pl.ANY, pltpu.HBM, pltpu.VMEM, pltpu.SMEM


def cost(flops, moved):
    return pl.CostEstimate(flops=flops, bytes_accessed=moved, transcendentals=0)


def call_plan(sz, own, mine, theirs):
    return pl.pallas_call(
        functools.partial(plan_kernel, sz),
        out_shape=[
            jax.ShapeDtypeStruct((sz.plan_rows, sz.lanes), jnp.int32),
            jax.ShapeDtypeStruct((sz.keep, BLK, BLK), jnp.bfloat16),
        ],
        in_specs=[spec(VMEM)] + [spec(ANY)] * 6,
        out_specs=[spec(VMEM), spec(ANY)],
        scratch_shapes=[pltpu.SemaphoreType.DMA((2 * sz.owned,))],
        compiler_params=pltpu.CompilerParams(vmem_limit_bytes=SMALL),
        cost_estimate=cost(1_000_000, 4_000_000),
        name="plan",
    )(own, *mine, *theirs)


def call_recv(sz, own, raws):
    return pl.pallas_call(
        functools.partial(recv_kernel, sz),
        out_shape=[
            jax.ShapeDtypeStruct((sz.recv_rows, sz.lanes), jnp.int32),
            jax.ShapeDtypeStruct((1, 1), jnp.int32),
        ],
        in_specs=[spec(VMEM)] * (1 + len(raws)),
        out_specs=[spec(VMEM)] * 2,
        compiler_params=pltpu.CompilerParams(vmem_limit_bytes=SMALL),
        cost_estimate=cost(1_000_000, 4_000_000),
        name="recv",
    )(own, *raws)


def call_turn(handed, arrived):
    return pl.pallas_call(
        lambda *_: None,
        out_shape=[jax.ShapeDtypeStruct(x.shape, x.dtype) for x in handed],
        in_specs=[spec(ANY)] * (len(handed) + len(arrived)),
        out_specs=[spec(ANY)] * len(handed),
        input_output_aliases={i: i for i in range(len(handed))},
        compiler_params=pltpu.CompilerParams(vmem_limit_bytes=SMALL),
        cost_estimate=cost(1000, 1000),
        name="turn",
    )(*handed, *arrived)


def blocks(n):
    return jax.ShapeDtypeStruct((n, BLK, BLK), jnp.bfloat16)


def held(scratch):
    return sum(s[0] * s[1] * s[2] * jnp.dtype(t).itemsize for s, t in scratch) + 2 * 1024 * 1024


def call_grads(sz, plan, tokens, cot, chunks):
    bf, f32 = jnp.bfloat16, jnp.float32
    A = sz.slots + 1
    out_shape = [blocks(sz.ring * sz.keep), blocks(sz.far * sz.keep), blocks((sz.ring - sz.far) * sz.keep), blocks(3 * A)]
    scratch = [
        ((3 * sz.room, sz.tok, BLK), bf),
        ((sz.blocks + 1, BLK, BLK), bf),
        ((sz.blocks + 1, BLK, BLK), bf),
        ((A, sz.tok, BLK), f32),
        ((A, sz.tok, BLK), f32),
        ((A, sz.tok, BLK), f32),
        ((3 * A, sz.tok, BLK), bf),
    ]
    return pl.pallas_call(
        functools.partial(grads_kernel, sz),
        out_shape=out_shape,
        in_specs=[spec(SMEM)] + [spec(HBM)] * 2 + [spec(ANY)] * len(chunks),
        out_specs=[spec(ANY)] * len(out_shape),
        scratch_shapes=[pltpu.VMEM(s, t) for s, t in scratch] + [
            pltpu.SemaphoreType.DMA((3 * sz.room,)),
            pltpu.SemaphoreType.DMA((len(chunks),)),
            pltpu.SemaphoreType.DMA((3 * sz.room,)),
            pltpu.SemaphoreType.DMA((3 * A,)),
        ],
        compiler_params=pltpu.CompilerParams(vmem_limit_bytes=held(scratch)),
        cost_estimate=cost(1_000_000_000, 20_000_000),
        name="grads",
    )(plan, pltpu.with_memory_space_constraint(tokens, HBM), pltpu.with_memory_space_constraint(cot, HBM), *chunks)


def call_terms(sz, plan, acts, chunks):
    T = sz.n_tensor
    bf, f32 = jnp.bfloat16, jnp.float32
    A = sz.slots + 1
    scratch = [
        ((sz.blocks + 1, BLK, BLK), bf),
        ((3 * A, sz.tok, BLK), bf),
        ((sz.all + 1, sz.tok, BLK), f32),
        ((T * sz.first, sz.tok, BLK), bf),
    ]
    return pl.pallas_call(
        functools.partial(terms_kernel, sz),
        out_shape=[blocks(sz.first)] * T,
        in_specs=[spec(SMEM)] + [spec(ANY)] * (1 + len(chunks)),
        out_specs=[spec(ANY)] * T,
        scratch_shapes=[pltpu.VMEM(s, t) for s, t in scratch] + [
            pltpu.SemaphoreType.DMA((max(len(chunks), T),)),
            pltpu.SemaphoreType.DMA((3 * A,)),
        ],
        compiler_params=pltpu.CompilerParams(vmem_limit_bytes=held(scratch)),
        cost_estimate=cost(400_000_000, 8_000_000),
        name="terms",
    )(plan, acts, *chunks)


def call_join(sz, plan, recv, firsts):
    half = jax.ShapeDtypeStruct((sz.tok, sz.width // sz.n_tensor), jnp.bfloat16)
    return pl.pallas_call(
        functools.partial(join_kernel, sz),
        out_shape=[half, half],
        in_specs=[spec(SMEM)] * 2 + [spec(VMEM)] * len(firsts),
        out_specs=[spec(VMEM), spec(VMEM)],
        compiler_params=pltpu.CompilerParams(vmem_limit_bytes=12 * 1024 * 1024),
        cost_estimate=cost(1_000_000, 6_000_000),
        name="join",
    )(plan, recv, *firsts)


def call_finish(sz, plan, terms):
    out = jax.ShapeDtypeStruct((1, sz.nb, BLK, BLK), jnp.bfloat16)
    return pl.pallas_call(
        functools.partial(finish_kernel, sz),
        out_shape=[out] * 3,
        in_specs=[spec(SMEM)] + [spec(VMEM)] * len(terms),
        out_specs=[spec(VMEM)] * 3,
        compiler_params=pltpu.CompilerParams(vmem_limit_bytes=SMALL),
        cost_estimate=cost(1_000_000, 1_000_000),
        name="finish",
    )(plan, *terms)


def gather_chunks(sz, chunk, recv):
    ahead, behind, swap = permutations(sz)
    same = {0: chunk}
    a = b = chunk
    for s in range(1, sz.top):
        a, b = lax.ppermute(a, "fsdp", ahead), lax.ppermute(b, "fsdp", behind)
        if s == 2:
            a, b = call_turn([a, b], [recv])
        same[sz.ring - s], same[s] = a, b
    other = {d: lax.ppermute(same[d], "fsdp", swap) for d in same}
    same[sz.top] = lax.ppermute(a, "fsdp", ahead)
    other[sz.top] = lax.ppermute(a, "fsdp", [(i, j ^ 1) for i, j in ahead])
    return [side[d] for side in (same, other) for d in sz.order]


def reduce_parts(sz, same, far, near, sent):
    ahead, behind, swap = permutations(sz)
    keep = sz.keep
    far, near = lax.ppermute(far, "fsdp", swap), lax.ppermute(near, "fsdp", swap)

    def term(d, *more):
        j = sz.order.index(d)
        pair = far[j * keep:(j + 1) * keep] if j < sz.far else near[(j - sz.far) * keep:][:keep]
        out = same[j * keep:(j + 1) * keep].astype(jnp.float32) + pair.astype(jnp.float32)
        for m in more:
            out = out + m.astype(jnp.float32)
        return out.astype(jnp.bfloat16)

    a, b = lax.optimization_barrier((term(sz.top), term(sz.top + 1)))
    for s in range(1, sz.top):
        if s == 2:
            a, b = call_turn([a, b], sent)
        a, b = lax.ppermute(a, "fsdp", ahead), lax.ppermute(b, "fsdp", behind)
        a = term(sz.top - s, a)
        if s + 1 < sz.top:
            a, b = lax.optimization_barrier((a, term(sz.top + 1 + s, b)))
    here = term(0)
    mine = [here, lax.ppermute(a, "fsdp", ahead), b]
    theirs = [
        lax.ppermute(here, "fsdp", swap),
        lax.ppermute(a, "fsdp", [(i, j ^ 1) for i, j in ahead]),
        lax.ppermute(b, "fsdp", swap),
    ]
    return mine + theirs


def program(sz, own, tokens, cotangent, mine):
    T = sz.n_tensor
    swap = permutations(sz)[-1]
    theirs = [lax.ppermute(b, "fsdp", swap) for b in mine]
    plan, chunk = call_plan(sz, own, mine, theirs)

    def exchange(array, s):
        return lax.ppermute(array, "tensor", [(i, (i + s) % T) for i in range(T)])

    recv, flag = call_recv(sz, own, [exchange(own, s) for s in range(1, T)])
    chunks = gather_chunks(sz, chunk, recv)
    same, far, near, acts = call_grads(sz, plan, tokens, cotangent, chunks)
    sent = call_terms(sz, plan, acts, chunks)
    firsts = [sent[0]] + [exchange(sent[s], s) for s in range(1, T)]
    terms = reduce_parts(sz, same, far, near, sent[1:])
    outputs, input_grads = call_join(sz, plan, recv, firsts)
    return (outputs, input_grads, *call_finish(sz, plan, terms)), flag


def shards(
    tokens,
    cotangent,
    gate_blocks,
    up_blocks,
    down_blocks,
    gate_where,
    up_where,
    down_where,
    block_counts,
):
    n_fsdp, n_tensor = lax.axis_size("fsdp"), lax.axis_size("tensor")
    f, rank = lax.axis_index("fsdp"), lax.axis_index("tensor")
    slots = gate_where.shape[1]
    full = Sizes(tokens, gate_blocks, slots, n_fsdp, n_tensor, False)
    own = jnp.concatenate([
        gate_where[0], up_where[0], down_where[0], block_counts[:, 0],
        f.astype(jnp.int32)[None], rank.astype(jnp.int32)[None]])
    own = jnp.pad(own, (0, full.lanes - own.shape[0]))[None]
    blocks_in = (gate_blocks, up_blocks, down_blocks)
    if slots >= full.cb:
        return program(full, own, tokens, cotangent, blocks_in)[0]
    lean = Sizes(tokens, gate_blocks, slots, n_fsdp, n_tensor, True)
    outs, flag = program(lean, own, tokens, cotangent, blocks_in)
    return lax.cond(
        flag[0, 0] > 0,
        lambda outs, *args: program(full, *args)[0],
        lambda outs, *args: outs,
        outs, own, tokens, cotangent, blocks_in)


def solution(mesh):
    placed = (
        P("fsdp", None),
        P("fsdp", None),
        P("tensor", "fsdp", None, None),
        P("tensor", "fsdp", None, None),
        P("tensor", "fsdp", None, None),
        P("tensor", None),
        P("tensor", None),
        P("tensor", None),
        P(None, "tensor"),
    )
    return jax.shard_map(
        shards,
        mesh=mesh,
        in_specs=placed,
        out_specs=(
            P("fsdp", "tensor"),
            P("fsdp", "tensor"),
            P("tensor", "fsdp", None, None),
            P("tensor", "fsdp", None, None),
            P("tensor", "fsdp", None, None),
        ),
        check_vma=False,
    )
```

```python
import functools

import jax
import jax.numpy as jnp
from jax import lax
from jax.experimental import pallas as pl
from jax.experimental.pallas import tpu as pltpu
from jax.sharding import PartitionSpec as P

FF = 14336
BLK = 128
GROUP = 2
FIRST_SEND = 18
LEAN_SLOTS = 4
SMALL = 4 * 1024 * 1024
PART, STRIP, CIDX, CWAS, OIDX, OWAS = range(6)
FIELDS = 6
COLS_ROW = 3 * FIELDS
HEAD_ROW = COLS_ROW + 1
MINE_ROW = COLS_ROW + 2
LISTS_ROW = COLS_ROW + 3
HEAD_COLS, HEAD_OVER, HEAD_LISTS = 3, 4, 8


class Sizes:
    def __init__(self, tokens, gate_blocks, slots, n_fsdp, n_tensor, lean):
        self.tok, self.width = tokens.shape
        self.n_fsdp, self.n_tensor = n_fsdp, n_tensor
        self.rb = self.width // BLK
        self.cb = FF // (BLK * n_tensor)
        self.slots = slots
        self.all = 3 * slots
        self.lanes = -(-(self.all + GROUP) // 128) * 128
        self.nb = gate_blocks.shape[1]
        self.owned = 3 * self.nb
        self.ring = n_fsdp // 2
        self.top = self.ring // 2
        self.rbt = self.rb // n_tensor
        self.order = [self.top]
        for d in range(1, self.top):
            self.order += [self.top + d, self.top - d]
        self.order.append(0)
        self.far = min(4, self.ring - 1)
        self.keep = min(LEAN_SLOTS, self.owned) if lean else self.owned
        self.send_all = 2 * self.rbt
        self.first = min(FIRST_SEND, self.send_all) if lean else self.send_all
        self.blocks = 2 * self.ring * self.keep
        self.plan_rows = -(-(LISTS_ROW + 2 * n_tensor) // 8) * 8
        self.note_n, self.note_over = self.lanes - 1, self.lanes - 2
        self.room = slots + GROUP


def permutations(sz):
    seq = list(range(0, sz.ring, 2)) + list(range(sz.ring - 1, 0, -2))
    ahead, behind, swap = [], [], []
    for i, q in enumerate(seq):
        up, down = seq[(i + 1) % sz.ring], seq[i - 1]
        ahead += [(q * 2, up * 2), (q * 2 + 1, down * 2 + 1)]
        behind += [(q * 2, down * 2), (q * 2 + 1, up * 2 + 1)]
        swap += [(q * 2, q * 2 + 1), (q * 2 + 1, q * 2)]
    return ahead, behind, swap


def ratio(x, d):
    return jnp.floor((x + 0.5) * (1.0 / d))


def rest_of(x, d):
    return x - d * ratio(x, d)


def ring_position(sz, chip):
    return jnp.where(rest_of(chip, 2) == 0, ratio(chip, 2), sz.ring - 1 - ratio(chip, 2))


class Marks:
    def __init__(self, sz, own):
        N, L, S = sz.all, sz.lanes, sz.slots
        f32 = jnp.float32
        self.sz = sz
        self.sub = lax.broadcasted_iota(jnp.int32, (N, L), 0)
        self.lane = lax.broadcasted_iota(jnp.int32, (N, L), 1)
        self.same = self.sub == self.lane
        sub_c = self.sub[:, :1].astype(f32)
        lane_r = lax.broadcasted_iota(jnp.int32, (1, L), 1).astype(f32)
        self.sub_c, self.lane_r = sub_c, lane_r
        raw_r = own[...].astype(f32)

        def single(row, at):
            return jnp.sum(jnp.where(lane_r == at, row, 0.0), axis=1, keepdims=True)

        self.f, self.rank = single(raw_r, N + 3), single(raw_r, N + 4)

        def kind(x):
            return (x >= S).astype(f32) + (x >= 2 * S).astype(f32)

        self.kind_c, self.kind_r = kind(sub_c), kind(lane_r)
        self.n_r = lane_r - S * self.kind_r
        self.n_c = sub_c - S * self.kind_c
        limit = jnp.zeros((1, L), f32)
        for k in range(3):
            limit = limit + jnp.where(self.kind_r == k, single(raw_r, N + k), 0.0)
        live_r = jnp.where((lane_r < N) & (self.n_r < limit), 1.0, 0.0)
        w_c = self.col(raw_r)
        live_c = self.col(live_r)

        def place(w, k):
            gate, down = ratio(w, sz.cb), ratio(w, sz.rb)
            is_down = k == 2
            return jnp.where(is_down, w - down * sz.rb, gate), jnp.where(is_down, down, w - gate * sz.cb)

        self.row_c, col_c = place(w_c, self.kind_c)
        self.row_r, col_r = place(raw_r, self.kind_r)
        self.chip_c, chip_r = ratio(self.n_c, 2 * sz.nb), ratio(self.n_r, 2 * sz.nb)
        self.same_chip = (self.chip_c == chip_r).astype(f32)
        self.same_col = (col_c == col_r).astype(f32)
        act_c, act_r = live_c, live_r
        for k in range(3):
            lanes = self.same_col * (live_r * (self.kind_r == k).astype(f32))
            act_c = act_c * jnp.max(lanes, axis=1, keepdims=True)
            subs = self.same_col * (live_c * (self.kind_c == k).astype(f32))
            act_r = act_r * jnp.max(subs, axis=0, keepdims=True)
        self.act_c, self.act_r = act_c, act_r
        out_c = jnp.where(self.kind_c == 2, 0.0, f32(sz.rb)) + self.row_c
        out_r = jnp.where(self.kind_r == 2, 0.0, f32(sz.rb)) + self.row_r
        self.same_out = (out_c == out_r).astype(f32)
        self.before = (self.lane < self.sub).astype(f32)
        self.after = (self.sub < self.lane).astype(f32)
        self.owas_c = jnp.max(self.same_out * self.before * act_r, axis=1, keepdims=True)
        self.owas_r = jnp.max(self.same_out * self.after * act_c, axis=0, keepdims=True)
        self.lead_c = act_c * (1.0 - self.owas_c)
        self.lead_r = act_r * (1.0 - self.owas_r)

        def shift(row):
            away = ratio(row, sz.rbt) - self.rank
            return jnp.where(away < 0, away + sz.n_tensor, away)

        self.shift_c, self.shift_r = shift(self.row_c), shift(self.row_r)
        self.local_c = jnp.where(self.kind_c == 2, 0.0, f32(sz.rbt)) + rest_of(self.row_c, sz.rbt)

    def col(self, row):
        return jnp.sum(jnp.where(self.same, row, 0.0), axis=1, keepdims=True)

    def carried(self):
        sz = self.sz
        rank = jnp.sum(self.before * self.same_chip * self.act_r, axis=1, keepdims=True)
        core = rest_of(rank, 2)
        away = ring_position(sz, self.chip_c) - ring_position(sz, ratio(self.f, 2))
        away = jnp.where(core == 0, away, -away)
        rel = jnp.where(away < 0, away + sz.ring, away)
        j = jnp.where(rel > sz.top, 2 * (rel - sz.top) - 1, 2 * (sz.top - rel))
        j = jnp.where(rel == 0, sz.ring - 1.0, j)
        return core, ratio(rank, 2), j + jnp.where(core == rest_of(self.f, 2), 0.0, float(sz.ring))

    def ranks(self, chosen_r):
        return jnp.sum(self.before * chosen_r, axis=1, keepdims=True)

    def listed(self, chosen_c, rank_c, value_c, lo=0, hi=None):
        at = rank_c[lo:hi] == self.lane[lo:hi].astype(jnp.float32)
        return jnp.sum(jnp.where(at, chosen_c[lo:hi] * value_c[lo:hi], 0.0), axis=0, keepdims=True)

    def most_on_chip(self):
        return jnp.max(jnp.sum(self.same_chip * self.act_r, axis=1, keepdims=True), axis=0, keepdims=True)


def total(x):
    return jnp.sum(x, axis=0, keepdims=True)


def head_row(sz, entries):
    lane = lax.broadcasted_iota(jnp.int32, (1, sz.lanes), 1)
    row = jnp.zeros((1, sz.lanes), jnp.float32)
    for i, value in entries:
        row = jnp.where(lane == i, value, row)
    return row


def plan_kernel(sz, own, *refs):
    mine, theirs, (plan, chunk, *notes, sems) = refs[:3], refs[3:6], refs[6:]
    S, N = sz.slots, sz.all
    m = Marks(sz, own)
    f32 = jnp.float32
    lane_r, sub_c = m.lane_r, m.sub_c
    core_c, pos_c, base_c = m.carried()
    own_core = core_c == rest_of(m.f, 2)

    pair = jnp.where(rest_of(m.f, 2) == 0, m.f + 1, m.f - 1)
    i_r = rest_of(lane_r, sz.owned)
    owner_r = jnp.where(lane_r < sz.owned, m.f, pair)
    slot_r = ratio(i_r, sz.nb) * S + owner_r * sz.nb + rest_of(i_r, sz.nb)
    at_r = jnp.sum(
        jnp.where((sub_c == slot_r) & own_core, m.act_c * (pos_c + 1.0), 0.0), axis=0, keepdims=True)
    copies = []
    for i in range(2 * sz.owned):
        side, k, a = i // sz.owned, i % sz.owned // sz.nb, i % sz.nb
        at = jnp.max(jnp.where(lane_r == i, at_r, 0.0)).astype(jnp.int32)
        fits = (at > 0) & (at <= sz.keep)
        place = jnp.minimum(jnp.maximum(at - 1, 0), sz.keep - 1)
        copy = pltpu.make_async_copy((mine, theirs)[side][k].at[0, a], chunk.at[place], sems.at[i])
        copies.append((fits, copy))
    for fits, copy in copies:
        pl.when(fits)(copy.start)

    same_kind = (m.kind_c == m.kind_r).astype(f32)
    rank_c = jnp.sum(m.before * same_kind * m.act_r, axis=1, keepdims=True)
    cwas_c = jnp.max(m.before * same_kind * m.same_col * m.act_r, axis=1, keepdims=True)
    cwas_r = jnp.max(m.after * same_kind * m.same_col * m.act_c, axis=0, keepdims=True)
    big = f32(4 * N)
    lanes_f = m.lane.astype(f32)
    gates_r = m.act_r * (m.kind_r == 0).astype(f32)
    cidx_c = jnp.min(jnp.where(m.same_col * gates_r > 0, lanes_f, big), axis=1, keepdims=True)
    oidx_c = jnp.min(jnp.where(m.same_out * m.act_r > 0, lanes_f, big), axis=1, keepdims=True)
    part_c = jnp.where(pos_c < sz.keep, base_c * sz.keep + pos_c, f32(sz.blocks))
    fields = [(part_c, sz.blocks), (m.row_c, 0), (cidx_c, S), (cwas_c, 0), (oidx_c, N), (m.owas_c, 0)]
    rows = []
    head = []
    for k in range(3):
        lo, hi = k * S, (k + 1) * S
        n_k = total(m.act_c[lo:hi])
        head.append((k, n_k))
        for value, spare in fields:
            row = m.listed(m.act_c, rank_c, value, lo, hi)
            rows.append(jnp.where(lane_r < n_k, row, f32(spare)))
    leader_c = m.act_c * (1.0 - cwas_c) * (m.kind_c == 0).astype(f32)
    leader_r = m.act_r * (1.0 - cwas_r) * (m.kind_r == 0).astype(f32)
    rows.append(m.listed(leader_c, m.ranks(leader_r), sub_c, 0, S))
    head.append((HEAD_COLS, total(leader_c)))
    lists, sent = [], []
    over = (m.most_on_chip() > 2 * sz.keep).astype(f32)
    for s in range(sz.n_tensor):
        chosen_c = m.lead_c * (m.shift_c == s).astype(f32)
        chosen_r = m.lead_r * (m.shift_r == s).astype(f32)
        rank = m.ranks(chosen_r)
        lists.append(m.listed(chosen_c, rank, sub_c))
        lists.append(m.listed(chosen_c, rank, m.local_c))
        n = total(chosen_c)
        head.append((HEAD_LISTS + s, n))
        sent.append(n)
        over = jnp.maximum(over, (n > sz.first).astype(f32))
    head.append((HEAD_OVER, over))
    for s in range(1, sz.n_tensor):
        note = jnp.where(lane_r == sz.note_n, sent[s], lists[2 * s + 1])
        notes[s - 1][...] = jnp.where(lane_r == sz.note_over, over, note).astype(jnp.int32)
    rows.append(head_row(sz, head))
    held_c = pos_c + 1.0 + jnp.where(own_core, 0.0, float(sz.keep))
    rows.append(jnp.sum(
        jnp.where((sub_c == slot_r) & (lane_r < sz.owned), m.act_c * held_c, 0.0), axis=0, keepdims=True))
    rows += lists
    for i, row in enumerate(rows):
        plan[i:i + 1, :] = row.astype(jnp.int32)
    for fits, copy in copies:
        pl.when(fits)(copy.wait)


def dot(a, b, ca, cb):
    return lax.dot_general(a, b, (((ca,), (cb,)), ((), ())), preferred_element_type=jnp.float32)


def field(sz, plan, k, j, e):
    return plan[k * FIELDS + j, e]


def walk(plan, k, body):
    steps = (plan[HEAD_ROW, k] + (GROUP - 1)) // GROUP
    lax.fori_loop(0, steps, lambda p, _: body(p * GROUP), None)


def each(plan, k, body):
    lax.fori_loop(0, plan[HEAD_ROW, k], lambda e, _: body(e), None)


def compute_kernel(sz, plan, tokens, cot, *refs):
    n_chunks, T = 2 * sz.ring, sz.n_tensor
    chunks, refs = refs[:n_chunks], refs[n_chunks:]
    same, far, near = refs[:3]
    firsts, refs = refs[3:3 + T], refs[3 + T:]
    xs, wbuf, parts, gate_acc, up_acc, hg_acc, gate_d, up_d, hid, out_acc, stage, strip_sems, sems = refs
    get = functools.partial(field, sz, plan)

    def strip_copy(k, e):
        src = cot if k == 2 else tokens
        cols = pl.ds(pl.multiple_of(get(k, STRIP, e) * BLK, BLK), BLK)
        return pltpu.make_async_copy(src.at[:, cols], xs.at[k * sz.room + e], strip_sems.at[k * sz.room + e])

    loads = [
        pltpu.make_async_copy(chunk, wbuf.at[pl.ds(i * sz.keep, sz.keep)], sems.at[i])
        for i, chunk in enumerate(chunks)
    ]
    for k in range(3):
        each(plan, k, lambda e, k=k: strip_copy(k, e).start())
    for c in loads:
        c.start()
    for k in range(3):
        each(plan, k, lambda e, k=k: strip_copy(k, e).wait())
    for c in loads:
        c.wait()

    def forward(k, acc, w_dim):
        def body(e0):
            prods = [
                dot(xs[k * sz.room + e0 + u], wbuf[get(k, PART, e0 + u)], 1, w_dim) for u in range(GROUP)]
            for u in range(GROUP):
                c = get(k, CIDX, e0 + u)
                acc[c] = prods[u] + jnp.where(get(k, CWAS, e0 + u) == 0, 0.0, acc[c])

        walk(plan, k, body)

    forward(0, gate_acc, 0)
    forward(1, up_acc, 0)
    forward(2, hg_acc, 1)

    def column(i, _):
        c = plan[COLS_ROW, i]
        g, u, h = gate_acc[c], up_acc[c], hg_acc[c]
        s = lax.logistic(g)
        silu = g * s
        gate_d[c] = (h * u * s * (1.0 + g * (1.0 - s))).astype(jnp.bfloat16)
        up_d[c] = (h * silu).astype(jnp.bfloat16)
        hid[c] = (silu * u).astype(jnp.bfloat16)

    lax.fori_loop(0, plan[HEAD_ROW, HEAD_COLS], column, None)

    def gradients(k, act):
        def body(e0):
            for u in range(GROUP):
                a, x = act[get(k, CIDX, e0 + u)], xs[k * sz.room + e0 + u]
                grad = dot(a, x, 0, 0) if k == 2 else dot(x, a, 0, 0)
                parts[get(k, PART, e0 + u)] = grad.astype(jnp.bfloat16)

        walk(plan, k, body)

    gradients(2, hid)
    gradients(0, gate_d)
    gradients(1, up_d)

    split = sz.ring * sz.keep
    cut = split + sz.far * sz.keep
    outs = [
        pltpu.make_async_copy(parts.at[pl.ds(split, cut - split)], far, sems.at[0]),
        pltpu.make_async_copy(parts.at[pl.ds(0, split)], same, sems.at[1]),
        pltpu.make_async_copy(parts.at[pl.ds(cut, sz.blocks - cut)], near, sems.at[2]),
    ]
    for c in outs:
        c.start()

    def terms(k, act, w_dim):
        def body(e0):
            prods = [
                dot(act[get(k, CIDX, e0 + u)], wbuf[get(k, PART, e0 + u)], 1, w_dim) for u in range(GROUP)]
            for u in range(GROUP):
                at = get(k, OIDX, e0 + u)
                out_acc[at] = prods[u] + jnp.where(get(k, OWAS, e0 + u) == 0, 0.0, out_acc[at])

        walk(plan, k, body)

    terms(2, hid, 0)
    terms(0, gate_d, 1)
    terms(1, up_d, 1)

    for s in reversed(range(T)):
        def staged(i, _, s=s):
            stage[s * sz.first + i] = out_acc[plan[LISTS_ROW + 2 * s, i]].astype(jnp.bfloat16)

        lax.fori_loop(0, jnp.minimum(plan[HEAD_ROW, HEAD_LISTS + s], sz.first), staged, None)
        copy = pltpu.make_async_copy(stage.at[pl.ds(s * sz.first, sz.first)], firsts[s], sems.at[3 + s])
        copy.start()
        outs.append(copy)
    for c in outs:
        c.wait()


def join_kernel(sz, plan, *refs):
    T = sz.n_tensor
    notes, firsts, (outputs, input_grads, flag) = refs[:T - 1], refs[T - 1:2 * T - 1], refs[2 * T - 1:]
    over = plan[HEAD_ROW, HEAD_OVER]
    for note in notes:
        over = jnp.maximum(over, note[0, sz.note_over])
    flag[0] = over
    outputs[...] = jnp.zeros_like(outputs)
    input_grads[...] = jnp.zeros_like(input_grads)

    def add(at, value):
        def into(ref, w):
            cols = pl.ds(pl.multiple_of(w * BLK, BLK), BLK)
            ref[:, cols] = (ref[:, cols].astype(jnp.float32) + value.astype(jnp.float32)).astype(jnp.bfloat16)

        @pl.when(at < sz.rbt)
        def _():
            into(outputs, at)

        @pl.when(at >= sz.rbt)
        def _():
            into(input_grads, at - sz.rbt)

    for s in range(T):
        n = notes[s - 1][0, sz.note_n] if s else plan[HEAD_ROW, HEAD_LISTS]

        def step(i, _, s=s):
            add(notes[s - 1][0, i] if s else plan[LISTS_ROW + 1, i], firsts[s][i])

        lax.fori_loop(0, jnp.minimum(n, sz.first), step, None)


def finish_kernel(sz, plan, *refs):
    mine, theirs, outs = refs[:3], refs[3:6], refs[6:]
    for k in range(3):
        for a in range(sz.nb):
            at = plan[MINE_ROW, k * sz.nb + a]

            def value(terms, p):
                p = jnp.minimum(jnp.maximum(p, 0), sz.keep - 1)
                return sum(t[p].astype(jnp.float32) for t in terms)

            out = jnp.where(at > sz.keep, value(theirs, at - 1 - sz.keep), value(mine, at - 1))
            outs[k][0, a] = jnp.where(at > 0, out, 0.0).astype(jnp.bfloat16)


def spec(space):
    return pl.BlockSpec(memory_space=space)


ANY, HBM, VMEM, SMEM = pl.ANY, pltpu.HBM, pltpu.VMEM, pltpu.SMEM


def cost(flops, moved):
    return pl.CostEstimate(flops=flops, bytes_accessed=moved, transcendentals=0)


def call_plan(sz, own, mine, theirs):
    return pl.pallas_call(
        functools.partial(plan_kernel, sz),
        out_shape=[
            jax.ShapeDtypeStruct((sz.plan_rows, sz.lanes), jnp.int32),
            jax.ShapeDtypeStruct((sz.keep, BLK, BLK), jnp.bfloat16),
        ] + [jax.ShapeDtypeStruct((1, sz.lanes), jnp.int32)] * (sz.n_tensor - 1),
        in_specs=[spec(VMEM)] + [spec(ANY)] * 6,
        out_specs=[spec(VMEM), spec(ANY)] + [spec(VMEM)] * (sz.n_tensor - 1),
        scratch_shapes=[pltpu.SemaphoreType.DMA((2 * sz.owned,))],
        compiler_params=pltpu.CompilerParams(vmem_limit_bytes=SMALL),
        cost_estimate=cost(1_000_000, 4_000_000),
        name="plan",
    )(own, *mine, *theirs)


def call_turn(handed, arrived):
    return pl.pallas_call(
        lambda *_: None,
        out_shape=[jax.ShapeDtypeStruct(x.shape, x.dtype) for x in handed],
        in_specs=[spec(ANY)] * (len(handed) + len(arrived)),
        out_specs=[spec(ANY)] * len(handed),
        input_output_aliases={i: i for i in range(len(handed))},
        compiler_params=pltpu.CompilerParams(vmem_limit_bytes=SMALL),
        cost_estimate=cost(1000, 1000),
        name="turn",
    )(*handed, *arrived)


def blocks(n):
    return jax.ShapeDtypeStruct((n, BLK, BLK), jnp.bfloat16)


def held(scratch):
    return sum(s[0] * s[1] * s[2] * jnp.dtype(t).itemsize for s, t in scratch) + 2 * 1024 * 1024


def call_compute(sz, plan, tokens, cot, chunks):
    bf, f32 = jnp.bfloat16, jnp.float32
    T, A = sz.n_tensor, sz.slots + 1
    out_shape = [blocks(sz.ring * sz.keep), blocks(sz.far * sz.keep), blocks((sz.ring - sz.far) * sz.keep)]
    out_shape += [blocks(sz.first)] * T
    scratch = [
        ((3 * sz.room, sz.tok, BLK), bf),
        ((sz.blocks + 1, BLK, BLK), bf),
        ((sz.blocks + 1, BLK, BLK), bf),
        ((A, sz.tok, BLK), f32),
        ((A, sz.tok, BLK), f32),
        ((A, sz.tok, BLK), f32),
        ((A, sz.tok, BLK), bf),
        ((A, sz.tok, BLK), bf),
        ((A, sz.tok, BLK), bf),
        ((sz.all + 1, sz.tok, BLK), f32),
        ((T * sz.first, sz.tok, BLK), bf),
    ]
    return pl.pallas_call(
        functools.partial(compute_kernel, sz),
        out_shape=out_shape,
        in_specs=[spec(SMEM)] + [spec(HBM)] * 2 + [spec(ANY)] * len(chunks),
        out_specs=[spec(ANY)] * len(out_shape),
        scratch_shapes=[pltpu.VMEM(s, t) for s, t in scratch] + [
            pltpu.SemaphoreType.DMA((3 * sz.room,)),
            pltpu.SemaphoreType.DMA((max(len(chunks), 3 + T),)),
        ],
        compiler_params=pltpu.CompilerParams(vmem_limit_bytes=held(scratch)),
        cost_estimate=cost(1_000_000_000, 20_000_000),
        name="compute",
    )(plan, pltpu.with_memory_space_constraint(tokens, HBM), pltpu.with_memory_space_constraint(cot, HBM), *chunks)


def call_join(sz, plan, notes, firsts):
    half = jax.ShapeDtypeStruct((sz.tok, sz.width // sz.n_tensor), jnp.bfloat16)
    return pl.pallas_call(
        functools.partial(join_kernel, sz),
        out_shape=[half, half, jax.ShapeDtypeStruct((1,), jnp.int32)],
        in_specs=[spec(SMEM)] * (1 + len(notes)) + [spec(VMEM)] * len(firsts),
        out_specs=[spec(VMEM), spec(VMEM), spec(SMEM)],
        compiler_params=pltpu.CompilerParams(vmem_limit_bytes=12 * 1024 * 1024),
        cost_estimate=cost(1_000_000, 6_000_000),
        name="join",
    )(plan, *notes, *firsts)


def call_finish(sz, plan, terms):
    out = jax.ShapeDtypeStruct((1, sz.nb, BLK, BLK), jnp.bfloat16)
    return pl.pallas_call(
        functools.partial(finish_kernel, sz),
        out_shape=[out] * 3,
        in_specs=[spec(SMEM)] + [spec(VMEM)] * len(terms),
        out_specs=[spec(VMEM)] * 3,
        compiler_params=pltpu.CompilerParams(vmem_limit_bytes=SMALL),
        cost_estimate=cost(1_000_000, 1_000_000),
        name="finish",
    )(plan, *terms)


def gather_chunks(sz, chunk, notes):
    ahead, behind, swap = permutations(sz)
    same = {0: chunk}
    a = b = chunk
    for s in range(1, sz.top):
        a, b = lax.ppermute(a, "fsdp", ahead), lax.ppermute(b, "fsdp", behind)
        if s == 1:
            a, b = call_turn([a, b], notes)
        same[sz.ring - s], same[s] = a, b
    other = {d: lax.ppermute(same[d], "fsdp", swap) for d in same}
    same[sz.top] = lax.ppermute(a, "fsdp", ahead)
    other[sz.top] = lax.ppermute(a, "fsdp", [(i, j ^ 1) for i, j in ahead])
    return [side[d] for side in (same, other) for d in sz.order]


def reduce_parts(sz, same, far, near):
    ahead, behind, swap = permutations(sz)
    keep = sz.keep
    far, near = lax.ppermute(far, "fsdp", swap), lax.ppermute(near, "fsdp", swap)

    def term(d, *more):
        j = sz.order.index(d)
        pair = far[j * keep:(j + 1) * keep] if j < sz.far else near[(j - sz.far) * keep:][:keep]
        out = same[j * keep:(j + 1) * keep].astype(jnp.float32) + pair.astype(jnp.float32)
        for m in more:
            out = out + m.astype(jnp.float32)
        return out.astype(jnp.bfloat16)

    a, b = lax.optimization_barrier((term(sz.top), term(sz.top + 1)))
    for s in range(1, sz.top):
        a, b = lax.ppermute(a, "fsdp", ahead), lax.ppermute(b, "fsdp", behind)
        a = term(sz.top - s, a)
        if s + 1 < sz.top:
            a, b = lax.optimization_barrier((a, term(sz.top + 1 + s, b)))
    here = term(0)
    mine = [here, lax.ppermute(a, "fsdp", ahead), b]
    theirs = [
        lax.ppermute(here, "fsdp", swap),
        lax.ppermute(a, "fsdp", [(i, j ^ 1) for i, j in ahead]),
        lax.ppermute(b, "fsdp", swap),
    ]
    return mine + theirs


def program(sz, own, tokens, cotangent, mine):
    T = sz.n_tensor
    swap = permutations(sz)[-1]
    theirs = [lax.ppermute(b, "fsdp", swap) for b in mine]
    plan, chunk, *notes = call_plan(sz, own, mine, theirs)

    def exchange(array, s):
        return lax.ppermute(array, "tensor", [(i, (i + s) % T) for i in range(T)])

    notes = [exchange(note, s) for s, note in enumerate(notes, 1)]
    chunks = gather_chunks(sz, chunk, notes)
    same, far, near, *firsts = call_compute(sz, plan, tokens, cotangent, chunks)
    firsts = [firsts[0]] + [exchange(firsts[s], s) for s in range(1, T)]
    terms = reduce_parts(sz, same, far, near)
    outputs, input_grads, flag = call_join(sz, plan, notes, firsts)
    return (outputs, input_grads, *call_finish(sz, plan, terms)), flag


def shards(
    tokens,
    cotangent,
    gate_blocks,
    up_blocks,
    down_blocks,
    gate_where,
    up_where,
    down_where,
    block_counts,
):
    n_fsdp, n_tensor = lax.axis_size("fsdp"), lax.axis_size("tensor")
    f, rank = lax.axis_index("fsdp"), lax.axis_index("tensor")
    slots = gate_where.shape[1]
    full = Sizes(tokens, gate_blocks, slots, n_fsdp, n_tensor, False)
    own = jnp.concatenate([
        gate_where[0], up_where[0], down_where[0], block_counts[:, 0],
        f.astype(jnp.int32)[None], rank.astype(jnp.int32)[None]])
    own = jnp.pad(own, (0, full.lanes - own.shape[0]))[None]
    blocks_in = (gate_blocks, up_blocks, down_blocks)
    if slots >= full.cb:
        return program(full, own, tokens, cotangent, blocks_in)[0]
    lean = Sizes(tokens, gate_blocks, slots, n_fsdp, n_tensor, True)
    outs, flag = program(lean, own, tokens, cotangent, blocks_in)
    return lax.cond(
        flag[0] > 0,
        lambda outs, *args: program(full, *args)[0],
        lambda outs, *args: outs,
        outs, own, tokens, cotangent, blocks_in)


def solution(mesh):
    placed = (
        P("fsdp", None),
        P("fsdp", None),
        P("tensor", "fsdp", None, None),
        P("tensor", "fsdp", None, None),
        P("tensor", "fsdp", None, None),
        P("tensor", None),
        P("tensor", None),
        P("tensor", None),
        P(None, "tensor"),
    )
    return jax.shard_map(
        shards,
        mesh=mesh,
        in_specs=placed,
        out_specs=(
            P("fsdp", "tensor"),
            P("fsdp", "tensor"),
            P("tensor", "fsdp", None, None),
            P("tensor", "fsdp", None, None),
            P("tensor", "fsdp", None, None),
        ),
        check_vma=False,
    )
```

```python
import functools

import jax
import jax.numpy as jnp
from jax import lax
from jax.experimental import pallas as pl
from jax.experimental.pallas import tpu as pltpu
from jax.sharding import PartitionSpec as P

FF = 14336
BLK = 128
GROUP = 4
FIRST_SEND = 18
LEAN_SLOTS = 4
SMALL = 4 * 1024 * 1024
PART, STRIP, CIDX, CWAS, OIDX, OWAS = range(6)
FIELDS = 6
COLS_ROW = 3 * FIELDS
HEAD_ROW = COLS_ROW + 1
MINE_ROW = COLS_ROW + 2
LISTS_ROW = COLS_ROW + 3
HEAD_COLS, HEAD_OVER, HEAD_LISTS = 3, 4, 8


class Sizes:
    def __init__(self, tokens, gate_blocks, slots, n_fsdp, n_tensor, lean):
        self.tok, self.width = tokens.shape
        self.n_fsdp, self.n_tensor = n_fsdp, n_tensor
        self.rb = self.width // BLK
        self.cb = FF // (BLK * n_tensor)
        self.slots = slots
        self.all = 3 * slots
        self.lanes = -(-(self.all + GROUP) // 128) * 128
        self.nb = gate_blocks.shape[1]
        self.owned = 3 * self.nb
        self.ring = n_fsdp // 2
        self.top = self.ring // 2
        self.rbt = self.rb // n_tensor
        self.order = [self.top]
        for d in range(1, self.top):
            self.order += [self.top + d, self.top - d]
        self.order.append(0)
        self.far = min(4, self.ring - 1)
        self.keep = min(LEAN_SLOTS, self.owned) if lean else self.owned
        self.send_all = 2 * self.rbt
        self.first = min(FIRST_SEND, self.send_all) if lean else self.send_all
        self.blocks = 2 * self.ring * self.keep
        self.plan_rows = -(-(LISTS_ROW + 2 * n_tensor) // 8) * 8
        self.note_n, self.note_over = self.lanes - 1, self.lanes - 2
        self.room = slots + GROUP


def permutations(sz):
    seq = list(range(0, sz.ring, 2)) + list(range(sz.ring - 1, 0, -2))
    ahead, behind, swap = [], [], []
    for i, q in enumerate(seq):
        up, down = seq[(i + 1) % sz.ring], seq[i - 1]
        ahead += [(q * 2, up * 2), (q * 2 + 1, down * 2 + 1)]
        behind += [(q * 2, down * 2), (q * 2 + 1, up * 2 + 1)]
        swap += [(q * 2, q * 2 + 1), (q * 2 + 1, q * 2)]
    return ahead, behind, swap


def ratio(x, d):
    return jnp.floor((x + 0.5) * (1.0 / d))


def rest_of(x, d):
    return x - d * ratio(x, d)


def ring_position(sz, chip):
    return jnp.where(rest_of(chip, 2) == 0, ratio(chip, 2), sz.ring - 1 - ratio(chip, 2))


class Marks:
    def __init__(self, sz, own):
        N, L, S = sz.all, sz.lanes, sz.slots
        f32 = jnp.float32
        self.sz = sz
        self.sub = lax.broadcasted_iota(jnp.int32, (N, L), 0)
        self.lane = lax.broadcasted_iota(jnp.int32, (N, L), 1)
        self.same = self.sub == self.lane
        sub_c = self.sub[:, :1].astype(f32)
        lane_r = lax.broadcasted_iota(jnp.int32, (1, L), 1).astype(f32)
        self.sub_c, self.lane_r = sub_c, lane_r
        raw_r = own[...].astype(f32)

        def single(row, at):
            return jnp.sum(jnp.where(lane_r == at, row, 0.0), axis=1, keepdims=True)

        self.f, self.rank = single(raw_r, N + 3), single(raw_r, N + 4)

        def kind(x):
            return (x >= S).astype(f32) + (x >= 2 * S).astype(f32)

        self.kind_c, self.kind_r = kind(sub_c), kind(lane_r)
        self.n_r = lane_r - S * self.kind_r
        self.n_c = sub_c - S * self.kind_c
        limit = jnp.zeros((1, L), f32)
        for k in range(3):
            limit = limit + jnp.where(self.kind_r == k, single(raw_r, N + k), 0.0)
        live_r = jnp.where((lane_r < N) & (self.n_r < limit), 1.0, 0.0)
        w_c = self.col(raw_r)
        live_c = self.col(live_r)

        def place(w, k):
            gate, down = ratio(w, sz.cb), ratio(w, sz.rb)
            is_down = k == 2
            return jnp.where(is_down, w - down * sz.rb, gate), jnp.where(is_down, down, w - gate * sz.cb)

        self.row_c, col_c = place(w_c, self.kind_c)
        self.row_r, col_r = place(raw_r, self.kind_r)
        self.chip_c, chip_r = ratio(self.n_c, 2 * sz.nb), ratio(self.n_r, 2 * sz.nb)
        self.same_chip = (self.chip_c == chip_r).astype(f32)
        self.same_col = (col_c == col_r).astype(f32)
        act_c, act_r = live_c, live_r
        for k in range(3):
            lanes = self.same_col * (live_r * (self.kind_r == k).astype(f32))
            act_c = act_c * jnp.max(lanes, axis=1, keepdims=True)
            subs = self.same_col * (live_c * (self.kind_c == k).astype(f32))
            act_r = act_r * jnp.max(subs, axis=0, keepdims=True)
        self.act_c, self.act_r = act_c, act_r
        out_c = jnp.where(self.kind_c == 2, 0.0, f32(sz.rb)) + self.row_c
        out_r = jnp.where(self.kind_r == 2, 0.0, f32(sz.rb)) + self.row_r
        self.same_out = (out_c == out_r).astype(f32)
        self.before = (self.lane < self.sub).astype(f32)
        self.after = (self.sub < self.lane).astype(f32)
        self.owas_c = jnp.max(self.same_out * self.before * act_r, axis=1, keepdims=True)
        self.owas_r = jnp.max(self.same_out * self.after * act_c, axis=0, keepdims=True)
        self.lead_c = act_c * (1.0 - self.owas_c)
        self.lead_r = act_r * (1.0 - self.owas_r)

        def shift(row):
            away = ratio(row, sz.rbt) - self.rank
            return jnp.where(away < 0, away + sz.n_tensor, away)

        self.shift_c, self.shift_r = shift(self.row_c), shift(self.row_r)
        self.local_c = jnp.where(self.kind_c == 2, 0.0, f32(sz.rbt)) + rest_of(self.row_c, sz.rbt)

    def col(self, row):
        return jnp.sum(jnp.where(self.same, row, 0.0), axis=1, keepdims=True)

    def carried(self):
        sz = self.sz
        rank = jnp.sum(self.before * self.same_chip * self.act_r, axis=1, keepdims=True)
        core = rest_of(rank, 2)
        away = ring_position(sz, self.chip_c) - ring_position(sz, ratio(self.f, 2))
        away = jnp.where(core == 0, away, -away)
        rel = jnp.where(away < 0, away + sz.ring, away)
        j = jnp.where(rel > sz.top, 2 * (rel - sz.top) - 1, 2 * (sz.top - rel))
        j = jnp.where(rel == 0, sz.ring - 1.0, j)
        return core, ratio(rank, 2), j + jnp.where(core == rest_of(self.f, 2), 0.0, float(sz.ring))

    def ranks(self, chosen_r):
        return jnp.sum(self.before * chosen_r, axis=1, keepdims=True)

    def listed(self, chosen_c, rank_c, value_c, lo=0, hi=None):
        at = rank_c[lo:hi] == self.lane[lo:hi].astype(jnp.float32)
        return jnp.sum(jnp.where(at, chosen_c[lo:hi] * value_c[lo:hi], 0.0), axis=0, keepdims=True)

    def most_on_chip(self):
        return jnp.max(jnp.sum(self.same_chip * self.act_r, axis=1, keepdims=True), axis=0, keepdims=True)


def total(x):
    return jnp.sum(x, axis=0, keepdims=True)


def head_row(sz, entries):
    lane = lax.broadcasted_iota(jnp.int32, (1, sz.lanes), 1)
    row = jnp.zeros((1, sz.lanes), jnp.float32)
    for i, value in entries:
        row = jnp.where(lane == i, value, row)
    return row


def plan_kernel(sz, own, *refs):
    mine, theirs, (plan, chunk, *notes, sems) = refs[:3], refs[3:6], refs[6:]
    S, N = sz.slots, sz.all
    m = Marks(sz, own)
    f32 = jnp.float32
    lane_r, sub_c = m.lane_r, m.sub_c
    core_c, pos_c, base_c = m.carried()
    own_core = core_c == rest_of(m.f, 2)

    pair = jnp.where(rest_of(m.f, 2) == 0, m.f + 1, m.f - 1)
    i_r = rest_of(lane_r, sz.owned)
    owner_r = jnp.where(lane_r < sz.owned, m.f, pair)
    slot_r = ratio(i_r, sz.nb) * S + owner_r * sz.nb + rest_of(i_r, sz.nb)
    at_r = jnp.sum(
        jnp.where((sub_c == slot_r) & own_core, m.act_c * (pos_c + 1.0), 0.0), axis=0, keepdims=True)
    copies = []
    for i in range(2 * sz.owned):
        side, k, a = i // sz.owned, i % sz.owned // sz.nb, i % sz.nb
        at = jnp.max(jnp.where(lane_r == i, at_r, 0.0)).astype(jnp.int32)
        fits = (at > 0) & (at <= sz.keep)
        place = jnp.minimum(jnp.maximum(at - 1, 0), sz.keep - 1)
        copy = pltpu.make_async_copy((mine, theirs)[side][k].at[0, a], chunk.at[place], sems.at[i])
        copies.append((fits, copy))
    for fits, copy in copies:
        pl.when(fits)(copy.start)

    same_kind = (m.kind_c == m.kind_r).astype(f32)
    rank_c = jnp.sum(m.before * same_kind * m.act_r, axis=1, keepdims=True)
    cwas_c = jnp.max(m.before * same_kind * m.same_col * m.act_r, axis=1, keepdims=True)
    cwas_r = jnp.max(m.after * same_kind * m.same_col * m.act_c, axis=0, keepdims=True)
    big = f32(4 * N)
    lanes_f = m.lane.astype(f32)
    gates_r = m.act_r * (m.kind_r == 0).astype(f32)
    cidx_c = jnp.min(jnp.where(m.same_col * gates_r > 0, lanes_f, big), axis=1, keepdims=True)
    oidx_c = jnp.min(jnp.where(m.same_out * m.act_r > 0, lanes_f, big), axis=1, keepdims=True)
    rank_r = jnp.sum(m.after * same_kind * m.act_c, axis=0, keepdims=True)
    turn_c = ratio(rank_c, GROUP) * 3 + m.kind_c
    turn_r = ratio(rank_r, GROUP) * 3 + m.kind_r
    ahead = ((turn_r < turn_c) | ((turn_r == turn_c) & (rank_r < rank_c))).astype(f32)
    owas_c = jnp.max(m.same_out * ahead * m.act_r, axis=1, keepdims=True)
    part_c = jnp.where(pos_c < sz.keep, base_c * sz.keep + pos_c, f32(sz.blocks))
    fields = [(part_c, sz.blocks), (m.row_c, 0), (cidx_c, S), (cwas_c, 0), (oidx_c, N), (owas_c, 0)]
    rows = []
    head = []
    for k in range(3):
        lo, hi = k * S, (k + 1) * S
        n_k = total(m.act_c[lo:hi])
        head.append((k, n_k))
        for value, spare in fields:
            row = m.listed(m.act_c, rank_c, value, lo, hi)
            rows.append(jnp.where(lane_r < n_k, row, f32(spare)))
    leader_c = m.act_c * (1.0 - cwas_c) * (m.kind_c == 0).astype(f32)
    leader_r = m.act_r * (1.0 - cwas_r) * (m.kind_r == 0).astype(f32)
    n_cols = total(leader_c)
    cols = m.listed(leader_c, m.ranks(leader_r), sub_c, 0, S)
    rows.append(jnp.where(lane_r < n_cols, cols, f32(S)))
    head.append((HEAD_COLS, n_cols))
    lists, sent = [], []
    over = (m.most_on_chip() > 2 * sz.keep).astype(f32)
    for s in range(sz.n_tensor):
        chosen_c = m.lead_c * (m.shift_c == s).astype(f32)
        chosen_r = m.lead_r * (m.shift_r == s).astype(f32)
        rank = m.ranks(chosen_r)
        lists.append(m.listed(chosen_c, rank, sub_c))
        lists.append(m.listed(chosen_c, rank, m.local_c))
        n = total(chosen_c)
        head.append((HEAD_LISTS + s, n))
        sent.append(n)
        over = jnp.maximum(over, (n > sz.first).astype(f32))
    head.append((HEAD_OVER, over))
    for s in range(1, sz.n_tensor):
        note = jnp.where(lane_r == sz.note_n, sent[s], lists[2 * s + 1])
        notes[s - 1][...] = jnp.where(lane_r == sz.note_over, over, note).astype(jnp.int32)
    rows.append(head_row(sz, head))
    held_c = pos_c + 1.0 + jnp.where(own_core, 0.0, float(sz.keep))
    rows.append(jnp.sum(
        jnp.where((sub_c == slot_r) & (lane_r < sz.owned), m.act_c * held_c, 0.0), axis=0, keepdims=True))
    rows += lists
    for i, row in enumerate(rows):
        plan[i:i + 1, :] = row.astype(jnp.int32)
    for fits, copy in copies:
        pl.when(fits)(copy.wait)


def dot(a, b, ca, cb):
    return lax.dot_general(a, b, (((ca,), (cb,)), ((), ())), preferred_element_type=jnp.float32)


def field(sz, plan, k, j, e):
    return plan[k * FIELDS + j, e]


def walk(plan, body):
    most = jnp.maximum(jnp.maximum(plan[HEAD_ROW, 0], plan[HEAD_ROW, 1]), plan[HEAD_ROW, 2])
    lax.fori_loop(0, (most + (GROUP - 1)) // GROUP, lambda p, _: body(p * GROUP), None)


def each(plan, k, body):
    lax.fori_loop(0, plan[HEAD_ROW, k], lambda e, _: body(e), None)


def compute_kernel(sz, plan, tokens, cot, *refs):
    n_chunks, T = 2 * sz.ring, sz.n_tensor
    chunks, refs = refs[:n_chunks], refs[n_chunks:]
    same, far, near = refs[:3]
    firsts, refs = refs[3:3 + T], refs[3 + T:]
    xs, wbuf, parts, gate_acc, up_acc, hg_acc, acts, out_acc, stage, strip_sems, sems = refs
    A = sz.slots + 1
    get = functools.partial(field, sz, plan)

    def strip_copy(k, e):
        src = cot if k == 2 else tokens
        cols = pl.ds(pl.multiple_of(get(k, STRIP, e) * BLK, BLK), BLK)
        return pltpu.make_async_copy(src.at[:, cols], xs.at[k * sz.room + e], strip_sems.at[k * sz.room + e])

    loads = [
        pltpu.make_async_copy(chunk, wbuf.at[pl.ds(i * sz.keep, sz.keep)], sems.at[i])
        for i, chunk in enumerate(chunks)
    ]
    for k in range(3):
        each(plan, k, lambda e, k=k: strip_copy(k, e).start())
    for c in loads:
        c.start()
    for k in range(3):
        each(plan, k, lambda e, k=k: strip_copy(k, e).wait())
    for c in loads:
        c.wait()

    group = [(k, u) for k in range(3) for u in range(GROUP)]

    def forward(e0):
        for k, u in group:
            e, acc = e0 + u, (gate_acc, up_acc, hg_acc)[k]
            prod = dot(xs[k * sz.room + e], wbuf[get(k, PART, e)], 1, 1 if k == 2 else 0)
            c = get(k, CIDX, e)
            acc[c] = prod + jnp.where(get(k, CWAS, e) == 0, 0.0, acc[c])

    walk(plan, forward)

    def columns(i, _):
        for j in range(GROUP):
            c = plan[COLS_ROW, i * GROUP + j]
            g, u, h = gate_acc[c], up_acc[c], hg_acc[c]
            s = lax.logistic(g)
            silu = g * s
            acts[c] = (h * u * s * (1.0 + g * (1.0 - s))).astype(jnp.bfloat16)
            acts[A + c] = (h * silu).astype(jnp.bfloat16)
            acts[2 * A + c] = (silu * u).astype(jnp.bfloat16)

    lax.fori_loop(0, (plan[HEAD_ROW, HEAD_COLS] + (GROUP - 1)) // GROUP, columns, None)

    def gradients(e0):
        for k, u in group:
            e = e0 + u
            a, x = acts[k * A + get(k, CIDX, e)], xs[k * sz.room + e]
            grad = dot(a, x, 0, 0) if k == 2 else dot(x, a, 0, 0)
            parts[get(k, PART, e)] = grad.astype(jnp.bfloat16)

    walk(plan, gradients)
    split = sz.ring * sz.keep
    cut = split + sz.far * sz.keep
    outs = [
        pltpu.make_async_copy(parts.at[pl.ds(split, cut - split)], far, sems.at[0]),
        pltpu.make_async_copy(parts.at[pl.ds(0, split)], same, sems.at[1]),
        pltpu.make_async_copy(parts.at[pl.ds(cut, sz.blocks - cut)], near, sems.at[2]),
    ]
    for c in outs:
        c.start()

    def terms(e0):
        for k, u in group:
            e = e0 + u
            prod = dot(acts[k * A + get(k, CIDX, e)], wbuf[get(k, PART, e)], 1, 0 if k == 2 else 1)
            at = get(k, OIDX, e)
            out_acc[at] = prod + jnp.where(get(k, OWAS, e) == 0, 0.0, out_acc[at])

    walk(plan, terms)

    for s in reversed(range(T)):
        def staged(i, _, s=s):
            stage[s * sz.first + i] = out_acc[plan[LISTS_ROW + 2 * s, i]].astype(jnp.bfloat16)

        lax.fori_loop(0, jnp.minimum(plan[HEAD_ROW, HEAD_LISTS + s], sz.first), staged, None)
        copy = pltpu.make_async_copy(stage.at[pl.ds(s * sz.first, sz.first)], firsts[s], sems.at[3 + s])
        copy.start()
        outs.append(copy)
    for c in outs:
        c.wait()


def strip_of(sz, at):
    w = jnp.where(at < sz.rbt, at, at - sz.rbt)
    return at < sz.rbt, pl.ds(pl.multiple_of(w * BLK, BLK), BLK)


def prepare_kernel(sz, plan, first, outputs, input_grads):
    outputs[...] = jnp.zeros_like(outputs)
    input_grads[...] = jnp.zeros_like(input_grads)

    def step(i, _):
        is_out, cols = strip_of(sz, plan[LISTS_ROW + 1, i])

        @pl.when(is_out)
        def _():
            outputs[:, cols] = first[i]

        @pl.when(jnp.logical_not(is_out))
        def _():
            input_grads[:, cols] = first[i]

    lax.fori_loop(0, jnp.minimum(plan[HEAD_ROW, HEAD_LISTS], sz.first), step, None)


def last_kernel(sz, plan, *refs):
    T = sz.n_tensor
    notes, refs = refs[:T - 1], refs[T - 1:]
    firsts, refs = refs[:T - 1], refs[T - 1:]
    mine, theirs, refs = refs[:3], refs[3:6], refs[8:]
    outputs, input_grads, grads, flag = refs[0], refs[1], refs[2:5], refs[5]
    strips, read_sems, write_sems = refs[6:]
    over = plan[HEAD_ROW, HEAD_OVER]
    for note in notes:
        over = jnp.maximum(over, note[0, sz.note_over])
    flag[0] = over

    def move(s, i, back, act):
        is_out, cols = strip_of(sz, notes[s][0, i])
        for ref, here in ((outputs, is_out), (input_grads, jnp.logical_not(is_out))):
            @pl.when(here)
            def _(ref=ref):
                there = ref.at[:, cols]
                if back:
                    act(pltpu.make_async_copy(strips.at[i], there, write_sems.at[i]))
                else:
                    act(pltpu.make_async_copy(there, strips.at[i], read_sems.at[i]))

    def loop(s, body):
        lax.fori_loop(0, jnp.minimum(notes[s][0, sz.note_n], sz.first), lambda i, _: body(i), None)

    def begin(s):
        loop(s, lambda i: move(s, i, False, lambda c: c.start()))

    def add(s):
        def step(i):
            move(s, i, False, lambda c: c.wait())
            value = strips[i].astype(jnp.float32) + firsts[s][i].astype(jnp.float32)
            strips[i] = value.astype(jnp.bfloat16)
            move(s, i, True, lambda c: c.start())

        loop(s, step)

    def end(s):
        loop(s, lambda i: move(s, i, True, lambda c: c.wait()))

    begin(0)
    for k in range(3):
        for a in range(sz.nb):
            at = plan[MINE_ROW, k * sz.nb + a]

            def value(terms, p):
                p = jnp.minimum(jnp.maximum(p, 0), sz.keep - 1)
                return sum(t[p].astype(jnp.float32) for t in terms)

            out = jnp.where(at > sz.keep, value(theirs, at - 1 - sz.keep), value(mine, at - 1))
            grads[k][0, a] = jnp.where(at > 0, out, 0.0).astype(jnp.bfloat16)
    add(0)
    end(0)
    for s in range(1, T - 1):
        begin(s)
        add(s)
        end(s)


def spec(space):
    return pl.BlockSpec(memory_space=space)


ANY, HBM, VMEM, SMEM = pl.ANY, pltpu.HBM, pltpu.VMEM, pltpu.SMEM


def cost(flops, moved):
    return pl.CostEstimate(flops=flops, bytes_accessed=moved, transcendentals=0)


def call_plan(sz, own, mine, theirs):
    return pl.pallas_call(
        functools.partial(plan_kernel, sz),
        out_shape=[
            jax.ShapeDtypeStruct((sz.plan_rows, sz.lanes), jnp.int32),
            jax.ShapeDtypeStruct((sz.keep, BLK, BLK), jnp.bfloat16),
        ] + [jax.ShapeDtypeStruct((1, sz.lanes), jnp.int32)] * (sz.n_tensor - 1),
        in_specs=[spec(VMEM)] + [spec(ANY)] * 6,
        out_specs=[spec(VMEM), spec(ANY)] + [spec(VMEM)] * (sz.n_tensor - 1),
        scratch_shapes=[pltpu.SemaphoreType.DMA((2 * sz.owned,))],
        compiler_params=pltpu.CompilerParams(vmem_limit_bytes=SMALL),
        cost_estimate=cost(1_000_000, 4_000_000),
        name="plan",
    )(own, *mine, *theirs)


def call_turn(handed, arrived):
    return pl.pallas_call(
        lambda *_: None,
        out_shape=[jax.ShapeDtypeStruct(x.shape, x.dtype) for x in handed],
        in_specs=[spec(ANY)] * (len(handed) + len(arrived)),
        out_specs=[spec(ANY)] * len(handed),
        input_output_aliases={i: i for i in range(len(handed))},
        compiler_params=pltpu.CompilerParams(vmem_limit_bytes=SMALL),
        cost_estimate=cost(1000, 1000),
        name="turn",
    )(*handed, *arrived)


def blocks(n):
    return jax.ShapeDtypeStruct((n, BLK, BLK), jnp.bfloat16)


def held(scratch):
    return sum(s[0] * s[1] * s[2] * jnp.dtype(t).itemsize for s, t in scratch) + 2 * 1024 * 1024


def call_compute(sz, plan, tokens, cot, chunks):
    bf, f32 = jnp.bfloat16, jnp.float32
    T, A = sz.n_tensor, sz.slots + 1
    out_shape = [blocks(sz.ring * sz.keep), blocks(sz.far * sz.keep), blocks((sz.ring - sz.far) * sz.keep)]
    out_shape += [blocks(sz.first)] * T
    scratch = [
        ((3 * sz.room, sz.tok, BLK), bf),
        ((sz.blocks + 1, BLK, BLK), bf),
        ((sz.blocks + 1, BLK, BLK), bf),
        ((A, sz.tok, BLK), f32),
        ((A, sz.tok, BLK), f32),
        ((A, sz.tok, BLK), f32),
        ((3 * A, sz.tok, BLK), bf),
        ((sz.all + 1, sz.tok, BLK), f32),
        ((T * sz.first, sz.tok, BLK), bf),
    ]
    return pl.pallas_call(
        functools.partial(compute_kernel, sz),
        out_shape=out_shape,
        in_specs=[spec(SMEM)] + [spec(HBM)] * 2 + [spec(ANY)] * len(chunks),
        out_specs=[spec(ANY)] * len(out_shape),
        scratch_shapes=[pltpu.VMEM(s, t) for s, t in scratch] + [
            pltpu.SemaphoreType.DMA((3 * sz.room,)),
            pltpu.SemaphoreType.DMA((max(len(chunks), 3 + T),)),
        ],
        compiler_params=pltpu.CompilerParams(vmem_limit_bytes=held(scratch)),
        cost_estimate=cost(1_000_000_000, 20_000_000),
        name="compute",
    )(plan, pltpu.with_memory_space_constraint(tokens, HBM), pltpu.with_memory_space_constraint(cot, HBM), *chunks)


def call_prepare(sz, plan, first):
    half = jax.ShapeDtypeStruct((sz.tok, sz.width // sz.n_tensor), jnp.bfloat16)
    return pl.pallas_call(
        functools.partial(prepare_kernel, sz),
        out_shape=[half, half],
        in_specs=[spec(SMEM), spec(VMEM)],
        out_specs=[spec(VMEM), spec(VMEM)],
        compiler_params=pltpu.CompilerParams(vmem_limit_bytes=10 * 1024 * 1024),
        cost_estimate=cost(1_000_000, 6_000_000),
        name="prepare",
    )(plan, first)


def call_last(sz, plan, notes, firsts, terms, partial):
    n = 1 + len(notes) + len(firsts) + len(terms)
    out = jax.ShapeDtypeStruct((1, sz.nb, BLK, BLK), jnp.bfloat16)
    return pl.pallas_call(
        functools.partial(last_kernel, sz),
        out_shape=[jax.ShapeDtypeStruct(p.shape, p.dtype) for p in partial] + [out] * 3 + [
            jax.ShapeDtypeStruct((1,), jnp.int32)],
        in_specs=[spec(SMEM)] * (1 + len(notes)) + [spec(VMEM)] * (len(firsts) + len(terms)) + [spec(ANY)] * 2,
        out_specs=[spec(ANY)] * 2 + [spec(VMEM)] * 3 + [spec(SMEM)],
        input_output_aliases={n: 0, n + 1: 1},
        scratch_shapes=[
            pltpu.VMEM((sz.first, sz.tok, BLK), jnp.bfloat16),
            pltpu.SemaphoreType.DMA((sz.first,)),
            pltpu.SemaphoreType.DMA((sz.first,)),
        ],
        compiler_params=pltpu.CompilerParams(vmem_limit_bytes=12 * 1024 * 1024),
        cost_estimate=cost(1_000_000, 3_000_000),
        name="last",
    )(plan, *notes, *firsts, *terms, *partial)


def gather_chunks(sz, chunk, notes):
    ahead, behind, swap = permutations(sz)
    same = {0: chunk}
    a = b = chunk
    for s in range(1, sz.top):
        a, b = lax.ppermute(a, "fsdp", ahead), lax.ppermute(b, "fsdp", behind)
        if s == 2:
            a, b = call_turn([a, b], notes)
        same[sz.ring - s], same[s] = a, b
    other = {d: lax.ppermute(same[d], "fsdp", swap) for d in same}
    same[sz.top] = lax.ppermute(a, "fsdp", ahead)
    other[sz.top] = lax.ppermute(a, "fsdp", [(i, j ^ 1) for i, j in ahead])
    return [side[d] for side in (same, other) for d in sz.order]


def reduce_parts(sz, same, far, near):
    ahead, behind, swap = permutations(sz)
    keep = sz.keep
    far, near = lax.ppermute(far, "fsdp", swap), lax.ppermute(near, "fsdp", swap)

    def term(d, *more):
        j = sz.order.index(d)
        pair = far[j * keep:(j + 1) * keep] if j < sz.far else near[(j - sz.far) * keep:][:keep]
        out = same[j * keep:(j + 1) * keep].astype(jnp.float32) + pair.astype(jnp.float32)
        for m in more:
            out = out + m.astype(jnp.float32)
        return out.astype(jnp.bfloat16)

    a, b = lax.optimization_barrier((term(sz.top), term(sz.top + 1)))
    for s in range(1, sz.top):
        a, b = lax.ppermute(a, "fsdp", ahead), lax.ppermute(b, "fsdp", behind)
        a = term(sz.top - s, a)
        if s + 1 < sz.top:
            a, b = lax.optimization_barrier((a, term(sz.top + 1 + s, b)))
    here = term(0)
    mine = [here, lax.ppermute(a, "fsdp", ahead), b]
    theirs = [
        lax.ppermute(here, "fsdp", swap),
        lax.ppermute(a, "fsdp", [(i, j ^ 1) for i, j in ahead]),
        lax.ppermute(b, "fsdp", swap),
    ]
    return mine + theirs


def program(sz, own, tokens, cotangent, mine):
    T = sz.n_tensor
    swap = permutations(sz)[-1]
    theirs = [lax.ppermute(b, "fsdp", swap) for b in mine]
    plan, chunk, *notes = call_plan(sz, own, mine, theirs)

    def exchange(array, s):
        return lax.ppermute(array, "tensor", [(i, (i + s) % T) for i in range(T)])

    notes = [exchange(note, s) for s, note in enumerate(notes, 1)]
    chunks = gather_chunks(sz, chunk, notes)
    same, far, near, *firsts = call_compute(sz, plan, tokens, cotangent, chunks)
    partial = call_prepare(sz, plan, firsts[0])
    firsts = [exchange(firsts[s], s) for s in range(1, T)]
    terms = reduce_parts(sz, same, far, near)
    *outs, flag = call_last(sz, plan, notes, firsts, terms, partial)
    return tuple(outs), flag


def shards(
    tokens,
    cotangent,
    gate_blocks,
    up_blocks,
    down_blocks,
    gate_where,
    up_where,
    down_where,
    block_counts,
):
    n_fsdp, n_tensor = lax.axis_size("fsdp"), lax.axis_size("tensor")
    f, rank = lax.axis_index("fsdp"), lax.axis_index("tensor")
    slots = gate_where.shape[1]
    full = Sizes(tokens, gate_blocks, slots, n_fsdp, n_tensor, False)
    own = jnp.concatenate([
        gate_where[0], up_where[0], down_where[0], block_counts[:, 0],
        f.astype(jnp.int32)[None], rank.astype(jnp.int32)[None]])
    own = jnp.pad(own, (0, full.lanes - own.shape[0]))[None]
    blocks_in = (gate_blocks, up_blocks, down_blocks)
    if slots >= full.cb:
        return program(full, own, tokens, cotangent, blocks_in)[0]
    lean = Sizes(tokens, gate_blocks, slots, n_fsdp, n_tensor, True)
    outs, flag = program(lean, own, tokens, cotangent, blocks_in)
    return lax.cond(
        flag[0] > 0,
        lambda outs, *args: program(full, *args)[0],
        lambda outs, *args: outs,
        outs, own, tokens, cotangent, blocks_in)


def solution(mesh):
    placed = (
        P("fsdp", None),
        P("fsdp", None),
        P("tensor", "fsdp", None, None),
        P("tensor", "fsdp", None, None),
        P("tensor", "fsdp", None, None),
        P("tensor", None),
        P("tensor", None),
        P("tensor", None),
        P(None, "tensor"),
    )
    return jax.shard_map(
        shards,
        mesh=mesh,
        in_specs=placed,
        out_specs=(
            P("fsdp", "tensor"),
            P("fsdp", "tensor"),
            P("tensor", "fsdp", None, None),
            P("tensor", "fsdp", None, None),
            P("tensor", "fsdp", None, None),
        ),
        check_vma=False,
    )
```

```python
import functools

import jax
import jax.numpy as jnp
from jax import lax
from jax.experimental import pallas as pl
from jax.experimental.pallas import tpu as pltpu
from jax.sharding import PartitionSpec as P

FF = 14336
BLK = 128
GROUP = 4
FIRST_SEND = 18
LEAN_SLOTS = 7
ROWS = BLK // 2
SMALL = 4 * 1024 * 1024
PART, STRIP, CIDX, CWAS, OIDX, OWAS = range(6)
FIELDS = 6
COLS_ROW = 3 * FIELDS
HEAD_ROW = COLS_ROW + 1
MINE_ROW = COLS_ROW + 2
LISTS_ROW = COLS_ROW + 3
HEAD_COLS, HEAD_OVER, HEAD_CORE, HEAD_LISTS = 3, 4, 5, 8


class Sizes:
    def __init__(self, tokens, gate_blocks, slots, n_fsdp, n_tensor, lean):
        self.tok, self.width = tokens.shape
        self.n_fsdp, self.n_tensor = n_fsdp, n_tensor
        self.rb = self.width // BLK
        self.cb = FF // (BLK * n_tensor)
        self.slots = slots
        self.all = 3 * slots
        self.lanes = -(-(self.all + GROUP) // 128) * 128
        self.nb = gate_blocks.shape[1]
        self.owned = 3 * self.nb
        self.ring = n_fsdp // 2
        self.top = self.ring // 2
        self.rbt = self.rb // n_tensor
        self.order = [self.top]
        for d in range(1, self.top):
            self.order += [self.top + d, self.top - d]
        self.order.append(0)
        self.far = min(2, self.ring - 1)
        self.keep = min(LEAN_SLOTS, 2 * self.owned) if lean else 2 * self.owned
        self.send_all = 2 * self.rbt
        self.first = min(FIRST_SEND, self.send_all) if lean else self.send_all
        self.blocks = self.ring * self.keep
        self.plan_rows = -(-(LISTS_ROW + 2 * n_tensor) // 8) * 8
        self.note_n, self.note_over = self.lanes - 1, self.lanes - 2
        self.room = slots + GROUP

    def place(self, d):
        return self.order.index(d) * self.keep

    def place_across(self, d):
        return self.place((self.ring - d) % self.ring)


def permutations(sz):
    seq = list(range(0, sz.ring, 2)) + list(range(sz.ring - 1, 0, -2))
    ahead, behind, swap = [], [], []
    for i, q in enumerate(seq):
        up, down = seq[(i + 1) % sz.ring], seq[i - 1]
        ahead += [(q * 2, up * 2), (q * 2 + 1, down * 2 + 1)]
        behind += [(q * 2, down * 2), (q * 2 + 1, up * 2 + 1)]
        swap += [(q * 2, q * 2 + 1), (q * 2 + 1, q * 2)]
    return ahead, behind, swap


def ratio(x, d):
    return jnp.floor((x + 0.5) * (1.0 / d))


def rest_of(x, d):
    return x - d * ratio(x, d)


def ring_position(sz, chip):
    return jnp.where(rest_of(chip, 2) == 0, ratio(chip, 2), sz.ring - 1 - ratio(chip, 2))


class Marks:
    def __init__(self, sz, own):
        N, L, S = sz.all, sz.lanes, sz.slots
        f32 = jnp.float32
        self.sz = sz
        self.sub = lax.broadcasted_iota(jnp.int32, (N, L), 0)
        self.lane = lax.broadcasted_iota(jnp.int32, (N, L), 1)
        self.same = self.sub == self.lane
        sub_c = self.sub[:, :1].astype(f32)
        lane_r = lax.broadcasted_iota(jnp.int32, (1, L), 1).astype(f32)
        self.sub_c, self.lane_r = sub_c, lane_r
        raw_r = own[...].astype(f32)

        def single(row, at):
            return jnp.sum(jnp.where(lane_r == at, row, 0.0), axis=1, keepdims=True)

        self.f, self.rank = single(raw_r, N + 3), single(raw_r, N + 4)

        def kind(x):
            return (x >= S).astype(f32) + (x >= 2 * S).astype(f32)

        self.kind_c, self.kind_r = kind(sub_c), kind(lane_r)
        self.n_r = lane_r - S * self.kind_r
        self.n_c = sub_c - S * self.kind_c
        limit = jnp.zeros((1, L), f32)
        for k in range(3):
            limit = limit + jnp.where(self.kind_r == k, single(raw_r, N + k), 0.0)
        live_r = jnp.where((lane_r < N) & (self.n_r < limit), 1.0, 0.0)
        w_c = self.col(raw_r)
        live_c = self.col(live_r)

        def place(w, k):
            gate, down = ratio(w, sz.cb), ratio(w, sz.rb)
            is_down = k == 2
            return jnp.where(is_down, w - down * sz.rb, gate), jnp.where(is_down, down, w - gate * sz.cb)

        self.row_c, col_c = place(w_c, self.kind_c)
        self.row_r, col_r = place(raw_r, self.kind_r)
        self.chip_c, chip_r = ratio(self.n_c, 2 * sz.nb), ratio(self.n_r, 2 * sz.nb)
        self.same_chip = (self.chip_c == chip_r).astype(f32)
        self.same_col = (col_c == col_r).astype(f32)
        act_c, act_r = live_c, live_r
        for k in range(3):
            lanes = self.same_col * (live_r * (self.kind_r == k).astype(f32))
            act_c = act_c * jnp.max(lanes, axis=1, keepdims=True)
            subs = self.same_col * (live_c * (self.kind_c == k).astype(f32))
            act_r = act_r * jnp.max(subs, axis=0, keepdims=True)
        self.act_c, self.act_r = act_c, act_r
        out_c = jnp.where(self.kind_c == 2, 0.0, f32(sz.rb)) + self.row_c
        out_r = jnp.where(self.kind_r == 2, 0.0, f32(sz.rb)) + self.row_r
        self.same_out = (out_c == out_r).astype(f32)
        self.before = (self.lane < self.sub).astype(f32)
        self.after = (self.sub < self.lane).astype(f32)
        self.owas_c = jnp.max(self.same_out * self.before * act_r, axis=1, keepdims=True)
        self.owas_r = jnp.max(self.same_out * self.after * act_c, axis=0, keepdims=True)
        self.lead_c = act_c * (1.0 - self.owas_c)
        self.lead_r = act_r * (1.0 - self.owas_r)

        def shift(row):
            away = ratio(row, sz.rbt) - self.rank
            return jnp.where(away < 0, away + sz.n_tensor, away)

        self.shift_c, self.shift_r = shift(self.row_c), shift(self.row_r)
        self.local_c = jnp.where(self.kind_c == 2, 0.0, f32(sz.rbt)) + rest_of(self.row_c, sz.rbt)

    def col(self, row):
        return jnp.sum(jnp.where(self.same, row, 0.0), axis=1, keepdims=True)

    def carried(self):
        sz = self.sz
        rank = jnp.sum(self.before * self.same_chip * self.act_r, axis=1, keepdims=True)
        away = ring_position(sz, self.chip_c) - ring_position(sz, ratio(self.f, 2))
        away = jnp.where(rest_of(self.f, 2) == 0, away, -away)
        rel = jnp.where(away < 0, away + sz.ring, away)
        j = jnp.where(rel > sz.top, 2 * (rel - sz.top) - 1, 2 * (sz.top - rel))
        return rank, jnp.where(rel == 0, sz.ring - 1.0, j)

    def ranks(self, chosen_r):
        return jnp.sum(self.before * chosen_r, axis=1, keepdims=True)

    def listed(self, chosen_c, rank_c, value_c, lo=0, hi=None):
        at = rank_c[lo:hi] == self.lane[lo:hi].astype(jnp.float32)
        return jnp.sum(jnp.where(at, chosen_c[lo:hi] * value_c[lo:hi], 0.0), axis=0, keepdims=True)

    def most_on_chip(self):
        return jnp.max(jnp.sum(self.same_chip * self.act_r, axis=1, keepdims=True), axis=0, keepdims=True)


def total(x):
    return jnp.sum(x, axis=0, keepdims=True)


def head_row(sz, entries):
    lane = lax.broadcasted_iota(jnp.int32, (1, sz.lanes), 1)
    row = jnp.zeros((1, sz.lanes), jnp.float32)
    for i, value in entries:
        row = jnp.where(lane == i, value, row)
    return row


def plan_kernel(sz, own, *refs):
    mine, theirs, (plan, chunk, *notes, sems) = refs[:3], refs[3:6], refs[6:]
    S, N = sz.slots, sz.all
    m = Marks(sz, own)
    f32 = jnp.float32
    lane_r, sub_c = m.lane_r, m.sub_c
    pos_c, base_c = m.carried()
    core = rest_of(m.f, 2)
    half = pl.ds(pl.multiple_of(jnp.max(core).astype(jnp.int32) * ROWS, ROWS), ROWS)

    pair = jnp.where(core == 0, m.f + 1, m.f - 1)
    i_r = rest_of(lane_r, sz.owned)
    owner_r = jnp.where(lane_r < sz.owned, m.f, pair)
    slot_r = ratio(i_r, sz.nb) * S + owner_r * sz.nb + rest_of(i_r, sz.nb)
    at_r = jnp.sum(jnp.where(sub_c == slot_r, m.act_c * (pos_c + 1.0), 0.0), axis=0, keepdims=True)
    copies = []
    for i in range(2 * sz.owned):
        side, k, a = i // sz.owned, i % sz.owned // sz.nb, i % sz.nb
        at = jnp.max(jnp.where(lane_r == i, at_r, 0.0)).astype(jnp.int32)
        fits = (at > 0) & (at <= sz.keep)
        place = jnp.minimum(jnp.maximum(at - 1, 0), sz.keep - 1)
        copy = pltpu.make_async_copy((mine, theirs)[side][k].at[0, a, half], chunk.at[place], sems.at[i])
        copies.append((fits, copy))
    for fits, copy in copies:
        pl.when(fits)(copy.start)

    same_kind = (m.kind_c == m.kind_r).astype(f32)
    rank_c = jnp.sum(m.before * same_kind * m.act_r, axis=1, keepdims=True)
    cwas_c = jnp.max(m.before * same_kind * m.same_col * m.act_r, axis=1, keepdims=True)
    cwas_r = jnp.max(m.after * same_kind * m.same_col * m.act_c, axis=0, keepdims=True)
    big = f32(4 * N)
    lanes_f = m.lane.astype(f32)
    gates_r = m.act_r * (m.kind_r == 0).astype(f32)
    cidx_c = jnp.min(jnp.where(m.same_col * gates_r > 0, lanes_f, big), axis=1, keepdims=True)
    oidx_c = jnp.min(jnp.where(m.same_out * m.act_r > 0, lanes_f, big), axis=1, keepdims=True)
    rank_r = jnp.sum(m.after * same_kind * m.act_c, axis=0, keepdims=True)
    turn_c = ratio(rank_c, GROUP) * 3 + m.kind_c
    turn_r = ratio(rank_r, GROUP) * 3 + m.kind_r
    ahead = ((turn_r < turn_c) | ((turn_r == turn_c) & (rank_r < rank_c))).astype(f32)
    owas_c = jnp.max(m.same_out * ahead * m.act_r, axis=1, keepdims=True)
    part_c = jnp.where(pos_c < sz.keep, base_c * sz.keep + pos_c, f32(sz.blocks))
    fields = [(part_c, sz.blocks), (m.row_c, 0), (cidx_c, S), (cwas_c, 0), (oidx_c, N), (owas_c, 0)]
    rows = []
    head = []
    for k in range(3):
        lo, hi = k * S, (k + 1) * S
        n_k = total(m.act_c[lo:hi])
        head.append((k, n_k))
        for value, spare in fields:
            row = m.listed(m.act_c, rank_c, value, lo, hi)
            rows.append(jnp.where(lane_r < n_k, row, f32(spare)))
    leader_c = m.act_c * (1.0 - cwas_c) * (m.kind_c == 0).astype(f32)
    leader_r = m.act_r * (1.0 - cwas_r) * (m.kind_r == 0).astype(f32)
    n_cols = total(leader_c)
    cols = m.listed(leader_c, m.ranks(leader_r), sub_c, 0, S)
    rows.append(jnp.where(lane_r < n_cols, cols, f32(S)))
    head.append((HEAD_COLS, n_cols))
    lists, sent = [], []
    over = (m.most_on_chip() > sz.keep).astype(f32)
    for s in range(sz.n_tensor):
        chosen_c = m.lead_c * (m.shift_c == s).astype(f32)
        chosen_r = m.lead_r * (m.shift_r == s).astype(f32)
        rank = m.ranks(chosen_r)
        lists.append(m.listed(chosen_c, rank, sub_c))
        lists.append(m.listed(chosen_c, rank, m.local_c))
        n = total(chosen_c)
        head.append((HEAD_LISTS + s, n))
        sent.append(n)
        over = jnp.maximum(over, (n > sz.first).astype(f32))
    head += [(HEAD_OVER, over), (HEAD_CORE, core)]
    for s in range(1, sz.n_tensor):
        note = jnp.where(lane_r == sz.note_n, sent[s], lists[2 * s + 1])
        notes[s - 1][...] = jnp.where(lane_r == sz.note_over, over, note).astype(jnp.int32)
    rows.append(head_row(sz, head))
    rows.append(at_r)
    rows += lists
    for i, row in enumerate(rows):
        plan[i:i + 1, :] = row.astype(jnp.int32)
    for fits, copy in copies:
        pl.when(fits)(copy.wait)


def dot(a, b, ca, cb):
    return lax.dot_general(a, b, (((ca,), (cb,)), ((), ())), preferred_element_type=jnp.float32)


def field(sz, plan, k, j, e):
    return plan[k * FIELDS + j, e]


def walk(plan, body):
    most = jnp.maximum(jnp.maximum(plan[HEAD_ROW, 0], plan[HEAD_ROW, 1]), plan[HEAD_ROW, 2])
    lax.fori_loop(0, (most + (GROUP - 1)) // GROUP, lambda p, _: body(p * GROUP), None)


def each(plan, k, body):
    lax.fori_loop(0, plan[HEAD_ROW, k], lambda e, _: body(e), None)


def compute_kernel(sz, plan, tokens, cot, *refs):
    n_chunks, T = 2 * sz.ring, sz.n_tensor
    chunks, refs = refs[:n_chunks], refs[n_chunks:]
    same, far, near = refs[:3]
    firsts, refs = refs[3:3 + T], refs[3 + T:]
    xs, wbuf, parts, gate_acc, up_acc, hg_acc, acts, out_acc, stage, strip_sems, sems = refs
    A = sz.slots + 1
    get = functools.partial(field, sz, plan)

    def strip_copy(k, e):
        src = cot if k == 2 else tokens
        cols = pl.ds(pl.multiple_of(get(k, STRIP, e) * BLK, BLK), BLK)
        return pltpu.make_async_copy(src.at[:, cols], xs.at[k * sz.room + e], strip_sems.at[k * sz.room + e])

    core = plan[HEAD_ROW, HEAD_CORE]
    sides = [pl.ds(pl.multiple_of(c * ROWS, ROWS), ROWS) for c in (core, 1 - core)]
    loads = []
    for side, place in enumerate((sz.place, sz.place_across)):
        for d in sz.order:
            i = len(loads)
            there = wbuf.at[pl.ds(place(d), sz.keep), sides[side]]
            loads.append(pltpu.make_async_copy(chunks[i], there, sems.at[i]))
    for k in range(3):
        each(plan, k, lambda e, k=k: strip_copy(k, e).start())
    for c in loads:
        c.start()
    for k in range(3):
        each(plan, k, lambda e, k=k: strip_copy(k, e).wait())
    for c in loads:
        c.wait()

    group = [(k, u) for k in range(3) for u in range(GROUP)]

    def forward(e0):
        for k, u in group:
            e, acc = e0 + u, (gate_acc, up_acc, hg_acc)[k]
            prod = dot(xs[k * sz.room + e], wbuf[get(k, PART, e)], 1, 1 if k == 2 else 0)
            c = get(k, CIDX, e)
            acc[c] = prod + jnp.where(get(k, CWAS, e) == 0, 0.0, acc[c])

    walk(plan, forward)

    def columns(i, _):
        for j in range(GROUP):
            c = plan[COLS_ROW, i * GROUP + j]
            g, u, h = gate_acc[c], up_acc[c], hg_acc[c]
            s = lax.logistic(g)
            silu = g * s
            acts[c] = (h * u * s * (1.0 + g * (1.0 - s))).astype(jnp.bfloat16)
            acts[A + c] = (h * silu).astype(jnp.bfloat16)
            acts[2 * A + c] = (silu * u).astype(jnp.bfloat16)

    lax.fori_loop(0, (plan[HEAD_ROW, HEAD_COLS] + (GROUP - 1)) // GROUP, columns, None)

    def gradients(e0):
        for k, u in group:
            e = e0 + u
            a, x = acts[k * A + get(k, CIDX, e)], xs[k * sz.room + e]
            grad = dot(a, x, 0, 0) if k == 2 else dot(x, a, 0, 0)
            parts[get(k, PART, e)] = grad.astype(jnp.bfloat16)

    walk(plan, gradients)
    outs = []
    for j, d in enumerate(sz.order):
        ref, at = (far, j) if j < sz.far else (near, j - sz.far)
        outs.append(pltpu.make_async_copy(
            parts.at[pl.ds(sz.place_across(d), sz.keep), sides[1]], ref.at[pl.ds(at * sz.keep, sz.keep)], sems.at[j]))
    outs.append(pltpu.make_async_copy(parts.at[pl.ds(0, sz.blocks), sides[0]], same, sems.at[sz.ring]))
    for c in outs:
        c.start()

    def terms(e0):
        for k, u in group:
            e = e0 + u
            prod = dot(acts[k * A + get(k, CIDX, e)], wbuf[get(k, PART, e)], 1, 0 if k == 2 else 1)
            at = get(k, OIDX, e)
            out_acc[at] = prod + jnp.where(get(k, OWAS, e) == 0, 0.0, out_acc[at])

    walk(plan, terms)

    for s in reversed(range(T)):
        def staged(i, _, s=s):
            stage[s * sz.first + i] = out_acc[plan[LISTS_ROW + 2 * s, i]].astype(jnp.bfloat16)

        lax.fori_loop(0, jnp.minimum(plan[HEAD_ROW, HEAD_LISTS + s], sz.first), staged, None)
        copy = pltpu.make_async_copy(stage.at[pl.ds(s * sz.first, sz.first)], firsts[s], sems.at[sz.ring + 1 + s])
        copy.start()
        outs.append(copy)
    for c in outs:
        c.wait()


def strip_of(sz, at):
    w = jnp.where(at < sz.rbt, at, at - sz.rbt)
    return at < sz.rbt, pl.ds(pl.multiple_of(w * BLK, BLK), BLK)


def prepare_kernel(sz, plan, note, first, outputs, input_grads, strips):
    outputs[...] = jnp.zeros_like(outputs)
    input_grads[...] = jnp.zeros_like(input_grads)

    def step(i, _):
        is_out, cols = strip_of(sz, plan[LISTS_ROW + 1, i])

        @pl.when(is_out)
        def _():
            outputs[:, cols] = first[i]

        @pl.when(jnp.logical_not(is_out))
        def _():
            input_grads[:, cols] = first[i]

    lax.fori_loop(0, jnp.minimum(plan[HEAD_ROW, HEAD_LISTS], sz.first), step, None)

    def pick(i, _):
        is_out, cols = strip_of(sz, note[0, i])

        @pl.when(is_out)
        def _():
            strips[i] = outputs[:, cols]

        @pl.when(jnp.logical_not(is_out))
        def _():
            strips[i] = input_grads[:, cols]

    lax.fori_loop(0, jnp.minimum(note[0, sz.note_n], sz.first), pick, None)


def last_kernel(sz, plan, *refs):
    T = sz.n_tensor
    notes, refs = refs[:T - 1], refs[T - 1:]
    firsts, refs = refs[:T - 1], refs[T - 1:]
    mine, theirs, held_strips, refs = refs[:3], refs[3:6], refs[6], refs[9:]
    outputs, input_grads, grads, flag = refs[0], refs[1], refs[2:5], refs[5]
    strips, read_sems, write_sems = refs[6:]
    over = plan[HEAD_ROW, HEAD_OVER]
    for note in notes:
        over = jnp.maximum(over, note[0, sz.note_over])
    flag[0] = over

    def move(s, i, back, act):
        is_out, cols = strip_of(sz, notes[s][0, i])
        for ref, here in ((outputs, is_out), (input_grads, jnp.logical_not(is_out))):
            @pl.when(here)
            def _(ref=ref):
                there = ref.at[:, cols]
                if back:
                    act(pltpu.make_async_copy(strips.at[i], there, write_sems.at[i]))
                else:
                    act(pltpu.make_async_copy(there, strips.at[i], read_sems.at[i]))

    def loop(s, body):
        lax.fori_loop(0, jnp.minimum(notes[s][0, sz.note_n], sz.first), lambda i, _: body(i), None)

    def begin(s):
        loop(s, lambda i: move(s, i, False, lambda c: c.start()))

    def add(s):
        def step(i):
            move(s, i, False, lambda c: c.wait())
            value = strips[i].astype(jnp.float32) + firsts[s][i].astype(jnp.float32)
            strips[i] = value.astype(jnp.bfloat16)
            move(s, i, True, lambda c: c.start())

        loop(s, step)

    def end(s):
        loop(s, lambda i: move(s, i, True, lambda c: c.wait()))

    def first_add(i):
        value = held_strips[i].astype(jnp.float32) + firsts[0][i].astype(jnp.float32)
        strips[i] = value.astype(jnp.bfloat16)
        move(0, i, True, lambda c: c.start())

    loop(0, first_add)
    core = plan[HEAD_ROW, HEAD_CORE]
    for k in range(3):
        for a in range(sz.nb):
            at = plan[MINE_ROW, k * sz.nb + a]
            p = jnp.minimum(jnp.maximum(at - 1, 0), sz.keep - 1)
            for terms, c in ((mine, core), (theirs, 1 - core)):
                value = sum(t[p].astype(jnp.float32) for t in terms)
                rows = pl.ds(pl.multiple_of(c * ROWS, ROWS), ROWS)
                grads[k][0, a, rows] = jnp.where(at > 0, value, 0.0).astype(jnp.bfloat16)
    end(0)
    for s in range(1, T - 1):
        begin(s)
        add(s)
        end(s)


def spec(space):
    return pl.BlockSpec(memory_space=space)


ANY, HBM, VMEM, SMEM = pl.ANY, pltpu.HBM, pltpu.VMEM, pltpu.SMEM


def cost(flops, moved):
    return pl.CostEstimate(flops=flops, bytes_accessed=moved, transcendentals=0)


def call_plan(sz, own, mine, theirs):
    return pl.pallas_call(
        functools.partial(plan_kernel, sz),
        out_shape=[
            jax.ShapeDtypeStruct((sz.plan_rows, sz.lanes), jnp.int32),
            halves(sz.keep),
        ] + [jax.ShapeDtypeStruct((1, sz.lanes), jnp.int32)] * (sz.n_tensor - 1),
        in_specs=[spec(VMEM)] + [spec(ANY)] * 6,
        out_specs=[spec(VMEM), spec(ANY)] + [spec(VMEM)] * (sz.n_tensor - 1),
        scratch_shapes=[pltpu.SemaphoreType.DMA((2 * sz.owned,))],
        compiler_params=pltpu.CompilerParams(vmem_limit_bytes=SMALL),
        cost_estimate=cost(1_000_000, 4_000_000),
        name="plan",
    )(own, *mine, *theirs)


def call_turn(handed, arrived):
    return pl.pallas_call(
        lambda *_: None,
        out_shape=[jax.ShapeDtypeStruct(x.shape, x.dtype) for x in handed],
        in_specs=[spec(ANY)] * (len(handed) + len(arrived)),
        out_specs=[spec(ANY)] * len(handed),
        input_output_aliases={i: i for i in range(len(handed))},
        compiler_params=pltpu.CompilerParams(vmem_limit_bytes=SMALL),
        cost_estimate=cost(1000, 1000),
        name="turn",
    )(*handed, *arrived)


def blocks(n):
    return jax.ShapeDtypeStruct((n, BLK, BLK), jnp.bfloat16)


def halves(n):
    return jax.ShapeDtypeStruct((n, ROWS, BLK), jnp.bfloat16)


def held(scratch):
    return sum(s[0] * s[1] * s[2] * jnp.dtype(t).itemsize for s, t in scratch) + 2 * 1024 * 1024


def call_compute(sz, plan, tokens, cot, chunks):
    bf, f32 = jnp.bfloat16, jnp.float32
    T, A = sz.n_tensor, sz.slots + 1
    out_shape = [halves(sz.ring * sz.keep), halves(sz.far * sz.keep), halves((sz.ring - sz.far) * sz.keep)]
    out_shape += [blocks(sz.first)] * T
    scratch = [
        ((3 * sz.room, sz.tok, BLK), bf),
        ((sz.blocks + 1, BLK, BLK), bf),
        ((sz.blocks + 1, BLK, BLK), bf),
        ((A, sz.tok, BLK), f32),
        ((A, sz.tok, BLK), f32),
        ((A, sz.tok, BLK), f32),
        ((3 * A, sz.tok, BLK), bf),
        ((sz.all + 1, sz.tok, BLK), f32),
        ((T * sz.first, sz.tok, BLK), bf),
    ]
    return pl.pallas_call(
        functools.partial(compute_kernel, sz),
        out_shape=out_shape,
        in_specs=[spec(SMEM)] + [spec(HBM)] * 2 + [spec(ANY)] * len(chunks),
        out_specs=[spec(ANY)] * len(out_shape),
        scratch_shapes=[pltpu.VMEM(s, t) for s, t in scratch] + [
            pltpu.SemaphoreType.DMA((3 * sz.room,)),
            pltpu.SemaphoreType.DMA((max(len(chunks), sz.ring + 1 + T),)),
        ],
        compiler_params=pltpu.CompilerParams(vmem_limit_bytes=held(scratch)),
        cost_estimate=cost(1_000_000_000, 20_000_000),
        name="compute",
    )(plan, pltpu.with_memory_space_constraint(tokens, HBM), pltpu.with_memory_space_constraint(cot, HBM), *chunks)


def call_prepare(sz, plan, note, first):
    half = jax.ShapeDtypeStruct((sz.tok, sz.width // sz.n_tensor), jnp.bfloat16)
    return pl.pallas_call(
        functools.partial(prepare_kernel, sz),
        out_shape=[half, half, blocks(sz.first)],
        in_specs=[spec(SMEM), spec(SMEM), spec(VMEM)],
        out_specs=[spec(VMEM)] * 3,
        compiler_params=pltpu.CompilerParams(vmem_limit_bytes=12 * 1024 * 1024),
        cost_estimate=cost(1_000_000, 6_000_000),
        name="prepare",
    )(plan, note, first)


def call_last(sz, plan, notes, firsts, terms, strips, partial):
    n = 2 + len(notes) + len(firsts) + len(terms)
    out = jax.ShapeDtypeStruct((1, sz.nb, BLK, BLK), jnp.bfloat16)
    return pl.pallas_call(
        functools.partial(last_kernel, sz),
        out_shape=[jax.ShapeDtypeStruct(p.shape, p.dtype) for p in partial] + [out] * 3 + [
            jax.ShapeDtypeStruct((1,), jnp.int32)],
        in_specs=[spec(SMEM)] * (1 + len(notes)) + [spec(VMEM)] * (len(firsts) + len(terms) + 1) + [spec(ANY)] * 2,
        out_specs=[spec(ANY)] * 2 + [spec(VMEM)] * 3 + [spec(SMEM)],
        input_output_aliases={n: 0, n + 1: 1},
        scratch_shapes=[
            pltpu.VMEM((sz.first, sz.tok, BLK), jnp.bfloat16),
            pltpu.SemaphoreType.DMA((sz.first,)),
            pltpu.SemaphoreType.DMA((sz.first,)),
        ],
        compiler_params=pltpu.CompilerParams(vmem_limit_bytes=12 * 1024 * 1024),
        cost_estimate=cost(1_000_000, 3_000_000),
        name="last",
    )(plan, *notes, *firsts, *terms, strips, *partial)


def gather_chunks(sz, chunk):
    ahead, behind, swap = permutations(sz)
    same = {0: chunk}
    a = b = chunk
    for s in range(1, sz.top):
        a, b = lax.ppermute(a, "fsdp", ahead), lax.ppermute(b, "fsdp", behind)
        same[sz.ring - s], same[s] = a, b
    other = {d: lax.ppermute(same[d], "fsdp", swap) for d in same}
    same[sz.top] = lax.ppermute(a, "fsdp", ahead)
    other[sz.top] = lax.ppermute(a, "fsdp", [(i, j ^ 1) for i, j in ahead])
    return [side[d] for side in (same, other) for d in sz.order]


def reduce_parts(sz, same, far, near, notes):
    ahead, behind, swap = permutations(sz)
    keep = sz.keep
    far = lax.ppermute(far, "fsdp", swap)
    near = lax.ppermute(call_turn([near], [far])[0], "fsdp", swap)

    def term(d, *more):
        j = sz.order.index(d)
        pair = far[j * keep:(j + 1) * keep] if j < sz.far else near[(j - sz.far) * keep:][:keep]
        out = same[j * keep:(j + 1) * keep].astype(jnp.float32) + pair.astype(jnp.float32)
        for m in more:
            out = out + m.astype(jnp.float32)
        return out.astype(jnp.bfloat16)

    a, b = lax.optimization_barrier((term(sz.top), term(sz.top + 1)))
    for s in range(1, sz.top):
        if s == 2:
            a, b = call_turn([a, b], notes)
        a, b = lax.ppermute(a, "fsdp", ahead), lax.ppermute(b, "fsdp", behind)
        a = term(sz.top - s, a)
        if s + 1 < sz.top:
            a, b = lax.optimization_barrier((a, term(sz.top + 1 + s, b)))
    here = term(0)
    mine = [here, lax.ppermute(a, "fsdp", ahead), b]
    theirs = [
        lax.ppermute(here, "fsdp", swap),
        lax.ppermute(a, "fsdp", [(i, j ^ 1) for i, j in ahead]),
        lax.ppermute(b, "fsdp", swap),
    ]
    return mine + theirs


def program(sz, own, tokens, cotangent, mine):
    T = sz.n_tensor
    swap = permutations(sz)[-1]
    theirs = [lax.ppermute(b, "fsdp", swap) for b in mine]
    plan, chunk, *notes = call_plan(sz, own, mine, theirs)

    def exchange(array, s):
        return lax.ppermute(array, "tensor", [(i, (i + s) % T) for i in range(T)])

    notes = [exchange(note, s) for s, note in enumerate(notes, 1)]
    chunks = gather_chunks(sz, chunk)
    same, far, near, *firsts = call_compute(sz, plan, tokens, cotangent, chunks)
    *partial, strips = call_prepare(sz, plan, notes[0], firsts[0])
    firsts = [exchange(firsts[s], s) for s in range(1, T)]
    terms = reduce_parts(sz, same, far, near, notes)
    *outs, flag = call_last(sz, plan, notes, firsts, terms, strips, partial)
    return tuple(outs), flag


def shards(
    tokens,
    cotangent,
    gate_blocks,
    up_blocks,
    down_blocks,
    gate_where,
    up_where,
    down_where,
    block_counts,
):
    n_fsdp, n_tensor = lax.axis_size("fsdp"), lax.axis_size("tensor")
    f, rank = lax.axis_index("fsdp"), lax.axis_index("tensor")
    slots = gate_where.shape[1]
    full = Sizes(tokens, gate_blocks, slots, n_fsdp, n_tensor, False)
    own = jnp.concatenate([
        gate_where[0], up_where[0], down_where[0], block_counts[:, 0],
        f.astype(jnp.int32)[None], rank.astype(jnp.int32)[None]])
    own = jnp.pad(own, (0, full.lanes - own.shape[0]))[None]
    blocks_in = (gate_blocks, up_blocks, down_blocks)
    if slots >= full.cb:
        return program(full, own, tokens, cotangent, blocks_in)[0]
    lean = Sizes(tokens, gate_blocks, slots, n_fsdp, n_tensor, True)
    outs, flag = program(lean, own, tokens, cotangent, blocks_in)
    return lax.cond(
        flag[0] > 0,
        lambda outs, *args: program(full, *args)[0],
        lambda outs, *args: outs,
        outs, own, tokens, cotangent, blocks_in)


def solution(mesh):
    placed = (
        P("fsdp", None),
        P("fsdp", None),
        P("tensor", "fsdp", None, None),
        P("tensor", "fsdp", None, None),
        P("tensor", "fsdp", None, None),
        P("tensor", None),
        P("tensor", None),
        P("tensor", None),
        P(None, "tensor"),
    )
    return jax.shard_map(
        shards,
        mesh=mesh,
        in_specs=placed,
        out_specs=(
            P("fsdp", "tensor"),
            P("fsdp", "tensor"),
            P("tensor", "fsdp", None, None),
            P("tensor", "fsdp", None, None),
            P("tensor", "fsdp", None, None),
        ),
        check_vma=False,
    )
```

```python
import functools

import jax
import jax.numpy as jnp
from jax import lax
from jax.experimental import pallas as pl
from jax.experimental.pallas import tpu as pltpu
from jax.sharding import PartitionSpec as P

FF = 14336
BLK = 128
GROUP = 4
FIRST_SEND = 18
LEAN_SLOTS = 7
ROWS = BLK // 2
SMALL = 4 * 1024 * 1024
PART, STRIP, CIDX, CWAS, OIDX, OWAS = range(6)
FIELDS = 6
COLS_ROW = 3 * FIELDS
HEAD_ROW = COLS_ROW + 1
MINE_ROW = COLS_ROW + 2
LISTS_ROW = COLS_ROW + 3
HEAD_COLS, HEAD_OVER, HEAD_CORE, HEAD_LISTS = 3, 4, 5, 8


class Sizes:
    def __init__(self, tokens, gate_blocks, slots, n_fsdp, n_tensor, lean):
        self.tok, self.width = tokens.shape
        self.n_fsdp, self.n_tensor = n_fsdp, n_tensor
        self.rb = self.width // BLK
        self.cb = FF // (BLK * n_tensor)
        self.slots = slots
        self.all = 3 * slots
        self.lanes = -(-(self.all + GROUP) // 128) * 128
        self.nb = gate_blocks.shape[1]
        self.owned = 3 * self.nb
        self.ring = n_fsdp // 2
        self.top = self.ring // 2
        self.rbt = self.rb // n_tensor
        self.order = [self.top]
        for d in range(1, self.top):
            self.order += [self.top + d, self.top - d]
        self.order.append(0)
        self.far = min(2, self.ring - 1)
        self.keep = min(LEAN_SLOTS, 2 * self.owned) if lean else 2 * self.owned
        self.send_all = 2 * self.rbt
        self.first = min(FIRST_SEND, self.send_all) if lean else self.send_all
        self.blocks = self.ring * self.keep
        self.plan_rows = -(-(LISTS_ROW + 2 * n_tensor) // 8) * 8
        self.note_n, self.note_over = self.lanes - 1, self.lanes - 2
        self.room = slots + GROUP

    def place(self, d):
        return self.order.index(d) * self.keep

    def place_across(self, d):
        return self.place((self.ring - d) % self.ring)


def permutations(sz):
    seq = list(range(0, sz.ring, 2)) + list(range(sz.ring - 1, 0, -2))
    ahead, behind, swap = [], [], []
    for i, q in enumerate(seq):
        up, down = seq[(i + 1) % sz.ring], seq[i - 1]
        ahead += [(q * 2, up * 2), (q * 2 + 1, down * 2 + 1)]
        behind += [(q * 2, down * 2), (q * 2 + 1, up * 2 + 1)]
        swap += [(q * 2, q * 2 + 1), (q * 2 + 1, q * 2)]
    return ahead, behind, swap


def ratio(x, d):
    return jnp.floor((x + 0.5) * (1.0 / d))


def rest_of(x, d):
    return x - d * ratio(x, d)


def ring_position(sz, chip):
    return jnp.where(rest_of(chip, 2) == 0, ratio(chip, 2), sz.ring - 1 - ratio(chip, 2))


class Marks:
    def __init__(self, sz, own):
        N, L, S = sz.all, sz.lanes, sz.slots
        f32 = jnp.float32
        self.sz = sz
        self.sub = lax.broadcasted_iota(jnp.int32, (N, L), 0)
        self.lane = lax.broadcasted_iota(jnp.int32, (N, L), 1)
        self.same = self.sub == self.lane
        sub_c = self.sub[:, :1].astype(f32)
        lane_r = lax.broadcasted_iota(jnp.int32, (1, L), 1).astype(f32)
        self.sub_c, self.lane_r = sub_c, lane_r
        raw_r = own[...].astype(f32)

        def single(row, at):
            return jnp.sum(jnp.where(lane_r == at, row, 0.0), axis=1, keepdims=True)

        self.f, self.rank = single(raw_r, N + 3), single(raw_r, N + 4)

        def kind(x):
            return (x >= S).astype(f32) + (x >= 2 * S).astype(f32)

        self.kind_c, self.kind_r = kind(sub_c), kind(lane_r)
        self.n_r = lane_r - S * self.kind_r
        self.n_c = sub_c - S * self.kind_c
        limit = jnp.zeros((1, L), f32)
        for k in range(3):
            limit = limit + jnp.where(self.kind_r == k, single(raw_r, N + k), 0.0)
        live_r = jnp.where((lane_r < N) & (self.n_r < limit), 1.0, 0.0)
        w_c = self.col(raw_r)
        live_c = self.col(live_r)

        def place(w, k):
            gate, down = ratio(w, sz.cb), ratio(w, sz.rb)
            is_down = k == 2
            return jnp.where(is_down, w - down * sz.rb, gate), jnp.where(is_down, down, w - gate * sz.cb)

        self.row_c, col_c = place(w_c, self.kind_c)
        self.row_r, col_r = place(raw_r, self.kind_r)
        self.chip_c, chip_r = ratio(self.n_c, 2 * sz.nb), ratio(self.n_r, 2 * sz.nb)
        self.same_chip = (self.chip_c == chip_r).astype(f32)
        self.same_col = (col_c == col_r).astype(f32)
        act_c, act_r = live_c, live_r
        for k in range(3):
            lanes = self.same_col * (live_r * (self.kind_r == k).astype(f32))
            act_c = act_c * jnp.max(lanes, axis=1, keepdims=True)
            subs = self.same_col * (live_c * (self.kind_c == k).astype(f32))
            act_r = act_r * jnp.max(subs, axis=0, keepdims=True)
        self.act_c, self.act_r = act_c, act_r
        out_c = jnp.where(self.kind_c == 2, 0.0, f32(sz.rb)) + self.row_c
        out_r = jnp.where(self.kind_r == 2, 0.0, f32(sz.rb)) + self.row_r
        self.same_out = (out_c == out_r).astype(f32)
        self.before = (self.lane < self.sub).astype(f32)
        self.after = (self.sub < self.lane).astype(f32)
        self.owas_c = jnp.max(self.same_out * self.before * act_r, axis=1, keepdims=True)
        self.owas_r = jnp.max(self.same_out * self.after * act_c, axis=0, keepdims=True)
        self.lead_c = act_c * (1.0 - self.owas_c)
        self.lead_r = act_r * (1.0 - self.owas_r)

        def shift(row):
            away = ratio(row, sz.rbt) - self.rank
            return jnp.where(away < 0, away + sz.n_tensor, away)

        self.shift_c, self.shift_r = shift(self.row_c), shift(self.row_r)
        self.local_c = jnp.where(self.kind_c == 2, 0.0, f32(sz.rbt)) + rest_of(self.row_c, sz.rbt)

    def col(self, row):
        return jnp.sum(jnp.where(self.same, row, 0.0), axis=1, keepdims=True)

    def carried(self):
        sz = self.sz
        rank = jnp.sum(self.before * self.same_chip * self.act_r, axis=1, keepdims=True)
        away = ring_position(sz, self.chip_c) - ring_position(sz, ratio(self.f, 2))
        away = jnp.where(rest_of(self.f, 2) == 0, away, -away)
        rel = jnp.where(away < 0, away + sz.ring, away)
        j = jnp.where(rel > sz.top, 2 * (rel - sz.top) - 1, 2 * (sz.top - rel))
        return rank, jnp.where(rel == 0, sz.ring - 1.0, j)

    def ranks(self, chosen_r):
        return jnp.sum(self.before * chosen_r, axis=1, keepdims=True)

    def listed(self, chosen_c, rank_c, value_c, lo=0, hi=None):
        at = rank_c[lo:hi] == self.lane[lo:hi].astype(jnp.float32)
        return jnp.sum(jnp.where(at, chosen_c[lo:hi] * value_c[lo:hi], 0.0), axis=0, keepdims=True)

    def most_on_chip(self):
        return jnp.max(jnp.sum(self.same_chip * self.act_r, axis=1, keepdims=True), axis=0, keepdims=True)


def total(x):
    return jnp.sum(x, axis=0, keepdims=True)


def head_row(sz, entries):
    lane = lax.broadcasted_iota(jnp.int32, (1, sz.lanes), 1)
    row = jnp.zeros((1, sz.lanes), jnp.float32)
    for i, value in entries:
        row = jnp.where(lane == i, value, row)
    return row


def plan_kernel(sz, own, *refs):
    mine, theirs, (plan, chunk, *notes, sems) = refs[:3], refs[3:6], refs[6:]
    S, N = sz.slots, sz.all
    m = Marks(sz, own)
    f32 = jnp.float32
    lane_r, sub_c = m.lane_r, m.sub_c
    pos_c, base_c = m.carried()
    core = rest_of(m.f, 2)
    half = pl.ds(pl.multiple_of(jnp.max(core).astype(jnp.int32) * ROWS, ROWS), ROWS)

    pair = jnp.where(core == 0, m.f + 1, m.f - 1)
    i_r = rest_of(lane_r, sz.owned)
    owner_r = jnp.where(lane_r < sz.owned, m.f, pair)
    slot_r = ratio(i_r, sz.nb) * S + owner_r * sz.nb + rest_of(i_r, sz.nb)
    at_r = jnp.sum(jnp.where(sub_c == slot_r, m.act_c * (pos_c + 1.0), 0.0), axis=0, keepdims=True)
    copies = []
    for i in range(2 * sz.owned):
        side, k, a = i // sz.owned, i % sz.owned // sz.nb, i % sz.nb
        at = jnp.max(jnp.where(lane_r == i, at_r, 0.0)).astype(jnp.int32)
        fits = (at > 0) & (at <= sz.keep)
        place = jnp.minimum(jnp.maximum(at - 1, 0), sz.keep - 1)
        copy = pltpu.make_async_copy((mine, theirs)[side][k].at[0, a, half], chunk.at[place], sems.at[i])
        copies.append((fits, copy))
    for fits, copy in copies:
        pl.when(fits)(copy.start)

    same_kind = (m.kind_c == m.kind_r).astype(f32)
    rank_c = jnp.sum(m.before * same_kind * m.act_r, axis=1, keepdims=True)
    cwas_c = jnp.max(m.before * same_kind * m.same_col * m.act_r, axis=1, keepdims=True)
    cwas_r = jnp.max(m.after * same_kind * m.same_col * m.act_c, axis=0, keepdims=True)
    big = f32(4 * N)
    lanes_f = m.lane.astype(f32)
    gates_r = m.act_r * (m.kind_r == 0).astype(f32)
    cidx_c = jnp.min(jnp.where(m.same_col * gates_r > 0, lanes_f, big), axis=1, keepdims=True)
    oidx_c = jnp.min(jnp.where(m.same_out * m.act_r > 0, lanes_f, big), axis=1, keepdims=True)
    rank_r = jnp.sum(m.after * same_kind * m.act_c, axis=0, keepdims=True)
    turn_c = ratio(rank_c, GROUP) * 3 + m.kind_c
    turn_r = ratio(rank_r, GROUP) * 3 + m.kind_r
    ahead = ((turn_r < turn_c) | ((turn_r == turn_c) & (rank_r < rank_c))).astype(f32)
    owas_c = jnp.max(m.same_out * ahead * m.act_r, axis=1, keepdims=True)
    part_c = jnp.where(pos_c < sz.keep, base_c * sz.keep + pos_c, f32(sz.blocks))
    fields = [(part_c, sz.blocks), (m.row_c, 0), (cidx_c, S), (cwas_c, 0), (oidx_c, N), (owas_c, 0)]
    rows = []
    head = []
    for k in range(3):
        lo, hi = k * S, (k + 1) * S
        n_k = total(m.act_c[lo:hi])
        head.append((k, n_k))
        for value, spare in fields:
            row = m.listed(m.act_c, rank_c, value, lo, hi)
            rows.append(jnp.where(lane_r < n_k, row, f32(spare)))
    leader_c = m.act_c * (1.0 - cwas_c) * (m.kind_c == 0).astype(f32)
    leader_r = m.act_r * (1.0 - cwas_r) * (m.kind_r == 0).astype(f32)
    n_cols = total(leader_c)
    cols = m.listed(leader_c, m.ranks(leader_r), sub_c, 0, S)
    rows.append(jnp.where(lane_r < n_cols, cols, f32(S)))
    head.append((HEAD_COLS, n_cols))
    lists, sent = [], []
    over = (m.most_on_chip() > sz.keep).astype(f32)
    for s in range(sz.n_tensor):
        chosen_c = m.lead_c * (m.shift_c == s).astype(f32)
        chosen_r = m.lead_r * (m.shift_r == s).astype(f32)
        rank = m.ranks(chosen_r)
        lists.append(m.listed(chosen_c, rank, sub_c))
        lists.append(m.listed(chosen_c, rank, m.local_c))
        n = total(chosen_c)
        head.append((HEAD_LISTS + s, n))
        sent.append(n)
        over = jnp.maximum(over, (n > sz.first).astype(f32))
    head += [(HEAD_OVER, over), (HEAD_CORE, core)]
    for s in range(1, sz.n_tensor):
        note = jnp.where(lane_r == sz.note_n, sent[s], lists[2 * s + 1])
        notes[s - 1][...] = jnp.where(lane_r == sz.note_over, over, note).astype(jnp.int32)
    rows.append(head_row(sz, head))
    rows.append(at_r)
    rows += lists
    for i, row in enumerate(rows):
        plan[i:i + 1, :] = row.astype(jnp.int32)
    for fits, copy in copies:
        pl.when(fits)(copy.wait)


def dot(a, b, ca, cb):
    return lax.dot_general(a, b, (((ca,), (cb,)), ((), ())), preferred_element_type=jnp.float32)


def field(sz, plan, k, j, e):
    return plan[k * FIELDS + j, e]


def walk(plan, body):
    most = jnp.maximum(jnp.maximum(plan[HEAD_ROW, 0], plan[HEAD_ROW, 1]), plan[HEAD_ROW, 2])
    lax.fori_loop(0, (most + (GROUP - 1)) // GROUP, lambda p, _: body(p * GROUP), None)


def each(plan, k, body):
    lax.fori_loop(0, plan[HEAD_ROW, k], lambda e, _: body(e), None)


def compute_kernel(sz, plan, tokens, cot, *refs):
    n_chunks, T = 2 * sz.ring, sz.n_tensor
    chunks, refs = refs[:n_chunks], refs[n_chunks:]
    same, far, near = refs[:3]
    firsts, refs = refs[3:3 + T], refs[3 + T:]
    xs, wbuf, parts, gate_acc, up_acc, hg_acc, acts, out_acc, stage, strip_sems, sems = refs
    A = sz.slots + 1
    get = functools.partial(field, sz, plan)

    def strip_copy(k, e):
        src = cot if k == 2 else tokens
        cols = pl.ds(pl.multiple_of(get(k, STRIP, e) * BLK, BLK), BLK)
        return pltpu.make_async_copy(src.at[:, cols], xs.at[k * sz.room + e], strip_sems.at[k * sz.room + e])

    core = plan[HEAD_ROW, HEAD_CORE]
    sides = [pl.ds(pl.multiple_of(c * ROWS, ROWS), ROWS) for c in (core, 1 - core)]
    loads = []
    for side, place in enumerate((sz.place, sz.place_across)):
        for d in sz.order:
            i = len(loads)
            there = wbuf.at[pl.ds(place(d), sz.keep), sides[side]]
            loads.append(pltpu.make_async_copy(chunks[i], there, sems.at[i]))
    for k in range(3):
        each(plan, k, lambda e, k=k: strip_copy(k, e).start())
    for c in loads:
        c.start()
    for k in range(3):
        each(plan, k, lambda e, k=k: strip_copy(k, e).wait())
    for c in loads:
        c.wait()

    group = [(k, u) for k in range(3) for u in range(GROUP)]

    def forward(e0):
        for k, u in group:
            e, acc = e0 + u, (gate_acc, up_acc, hg_acc)[k]
            prod = dot(xs[k * sz.room + e], wbuf[get(k, PART, e)], 1, 1 if k == 2 else 0)
            c = get(k, CIDX, e)
            acc[c] = prod + jnp.where(get(k, CWAS, e) == 0, 0.0, acc[c])

    walk(plan, forward)

    def columns(i, _):
        for j in range(GROUP):
            c = plan[COLS_ROW, i * GROUP + j]
            g, u, h = gate_acc[c], up_acc[c], hg_acc[c]
            s = lax.logistic(g)
            silu = g * s
            acts[c] = (h * u * s * (1.0 + g * (1.0 - s))).astype(jnp.bfloat16)
            acts[A + c] = (h * silu).astype(jnp.bfloat16)
            acts[2 * A + c] = (silu * u).astype(jnp.bfloat16)

    lax.fori_loop(0, (plan[HEAD_ROW, HEAD_COLS] + (GROUP - 1)) // GROUP, columns, None)

    def gradients(e0):
        for k, u in group:
            e = e0 + u
            a, x = acts[k * A + get(k, CIDX, e)], xs[k * sz.room + e]
            grad = dot(a, x, 0, 0) if k == 2 else dot(x, a, 0, 0)
            parts[get(k, PART, e)] = grad.astype(jnp.bfloat16)

    walk(plan, gradients)
    outs = []
    for j, d in enumerate(sz.order):
        ref, at = (far, j) if j < sz.far else (near, j - sz.far)
        outs.append(pltpu.make_async_copy(
            parts.at[pl.ds(sz.place_across(d), sz.keep), sides[1]], ref.at[pl.ds(at * sz.keep, sz.keep)], sems.at[j]))
    outs.append(pltpu.make_async_copy(parts.at[pl.ds(0, sz.blocks), sides[0]], same, sems.at[sz.ring]))
    for c in outs:
        c.start()

    def terms(e0):
        for k, u in group:
            e = e0 + u
            prod = dot(acts[k * A + get(k, CIDX, e)], wbuf[get(k, PART, e)], 1, 0 if k == 2 else 1)
            at = get(k, OIDX, e)
            out_acc[at] = prod + jnp.where(get(k, OWAS, e) == 0, 0.0, out_acc[at])

    walk(plan, terms)

    for s in reversed(range(T)):
        def staged(i, _, s=s):
            stage[s * sz.first + i] = out_acc[plan[LISTS_ROW + 2 * s, i]].astype(jnp.bfloat16)

        lax.fori_loop(0, jnp.minimum(plan[HEAD_ROW, HEAD_LISTS + s], sz.first), staged, None)
        copy = pltpu.make_async_copy(stage.at[pl.ds(s * sz.first, sz.first)], firsts[s], sems.at[sz.ring + 1 + s])
        copy.start()
        outs.append(copy)
    for c in outs:
        c.wait()


def strip_of(sz, at):
    w = jnp.where(at < sz.rbt, at, at - sz.rbt)
    return at < sz.rbt, pl.ds(pl.multiple_of(w * BLK, BLK), BLK)


def prepare_kernel(sz, plan, note, first, outputs, input_grads, strips):
    outputs[...] = jnp.zeros_like(outputs)
    input_grads[...] = jnp.zeros_like(input_grads)

    def step(i, _):
        is_out, cols = strip_of(sz, plan[LISTS_ROW + 1, i])

        @pl.when(is_out)
        def _():
            outputs[:, cols] = first[i]

        @pl.when(jnp.logical_not(is_out))
        def _():
            input_grads[:, cols] = first[i]

    lax.fori_loop(0, jnp.minimum(plan[HEAD_ROW, HEAD_LISTS], sz.first), step, None)

    def pick(i, _):
        is_out, cols = strip_of(sz, note[0, i])

        @pl.when(is_out)
        def _():
            strips[i] = outputs[:, cols]

        @pl.when(jnp.logical_not(is_out))
        def _():
            strips[i] = input_grads[:, cols]

    lax.fori_loop(0, jnp.minimum(note[0, sz.note_n], sz.first), pick, None)


def last_kernel(sz, plan, *refs):
    T = sz.n_tensor
    notes, refs = refs[:T - 1], refs[T - 1:]
    firsts, refs = refs[:T - 1], refs[T - 1:]
    mine, theirs, held_strips, refs = refs[:3], refs[3:6], refs[6], refs[9:]
    outputs, input_grads, grads, flag = refs[0], refs[1], refs[2:5], refs[5]
    strips, read_sems, write_sems = refs[6:]
    over = plan[HEAD_ROW, HEAD_OVER]
    for note in notes:
        over = jnp.maximum(over, note[0, sz.note_over])
    flag[0] = over

    def move(s, i, back, act):
        is_out, cols = strip_of(sz, notes[s][0, i])
        for ref, here in ((outputs, is_out), (input_grads, jnp.logical_not(is_out))):
            @pl.when(here)
            def _(ref=ref):
                there = ref.at[:, cols]
                if back:
                    act(pltpu.make_async_copy(strips.at[i], there, write_sems.at[i]))
                else:
                    act(pltpu.make_async_copy(there, strips.at[i], read_sems.at[i]))

    def loop(s, body):
        lax.fori_loop(0, jnp.minimum(notes[s][0, sz.note_n], sz.first), lambda i, _: body(i), None)

    def begin(s):
        loop(s, lambda i: move(s, i, False, lambda c: c.start()))

    def add(s):
        def step(i):
            move(s, i, False, lambda c: c.wait())
            value = strips[i].astype(jnp.float32) + firsts[s][i].astype(jnp.float32)
            strips[i] = value.astype(jnp.bfloat16)
            move(s, i, True, lambda c: c.start())

        loop(s, step)

    def end(s):
        loop(s, lambda i: move(s, i, True, lambda c: c.wait()))

    def first_add(i):
        value = held_strips[i].astype(jnp.float32) + firsts[0][i].astype(jnp.float32)
        strips[i] = value.astype(jnp.bfloat16)
        move(0, i, True, lambda c: c.start())

    loop(0, first_add)
    core = plan[HEAD_ROW, HEAD_CORE]
    for k in range(3):
        for a in range(sz.nb):
            at = plan[MINE_ROW, k * sz.nb + a]
            p = jnp.minimum(jnp.maximum(at - 1, 0), sz.keep - 1)
            for terms, c in ((mine, core), (theirs, 1 - core)):
                value = sum(t[p].astype(jnp.float32) for t in terms)
                rows = pl.ds(pl.multiple_of(c * ROWS, ROWS), ROWS)
                grads[k][0, a, rows] = jnp.where(at > 0, value, 0.0).astype(jnp.bfloat16)
    end(0)
    for s in range(1, T - 1):
        begin(s)
        add(s)
        end(s)


def spec(space):
    return pl.BlockSpec(memory_space=space)


ANY, HBM, VMEM, SMEM = pl.ANY, pltpu.HBM, pltpu.VMEM, pltpu.SMEM


def cost(flops, moved):
    return pl.CostEstimate(flops=flops, bytes_accessed=moved, transcendentals=0)


def call_plan(sz, own, mine, theirs):
    return pl.pallas_call(
        functools.partial(plan_kernel, sz),
        out_shape=[
            jax.ShapeDtypeStruct((sz.plan_rows, sz.lanes), jnp.int32),
            halves(sz.keep),
        ] + [jax.ShapeDtypeStruct((1, sz.lanes), jnp.int32)] * (sz.n_tensor - 1),
        in_specs=[spec(VMEM)] + [spec(ANY)] * 6,
        out_specs=[spec(VMEM), spec(ANY)] + [spec(VMEM)] * (sz.n_tensor - 1),
        scratch_shapes=[pltpu.SemaphoreType.DMA((2 * sz.owned,))],
        compiler_params=pltpu.CompilerParams(vmem_limit_bytes=SMALL),
        cost_estimate=cost(1_000_000, 4_000_000),
        name="plan",
    )(own, *mine, *theirs)


def call_turn(handed, arrived):
    return pl.pallas_call(
        lambda *_: None,
        out_shape=[jax.ShapeDtypeStruct(x.shape, x.dtype) for x in handed],
        in_specs=[spec(ANY)] * (len(handed) + len(arrived)),
        out_specs=[spec(ANY)] * len(handed),
        input_output_aliases={i: i for i in range(len(handed))},
        compiler_params=pltpu.CompilerParams(vmem_limit_bytes=SMALL),
        cost_estimate=cost(1000, 1000),
        name="turn",
    )(*handed, *arrived)


def blocks(n):
    return jax.ShapeDtypeStruct((n, BLK, BLK), jnp.bfloat16)


def halves(n):
    return jax.ShapeDtypeStruct((n, ROWS, BLK), jnp.bfloat16)


def held(scratch):
    return sum(s[0] * s[1] * s[2] * jnp.dtype(t).itemsize for s, t in scratch) + 2 * 1024 * 1024


def call_compute(sz, plan, tokens, cot, chunks):
    bf, f32 = jnp.bfloat16, jnp.float32
    T, A = sz.n_tensor, sz.slots + 1
    out_shape = [halves(sz.ring * sz.keep), halves(sz.far * sz.keep), halves((sz.ring - sz.far) * sz.keep)]
    out_shape += [blocks(sz.first)] * T
    scratch = [
        ((3 * sz.room, sz.tok, BLK), bf),
        ((sz.blocks + 1, BLK, BLK), bf),
        ((sz.blocks + 1, BLK, BLK), bf),
        ((A, sz.tok, BLK), f32),
        ((A, sz.tok, BLK), f32),
        ((A, sz.tok, BLK), f32),
        ((3 * A, sz.tok, BLK), bf),
        ((sz.all + 1, sz.tok, BLK), f32),
        ((T * sz.first, sz.tok, BLK), bf),
    ]
    return pl.pallas_call(
        functools.partial(compute_kernel, sz),
        out_shape=out_shape,
        in_specs=[spec(SMEM)] + [spec(HBM)] * 2 + [spec(ANY)] * len(chunks),
        out_specs=[spec(ANY)] * len(out_shape),
        scratch_shapes=[pltpu.VMEM(s, t) for s, t in scratch] + [
            pltpu.SemaphoreType.DMA((3 * sz.room,)),
            pltpu.SemaphoreType.DMA((max(len(chunks), sz.ring + 1 + T),)),
        ],
        compiler_params=pltpu.CompilerParams(vmem_limit_bytes=held(scratch)),
        cost_estimate=cost(1_000_000_000, 20_000_000),
        name="compute",
    )(plan, pltpu.with_memory_space_constraint(tokens, HBM), pltpu.with_memory_space_constraint(cot, HBM), *chunks)


def call_prepare(sz, plan, note, first):
    half = jax.ShapeDtypeStruct((sz.tok, sz.width // sz.n_tensor), jnp.bfloat16)
    return pl.pallas_call(
        functools.partial(prepare_kernel, sz),
        out_shape=[half, half, blocks(sz.first)],
        in_specs=[spec(SMEM), spec(SMEM), spec(VMEM)],
        out_specs=[spec(VMEM)] * 3,
        compiler_params=pltpu.CompilerParams(vmem_limit_bytes=12 * 1024 * 1024),
        cost_estimate=cost(1_000_000, 6_000_000),
        name="prepare",
    )(plan, note, first)


def call_last(sz, plan, notes, firsts, terms, strips, partial):
    n = 2 + len(notes) + len(firsts) + len(terms)
    out = jax.ShapeDtypeStruct((1, sz.nb, BLK, BLK), jnp.bfloat16)
    return pl.pallas_call(
        functools.partial(last_kernel, sz),
        out_shape=[jax.ShapeDtypeStruct(p.shape, p.dtype) for p in partial] + [out] * 3 + [
            jax.ShapeDtypeStruct((1,), jnp.int32)],
        in_specs=[spec(SMEM)] * (1 + len(notes)) + [spec(VMEM)] * (len(firsts) + len(terms) + 1) + [spec(ANY)] * 2,
        out_specs=[spec(ANY)] * 2 + [spec(VMEM)] * 3 + [spec(SMEM)],
        input_output_aliases={n: 0, n + 1: 1},
        scratch_shapes=[
            pltpu.VMEM((sz.first, sz.tok, BLK), jnp.bfloat16),
            pltpu.SemaphoreType.DMA((sz.first,)),
            pltpu.SemaphoreType.DMA((sz.first,)),
        ],
        compiler_params=pltpu.CompilerParams(vmem_limit_bytes=12 * 1024 * 1024),
        cost_estimate=cost(1_000_000, 3_000_000),
        name="last",
    )(plan, *notes, *firsts, *terms, strips, *partial)


def gather_chunks(sz, chunk):
    ahead, behind, swap = permutations(sz)
    same = {0: chunk}
    a = b = chunk
    for s in range(1, sz.top):
        a, b = lax.ppermute(a, "fsdp", ahead), lax.ppermute(b, "fsdp", behind)
        same[sz.ring - s], same[s] = a, b
    other = {d: lax.ppermute(same[d], "fsdp", swap) for d in same}
    same[sz.top] = lax.ppermute(a, "fsdp", ahead)
    other[sz.top] = lax.ppermute(a, "fsdp", [(i, j ^ 1) for i, j in ahead])
    return [side[d] for side in (same, other) for d in sz.order]


def reduce_parts(sz, same, far, near, notes):
    ahead, behind, swap = permutations(sz)
    keep = sz.keep
    far = lax.ppermute(far, "fsdp", swap)
    near = lax.ppermute(call_turn([near], [far])[0], "fsdp", swap)

    def term(d, *more):
        j = sz.order.index(d)
        pair = far[j * keep:(j + 1) * keep] if j < sz.far else near[(j - sz.far) * keep:][:keep]
        out = same[j * keep:(j + 1) * keep].astype(jnp.float32) + pair.astype(jnp.float32)
        for m in more:
            out = out + m.astype(jnp.float32)
        return out.astype(jnp.bfloat16)

    a, b = lax.optimization_barrier((term(sz.top), term(sz.top + 1)))
    for s in range(1, sz.top):
        last_b = b
        a, b = lax.ppermute(a, "fsdp", ahead), lax.ppermute(b, "fsdp", behind)
        if s == 1:
            a, b = call_turn([a, b], notes)
        else:
            a = call_turn([a], [last_b])[0]
        a = term(sz.top - s, a)
        if s + 1 < sz.top:
            b = term(sz.top + 1 + s, call_turn([b], [a])[0])
    here = term(0)

    def across(pairs):
        return [(i, j ^ 1) for i, j in pairs]

    mine = [here, lax.ppermute(a, "fsdp", ahead), b]
    theirs = [
        lax.ppermute(here, "fsdp", swap),
        lax.ppermute(a, "fsdp", across(ahead)),
        lax.ppermute(last_b, "fsdp", across(behind)),
    ]
    return mine + theirs


def program(sz, own, tokens, cotangent, mine):
    T = sz.n_tensor
    swap = permutations(sz)[-1]
    theirs = [lax.ppermute(b, "fsdp", swap) for b in mine]
    plan, chunk, *notes = call_plan(sz, own, mine, theirs)

    def exchange(array, s):
        return lax.ppermute(array, "tensor", [(i, (i + s) % T) for i in range(T)])

    notes = [exchange(note, s) for s, note in enumerate(notes, 1)]
    chunks = gather_chunks(sz, chunk)
    same, far, near, *firsts = call_compute(sz, plan, tokens, cotangent, chunks)
    *partial, strips = call_prepare(sz, plan, notes[0], firsts[0])
    firsts = [exchange(firsts[s], s) for s in range(1, T)]
    terms = reduce_parts(sz, same, far, near, notes)
    *outs, flag = call_last(sz, plan, notes, firsts, terms, strips, partial)
    return tuple(outs), flag


def shards(
    tokens,
    cotangent,
    gate_blocks,
    up_blocks,
    down_blocks,
    gate_where,
    up_where,
    down_where,
    block_counts,
):
    n_fsdp, n_tensor = lax.axis_size("fsdp"), lax.axis_size("tensor")
    f, rank = lax.axis_index("fsdp"), lax.axis_index("tensor")
    slots = gate_where.shape[1]
    full = Sizes(tokens, gate_blocks, slots, n_fsdp, n_tensor, False)
    own = jnp.concatenate([
        gate_where[0], up_where[0], down_where[0], block_counts[:, 0],
        f.astype(jnp.int32)[None], rank.astype(jnp.int32)[None]])
    own = jnp.pad(own, (0, full.lanes - own.shape[0]))[None]
    blocks_in = (gate_blocks, up_blocks, down_blocks)
    if slots >= full.cb:
        return program(full, own, tokens, cotangent, blocks_in)[0]
    lean = Sizes(tokens, gate_blocks, slots, n_fsdp, n_tensor, True)
    outs, flag = program(lean, own, tokens, cotangent, blocks_in)
    return lax.cond(
        flag[0] > 0,
        lambda outs, *args: program(full, *args)[0],
        lambda outs, *args: outs,
        outs, own, tokens, cotangent, blocks_in)


def solution(mesh):
    placed = (
        P("fsdp", None),
        P("fsdp", None),
        P("tensor", "fsdp", None, None),
        P("tensor", "fsdp", None, None),
        P("tensor", "fsdp", None, None),
        P("tensor", None),
        P("tensor", None),
        P("tensor", None),
        P(None, "tensor"),
    )
    return jax.shard_map(
        shards,
        mesh=mesh,
        in_specs=placed,
        out_specs=(
            P("fsdp", "tensor"),
            P("fsdp", "tensor"),
            P("tensor", "fsdp", None, None),
            P("tensor", "fsdp", None, None),
            P("tensor", "fsdp", None, None),
        ),
        check_vma=False,
    )
```

```python
import functools

import jax
import jax.numpy as jnp
from jax import lax
from jax.experimental import pallas as pl
from jax.experimental.pallas import tpu as pltpu
from jax.sharding import PartitionSpec as P

FF = 14336
BLK = 128
GROUP = 4
FIRST_SEND = 18
LEAN_SLOTS = 7
ROWS = BLK // 2
SMALL = 4 * 1024 * 1024
PART, STRIP, CIDX, CWAS, OIDX, OWAS = range(6)
FIELDS = 6
COLS_ROW = 3 * FIELDS
HEAD_ROW = COLS_ROW + 1
MINE_ROW = COLS_ROW + 2
LISTS_ROW = COLS_ROW + 3
HEAD_COLS, HEAD_OVER, HEAD_CORE, HEAD_LISTS = 3, 4, 5, 8


class Sizes:
    def __init__(self, tokens, gate_blocks, slots, n_fsdp, n_tensor, lean):
        self.tok, self.width = tokens.shape
        self.n_fsdp, self.n_tensor = n_fsdp, n_tensor
        self.rb = self.width // BLK
        self.cb = FF // (BLK * n_tensor)
        self.slots = slots
        self.all = 3 * slots
        self.lanes = -(-(self.all + GROUP) // 128) * 128
        self.nb = gate_blocks.shape[1]
        self.owned = 3 * self.nb
        self.ring = n_fsdp // 2
        self.top = self.ring // 2
        self.rbt = self.rb // n_tensor
        self.order = [self.top]
        for d in range(1, self.top):
            self.order += [self.top + d, self.top - d]
        self.order.append(0)
        self.far = min(2, self.ring - 1)
        self.keep = min(LEAN_SLOTS, 2 * self.owned) if lean else 2 * self.owned
        self.send_all = 2 * self.rbt
        self.first = min(FIRST_SEND, self.send_all) if lean else self.send_all
        self.blocks = self.ring * self.keep
        self.plan_rows = -(-(LISTS_ROW + 2 * n_tensor) // 8) * 8
        self.note_n, self.note_over = self.lanes - 1, self.lanes - 2
        self.room = slots + GROUP

    def place(self, d):
        return self.order.index(d) * self.keep

    def place_across(self, d):
        return self.place((self.ring - d) % self.ring)


def permutations(sz):
    seq = list(range(0, sz.ring, 2)) + list(range(sz.ring - 1, 0, -2))
    ahead, behind, swap = [], [], []
    for i, q in enumerate(seq):
        up, down = seq[(i + 1) % sz.ring], seq[i - 1]
        ahead += [(q * 2, up * 2), (q * 2 + 1, down * 2 + 1)]
        behind += [(q * 2, down * 2), (q * 2 + 1, up * 2 + 1)]
        swap += [(q * 2, q * 2 + 1), (q * 2 + 1, q * 2)]
    return ahead, behind, swap


def ratio(x, d):
    return jnp.floor((x + 0.5) * (1.0 / d))


def rest_of(x, d):
    return x - d * ratio(x, d)


def ring_position(sz, chip):
    return jnp.where(rest_of(chip, 2) == 0, ratio(chip, 2), sz.ring - 1 - ratio(chip, 2))


class Marks:
    def __init__(self, sz, own):
        N, L, S = sz.all, sz.lanes, sz.slots
        f32 = jnp.float32
        self.sz = sz
        self.sub = lax.broadcasted_iota(jnp.int32, (N, L), 0)
        self.lane = lax.broadcasted_iota(jnp.int32, (N, L), 1)
        self.same = self.sub == self.lane
        sub_c = self.sub[:, :1].astype(f32)
        lane_r = lax.broadcasted_iota(jnp.int32, (1, L), 1).astype(f32)
        self.sub_c, self.lane_r = sub_c, lane_r
        raw_r = own[...].astype(f32)

        def single(row, at):
            return jnp.sum(jnp.where(lane_r == at, row, 0.0), axis=1, keepdims=True)

        self.f, self.rank = single(raw_r, N + 3), single(raw_r, N + 4)

        def kind(x):
            return (x >= S).astype(f32) + (x >= 2 * S).astype(f32)

        self.kind_c, self.kind_r = kind(sub_c), kind(lane_r)
        self.n_r = lane_r - S * self.kind_r
        self.n_c = sub_c - S * self.kind_c
        limit = jnp.zeros((1, L), f32)
        for k in range(3):
            limit = limit + jnp.where(self.kind_r == k, single(raw_r, N + k), 0.0)
        live_r = jnp.where((lane_r < N) & (self.n_r < limit), 1.0, 0.0)
        w_c = self.col(raw_r)
        live_c = self.col(live_r)

        def place(w, k):
            gate, down = ratio(w, sz.cb), ratio(w, sz.rb)
            is_down = k == 2
            return jnp.where(is_down, w - down * sz.rb, gate), jnp.where(is_down, down, w - gate * sz.cb)

        self.row_c, col_c = place(w_c, self.kind_c)
        self.row_r, col_r = place(raw_r, self.kind_r)
        self.chip_c, chip_r = ratio(self.n_c, 2 * sz.nb), ratio(self.n_r, 2 * sz.nb)
        self.same_chip = (self.chip_c == chip_r).astype(f32)
        self.same_col = (col_c == col_r).astype(f32)
        act_c, act_r = live_c, live_r
        for k in range(3):
            lanes = self.same_col * (live_r * (self.kind_r == k).astype(f32))
            act_c = act_c * jnp.max(lanes, axis=1, keepdims=True)
            subs = self.same_col * (live_c * (self.kind_c == k).astype(f32))
            act_r = act_r * jnp.max(subs, axis=0, keepdims=True)
        self.act_c, self.act_r = act_c, act_r
        out_c = jnp.where(self.kind_c == 2, 0.0, f32(sz.rb)) + self.row_c
        out_r = jnp.where(self.kind_r == 2, 0.0, f32(sz.rb)) + self.row_r
        self.same_out = (out_c == out_r).astype(f32)
        self.before = (self.lane < self.sub).astype(f32)
        self.after = (self.sub < self.lane).astype(f32)
        self.owas_c = jnp.max(self.same_out * self.before * act_r, axis=1, keepdims=True)
        self.owas_r = jnp.max(self.same_out * self.after * act_c, axis=0, keepdims=True)
        self.lead_c = act_c * (1.0 - self.owas_c)
        self.lead_r = act_r * (1.0 - self.owas_r)

        def shift(row):
            away = ratio(row, sz.rbt) - self.rank
            return jnp.where(away < 0, away + sz.n_tensor, away)

        self.shift_c, self.shift_r = shift(self.row_c), shift(self.row_r)
        self.local_c = jnp.where(self.kind_c == 2, 0.0, f32(sz.rbt)) + rest_of(self.row_c, sz.rbt)

    def col(self, row):
        return jnp.sum(jnp.where(self.same, row, 0.0), axis=1, keepdims=True)

    def carried(self):
        sz = self.sz
        rank = jnp.sum(self.before * self.same_chip * self.act_r, axis=1, keepdims=True)
        away = ring_position(sz, self.chip_c) - ring_position(sz, ratio(self.f, 2))
        away = jnp.where(rest_of(self.f, 2) == 0, away, -away)
        rel = jnp.where(away < 0, away + sz.ring, away)
        j = jnp.where(rel > sz.top, 2 * (rel - sz.top) - 1, 2 * (sz.top - rel))
        return rank, jnp.where(rel == 0, sz.ring - 1.0, j)

    def ranks(self, chosen_r):
        return jnp.sum(self.before * chosen_r, axis=1, keepdims=True)

    def listed(self, chosen_c, rank_c, value_c, lo=0, hi=None):
        at = rank_c[lo:hi] == self.lane[lo:hi].astype(jnp.float32)
        return jnp.sum(jnp.where(at, chosen_c[lo:hi] * value_c[lo:hi], 0.0), axis=0, keepdims=True)

    def most_on_chip(self):
        return jnp.max(jnp.sum(self.same_chip * self.act_r, axis=1, keepdims=True), axis=0, keepdims=True)


def total(x):
    return jnp.sum(x, axis=0, keepdims=True)


def head_row(sz, entries):
    lane = lax.broadcasted_iota(jnp.int32, (1, sz.lanes), 1)
    row = jnp.zeros((1, sz.lanes), jnp.float32)
    for i, value in entries:
        row = jnp.where(lane == i, value, row)
    return row


def plan_kernel(sz, own, *refs):
    mine, theirs, (plan, chunk, *notes, sems) = refs[:3], refs[3:6], refs[6:]
    S, N = sz.slots, sz.all
    m = Marks(sz, own)
    f32 = jnp.float32
    lane_r, sub_c = m.lane_r, m.sub_c
    pos_c, base_c = m.carried()
    core = rest_of(m.f, 2)
    half = pl.ds(pl.multiple_of(jnp.max(core).astype(jnp.int32) * ROWS, ROWS), ROWS)

    pair = jnp.where(core == 0, m.f + 1, m.f - 1)
    i_r = rest_of(lane_r, sz.owned)
    owner_r = jnp.where(lane_r < sz.owned, m.f, pair)
    slot_r = ratio(i_r, sz.nb) * S + owner_r * sz.nb + rest_of(i_r, sz.nb)
    at_r = jnp.sum(jnp.where(sub_c == slot_r, m.act_c * (pos_c + 1.0), 0.0), axis=0, keepdims=True)
    copies = []
    for i in range(2 * sz.owned):
        side, k, a = i // sz.owned, i % sz.owned // sz.nb, i % sz.nb
        at = jnp.max(jnp.where(lane_r == i, at_r, 0.0)).astype(jnp.int32)
        fits = (at > 0) & (at <= sz.keep)
        place = jnp.minimum(jnp.maximum(at - 1, 0), sz.keep - 1)
        copy = pltpu.make_async_copy((mine, theirs)[side][k].at[0, a, half], chunk.at[place], sems.at[i])
        copies.append((fits, copy))
    for fits, copy in copies:
        pl.when(fits)(copy.start)

    same_kind = (m.kind_c == m.kind_r).astype(f32)
    rank_c = jnp.sum(m.before * same_kind * m.act_r, axis=1, keepdims=True)
    cwas_c = jnp.max(m.before * same_kind * m.same_col * m.act_r, axis=1, keepdims=True)
    cwas_r = jnp.max(m.after * same_kind * m.same_col * m.act_c, axis=0, keepdims=True)
    big = f32(4 * N)
    lanes_f = m.lane.astype(f32)
    gates_r = m.act_r * (m.kind_r == 0).astype(f32)
    cidx_c = jnp.min(jnp.where(m.same_col * gates_r > 0, lanes_f, big), axis=1, keepdims=True)
    oidx_c = jnp.min(jnp.where(m.same_out * m.act_r > 0, lanes_f, big), axis=1, keepdims=True)
    rank_r = jnp.sum(m.after * same_kind * m.act_c, axis=0, keepdims=True)
    turn_c = ratio(rank_c, GROUP) * 3 + m.kind_c
    turn_r = ratio(rank_r, GROUP) * 3 + m.kind_r
    ahead = ((turn_r < turn_c) | ((turn_r == turn_c) & (rank_r < rank_c))).astype(f32)
    owas_c = jnp.max(m.same_out * ahead * m.act_r, axis=1, keepdims=True)
    part_c = jnp.where(pos_c < sz.keep, base_c * sz.keep + pos_c, f32(sz.blocks))
    fields = [(part_c, sz.blocks), (m.row_c, 0), (cidx_c, S), (cwas_c, 0), (oidx_c, N), (owas_c, 0)]
    rows = []
    head = []
    for k in range(3):
        lo, hi = k * S, (k + 1) * S
        n_k = total(m.act_c[lo:hi])
        head.append((k, n_k))
        for value, spare in fields:
            row = m.listed(m.act_c, rank_c, value, lo, hi)
            rows.append(jnp.where(lane_r < n_k, row, f32(spare)))
    leader_c = m.act_c * (1.0 - cwas_c) * (m.kind_c == 0).astype(f32)
    leader_r = m.act_r * (1.0 - cwas_r) * (m.kind_r == 0).astype(f32)
    n_cols = total(leader_c)
    cols = m.listed(leader_c, m.ranks(leader_r), sub_c, 0, S)
    rows.append(jnp.where(lane_r < n_cols, cols, f32(S)))
    head.append((HEAD_COLS, n_cols))
    lists, sent = [], []
    over = (m.most_on_chip() > sz.keep).astype(f32)
    for s in range(sz.n_tensor):
        chosen_c = m.lead_c * (m.shift_c == s).astype(f32)
        chosen_r = m.lead_r * (m.shift_r == s).astype(f32)
        rank = m.ranks(chosen_r)
        lists.append(m.listed(chosen_c, rank, sub_c))
        lists.append(m.listed(chosen_c, rank, m.local_c))
        n = total(chosen_c)
        head.append((HEAD_LISTS + s, n))
        sent.append(n)
        over = jnp.maximum(over, (n > sz.first).astype(f32))
    head += [(HEAD_OVER, over), (HEAD_CORE, core)]
    for s in range(1, sz.n_tensor):
        note = jnp.where(lane_r == sz.note_n, sent[s], lists[2 * s + 1])
        notes[s - 1][...] = jnp.where(lane_r == sz.note_over, over, note).astype(jnp.int32)
    rows.append(head_row(sz, head))
    rows.append(at_r)
    rows += lists
    for i, row in enumerate(rows):
        plan[i:i + 1, :] = row.astype(jnp.int32)
    for fits, copy in copies:
        pl.when(fits)(copy.wait)


def dot(a, b, ca, cb):
    return lax.dot_general(a, b, (((ca,), (cb,)), ((), ())), preferred_element_type=jnp.float32)


def field(sz, plan, k, j, e):
    return plan[k * FIELDS + j, e]


def walk(plan, body):
    most = jnp.maximum(jnp.maximum(plan[HEAD_ROW, 0], plan[HEAD_ROW, 1]), plan[HEAD_ROW, 2])
    lax.fori_loop(0, (most + (GROUP - 1)) // GROUP, lambda p, _: body(p * GROUP), None)


def each(plan, k, body):
    lax.fori_loop(0, plan[HEAD_ROW, k], lambda e, _: body(e), None)


def compute_kernel(sz, plan, tokens, cot, *refs):
    n_chunks, T = 2 * sz.ring, sz.n_tensor
    chunks, refs = refs[:n_chunks], refs[n_chunks:]
    same, far, near = refs[:3]
    firsts, refs = refs[3:3 + T], refs[3 + T:]
    xs, wbuf, parts, gate_acc, up_acc, hg_acc, acts, out_acc, stage, strip_sems, sems = refs
    A = sz.slots + 1
    get = functools.partial(field, sz, plan)

    def strip_copy(k, e):
        src = cot if k == 2 else tokens
        cols = pl.ds(pl.multiple_of(get(k, STRIP, e) * BLK, BLK), BLK)
        return pltpu.make_async_copy(src.at[:, cols], xs.at[k * sz.room + e], strip_sems.at[k * sz.room + e])

    core = plan[HEAD_ROW, HEAD_CORE]
    sides = [pl.ds(pl.multiple_of(c * ROWS, ROWS), ROWS) for c in (core, 1 - core)]
    loads = []
    for side, place in enumerate((sz.place, sz.place_across)):
        for d in sz.order:
            i = len(loads)
            there = wbuf.at[pl.ds(place(d), sz.keep), sides[side]]
            loads.append(pltpu.make_async_copy(chunks[i], there, sems.at[i]))
    for k in range(3):
        each(plan, k, lambda e, k=k: strip_copy(k, e).start())
    for c in loads:
        c.start()
    for k in range(3):
        each(plan, k, lambda e, k=k: strip_copy(k, e).wait())
    for c in loads:
        c.wait()

    group = [(k, u) for k in range(3) for u in range(GROUP)]

    def forward(e0):
        for k, u in group:
            e, acc = e0 + u, (gate_acc, up_acc, hg_acc)[k]
            prod = dot(xs[k * sz.room + e], wbuf[get(k, PART, e)], 1, 1 if k == 2 else 0)
            c = get(k, CIDX, e)
            acc[c] = prod + jnp.where(get(k, CWAS, e) == 0, 0.0, acc[c])

    walk(plan, forward)

    def columns(i, _):
        for j in range(GROUP):
            c = plan[COLS_ROW, i * GROUP + j]
            g, u, h = gate_acc[c], up_acc[c], hg_acc[c]
            s = lax.logistic(g)
            silu = g * s
            acts[c] = (h * u * s * (1.0 + g * (1.0 - s))).astype(jnp.bfloat16)
            acts[A + c] = (h * silu).astype(jnp.bfloat16)
            acts[2 * A + c] = (silu * u).astype(jnp.bfloat16)

    lax.fori_loop(0, (plan[HEAD_ROW, HEAD_COLS] + (GROUP - 1)) // GROUP, columns, None)

    def gradients(e0):
        for k, u in group:
            e = e0 + u
            a, x = acts[k * A + get(k, CIDX, e)], xs[k * sz.room + e]
            grad = dot(a, x, 0, 0) if k == 2 else dot(x, a, 0, 0)
            parts[get(k, PART, e)] = grad.astype(jnp.bfloat16)

    walk(plan, gradients)
    outs = []
    for j, d in enumerate(sz.order):
        ref, at = (far, j) if j < sz.far else (near, j - sz.far)
        outs.append(pltpu.make_async_copy(
            parts.at[pl.ds(sz.place_across(d), sz.keep), sides[1]], ref.at[pl.ds(at * sz.keep, sz.keep)], sems.at[j]))
    outs.append(pltpu.make_async_copy(parts.at[pl.ds(0, sz.blocks), sides[0]], same, sems.at[sz.ring]))
    for c in outs:
        c.start()

    def terms(e0):
        for k, u in group:
            e = e0 + u
            prod = dot(acts[k * A + get(k, CIDX, e)], wbuf[get(k, PART, e)], 1, 0 if k == 2 else 1)
            at = get(k, OIDX, e)
            out_acc[at] = prod + jnp.where(get(k, OWAS, e) == 0, 0.0, out_acc[at])

    walk(plan, terms)

    for s in reversed(range(T)):
        def staged(i, _, s=s):
            stage[s * sz.first + i] = out_acc[plan[LISTS_ROW + 2 * s, i]].astype(jnp.bfloat16)

        lax.fori_loop(0, jnp.minimum(plan[HEAD_ROW, HEAD_LISTS + s], sz.first), staged, None)
        copy = pltpu.make_async_copy(stage.at[pl.ds(s * sz.first, sz.first)], firsts[s], sems.at[sz.ring + 1 + s])
        copy.start()
        outs.append(copy)
    for c in outs:
        c.wait()


def strip_of(sz, at):
    w = jnp.where(at < sz.rbt, at, at - sz.rbt)
    return at < sz.rbt, pl.ds(pl.multiple_of(w * BLK, BLK), BLK)


def prepare_kernel(sz, plan, note, first, outputs, input_grads, strips):
    outputs[...] = jnp.zeros_like(outputs)
    input_grads[...] = jnp.zeros_like(input_grads)

    def step(i, _):
        is_out, cols = strip_of(sz, plan[LISTS_ROW + 1, i])

        @pl.when(is_out)
        def _():
            outputs[:, cols] = first[i]

        @pl.when(jnp.logical_not(is_out))
        def _():
            input_grads[:, cols] = first[i]

    lax.fori_loop(0, jnp.minimum(plan[HEAD_ROW, HEAD_LISTS], sz.first), step, None)

    def pick(i, _):
        is_out, cols = strip_of(sz, note[0, i])

        @pl.when(is_out)
        def _():
            strips[i] = outputs[:, cols]

        @pl.when(jnp.logical_not(is_out))
        def _():
            strips[i] = input_grads[:, cols]

    lax.fori_loop(0, jnp.minimum(note[0, sz.note_n], sz.first), pick, None)


def last_kernel(sz, plan, *refs):
    T = sz.n_tensor
    notes, refs = refs[:T - 1], refs[T - 1:]
    firsts, refs = refs[:T - 1], refs[T - 1:]
    mine, theirs, held_strips, refs = refs[:3], refs[3:6], refs[6], refs[9:]
    outputs, input_grads, grads, flag = refs[0], refs[1], refs[2:5], refs[5]
    strips, read_sems, write_sems = refs[6:]
    over = plan[HEAD_ROW, HEAD_OVER]
    for note in notes:
        over = jnp.maximum(over, note[0, sz.note_over])
    flag[0] = over

    def move(s, i, back, act):
        is_out, cols = strip_of(sz, notes[s][0, i])
        for ref, here in ((outputs, is_out), (input_grads, jnp.logical_not(is_out))):
            @pl.when(here)
            def _(ref=ref):
                there = ref.at[:, cols]
                if back:
                    act(pltpu.make_async_copy(strips.at[i], there, write_sems.at[i]))
                else:
                    act(pltpu.make_async_copy(there, strips.at[i], read_sems.at[i]))

    def loop(s, body):
        lax.fori_loop(0, jnp.minimum(notes[s][0, sz.note_n], sz.first), lambda i, _: body(i), None)

    def begin(s):
        loop(s, lambda i: move(s, i, False, lambda c: c.start()))

    def add(s):
        def step(i):
            move(s, i, False, lambda c: c.wait())
            value = strips[i].astype(jnp.float32) + firsts[s][i].astype(jnp.float32)
            strips[i] = value.astype(jnp.bfloat16)
            move(s, i, True, lambda c: c.start())

        loop(s, step)

    def end(s):
        loop(s, lambda i: move(s, i, True, lambda c: c.wait()))

    def first_add(i):
        value = held_strips[i].astype(jnp.float32) + firsts[0][i].astype(jnp.float32)
        strips[i] = value.astype(jnp.bfloat16)
        move(0, i, True, lambda c: c.start())

    loop(0, first_add)
    core = plan[HEAD_ROW, HEAD_CORE]
    for k in range(3):
        for a in range(sz.nb):
            at = plan[MINE_ROW, k * sz.nb + a]
            p = jnp.minimum(jnp.maximum(at - 1, 0), sz.keep - 1)
            for terms, c in ((mine, core), (theirs, 1 - core)):
                value = sum(t[p].astype(jnp.float32) for t in terms)
                rows = pl.ds(pl.multiple_of(c * ROWS, ROWS), ROWS)
                grads[k][0, a, rows] = jnp.where(at > 0, value, 0.0).astype(jnp.bfloat16)
    end(0)
    for s in range(1, T - 1):
        begin(s)
        add(s)
        end(s)


def spec(space):
    return pl.BlockSpec(memory_space=space)


ANY, HBM, VMEM, SMEM = pl.ANY, pltpu.HBM, pltpu.VMEM, pltpu.SMEM


def cost(flops, moved):
    return pl.CostEstimate(flops=flops, bytes_accessed=moved, transcendentals=0)


def call_plan(sz, own, mine, theirs):
    return pl.pallas_call(
        functools.partial(plan_kernel, sz),
        out_shape=[
            jax.ShapeDtypeStruct((sz.plan_rows, sz.lanes), jnp.int32),
            halves(sz.keep),
        ] + [jax.ShapeDtypeStruct((1, sz.lanes), jnp.int32)] * (sz.n_tensor - 1),
        in_specs=[spec(VMEM)] + [spec(ANY)] * 6,
        out_specs=[spec(VMEM), spec(ANY)] + [spec(VMEM)] * (sz.n_tensor - 1),
        scratch_shapes=[pltpu.SemaphoreType.DMA((2 * sz.owned,))],
        compiler_params=pltpu.CompilerParams(vmem_limit_bytes=SMALL),
        cost_estimate=cost(1_000_000, 4_000_000),
        name="plan",
    )(own, *mine, *theirs)


def call_turn(handed, arrived):
    return pl.pallas_call(
        lambda *_: None,
        out_shape=[jax.ShapeDtypeStruct(x.shape, x.dtype) for x in handed],
        in_specs=[spec(ANY)] * (len(handed) + len(arrived)),
        out_specs=[spec(ANY)] * len(handed),
        input_output_aliases={i: i for i in range(len(handed))},
        compiler_params=pltpu.CompilerParams(vmem_limit_bytes=SMALL),
        cost_estimate=cost(1000, 1000),
        name="turn",
    )(*handed, *arrived)


def blocks(n):
    return jax.ShapeDtypeStruct((n, BLK, BLK), jnp.bfloat16)


def halves(n):
    return jax.ShapeDtypeStruct((n, ROWS, BLK), jnp.bfloat16)


def held(scratch):
    return sum(s[0] * s[1] * s[2] * jnp.dtype(t).itemsize for s, t in scratch) + 2 * 1024 * 1024


def call_compute(sz, plan, tokens, cot, chunks):
    bf, f32 = jnp.bfloat16, jnp.float32
    T, A = sz.n_tensor, sz.slots + 1
    out_shape = [halves(sz.ring * sz.keep), halves(sz.far * sz.keep), halves((sz.ring - sz.far) * sz.keep)]
    out_shape += [blocks(sz.first)] * T
    scratch = [
        ((3 * sz.room, sz.tok, BLK), bf),
        ((sz.blocks + 1, BLK, BLK), bf),
        ((sz.blocks + 1, BLK, BLK), bf),
        ((A, sz.tok, BLK), f32),
        ((A, sz.tok, BLK), f32),
        ((A, sz.tok, BLK), f32),
        ((3 * A, sz.tok, BLK), bf),
        ((sz.all + 1, sz.tok, BLK), f32),
        ((T * sz.first, sz.tok, BLK), bf),
    ]
    return pl.pallas_call(
        functools.partial(compute_kernel, sz),
        out_shape=out_shape,
        in_specs=[spec(SMEM)] + [spec(HBM)] * 2 + [spec(ANY)] * len(chunks),
        out_specs=[spec(ANY)] * len(out_shape),
        scratch_shapes=[pltpu.VMEM(s, t) for s, t in scratch] + [
            pltpu.SemaphoreType.DMA((3 * sz.room,)),
            pltpu.SemaphoreType.DMA((max(len(chunks), sz.ring + 1 + T),)),
        ],
        compiler_params=pltpu.CompilerParams(vmem_limit_bytes=held(scratch)),
        cost_estimate=cost(1_000_000_000, 20_000_000),
        name="compute",
    )(plan, pltpu.with_memory_space_constraint(tokens, HBM), pltpu.with_memory_space_constraint(cot, HBM), *chunks)


def call_prepare(sz, plan, note, first):
    half = jax.ShapeDtypeStruct((sz.tok, sz.width // sz.n_tensor), jnp.bfloat16)
    return pl.pallas_call(
        functools.partial(prepare_kernel, sz),
        out_shape=[half, half, blocks(sz.first)],
        in_specs=[spec(SMEM), spec(SMEM), spec(VMEM)],
        out_specs=[spec(VMEM)] * 3,
        compiler_params=pltpu.CompilerParams(vmem_limit_bytes=12 * 1024 * 1024),
        cost_estimate=cost(1_000_000, 6_000_000),
        name="prepare",
    )(plan, note, first)


def call_last(sz, plan, notes, firsts, terms, strips, partial):
    n = 2 + len(notes) + len(firsts) + len(terms)
    out = jax.ShapeDtypeStruct((1, sz.nb, BLK, BLK), jnp.bfloat16)
    return pl.pallas_call(
        functools.partial(last_kernel, sz),
        out_shape=[jax.ShapeDtypeStruct(p.shape, p.dtype) for p in partial] + [out] * 3 + [
            jax.ShapeDtypeStruct((1,), jnp.int32)],
        in_specs=[spec(SMEM)] * (1 + len(notes)) + [spec(VMEM)] * (len(firsts) + len(terms) + 1) + [spec(ANY)] * 2,
        out_specs=[spec(ANY)] * 2 + [spec(VMEM)] * 3 + [spec(SMEM)],
        input_output_aliases={n: 0, n + 1: 1},
        scratch_shapes=[
            pltpu.VMEM((sz.first, sz.tok, BLK), jnp.bfloat16),
            pltpu.SemaphoreType.DMA((sz.first,)),
            pltpu.SemaphoreType.DMA((sz.first,)),
        ],
        compiler_params=pltpu.CompilerParams(vmem_limit_bytes=12 * 1024 * 1024),
        cost_estimate=cost(1_000_000, 3_000_000),
        name="last",
    )(plan, *notes, *firsts, *terms, strips, *partial)


def across(pairs):
    return [(i, j ^ 1) for i, j in pairs]


def gather_chunks(sz, chunk):
    ahead, behind, swap = permutations(sz)
    same = {0: chunk}
    a = b = chunk
    for s in range(1, sz.top):
        a, b = lax.ppermute(a, "fsdp", ahead), lax.ppermute(b, "fsdp", behind)
        same[sz.ring - s], same[s] = a, b
    other = {d: lax.ppermute(same[d], "fsdp", swap) for d in same}
    same[sz.top] = lax.ppermute(a, "fsdp", ahead)
    other[sz.top] = lax.ppermute(a, "fsdp", across(ahead))
    return [side[d] for side in (same, other) for d in sz.order]


def reduce_parts(sz, same, far, near, notes, prepare):
    ahead, behind, swap = permutations(sz)
    keep = sz.keep
    far = lax.ppermute(far, "fsdp", swap)
    near = lax.ppermute(call_turn([near], [far])[0], "fsdp", swap)

    def term(d, *more):
        j = sz.order.index(d)
        pair = far[j * keep:(j + 1) * keep] if j < sz.far else near[(j - sz.far) * keep:][:keep]
        out = same[j * keep:(j + 1) * keep].astype(jnp.float32) + pair.astype(jnp.float32)
        for m in more:
            out = out + m.astype(jnp.float32)
        return out.astype(jnp.bfloat16)

    a, b = lax.optimization_barrier((term(sz.top), term(sz.top + 1)))
    here = term(0)
    here_across = lax.ppermute(here, "fsdp", swap)
    prepared = prepare(here_across)
    for s in range(1, sz.top):
        last_b = b
        a, b = lax.ppermute(a, "fsdp", ahead), lax.ppermute(b, "fsdp", behind)
        if s == 1:
            a, b = call_turn([a, b], notes)
        else:
            a = call_turn([a], [last_b] + (list(prepared[2:]) if s == 2 else []))[0]
        a = term(sz.top - s, a)
        if s + 1 < sz.top:
            b = term(sz.top + 1 + s, call_turn([b], [a])[0])
    mine = [here, lax.ppermute(a, "fsdp", ahead), b]
    theirs = [
        here_across,
        lax.ppermute(a, "fsdp", across(ahead)),
        lax.ppermute(last_b, "fsdp", across(behind)),
    ]
    return mine + theirs, prepared


def program(sz, own, tokens, cotangent, mine):
    T = sz.n_tensor
    swap = permutations(sz)[-1]
    theirs = [lax.ppermute(b, "fsdp", swap) for b in mine]
    plan, chunk, *notes = call_plan(sz, own, mine, theirs)

    def exchange(array, s):
        return lax.ppermute(array, "tensor", [(i, (i + s) % T) for i in range(T)])

    notes = [exchange(note, s) for s, note in enumerate(notes, 1)]
    chunks = gather_chunks(sz, chunk)
    same, far, near, *firsts = call_compute(sz, plan, tokens, cotangent, chunks)

    def prepare(after):
        return call_prepare(sz, plan, notes[0], call_turn([firsts[0]], [after])[0])

    sent = [exchange(firsts[s], s) for s in range(1, T)]
    terms, (*partial, strips) = reduce_parts(sz, same, far, near, notes, prepare)
    *outs, flag = call_last(sz, plan, notes, sent, terms, strips, partial)
    return tuple(outs), flag


def shards(
    tokens,
    cotangent,
    gate_blocks,
    up_blocks,
    down_blocks,
    gate_where,
    up_where,
    down_where,
    block_counts,
):
    n_fsdp, n_tensor = lax.axis_size("fsdp"), lax.axis_size("tensor")
    f, rank = lax.axis_index("fsdp"), lax.axis_index("tensor")
    slots = gate_where.shape[1]
    full = Sizes(tokens, gate_blocks, slots, n_fsdp, n_tensor, False)
    own = jnp.concatenate([
        gate_where[0], up_where[0], down_where[0], block_counts[:, 0],
        f.astype(jnp.int32)[None], rank.astype(jnp.int32)[None]])
    own = jnp.pad(own, (0, full.lanes - own.shape[0]))[None]
    blocks_in = (gate_blocks, up_blocks, down_blocks)
    if slots >= full.cb:
        return program(full, own, tokens, cotangent, blocks_in)[0]
    lean = Sizes(tokens, gate_blocks, slots, n_fsdp, n_tensor, True)
    outs, flag = program(lean, own, tokens, cotangent, blocks_in)
    return lax.cond(
        flag[0] > 0,
        lambda outs, *args: program(full, *args)[0],
        lambda outs, *args: outs,
        outs, own, tokens, cotangent, blocks_in)


def solution(mesh):
    placed = (
        P("fsdp", None),
        P("fsdp", None),
        P("tensor", "fsdp", None, None),
        P("tensor", "fsdp", None, None),
        P("tensor", "fsdp", None, None),
        P("tensor", None),
        P("tensor", None),
        P("tensor", None),
        P(None, "tensor"),
    )
    return jax.shard_map(
        shards,
        mesh=mesh,
        in_specs=placed,
        out_specs=(
            P("fsdp", "tensor"),
            P("fsdp", "tensor"),
            P("tensor", "fsdp", None, None),
            P("tensor", "fsdp", None, None),
            P("tensor", "fsdp", None, None),
        ),
        check_vma=False,
    )
```

```python
import functools

import jax
import jax.numpy as jnp
from jax import lax
from jax.experimental import pallas as pl
from jax.experimental.pallas import tpu as pltpu
from jax.sharding import PartitionSpec as P

FF = 14336
BLK = 128
GROUP = 4
FIRST_SEND = 18
LEAN_SLOTS = 7
ROWS = BLK // 2
PIECE = 3
SMALL = 4 * 1024 * 1024
PART, STRIP, CIDX, CWAS, OIDX, OWAS = range(6)
FIELDS = 6
COLS_ROW = 3 * FIELDS
HEAD_ROW = COLS_ROW + 1
MINE_ROW = COLS_ROW + 2
LISTS_ROW = COLS_ROW + 3
HEAD_COLS, HEAD_OVER, HEAD_CORE, HEAD_LISTS = 3, 4, 5, 8


class Sizes:
    def __init__(self, tokens, gate_blocks, slots, n_fsdp, n_tensor, lean):
        self.tok, self.width = tokens.shape
        self.n_fsdp, self.n_tensor = n_fsdp, n_tensor
        self.rb = self.width // BLK
        self.cb = FF // (BLK * n_tensor)
        self.slots = slots
        self.all = 3 * slots
        self.lanes = -(-(self.all + GROUP) // 128) * 128
        self.nb = gate_blocks.shape[1]
        self.owned = 3 * self.nb
        self.ring = n_fsdp // 2
        self.top = self.ring // 2
        self.rbt = self.rb // n_tensor
        self.order = [self.top]
        for d in range(1, self.top):
            self.order += [self.top + d, self.top - d]
        self.order.append(0)
        self.far = min(2, self.ring - 1)
        self.keep = min(LEAN_SLOTS, 2 * self.owned) if lean else 2 * self.owned
        self.send_all = 2 * self.rbt
        self.first = min(FIRST_SEND, self.send_all) if lean else self.send_all
        self.blocks = self.ring * self.keep
        self.plan_rows = -(-(LISTS_ROW + 2 * n_tensor) // 8) * 8
        self.note_n, self.note_over = self.lanes - 1, self.lanes - 2
        self.room = slots + GROUP

    def place(self, d):
        return self.order.index(d) * self.keep

    def place_across(self, d):
        return self.place((self.ring - d) % self.ring)


def permutations(sz):
    seq = list(range(0, sz.ring, 2)) + list(range(sz.ring - 1, 0, -2))
    ahead, behind, swap = [], [], []
    for i, q in enumerate(seq):
        up, down = seq[(i + 1) % sz.ring], seq[i - 1]
        ahead += [(q * 2, up * 2), (q * 2 + 1, down * 2 + 1)]
        behind += [(q * 2, down * 2), (q * 2 + 1, up * 2 + 1)]
        swap += [(q * 2, q * 2 + 1), (q * 2 + 1, q * 2)]
    return ahead, behind, swap


def ratio(x, d):
    return jnp.floor((x + 0.5) * (1.0 / d))


def rest_of(x, d):
    return x - d * ratio(x, d)


def ring_position(sz, chip):
    return jnp.where(rest_of(chip, 2) == 0, ratio(chip, 2), sz.ring - 1 - ratio(chip, 2))


class Marks:
    def __init__(self, sz, own):
        N, L, S = sz.all, sz.lanes, sz.slots
        f32 = jnp.float32
        self.sz = sz
        self.sub = lax.broadcasted_iota(jnp.int32, (N, L), 0)
        self.lane = lax.broadcasted_iota(jnp.int32, (N, L), 1)
        self.same = self.sub == self.lane
        sub_c = self.sub[:, :1].astype(f32)
        lane_r = lax.broadcasted_iota(jnp.int32, (1, L), 1).astype(f32)
        self.sub_c, self.lane_r = sub_c, lane_r
        raw_r = own[...].astype(f32)

        def single(row, at):
            return jnp.sum(jnp.where(lane_r == at, row, 0.0), axis=1, keepdims=True)

        self.f, self.rank = single(raw_r, N + 3), single(raw_r, N + 4)

        def kind(x):
            return (x >= S).astype(f32) + (x >= 2 * S).astype(f32)

        self.kind_c, self.kind_r = kind(sub_c), kind(lane_r)
        self.n_r = lane_r - S * self.kind_r
        self.n_c = sub_c - S * self.kind_c
        limit = jnp.zeros((1, L), f32)
        for k in range(3):
            limit = limit + jnp.where(self.kind_r == k, single(raw_r, N + k), 0.0)
        live_r = jnp.where((lane_r < N) & (self.n_r < limit), 1.0, 0.0)
        w_c = self.col(raw_r)
        live_c = self.col(live_r)

        def place(w, k):
            gate, down = ratio(w, sz.cb), ratio(w, sz.rb)
            is_down = k == 2
            return jnp.where(is_down, w - down * sz.rb, gate), jnp.where(is_down, down, w - gate * sz.cb)

        self.row_c, col_c = place(w_c, self.kind_c)
        self.row_r, col_r = place(raw_r, self.kind_r)
        self.chip_c, chip_r = ratio(self.n_c, 2 * sz.nb), ratio(self.n_r, 2 * sz.nb)
        self.same_chip = (self.chip_c == chip_r).astype(f32)
        self.same_col = (col_c == col_r).astype(f32)
        act_c, act_r = live_c, live_r
        for k in range(3):
            lanes = self.same_col * (live_r * (self.kind_r == k).astype(f32))
            act_c = act_c * jnp.max(lanes, axis=1, keepdims=True)
            subs = self.same_col * (live_c * (self.kind_c == k).astype(f32))
            act_r = act_r * jnp.max(subs, axis=0, keepdims=True)
        self.act_c, self.act_r = act_c, act_r
        out_c = jnp.where(self.kind_c == 2, 0.0, f32(sz.rb)) + self.row_c
        out_r = jnp.where(self.kind_r == 2, 0.0, f32(sz.rb)) + self.row_r
        self.same_out = (out_c == out_r).astype(f32)
        self.before = (self.lane < self.sub).astype(f32)
        self.after = (self.sub < self.lane).astype(f32)
        self.owas_c = jnp.max(self.same_out * self.before * act_r, axis=1, keepdims=True)
        self.owas_r = jnp.max(self.same_out * self.after * act_c, axis=0, keepdims=True)
        self.lead_c = act_c * (1.0 - self.owas_c)
        self.lead_r = act_r * (1.0 - self.owas_r)

        def shift(row):
            away = ratio(row, sz.rbt) - self.rank
            return jnp.where(away < 0, away + sz.n_tensor, away)

        self.shift_c, self.shift_r = shift(self.row_c), shift(self.row_r)
        self.local_c = jnp.where(self.kind_c == 2, 0.0, f32(sz.rbt)) + rest_of(self.row_c, sz.rbt)

    def col(self, row):
        return jnp.sum(jnp.where(self.same, row, 0.0), axis=1, keepdims=True)

    def carried(self):
        sz = self.sz
        rank = jnp.sum(self.before * self.same_chip * self.act_r, axis=1, keepdims=True)
        away = ring_position(sz, self.chip_c) - ring_position(sz, ratio(self.f, 2))
        away = jnp.where(rest_of(self.f, 2) == 0, away, -away)
        rel = jnp.where(away < 0, away + sz.ring, away)
        j = jnp.where(rel > sz.top, 2 * (rel - sz.top) - 1, 2 * (sz.top - rel))
        return rank, jnp.where(rel == 0, sz.ring - 1.0, j)

    def ranks(self, chosen_r):
        return jnp.sum(self.before * chosen_r, axis=1, keepdims=True)

    def listed(self, chosen_c, rank_c, value_c, lo=0, hi=None):
        at = rank_c[lo:hi] == self.lane[lo:hi].astype(jnp.float32)
        return jnp.sum(jnp.where(at, chosen_c[lo:hi] * value_c[lo:hi], 0.0), axis=0, keepdims=True)

    def most_on_chip(self):
        return jnp.max(jnp.sum(self.same_chip * self.act_r, axis=1, keepdims=True), axis=0, keepdims=True)


def total(x):
    return jnp.sum(x, axis=0, keepdims=True)


def head_row(sz, entries):
    lane = lax.broadcasted_iota(jnp.int32, (1, sz.lanes), 1)
    row = jnp.zeros((1, sz.lanes), jnp.float32)
    for i, value in entries:
        row = jnp.where(lane == i, value, row)
    return row


def plan_kernel(sz, own, *refs):
    mine, theirs, (plan, chunk, *notes, sems) = refs[:3], refs[3:6], refs[6:]
    S, N = sz.slots, sz.all
    m = Marks(sz, own)
    f32 = jnp.float32
    lane_r, sub_c = m.lane_r, m.sub_c
    pos_c, base_c = m.carried()
    core = rest_of(m.f, 2)
    half = pl.ds(pl.multiple_of(jnp.max(core).astype(jnp.int32) * ROWS, ROWS), ROWS)

    pair = jnp.where(core == 0, m.f + 1, m.f - 1)
    i_r = rest_of(lane_r, sz.owned)
    owner_r = jnp.where(lane_r < sz.owned, m.f, pair)
    slot_r = ratio(i_r, sz.nb) * S + owner_r * sz.nb + rest_of(i_r, sz.nb)
    at_r = jnp.sum(jnp.where(sub_c == slot_r, m.act_c * (pos_c + 1.0), 0.0), axis=0, keepdims=True)
    copies = []
    for i in range(2 * sz.owned):
        side, k, a = i // sz.owned, i % sz.owned // sz.nb, i % sz.nb
        at = jnp.max(jnp.where(lane_r == i, at_r, 0.0)).astype(jnp.int32)
        fits = (at > 0) & (at <= sz.keep)
        place = jnp.minimum(jnp.maximum(at - 1, 0), sz.keep - 1)
        copy = pltpu.make_async_copy((mine, theirs)[side][k].at[0, a, half], chunk.at[place], sems.at[i])
        copies.append((fits, copy))
    for fits, copy in copies:
        pl.when(fits)(copy.start)

    same_kind = (m.kind_c == m.kind_r).astype(f32)
    rank_c = jnp.sum(m.before * same_kind * m.act_r, axis=1, keepdims=True)
    cwas_c = jnp.max(m.before * same_kind * m.same_col * m.act_r, axis=1, keepdims=True)
    cwas_r = jnp.max(m.after * same_kind * m.same_col * m.act_c, axis=0, keepdims=True)
    big = f32(4 * N)
    lanes_f = m.lane.astype(f32)
    gates_r = m.act_r * (m.kind_r == 0).astype(f32)
    cidx_c = jnp.min(jnp.where(m.same_col * gates_r > 0, lanes_f, big), axis=1, keepdims=True)
    oidx_c = jnp.min(jnp.where(m.same_out * m.act_r > 0, lanes_f, big), axis=1, keepdims=True)
    rank_r = jnp.sum(m.after * same_kind * m.act_c, axis=0, keepdims=True)
    turn_c = ratio(rank_c, GROUP) * 3 + m.kind_c
    turn_r = ratio(rank_r, GROUP) * 3 + m.kind_r
    ahead = ((turn_r < turn_c) | ((turn_r == turn_c) & (rank_r < rank_c))).astype(f32)
    owas_c = jnp.max(m.same_out * ahead * m.act_r, axis=1, keepdims=True)
    part_c = jnp.where(pos_c < sz.keep, base_c * sz.keep + pos_c, f32(sz.blocks))
    fields = [(part_c, sz.blocks), (m.row_c, 0), (cidx_c, S), (cwas_c, 0), (oidx_c, N), (owas_c, 0)]
    rows = []
    head = []
    for k in range(3):
        lo, hi = k * S, (k + 1) * S
        n_k = total(m.act_c[lo:hi])
        head.append((k, n_k))
        for value, spare in fields:
            row = m.listed(m.act_c, rank_c, value, lo, hi)
            rows.append(jnp.where(lane_r < n_k, row, f32(spare)))
    leader_c = m.act_c * (1.0 - cwas_c) * (m.kind_c == 0).astype(f32)
    leader_r = m.act_r * (1.0 - cwas_r) * (m.kind_r == 0).astype(f32)
    n_cols = total(leader_c)
    cols = m.listed(leader_c, m.ranks(leader_r), sub_c, 0, S)
    rows.append(jnp.where(lane_r < n_cols, cols, f32(S)))
    head.append((HEAD_COLS, n_cols))
    lists, sent = [], []
    over = (m.most_on_chip() > sz.keep).astype(f32)
    for s in range(sz.n_tensor):
        chosen_c = m.lead_c * (m.shift_c == s).astype(f32)
        chosen_r = m.lead_r * (m.shift_r == s).astype(f32)
        rank = m.ranks(chosen_r)
        lists.append(m.listed(chosen_c, rank, sub_c))
        lists.append(m.listed(chosen_c, rank, m.local_c))
        n = total(chosen_c)
        head.append((HEAD_LISTS + s, n))
        sent.append(n)
        over = jnp.maximum(over, (n > sz.first).astype(f32))
    head += [(HEAD_OVER, over), (HEAD_CORE, core)]
    for s in range(1, sz.n_tensor):
        note = jnp.where(lane_r == sz.note_n, sent[s], lists[2 * s + 1])
        notes[s - 1][...] = jnp.where(lane_r == sz.note_over, over, note).astype(jnp.int32)
    rows.append(head_row(sz, head))
    rows.append(at_r)
    rows += lists
    for i, row in enumerate(rows):
        plan[i:i + 1, :] = row.astype(jnp.int32)
    for fits, copy in copies:
        pl.when(fits)(copy.wait)


def dot(a, b, ca, cb):
    return lax.dot_general(a, b, (((ca,), (cb,)), ((), ())), preferred_element_type=jnp.float32)


def field(sz, plan, k, j, e):
    return plan[k * FIELDS + j, e]


def walk(plan, body):
    most = jnp.maximum(jnp.maximum(plan[HEAD_ROW, 0], plan[HEAD_ROW, 1]), plan[HEAD_ROW, 2])
    lax.fori_loop(0, (most + (GROUP - 1)) // GROUP, lambda p, _: body(p * GROUP), None)


def each(plan, k, body):
    lax.fori_loop(0, plan[HEAD_ROW, k], lambda e, _: body(e), None)


def compute_kernel(sz, plan, tokens, cot, *refs):
    n_chunks, T = 2 * sz.ring, sz.n_tensor
    chunks, refs = refs[:n_chunks], refs[n_chunks:]
    same, far, near = refs[:3]
    firsts, refs = refs[3:3 + T], refs[3 + T:]
    xs, wbuf, parts, gate_acc, up_acc, hg_acc, acts, out_acc, stage, strip_sems, sems = refs
    A = sz.slots + 1
    get = functools.partial(field, sz, plan)

    def strip_copy(k, e):
        src = cot if k == 2 else tokens
        cols = pl.ds(pl.multiple_of(get(k, STRIP, e) * BLK, BLK), BLK)
        return pltpu.make_async_copy(src.at[:, cols], xs.at[k * sz.room + e], strip_sems.at[k * sz.room + e])

    core = plan[HEAD_ROW, HEAD_CORE]
    sides = [pl.ds(pl.multiple_of(c * ROWS, ROWS), ROWS) for c in (core, 1 - core)]
    loads = []
    for side, place in enumerate((sz.place, sz.place_across)):
        for d in sz.order:
            i = len(loads)
            there = wbuf.at[pl.ds(place(d), sz.keep), sides[side]]
            loads.append(pltpu.make_async_copy(chunks[i], there, sems.at[i]))
    for k in range(3):
        each(plan, k, lambda e, k=k: strip_copy(k, e).start())
    for c in loads:
        c.start()
    for k in range(3):
        each(plan, k, lambda e, k=k: strip_copy(k, e).wait())
    for c in loads:
        c.wait()

    group = [(k, u) for k in range(3) for u in range(GROUP)]

    def forward(e0):
        for k, u in group:
            e, acc = e0 + u, (gate_acc, up_acc, hg_acc)[k]
            prod = dot(xs[k * sz.room + e], wbuf[get(k, PART, e)], 1, 1 if k == 2 else 0)
            c = get(k, CIDX, e)
            acc[c] = prod + jnp.where(get(k, CWAS, e) == 0, 0.0, acc[c])

    walk(plan, forward)

    def columns(i, _):
        for j in range(GROUP):
            c = plan[COLS_ROW, i * GROUP + j]
            g, u, h = gate_acc[c], up_acc[c], hg_acc[c]
            s = lax.logistic(g)
            silu = g * s
            acts[c] = (h * u * s * (1.0 + g * (1.0 - s))).astype(jnp.bfloat16)
            acts[A + c] = (h * silu).astype(jnp.bfloat16)
            acts[2 * A + c] = (silu * u).astype(jnp.bfloat16)

    lax.fori_loop(0, (plan[HEAD_ROW, HEAD_COLS] + (GROUP - 1)) // GROUP, columns, None)

    def gradients(e0):
        for k, u in group:
            e = e0 + u
            a, x = acts[k * A + get(k, CIDX, e)], xs[k * sz.room + e]
            grad = dot(a, x, 0, 0) if k == 2 else dot(x, a, 0, 0)
            parts[get(k, PART, e)] = grad.astype(jnp.bfloat16)

    walk(plan, gradients)
    outs = []
    for j, d in enumerate(sz.order):
        ref, at = (far, j) if j < sz.far else (near, j - sz.far)
        outs.append(pltpu.make_async_copy(
            parts.at[pl.ds(sz.place_across(d), sz.keep), sides[1]], ref.at[pl.ds(at * sz.keep, sz.keep)], sems.at[j]))
        mine = pl.ds(j * sz.keep, sz.keep)
        outs.append(pltpu.make_async_copy(parts.at[mine, sides[0]], same.at[mine], sems.at[sz.ring + j]))
    for c in outs:
        c.start()

    def terms(e0):
        for k, u in group:
            e = e0 + u
            prod = dot(acts[k * A + get(k, CIDX, e)], wbuf[get(k, PART, e)], 1, 0 if k == 2 else 1)
            at = get(k, OIDX, e)
            out_acc[at] = prod + jnp.where(get(k, OWAS, e) == 0, 0.0, out_acc[at])

    walk(plan, terms)

    for s in reversed(range(T)):
        def staged(i, _, s=s):
            stage[s * sz.first + i] = out_acc[plan[LISTS_ROW + 2 * s, i]].astype(jnp.bfloat16)

        lax.fori_loop(0, jnp.minimum(plan[HEAD_ROW, HEAD_LISTS + s], sz.first), staged, None)
        for lo in range(0, sz.first, PIECE):
            n = min(PIECE, sz.first - lo)
            piece = stage.at[pl.ds(s * sz.first + lo, n)]
            copy = pltpu.make_async_copy(piece, firsts[s].at[pl.ds(lo, n)], sems.at[len(outs)])
            copy.start()
            outs.append(copy)
    for c in outs:
        c.wait()


def strip_of(sz, at):
    w = jnp.where(at < sz.rbt, at, at - sz.rbt)
    return at < sz.rbt, pl.ds(pl.multiple_of(w * BLK, BLK), BLK)


def prepare_kernel(sz, plan, note, first, outputs, input_grads, strips):
    outputs[...] = jnp.zeros_like(outputs)
    input_grads[...] = jnp.zeros_like(input_grads)

    def step(i, _):
        is_out, cols = strip_of(sz, plan[LISTS_ROW + 1, i])

        @pl.when(is_out)
        def _():
            outputs[:, cols] = first[i]

        @pl.when(jnp.logical_not(is_out))
        def _():
            input_grads[:, cols] = first[i]

    lax.fori_loop(0, jnp.minimum(plan[HEAD_ROW, HEAD_LISTS], sz.first), step, None)

    def pick(i, _):
        is_out, cols = strip_of(sz, note[0, i])

        @pl.when(is_out)
        def _():
            strips[i] = outputs[:, cols]

        @pl.when(jnp.logical_not(is_out))
        def _():
            strips[i] = input_grads[:, cols]

    lax.fori_loop(0, jnp.minimum(note[0, sz.note_n], sz.first), pick, None)


def last_kernel(sz, plan, *refs):
    T = sz.n_tensor
    notes, refs = refs[:T - 1], refs[T - 1:]
    firsts, refs = refs[:T - 1], refs[T - 1:]
    mine, theirs, held_strips, refs = refs[:3], refs[3:6], refs[6], refs[9:]
    outputs, input_grads, grads, flag = refs[0], refs[1], refs[2:5], refs[5]
    strips, arrived, read_sems, write_sems, arrive_sems = refs[6:]
    over = plan[HEAD_ROW, HEAD_OVER]
    for note in notes:
        over = jnp.maximum(over, note[0, sz.note_over])
    flag[0] = over

    def move(s, i, back, act):
        is_out, cols = strip_of(sz, notes[s][0, i])
        for ref, here in ((outputs, is_out), (input_grads, jnp.logical_not(is_out))):
            @pl.when(here)
            def _(ref=ref):
                there = ref.at[:, cols]
                if back:
                    act(pltpu.make_async_copy(strips.at[i], there, write_sems.at[i]))
                else:
                    act(pltpu.make_async_copy(there, strips.at[i], read_sems.at[i]))

    def loop(s, body):
        lax.fori_loop(0, jnp.minimum(notes[s][0, sz.note_n], sz.first), lambda i, _: body(i), None)

    def fetch(s, i, act):
        act(pltpu.make_async_copy(firsts[s].at[i], arrived.at[i], arrive_sems.at[i]))
        if s:
            move(s, i, False, act)
        else:
            act(pltpu.make_async_copy(held_strips.at[i], strips.at[i], read_sems.at[i]))

    def begin(s):
        loop(s, lambda i: fetch(s, i, lambda c: c.start()))

    def add(s):
        def step(i):
            fetch(s, i, lambda c: c.wait())
            value = strips[i].astype(jnp.float32) + arrived[i].astype(jnp.float32)
            strips[i] = value.astype(jnp.bfloat16)
            move(s, i, True, lambda c: c.start())

        loop(s, step)

    def end(s):
        loop(s, lambda i: move(s, i, True, lambda c: c.wait()))

    begin(0)
    core = plan[HEAD_ROW, HEAD_CORE]
    for k in range(3):
        for a in range(sz.nb):
            at = plan[MINE_ROW, k * sz.nb + a]
            p = jnp.minimum(jnp.maximum(at - 1, 0), sz.keep - 1)
            for terms, c in ((mine, core), (theirs, 1 - core)):
                value = sum(t[p].astype(jnp.float32) for t in terms)
                rows = pl.ds(pl.multiple_of(c * ROWS, ROWS), ROWS)
                grads[k][0, a, rows] = jnp.where(at > 0, value, 0.0).astype(jnp.bfloat16)
    add(0)
    end(0)
    for s in range(1, T - 1):
        begin(s)
        add(s)
        end(s)


def spec(space):
    return pl.BlockSpec(memory_space=space)


ANY, HBM, VMEM, SMEM = pl.ANY, pltpu.HBM, pltpu.VMEM, pltpu.SMEM


def cost(flops, moved):
    return pl.CostEstimate(flops=flops, bytes_accessed=moved, transcendentals=0)


def call_plan(sz, own, mine, theirs):
    return pl.pallas_call(
        functools.partial(plan_kernel, sz),
        out_shape=[
            jax.ShapeDtypeStruct((sz.plan_rows, sz.lanes), jnp.int32),
            halves(sz.keep),
        ] + [jax.ShapeDtypeStruct((1, sz.lanes), jnp.int32)] * (sz.n_tensor - 1),
        in_specs=[spec(VMEM)] + [spec(ANY)] * 6,
        out_specs=[spec(VMEM), spec(ANY)] + [spec(VMEM)] * (sz.n_tensor - 1),
        scratch_shapes=[pltpu.SemaphoreType.DMA((2 * sz.owned,))],
        compiler_params=pltpu.CompilerParams(vmem_limit_bytes=SMALL),
        cost_estimate=cost(1_000_000, 4_000_000),
        name="plan",
    )(own, *mine, *theirs)


def call_turn(handed, arrived):
    return pl.pallas_call(
        lambda *_: None,
        out_shape=[jax.ShapeDtypeStruct(x.shape, x.dtype) for x in handed],
        in_specs=[spec(ANY)] * (len(handed) + len(arrived)),
        out_specs=[spec(ANY)] * len(handed),
        input_output_aliases={i: i for i in range(len(handed))},
        compiler_params=pltpu.CompilerParams(vmem_limit_bytes=SMALL),
        cost_estimate=cost(1000, 1000),
        name="turn",
    )(*handed, *arrived)


def blocks(n):
    return jax.ShapeDtypeStruct((n, BLK, BLK), jnp.bfloat16)


def halves(n):
    return jax.ShapeDtypeStruct((n, ROWS, BLK), jnp.bfloat16)


def held(scratch):
    return sum(s[0] * s[1] * s[2] * jnp.dtype(t).itemsize for s, t in scratch) + 2 * 1024 * 1024


def call_compute(sz, plan, tokens, cot, chunks):
    bf, f32 = jnp.bfloat16, jnp.float32
    T, A = sz.n_tensor, sz.slots + 1
    out_shape = [halves(sz.ring * sz.keep), halves(sz.far * sz.keep), halves((sz.ring - sz.far) * sz.keep)]
    out_shape += [blocks(sz.first)] * T
    scratch = [
        ((3 * sz.room, sz.tok, BLK), bf),
        ((sz.blocks + 1, BLK, BLK), bf),
        ((sz.blocks + 1, BLK, BLK), bf),
        ((A, sz.tok, BLK), f32),
        ((A, sz.tok, BLK), f32),
        ((A, sz.tok, BLK), f32),
        ((3 * A, sz.tok, BLK), bf),
        ((sz.all + 1, sz.tok, BLK), f32),
        ((T * sz.first, sz.tok, BLK), bf),
    ]
    return pl.pallas_call(
        functools.partial(compute_kernel, sz),
        out_shape=out_shape,
        in_specs=[spec(SMEM)] + [spec(HBM)] * 2 + [spec(ANY)] * len(chunks),
        out_specs=[spec(ANY)] * len(out_shape),
        scratch_shapes=[pltpu.VMEM(s, t) for s, t in scratch] + [
            pltpu.SemaphoreType.DMA((3 * sz.room,)),
            pltpu.SemaphoreType.DMA((2 * sz.ring + T * -(-sz.first // PIECE),)),
        ],
        compiler_params=pltpu.CompilerParams(vmem_limit_bytes=held(scratch)),
        cost_estimate=cost(1_000_000_000, 20_000_000),
        name="compute",
    )(plan, pltpu.with_memory_space_constraint(tokens, HBM), pltpu.with_memory_space_constraint(cot, HBM), *chunks)


def call_prepare(sz, plan, note, first):
    half = jax.ShapeDtypeStruct((sz.tok, sz.width // sz.n_tensor), jnp.bfloat16)
    return pl.pallas_call(
        functools.partial(prepare_kernel, sz),
        out_shape=[half, half, blocks(sz.first)],
        in_specs=[spec(SMEM), spec(SMEM), spec(VMEM)],
        out_specs=[spec(VMEM)] * 3,
        compiler_params=pltpu.CompilerParams(vmem_limit_bytes=12 * 1024 * 1024),
        cost_estimate=cost(1_000_000, 6_000_000),
        name="prepare",
    )(plan, note, first)


def call_last(sz, plan, notes, firsts, terms, strips, partial):
    n = 2 + len(notes) + len(firsts) + len(terms)
    out = jax.ShapeDtypeStruct((1, sz.nb, BLK, BLK), jnp.bfloat16)
    return pl.pallas_call(
        functools.partial(last_kernel, sz),
        out_shape=[jax.ShapeDtypeStruct(p.shape, p.dtype) for p in partial] + [out] * 3 + [
            jax.ShapeDtypeStruct((1,), jnp.int32)],
        in_specs=[spec(SMEM)] * (1 + len(notes)) + [spec(ANY)] * len(firsts) + [spec(VMEM)] * len(terms) + [spec(ANY)] * 3,
        out_specs=[spec(ANY)] * 2 + [spec(VMEM)] * 3 + [spec(SMEM)],
        input_output_aliases={n: 0, n + 1: 1},
        scratch_shapes=[
            pltpu.VMEM((sz.first, sz.tok, BLK), jnp.bfloat16),
            pltpu.VMEM((sz.first, sz.tok, BLK), jnp.bfloat16),
            pltpu.SemaphoreType.DMA((sz.first,)),
            pltpu.SemaphoreType.DMA((sz.first,)),
            pltpu.SemaphoreType.DMA((sz.first,)),
        ],
        compiler_params=pltpu.CompilerParams(vmem_limit_bytes=12 * 1024 * 1024),
        cost_estimate=cost(1_000_000, 3_000_000),
        name="last",
    )(plan, *notes, *firsts, *terms, strips, *partial)


def across(pairs):
    return [(i, j ^ 1) for i, j in pairs]


def gather_chunks(sz, chunk):
    ahead, behind, swap = permutations(sz)
    same = {0: chunk}
    a = b = chunk
    for s in range(1, sz.top):
        a, b = lax.ppermute(a, "fsdp", ahead), lax.ppermute(b, "fsdp", behind)
        same[sz.ring - s], same[s] = a, b
    other = {d: lax.ppermute(same[d], "fsdp", swap) for d in same}
    same[sz.top] = lax.ppermute(a, "fsdp", ahead)
    other[sz.top] = lax.ppermute(a, "fsdp", across(ahead))
    return [side[d] for side in (same, other) for d in sz.order]


def reduce_parts(sz, same, far, near, notes, prepare):
    ahead, behind, swap = permutations(sz)
    keep = sz.keep
    far = lax.ppermute(far, "fsdp", swap)
    near = lax.ppermute(call_turn([near], [far])[0], "fsdp", swap)

    def term(d, *more):
        j = sz.order.index(d)
        pair = far[j * keep:(j + 1) * keep] if j < sz.far else near[(j - sz.far) * keep:][:keep]
        out = same[j * keep:(j + 1) * keep].astype(jnp.float32) + pair.astype(jnp.float32)
        for m in more:
            out = out + m.astype(jnp.float32)
        return out.astype(jnp.bfloat16)

    a, b = lax.optimization_barrier((term(sz.top), term(sz.top + 1)))
    here = term(0)
    here_across = lax.ppermute(here, "fsdp", swap)
    prepared = prepare(here_across)
    for s in range(1, sz.top):
        last_b = b
        a, b = lax.ppermute(a, "fsdp", ahead), lax.ppermute(b, "fsdp", behind)
        if s == 1:
            a, b = call_turn([a, b], notes)
        else:
            a = call_turn([a], [last_b] + (list(prepared[2:]) if s == 2 else []))[0]
        a = term(sz.top - s, a)
        if s + 1 < sz.top:
            b = term(sz.top + 1 + s, call_turn([b], [a])[0])
    mine = [here, lax.ppermute(a, "fsdp", ahead), b]
    theirs = [
        here_across,
        lax.ppermute(a, "fsdp", across(ahead)),
        lax.ppermute(last_b, "fsdp", across(behind)),
    ]
    return mine + theirs, prepared


def program(sz, own, tokens, cotangent, mine):
    T = sz.n_tensor
    swap = permutations(sz)[-1]
    theirs = [lax.ppermute(b, "fsdp", swap) for b in mine]
    plan, chunk, *notes = call_plan(sz, own, mine, theirs)

    def exchange(array, s):
        return lax.ppermute(array, "tensor", [(i, (i + s) % T) for i in range(T)])

    notes = [exchange(note, s) for s, note in enumerate(notes, 1)]
    chunks = gather_chunks(sz, chunk)
    same, far, near, *firsts = call_compute(sz, plan, tokens, cotangent, chunks)

    def prepare(after):
        return call_prepare(sz, plan, notes[0], call_turn([firsts[0]], [after])[0])

    sent = [exchange(firsts[s], s) for s in range(1, T)]
    terms, (*partial, strips) = reduce_parts(sz, same, far, near, notes, prepare)
    *outs, flag = call_last(sz, plan, notes, sent, terms, strips, partial)
    return tuple(outs), flag


def shards(
    tokens,
    cotangent,
    gate_blocks,
    up_blocks,
    down_blocks,
    gate_where,
    up_where,
    down_where,
    block_counts,
):
    n_fsdp, n_tensor = lax.axis_size("fsdp"), lax.axis_size("tensor")
    f, rank = lax.axis_index("fsdp"), lax.axis_index("tensor")
    slots = gate_where.shape[1]
    full = Sizes(tokens, gate_blocks, slots, n_fsdp, n_tensor, False)
    own = jnp.concatenate([
        gate_where[0], up_where[0], down_where[0], block_counts[:, 0],
        f.astype(jnp.int32)[None], rank.astype(jnp.int32)[None]])
    own = jnp.pad(own, (0, full.lanes - own.shape[0]))[None]
    blocks_in = (gate_blocks, up_blocks, down_blocks)
    if slots >= full.cb:
        return program(full, own, tokens, cotangent, blocks_in)[0]
    lean = Sizes(tokens, gate_blocks, slots, n_fsdp, n_tensor, True)
    outs, flag = program(lean, own, tokens, cotangent, blocks_in)
    return lax.cond(
        flag[0] > 0,
        lambda outs, *args: program(full, *args)[0],
        lambda outs, *args: outs,
        outs, own, tokens, cotangent, blocks_in)


def solution(mesh):
    placed = (
        P("fsdp", None),
        P("fsdp", None),
        P("tensor", "fsdp", None, None),
        P("tensor", "fsdp", None, None),
        P("tensor", "fsdp", None, None),
        P("tensor", None),
        P("tensor", None),
        P("tensor", None),
        P(None, "tensor"),
    )
    return jax.shard_map(
        shards,
        mesh=mesh,
        in_specs=placed,
        out_specs=(
            P("fsdp", "tensor"),
            P("fsdp", "tensor"),
            P("tensor", "fsdp", None, None),
            P("tensor", "fsdp", None, None),
            P("tensor", "fsdp", None, None),
        ),
        check_vma=False,
    )
```

```python
import functools

import jax
import jax.numpy as jnp
from jax import lax
from jax.experimental import pallas as pl
from jax.experimental.pallas import tpu as pltpu
from jax.sharding import PartitionSpec as P

FF = 14336
BLK = 128
GROUP = 8
COLUMNS = 4
FIRST_SEND = 18
LEAN_SLOTS = 7
ROWS = BLK // 2
SMALL = 4 * 1024 * 1024
PART, STRIP, CIDX, CWAS, OIDX, OWAS = range(6)
FIELDS = 6
COLS_ROW = 3 * FIELDS
HEAD_ROW = COLS_ROW + 1
MINE_ROW = COLS_ROW + 2
LISTS_ROW = COLS_ROW + 3
HEAD_COLS, HEAD_OVER, HEAD_CORE, HEAD_LISTS = 3, 4, 5, 8


class Sizes:
    def __init__(self, tokens, gate_blocks, slots, n_fsdp, n_tensor, lean):
        self.tok, self.width = tokens.shape
        self.n_fsdp, self.n_tensor = n_fsdp, n_tensor
        self.rb = self.width // BLK
        self.cb = FF // (BLK * n_tensor)
        self.slots = slots
        self.all = 3 * slots
        self.lanes = -(-(self.all + GROUP) // 128) * 128
        self.nb = gate_blocks.shape[1]
        self.owned = 3 * self.nb
        self.ring = n_fsdp // 2
        self.top = self.ring // 2
        self.rbt = self.rb // n_tensor
        self.order = [self.top]
        for d in range(1, self.top):
            self.order += [self.top + d, self.top - d]
        self.order.append(0)
        self.far = min(2, self.ring - 1)
        self.keep = min(LEAN_SLOTS, 2 * self.owned) if lean else 2 * self.owned
        self.send_all = 2 * self.rbt
        self.first = min(FIRST_SEND, self.send_all) if lean else self.send_all
        self.blocks = self.ring * self.keep
        self.plan_rows = -(-(LISTS_ROW + 2 * n_tensor) // 8) * 8
        self.note_n, self.note_over = self.lanes - 1, self.lanes - 2
        self.room = slots + GROUP

    def place(self, d):
        return self.order.index(d) * self.keep

    def place_across(self, d):
        return self.place((self.ring - d) % self.ring)


def permutations(sz):
    seq = list(range(0, sz.ring, 2)) + list(range(sz.ring - 1, 0, -2))
    ahead, behind, swap = [], [], []
    for i, q in enumerate(seq):
        up, down = seq[(i + 1) % sz.ring], seq[i - 1]
        ahead += [(q * 2, up * 2), (q * 2 + 1, down * 2 + 1)]
        behind += [(q * 2, down * 2), (q * 2 + 1, up * 2 + 1)]
        swap += [(q * 2, q * 2 + 1), (q * 2 + 1, q * 2)]
    return ahead, behind, swap


def ratio(x, d):
    return jnp.floor((x + 0.5) * (1.0 / d))


def rest_of(x, d):
    return x - d * ratio(x, d)


def ring_position(sz, chip):
    return jnp.where(rest_of(chip, 2) == 0, ratio(chip, 2), sz.ring - 1 - ratio(chip, 2))


class Marks:
    def __init__(self, sz, own):
        N, L, S = sz.all, sz.lanes, sz.slots
        f32 = jnp.float32
        self.sz = sz
        self.sub = lax.broadcasted_iota(jnp.int32, (N, L), 0)
        self.lane = lax.broadcasted_iota(jnp.int32, (N, L), 1)
        self.same = self.sub == self.lane
        sub_c = self.sub[:, :1].astype(f32)
        lane_r = lax.broadcasted_iota(jnp.int32, (1, L), 1).astype(f32)
        self.sub_c, self.lane_r = sub_c, lane_r
        raw_r = own[...].astype(f32)

        def single(row, at):
            return jnp.sum(jnp.where(lane_r == at, row, 0.0), axis=1, keepdims=True)

        self.f, self.rank = single(raw_r, N + 3), single(raw_r, N + 4)

        def kind(x):
            return (x >= S).astype(f32) + (x >= 2 * S).astype(f32)

        self.kind_c, self.kind_r = kind(sub_c), kind(lane_r)
        self.n_r = lane_r - S * self.kind_r
        self.n_c = sub_c - S * self.kind_c
        limit = jnp.zeros((1, L), f32)
        for k in range(3):
            limit = limit + jnp.where(self.kind_r == k, single(raw_r, N + k), 0.0)
        live_r = jnp.where((lane_r < N) & (self.n_r < limit), 1.0, 0.0)
        w_c = self.col(raw_r)
        live_c = self.col(live_r)

        def place(w, k):
            gate, down = ratio(w, sz.cb), ratio(w, sz.rb)
            is_down = k == 2
            return jnp.where(is_down, w - down * sz.rb, gate), jnp.where(is_down, down, w - gate * sz.cb)

        self.row_c, col_c = place(w_c, self.kind_c)
        self.row_r, col_r = place(raw_r, self.kind_r)
        self.chip_c, chip_r = ratio(self.n_c, 2 * sz.nb), ratio(self.n_r, 2 * sz.nb)
        self.same_chip = (self.chip_c == chip_r).astype(f32)
        self.same_col = (col_c == col_r).astype(f32)
        act_c, act_r = live_c, live_r
        for k in range(3):
            lanes = self.same_col * (live_r * (self.kind_r == k).astype(f32))
            act_c = act_c * jnp.max(lanes, axis=1, keepdims=True)
            subs = self.same_col * (live_c * (self.kind_c == k).astype(f32))
            act_r = act_r * jnp.max(subs, axis=0, keepdims=True)
        self.act_c, self.act_r = act_c, act_r
        out_c = jnp.where(self.kind_c == 2, 0.0, f32(sz.rb)) + self.row_c
        out_r = jnp.where(self.kind_r == 2, 0.0, f32(sz.rb)) + self.row_r
        self.same_out = (out_c == out_r).astype(f32)
        self.before = (self.lane < self.sub).astype(f32)
        self.after = (self.sub < self.lane).astype(f32)
        self.owas_c = jnp.max(self.same_out * self.before * act_r, axis=1, keepdims=True)
        self.owas_r = jnp.max(self.same_out * self.after * act_c, axis=0, keepdims=True)
        self.lead_c = act_c * (1.0 - self.owas_c)
        self.lead_r = act_r * (1.0 - self.owas_r)

        def shift(row):
            away = ratio(row, sz.rbt) - self.rank
            return jnp.where(away < 0, away + sz.n_tensor, away)

        self.shift_c, self.shift_r = shift(self.row_c), shift(self.row_r)
        self.local_c = jnp.where(self.kind_c == 2, 0.0, f32(sz.rbt)) + rest_of(self.row_c, sz.rbt)

    def col(self, row):
        return jnp.sum(jnp.where(self.same, row, 0.0), axis=1, keepdims=True)

    def carried(self):
        sz = self.sz
        rank = jnp.sum(self.before * self.same_chip * self.act_r, axis=1, keepdims=True)
        away = ring_position(sz, self.chip_c) - ring_position(sz, ratio(self.f, 2))
        away = jnp.where(rest_of(self.f, 2) == 0, away, -away)
        rel = jnp.where(away < 0, away + sz.ring, away)
        j = jnp.where(rel > sz.top, 2 * (rel - sz.top) - 1, 2 * (sz.top - rel))
        return rank, jnp.where(rel == 0, sz.ring - 1.0, j)

    def ranks(self, chosen_r):
        return jnp.sum(self.before * chosen_r, axis=1, keepdims=True)

    def listed(self, chosen_c, rank_c, value_c, lo=0, hi=None):
        at = rank_c[lo:hi] == self.lane[lo:hi].astype(jnp.float32)
        return jnp.sum(jnp.where(at, chosen_c[lo:hi] * value_c[lo:hi], 0.0), axis=0, keepdims=True)

    def most_on_chip(self):
        return jnp.max(jnp.sum(self.same_chip * self.act_r, axis=1, keepdims=True), axis=0, keepdims=True)


def total(x):
    return jnp.sum(x, axis=0, keepdims=True)


def head_row(sz, entries):
    lane = lax.broadcasted_iota(jnp.int32, (1, sz.lanes), 1)
    row = jnp.zeros((1, sz.lanes), jnp.float32)
    for i, value in entries:
        row = jnp.where(lane == i, value, row)
    return row


def plan_kernel(sz, own, *refs):
    mine, theirs, (plan, chunk, *notes, sems) = refs[:3], refs[3:6], refs[6:]
    S, N = sz.slots, sz.all
    m = Marks(sz, own)
    f32 = jnp.float32
    lane_r, sub_c = m.lane_r, m.sub_c
    pos_c, base_c = m.carried()
    core = rest_of(m.f, 2)
    half = pl.ds(pl.multiple_of(jnp.max(core).astype(jnp.int32) * ROWS, ROWS), ROWS)

    pair = jnp.where(core == 0, m.f + 1, m.f - 1)
    i_r = rest_of(lane_r, sz.owned)
    owner_r = jnp.where(lane_r < sz.owned, m.f, pair)
    slot_r = ratio(i_r, sz.nb) * S + owner_r * sz.nb + rest_of(i_r, sz.nb)
    at_r = jnp.sum(jnp.where(sub_c == slot_r, m.act_c * (pos_c + 1.0), 0.0), axis=0, keepdims=True)
    copies = []
    for i in range(2 * sz.owned):
        side, k, a = i // sz.owned, i % sz.owned // sz.nb, i % sz.nb
        at = jnp.max(jnp.where(lane_r == i, at_r, 0.0)).astype(jnp.int32)
        fits = (at > 0) & (at <= sz.keep)
        place = jnp.minimum(jnp.maximum(at - 1, 0), sz.keep - 1)
        copy = pltpu.make_async_copy((mine, theirs)[side][k].at[0, a, half], chunk.at[place], sems.at[i])
        copies.append((fits, copy))
    for fits, copy in copies:
        pl.when(fits)(copy.start)

    same_kind = (m.kind_c == m.kind_r).astype(f32)
    rank_c = jnp.sum(m.before * same_kind * m.act_r, axis=1, keepdims=True)
    cwas_c = jnp.max(m.before * same_kind * m.same_col * m.act_r, axis=1, keepdims=True)
    cwas_r = jnp.max(m.after * same_kind * m.same_col * m.act_c, axis=0, keepdims=True)
    big = f32(4 * N)
    lanes_f = m.lane.astype(f32)
    gates_r = m.act_r * (m.kind_r == 0).astype(f32)
    cidx_c = jnp.min(jnp.where(m.same_col * gates_r > 0, lanes_f, big), axis=1, keepdims=True)
    oidx_c = jnp.min(jnp.where(m.same_out * m.act_r > 0, lanes_f, big), axis=1, keepdims=True)
    rank_r = jnp.sum(m.after * same_kind * m.act_c, axis=0, keepdims=True)
    turn_c = ratio(rank_c, GROUP) * 3 + m.kind_c
    turn_r = ratio(rank_r, GROUP) * 3 + m.kind_r
    ahead = ((turn_r < turn_c) | ((turn_r == turn_c) & (rank_r < rank_c))).astype(f32)
    owas_c = jnp.max(m.same_out * ahead * m.act_r, axis=1, keepdims=True)
    part_c = jnp.where(pos_c < sz.keep, base_c * sz.keep + pos_c, f32(sz.blocks))
    fields = [(part_c, sz.blocks), (m.row_c, 0), (cidx_c, S), (cwas_c, 0), (oidx_c, N), (owas_c, 0)]
    rows = []
    head = []
    for k in range(3):
        lo, hi = k * S, (k + 1) * S
        n_k = total(m.act_c[lo:hi])
        head.append((k, n_k))
        for value, spare in fields:
            row = m.listed(m.act_c, rank_c, value, lo, hi)
            rows.append(jnp.where(lane_r < n_k, row, f32(spare)))
    leader_c = m.act_c * (1.0 - cwas_c) * (m.kind_c == 0).astype(f32)
    leader_r = m.act_r * (1.0 - cwas_r) * (m.kind_r == 0).astype(f32)
    n_cols = total(leader_c)
    cols = m.listed(leader_c, m.ranks(leader_r), sub_c, 0, S)
    rows.append(jnp.where(lane_r < n_cols, cols, f32(S)))
    head.append((HEAD_COLS, n_cols))
    lists, sent = [], []
    over = (m.most_on_chip() > sz.keep).astype(f32)
    for s in range(sz.n_tensor):
        chosen_c = m.lead_c * (m.shift_c == s).astype(f32)
        chosen_r = m.lead_r * (m.shift_r == s).astype(f32)
        rank = m.ranks(chosen_r)
        lists.append(m.listed(chosen_c, rank, sub_c))
        lists.append(m.listed(chosen_c, rank, m.local_c))
        n = total(chosen_c)
        head.append((HEAD_LISTS + s, n))
        sent.append(n)
        over = jnp.maximum(over, (n > sz.first).astype(f32))
    head += [(HEAD_OVER, over), (HEAD_CORE, core)]
    for s in range(1, sz.n_tensor):
        note = jnp.where(lane_r == sz.note_n, sent[s], lists[2 * s + 1])
        notes[s - 1][...] = jnp.where(lane_r == sz.note_over, over, note).astype(jnp.int32)
    rows.append(head_row(sz, head))
    rows.append(at_r)
    rows += lists
    for i, row in enumerate(rows):
        plan[i:i + 1, :] = row.astype(jnp.int32)
    for fits, copy in copies:
        pl.when(fits)(copy.wait)


def dot(a, b, ca, cb):
    return lax.dot_general(a, b, (((ca,), (cb,)), ((), ())), preferred_element_type=jnp.float32)


def field(sz, plan, k, j, e):
    return plan[k * FIELDS + j, e]


def walk(plan, body):
    most = jnp.maximum(jnp.maximum(plan[HEAD_ROW, 0], plan[HEAD_ROW, 1]), plan[HEAD_ROW, 2])
    lax.fori_loop(0, (most + (GROUP - 1)) // GROUP, lambda p, _: body(p * GROUP), None)


def each(plan, k, body):
    lax.fori_loop(0, plan[HEAD_ROW, k], lambda e, _: body(e), None)


def compute_kernel(sz, plan, tokens, cot, *refs):
    n_chunks, T = 2 * sz.ring, sz.n_tensor
    chunks, refs = refs[:n_chunks], refs[n_chunks:]
    same, far, near = refs[:3]
    firsts, refs = refs[3:3 + T], refs[3 + T:]
    xs, wbuf, parts, gate_acc, up_acc, hg_acc, acts, out_acc, stage, strip_sems, sems = refs
    A = sz.slots + 1
    get = functools.partial(field, sz, plan)

    def strip_copy(k, e):
        src = cot if k == 2 else tokens
        cols = pl.ds(pl.multiple_of(get(k, STRIP, e) * BLK, BLK), BLK)
        return pltpu.make_async_copy(src.at[:, cols], xs.at[k * sz.room + e], strip_sems.at[k * sz.room + e])

    core = plan[HEAD_ROW, HEAD_CORE]
    sides = [pl.ds(pl.multiple_of(c * ROWS, ROWS), ROWS) for c in (core, 1 - core)]
    loads = []
    for side, place in enumerate((sz.place, sz.place_across)):
        for d in sz.order:
            i = len(loads)
            there = wbuf.at[pl.ds(place(d), sz.keep), sides[side]]
            loads.append(pltpu.make_async_copy(chunks[i], there, sems.at[i]))
    for k in range(3):
        each(plan, k, lambda e, k=k: strip_copy(k, e).start())
    for c in loads:
        c.start()
    for k in range(3):
        each(plan, k, lambda e, k=k: strip_copy(k, e).wait())
    for c in loads:
        c.wait()

    group = [(k, u) for k in range(3) for u in range(GROUP)]

    def forward(e0):
        for k, u in group:
            e, acc = e0 + u, (gate_acc, up_acc, hg_acc)[k]
            prod = dot(xs[k * sz.room + e], wbuf[get(k, PART, e)], 1, 1 if k == 2 else 0)
            c = get(k, CIDX, e)
            acc[c] = prod + jnp.where(get(k, CWAS, e) == 0, 0.0, acc[c])

    walk(plan, forward)

    def columns(i, _):
        for j in range(COLUMNS):
            c = plan[COLS_ROW, i * COLUMNS + j]
            g, u, h = gate_acc[c], up_acc[c], hg_acc[c]
            s = lax.logistic(g)
            silu = g * s
            acts[c] = (h * u * s * (1.0 + g * (1.0 - s))).astype(jnp.bfloat16)
            acts[A + c] = (h * silu).astype(jnp.bfloat16)
            acts[2 * A + c] = (silu * u).astype(jnp.bfloat16)

    lax.fori_loop(0, (plan[HEAD_ROW, HEAD_COLS] + (COLUMNS - 1)) // COLUMNS, columns, None)

    def gradients(e0):
        for k, u in group:
            e = e0 + u
            a, x = acts[k * A + get(k, CIDX, e)], xs[k * sz.room + e]
            grad = dot(a, x, 0, 0) if k == 2 else dot(x, a, 0, 0)
            parts[get(k, PART, e)] = grad.astype(jnp.bfloat16)

    walk(plan, gradients)
    outs = []
    for j, d in enumerate(sz.order):
        ref, at = (far, j) if j < sz.far else (near, j - sz.far)
        outs.append(pltpu.make_async_copy(
            parts.at[pl.ds(sz.place_across(d), sz.keep), sides[1]], ref.at[pl.ds(at * sz.keep, sz.keep)], sems.at[j]))
    outs.append(pltpu.make_async_copy(parts.at[pl.ds(0, sz.blocks), sides[0]], same, sems.at[sz.ring]))
    for c in outs:
        c.start()

    def terms(e0):
        for k, u in group:
            e = e0 + u
            prod = dot(acts[k * A + get(k, CIDX, e)], wbuf[get(k, PART, e)], 1, 0 if k == 2 else 1)
            at = get(k, OIDX, e)
            out_acc[at] = prod + jnp.where(get(k, OWAS, e) == 0, 0.0, out_acc[at])

    walk(plan, terms)

    for s in reversed(range(T)):
        def staged(i, _, s=s):
            stage[s * sz.first + i] = out_acc[plan[LISTS_ROW + 2 * s, i]].astype(jnp.bfloat16)

        lax.fori_loop(0, jnp.minimum(plan[HEAD_ROW, HEAD_LISTS + s], sz.first), staged, None)
        copy = pltpu.make_async_copy(stage.at[pl.ds(s * sz.first, sz.first)], firsts[s], sems.at[sz.ring + 1 + s])
        copy.start()
        outs.append(copy)
    for c in outs:
        c.wait()


def strip_of(sz, at):
    w = jnp.where(at < sz.rbt, at, at - sz.rbt)
    return at < sz.rbt, pl.ds(pl.multiple_of(w * BLK, BLK), BLK)


def prepare_kernel(sz, plan, note, first, outputs, input_grads, strips):
    outputs[...] = jnp.zeros_like(outputs)
    input_grads[...] = jnp.zeros_like(input_grads)

    def step(i, _):
        is_out, cols = strip_of(sz, plan[LISTS_ROW + 1, i])

        @pl.when(is_out)
        def _():
            outputs[:, cols] = first[i]

        @pl.when(jnp.logical_not(is_out))
        def _():
            input_grads[:, cols] = first[i]

    lax.fori_loop(0, jnp.minimum(plan[HEAD_ROW, HEAD_LISTS], sz.first), step, None)

    def pick(i, _):
        is_out, cols = strip_of(sz, note[0, i])

        @pl.when(is_out)
        def _():
            strips[i] = outputs[:, cols]

        @pl.when(jnp.logical_not(is_out))
        def _():
            strips[i] = input_grads[:, cols]

    lax.fori_loop(0, jnp.minimum(note[0, sz.note_n], sz.first), pick, None)


def last_kernel(sz, plan, *refs):
    T = sz.n_tensor
    notes, refs = refs[:T - 1], refs[T - 1:]
    firsts, refs = refs[:T - 1], refs[T - 1:]
    mine, theirs, held_strips, refs = refs[:3], refs[3:6], refs[6], refs[9:]
    outputs, input_grads, grads, flag = refs[0], refs[1], refs[2:5], refs[5]
    strips, read_sems, write_sems = refs[6:]
    over = plan[HEAD_ROW, HEAD_OVER]
    for note in notes:
        over = jnp.maximum(over, note[0, sz.note_over])
    flag[0] = over

    def move(s, i, back, act):
        is_out, cols = strip_of(sz, notes[s][0, i])
        for ref, here in ((outputs, is_out), (input_grads, jnp.logical_not(is_out))):
            @pl.when(here)
            def _(ref=ref):
                there = ref.at[:, cols]
                if back:
                    act(pltpu.make_async_copy(strips.at[i], there, write_sems.at[i]))
                else:
                    act(pltpu.make_async_copy(there, strips.at[i], read_sems.at[i]))

    def loop(s, body):
        lax.fori_loop(0, jnp.minimum(notes[s][0, sz.note_n], sz.first), lambda i, _: body(i), None)

    def begin(s):
        loop(s, lambda i: move(s, i, False, lambda c: c.start()))

    def add(s):
        def step(i):
            move(s, i, False, lambda c: c.wait())
            value = strips[i].astype(jnp.float32) + firsts[s][i].astype(jnp.float32)
            strips[i] = value.astype(jnp.bfloat16)
            move(s, i, True, lambda c: c.start())

        loop(s, step)

    def end(s):
        loop(s, lambda i: move(s, i, True, lambda c: c.wait()))

    def first_add(i):
        value = held_strips[i].astype(jnp.float32) + firsts[0][i].astype(jnp.float32)
        strips[i] = value.astype(jnp.bfloat16)
        move(0, i, True, lambda c: c.start())

    loop(0, first_add)
    core = plan[HEAD_ROW, HEAD_CORE]
    for k in range(3):
        for a in range(sz.nb):
            at = plan[MINE_ROW, k * sz.nb + a]
            p = jnp.minimum(jnp.maximum(at - 1, 0), sz.keep - 1)
            for terms, c in ((mine, core), (theirs, 1 - core)):
                value = sum(t[p].astype(jnp.float32) for t in terms)
                rows = pl.ds(pl.multiple_of(c * ROWS, ROWS), ROWS)
                grads[k][0, a, rows] = jnp.where(at > 0, value, 0.0).astype(jnp.bfloat16)
    end(0)
    for s in range(1, T - 1):
        begin(s)
        add(s)
        end(s)


def spec(space):
    return pl.BlockSpec(memory_space=space)


ANY, HBM, VMEM, SMEM = pl.ANY, pltpu.HBM, pltpu.VMEM, pltpu.SMEM


def cost(flops, moved):
    return pl.CostEstimate(flops=flops, bytes_accessed=moved, transcendentals=0)


def call_plan(sz, own, mine, theirs):
    return pl.pallas_call(
        functools.partial(plan_kernel, sz),
        out_shape=[
            jax.ShapeDtypeStruct((sz.plan_rows, sz.lanes), jnp.int32),
            halves(sz.keep),
        ] + [jax.ShapeDtypeStruct((1, sz.lanes), jnp.int32)] * (sz.n_tensor - 1),
        in_specs=[spec(VMEM)] + [spec(ANY)] * 6,
        out_specs=[spec(VMEM), spec(ANY)] + [spec(VMEM)] * (sz.n_tensor - 1),
        scratch_shapes=[pltpu.SemaphoreType.DMA((2 * sz.owned,))],
        compiler_params=pltpu.CompilerParams(vmem_limit_bytes=SMALL),
        cost_estimate=cost(1_000_000, 4_000_000),
        name="plan",
    )(own, *mine, *theirs)


def call_turn(handed, arrived):
    return pl.pallas_call(
        lambda *_: None,
        out_shape=[jax.ShapeDtypeStruct(x.shape, x.dtype) for x in handed],
        in_specs=[spec(ANY)] * (len(handed) + len(arrived)),
        out_specs=[spec(ANY)] * len(handed),
        input_output_aliases={i: i for i in range(len(handed))},
        compiler_params=pltpu.CompilerParams(vmem_limit_bytes=SMALL),
        cost_estimate=cost(1000, 1000),
        name="turn",
    )(*handed, *arrived)


def blocks(n):
    return jax.ShapeDtypeStruct((n, BLK, BLK), jnp.bfloat16)


def halves(n):
    return jax.ShapeDtypeStruct((n, ROWS, BLK), jnp.bfloat16)


def held(scratch):
    return sum(s[0] * s[1] * s[2] * jnp.dtype(t).itemsize for s, t in scratch) + 2 * 1024 * 1024


def call_compute(sz, plan, tokens, cot, chunks):
    bf, f32 = jnp.bfloat16, jnp.float32
    T, A = sz.n_tensor, sz.slots + 1
    out_shape = [halves(sz.ring * sz.keep), halves(sz.far * sz.keep), halves((sz.ring - sz.far) * sz.keep)]
    out_shape += [blocks(sz.first)] * T
    scratch = [
        ((3 * sz.room, sz.tok, BLK), bf),
        ((sz.blocks + 1, BLK, BLK), bf),
        ((sz.blocks + 1, BLK, BLK), bf),
        ((A, sz.tok, BLK), f32),
        ((A, sz.tok, BLK), f32),
        ((A, sz.tok, BLK), f32),
        ((3 * A, sz.tok, BLK), bf),
        ((sz.all + 1, sz.tok, BLK), f32),
        ((T * sz.first, sz.tok, BLK), bf),
    ]
    return pl.pallas_call(
        functools.partial(compute_kernel, sz),
        out_shape=out_shape,
        in_specs=[spec(SMEM)] + [spec(HBM)] * 2 + [spec(ANY)] * len(chunks),
        out_specs=[spec(ANY)] * len(out_shape),
        scratch_shapes=[pltpu.VMEM(s, t) for s, t in scratch] + [
            pltpu.SemaphoreType.DMA((3 * sz.room,)),
            pltpu.SemaphoreType.DMA((max(len(chunks), sz.ring + 1 + T),)),
        ],
        compiler_params=pltpu.CompilerParams(vmem_limit_bytes=held(scratch)),
        cost_estimate=cost(1_000_000_000, 20_000_000),
        name="compute",
    )(plan, pltpu.with_memory_space_constraint(tokens, HBM), pltpu.with_memory_space_constraint(cot, HBM), *chunks)


def call_prepare(sz, plan, note, first):
    half = jax.ShapeDtypeStruct((sz.tok, sz.width // sz.n_tensor), jnp.bfloat16)
    return pl.pallas_call(
        functools.partial(prepare_kernel, sz),
        out_shape=[half, half, blocks(sz.first)],
        in_specs=[spec(SMEM), spec(SMEM), spec(VMEM)],
        out_specs=[spec(VMEM)] * 3,
        compiler_params=pltpu.CompilerParams(vmem_limit_bytes=12 * 1024 * 1024),
        cost_estimate=cost(1_000_000, 6_000_000),
        name="prepare",
    )(plan, note, first)


def call_last(sz, plan, notes, firsts, terms, strips, partial):
    n = 2 + len(notes) + len(firsts) + len(terms)
    out = jax.ShapeDtypeStruct((1, sz.nb, BLK, BLK), jnp.bfloat16)
    return pl.pallas_call(
        functools.partial(last_kernel, sz),
        out_shape=[jax.ShapeDtypeStruct(p.shape, p.dtype) for p in partial] + [out] * 3 + [
            jax.ShapeDtypeStruct((1,), jnp.int32)],
        in_specs=[spec(SMEM)] * (1 + len(notes)) + [spec(VMEM)] * (len(firsts) + len(terms) + 1) + [spec(ANY)] * 2,
        out_specs=[spec(ANY)] * 2 + [spec(VMEM)] * 3 + [spec(SMEM)],
        input_output_aliases={n: 0, n + 1: 1},
        scratch_shapes=[
            pltpu.VMEM((sz.first, sz.tok, BLK), jnp.bfloat16),
            pltpu.SemaphoreType.DMA((sz.first,)),
            pltpu.SemaphoreType.DMA((sz.first,)),
        ],
        compiler_params=pltpu.CompilerParams(vmem_limit_bytes=12 * 1024 * 1024),
        cost_estimate=cost(1_000_000, 3_000_000),
        name="last",
    )(plan, *notes, *firsts, *terms, strips, *partial)


def across(pairs):
    return [(i, j ^ 1) for i, j in pairs]


def gather_chunks(sz, chunk):
    ahead, behind, swap = permutations(sz)
    same = {0: chunk}
    a = b = chunk
    for s in range(1, sz.top):
        a, b = lax.ppermute(a, "fsdp", ahead), lax.ppermute(b, "fsdp", behind)
        same[sz.ring - s], same[s] = a, b
    other = {d: lax.ppermute(same[d], "fsdp", swap) for d in same}
    same[sz.top] = lax.ppermute(a, "fsdp", ahead)
    other[sz.top] = lax.ppermute(a, "fsdp", across(ahead))
    return [side[d] for side in (same, other) for d in sz.order]


def reduce_parts(sz, same, far, near, notes, prepare):
    ahead, behind, swap = permutations(sz)
    keep = sz.keep
    far = lax.ppermute(far, "fsdp", swap)
    near = lax.ppermute(call_turn([near], [far])[0], "fsdp", swap)

    def term(d, *more):
        j = sz.order.index(d)
        pair = far[j * keep:(j + 1) * keep] if j < sz.far else near[(j - sz.far) * keep:][:keep]
        out = same[j * keep:(j + 1) * keep].astype(jnp.float32) + pair.astype(jnp.float32)
        for m in more:
            out = out + m.astype(jnp.float32)
        return out.astype(jnp.bfloat16)

    a, b = lax.optimization_barrier((term(sz.top), term(sz.top + 1)))
    here = term(0)
    here_across = lax.ppermute(here, "fsdp", swap)
    prepared = prepare(here_across)
    for s in range(1, sz.top):
        last_b = b
        a, b = lax.ppermute(a, "fsdp", ahead), lax.ppermute(b, "fsdp", behind)
        if s == 1:
            a, b = call_turn([a, b], notes)
        else:
            a = call_turn([a], [last_b] + (list(prepared[2:]) if s == 2 else []))[0]
        a = term(sz.top - s, a)
        if s + 1 < sz.top:
            b = term(sz.top + 1 + s, call_turn([b], [a])[0])
    mine = [here, lax.ppermute(a, "fsdp", ahead), b]
    theirs = [
        here_across,
        lax.ppermute(a, "fsdp", across(ahead)),
        lax.ppermute(last_b, "fsdp", across(behind)),
    ]
    return mine + theirs, prepared


def program(sz, own, tokens, cotangent, mine):
    T = sz.n_tensor
    swap = permutations(sz)[-1]
    theirs = [lax.ppermute(b, "fsdp", swap) for b in mine]
    plan, chunk, *notes = call_plan(sz, own, mine, theirs)

    def exchange(array, s):
        return lax.ppermute(array, "tensor", [(i, (i + s) % T) for i in range(T)])

    notes = [exchange(note, s) for s, note in enumerate(notes, 1)]
    chunks = gather_chunks(sz, chunk)
    same, far, near, *firsts = call_compute(sz, plan, tokens, cotangent, chunks)

    def prepare(after):
        return call_prepare(sz, plan, notes[0], call_turn([firsts[0]], [after])[0])

    sent = [exchange(firsts[s], s) for s in range(1, T)]
    terms, (*partial, strips) = reduce_parts(sz, same, far, near, notes, prepare)
    *outs, flag = call_last(sz, plan, notes, sent, terms, strips, partial)
    return tuple(outs), flag


def shards(
    tokens,
    cotangent,
    gate_blocks,
    up_blocks,
    down_blocks,
    gate_where,
    up_where,
    down_where,
    block_counts,
):
    n_fsdp, n_tensor = lax.axis_size("fsdp"), lax.axis_size("tensor")
    f, rank = lax.axis_index("fsdp"), lax.axis_index("tensor")
    slots = gate_where.shape[1]
    full = Sizes(tokens, gate_blocks, slots, n_fsdp, n_tensor, False)
    own = jnp.concatenate([
        gate_where[0], up_where[0], down_where[0], block_counts[:, 0],
        f.astype(jnp.int32)[None], rank.astype(jnp.int32)[None]])
    own = jnp.pad(own, (0, full.lanes - own.shape[0]))[None]
    blocks_in = (gate_blocks, up_blocks, down_blocks)
    if slots >= full.cb:
        return program(full, own, tokens, cotangent, blocks_in)[0]
    lean = Sizes(tokens, gate_blocks, slots, n_fsdp, n_tensor, True)
    outs, flag = program(lean, own, tokens, cotangent, blocks_in)
    return lax.cond(
        flag[0] > 0,
        lambda outs, *args: program(full, *args)[0],
        lambda outs, *args: outs,
        outs, own, tokens, cotangent, blocks_in)


def solution(mesh):
    placed = (
        P("fsdp", None),
        P("fsdp", None),
        P("tensor", "fsdp", None, None),
        P("tensor", "fsdp", None, None),
        P("tensor", "fsdp", None, None),
        P("tensor", None),
        P("tensor", None),
        P("tensor", None),
        P(None, "tensor"),
    )
    return jax.shard_map(
        shards,
        mesh=mesh,
        in_specs=placed,
        out_specs=(
            P("fsdp", "tensor"),
            P("fsdp", "tensor"),
            P("tensor", "fsdp", None, None),
            P("tensor", "fsdp", None, None),
            P("tensor", "fsdp", None, None),
        ),
        check_vma=False,
    )
```

```python
import functools

import jax
import jax.numpy as jnp
from jax import lax
from jax.experimental import pallas as pl
from jax.experimental.pallas import tpu as pltpu
from jax.sharding import PartitionSpec as P

FF = 14336
BLK = 128
GROUP = 8
COLUMNS = 4
FIRST_SEND = 18
LEAN_SLOTS = 7
ROWS = BLK // 2
SMALL = 4 * 1024 * 1024
PART, STRIP, CIDX, CWAS, OIDX, OWAS = range(6)
FIELDS = 6
COLS_ROW = 3 * FIELDS
HEAD_ROW = COLS_ROW + 1
MINE_ROW = COLS_ROW + 2
LISTS_ROW = COLS_ROW + 3
HEAD_COLS, HEAD_OVER, HEAD_CORE, HEAD_LISTS = 3, 4, 5, 8


class Sizes:
    def __init__(self, tokens, gate_blocks, slots, n_fsdp, n_tensor, lean):
        self.tok, self.width = tokens.shape
        self.n_fsdp, self.n_tensor = n_fsdp, n_tensor
        self.rb = self.width // BLK
        self.cb = FF // (BLK * n_tensor)
        self.slots = slots
        self.all = 3 * slots
        self.lanes = -(-(self.all + GROUP) // 128) * 128
        self.nb = gate_blocks.shape[1]
        self.owned = 3 * self.nb
        self.ring = n_fsdp // 2
        self.top = self.ring // 2
        self.rbt = self.rb // n_tensor
        self.order = [self.top]
        for d in range(1, self.top):
            self.order += [self.top + d, self.top - d]
        self.order.append(0)
        self.far = min(2, self.ring - 1)
        self.keep = min(LEAN_SLOTS, 2 * self.owned) if lean else 2 * self.owned
        self.send_all = 2 * self.rbt
        self.first = min(FIRST_SEND, self.send_all) if lean else self.send_all
        self.blocks = self.ring * self.keep
        self.plan_rows = -(-(LISTS_ROW + 2 * n_tensor) // 8) * 8
        self.note_n, self.note_over = self.lanes - 1, self.lanes - 2
        self.room = slots + GROUP

    def place(self, d):
        return self.order.index(d) * self.keep

    def place_across(self, d):
        return self.place((self.ring - d) % self.ring)


def permutations(sz):
    seq = list(range(0, sz.ring, 2)) + list(range(sz.ring - 1, 0, -2))
    ahead, behind, swap = [], [], []
    for i, q in enumerate(seq):
        up, down = seq[(i + 1) % sz.ring], seq[i - 1]
        ahead += [(q * 2, up * 2), (q * 2 + 1, down * 2 + 1)]
        behind += [(q * 2, down * 2), (q * 2 + 1, up * 2 + 1)]
        swap += [(q * 2, q * 2 + 1), (q * 2 + 1, q * 2)]
    return ahead, behind, swap


def ratio(x, d):
    return jnp.floor((x + 0.5) * (1.0 / d))


def rest_of(x, d):
    return x - d * ratio(x, d)


def ring_position(sz, chip):
    return jnp.where(rest_of(chip, 2) == 0, ratio(chip, 2), sz.ring - 1 - ratio(chip, 2))


class Marks:
    def __init__(self, sz, own):
        N, L, S = sz.all, sz.lanes, sz.slots
        f32 = jnp.float32
        self.sz = sz
        self.sub = lax.broadcasted_iota(jnp.int32, (N, L), 0)
        self.lane = lax.broadcasted_iota(jnp.int32, (N, L), 1)
        self.same = self.sub == self.lane
        sub_c = self.sub[:, :1].astype(f32)
        lane_r = lax.broadcasted_iota(jnp.int32, (1, L), 1).astype(f32)
        self.sub_c, self.lane_r = sub_c, lane_r
        raw_r = own[...].astype(f32)

        def single(row, at):
            return jnp.sum(jnp.where(lane_r == at, row, 0.0), axis=1, keepdims=True)

        self.f, self.rank = single(raw_r, N + 3), single(raw_r, N + 4)

        def kind(x):
            return (x >= S).astype(f32) + (x >= 2 * S).astype(f32)

        self.kind_c, self.kind_r = kind(sub_c), kind(lane_r)
        self.n_r = lane_r - S * self.kind_r
        self.n_c = sub_c - S * self.kind_c
        limit = jnp.zeros((1, L), f32)
        for k in range(3):
            limit = limit + jnp.where(self.kind_r == k, single(raw_r, N + k), 0.0)
        live_r = jnp.where((lane_r < N) & (self.n_r < limit), 1.0, 0.0)
        w_c = self.col(raw_r)
        live_c = self.col(live_r)

        def place(w, k):
            gate, down = ratio(w, sz.cb), ratio(w, sz.rb)
            is_down = k == 2
            return jnp.where(is_down, w - down * sz.rb, gate), jnp.where(is_down, down, w - gate * sz.cb)

        self.row_c, col_c = place(w_c, self.kind_c)
        self.row_r, col_r = place(raw_r, self.kind_r)
        self.chip_c, chip_r = ratio(self.n_c, 2 * sz.nb), ratio(self.n_r, 2 * sz.nb)
        self.same_chip = (self.chip_c == chip_r).astype(f32)
        self.same_col = (col_c == col_r).astype(f32)
        act_c, act_r = live_c, live_r
        for k in range(3):
            lanes = self.same_col * (live_r * (self.kind_r == k).astype(f32))
            act_c = act_c * jnp.max(lanes, axis=1, keepdims=True)
            subs = self.same_col * (live_c * (self.kind_c == k).astype(f32))
            act_r = act_r * jnp.max(subs, axis=0, keepdims=True)
        self.act_c, self.act_r = act_c, act_r
        out_c = jnp.where(self.kind_c == 2, 0.0, f32(sz.rb)) + self.row_c
        out_r = jnp.where(self.kind_r == 2, 0.0, f32(sz.rb)) + self.row_r
        self.same_out = (out_c == out_r).astype(f32)
        self.before = (self.lane < self.sub).astype(f32)
        self.after = (self.sub < self.lane).astype(f32)
        self.owas_c = jnp.max(self.same_out * self.before * act_r, axis=1, keepdims=True)
        self.owas_r = jnp.max(self.same_out * self.after * act_c, axis=0, keepdims=True)
        self.lead_c = act_c * (1.0 - self.owas_c)
        self.lead_r = act_r * (1.0 - self.owas_r)

        def shift(row):
            away = ratio(row, sz.rbt) - self.rank
            return jnp.where(away < 0, away + sz.n_tensor, away)

        self.shift_c, self.shift_r = shift(self.row_c), shift(self.row_r)
        self.local_c = jnp.where(self.kind_c == 2, 0.0, f32(sz.rbt)) + rest_of(self.row_c, sz.rbt)

    def col(self, row):
        return jnp.sum(jnp.where(self.same, row, 0.0), axis=1, keepdims=True)

    def carried(self):
        sz = self.sz
        rank = jnp.sum(self.before * self.same_chip * self.act_r, axis=1, keepdims=True)
        away = ring_position(sz, self.chip_c) - ring_position(sz, ratio(self.f, 2))
        away = jnp.where(rest_of(self.f, 2) == 0, away, -away)
        rel = jnp.where(away < 0, away + sz.ring, away)
        j = jnp.where(rel > sz.top, 2 * (rel - sz.top) - 1, 2 * (sz.top - rel))
        return rank, jnp.where(rel == 0, sz.ring - 1.0, j)

    def ranks(self, chosen_r):
        return jnp.sum(self.before * chosen_r, axis=1, keepdims=True)

    def listed(self, chosen_c, rank_c, value_c, lo=0, hi=None):
        at = rank_c[lo:hi] == self.lane[lo:hi].astype(jnp.float32)
        return jnp.sum(jnp.where(at, chosen_c[lo:hi] * value_c[lo:hi], 0.0), axis=0, keepdims=True)

    def most_on_chip(self):
        return jnp.max(jnp.sum(self.same_chip * self.act_r, axis=1, keepdims=True), axis=0, keepdims=True)


def total(x):
    return jnp.sum(x, axis=0, keepdims=True)


def head_row(sz, entries):
    lane = lax.broadcasted_iota(jnp.int32, (1, sz.lanes), 1)
    row = jnp.zeros((1, sz.lanes), jnp.float32)
    for i, value in entries:
        row = jnp.where(lane == i, value, row)
    return row


def plan_kernel(sz, own, *refs):
    mine, theirs, (plan, chunk, *notes, sems) = refs[:3], refs[3:6], refs[6:]
    S, N = sz.slots, sz.all
    m = Marks(sz, own)
    f32 = jnp.float32
    lane_r, sub_c = m.lane_r, m.sub_c
    pos_c, base_c = m.carried()
    core = rest_of(m.f, 2)
    half = pl.ds(pl.multiple_of(jnp.max(core).astype(jnp.int32) * ROWS, ROWS), ROWS)

    pair = jnp.where(core == 0, m.f + 1, m.f - 1)
    i_r = rest_of(lane_r, sz.owned)
    owner_r = jnp.where(lane_r < sz.owned, m.f, pair)
    slot_r = ratio(i_r, sz.nb) * S + owner_r * sz.nb + rest_of(i_r, sz.nb)
    at_r = jnp.sum(jnp.where(sub_c == slot_r, m.act_c * (pos_c + 1.0), 0.0), axis=0, keepdims=True)
    copies = []
    for i in range(2 * sz.owned):
        side, k, a = i // sz.owned, i % sz.owned // sz.nb, i % sz.nb
        at = jnp.max(jnp.where(lane_r == i, at_r, 0.0)).astype(jnp.int32)
        fits = (at > 0) & (at <= sz.keep)
        place = jnp.minimum(jnp.maximum(at - 1, 0), sz.keep - 1)
        copy = pltpu.make_async_copy((mine, theirs)[side][k].at[0, a, half], chunk.at[place], sems.at[i])
        copies.append((fits, copy))
    for fits, copy in copies:
        pl.when(fits)(copy.start)

    same_kind = (m.kind_c == m.kind_r).astype(f32)
    rank_c = jnp.sum(m.before * same_kind * m.act_r, axis=1, keepdims=True)
    cwas_c = jnp.max(m.before * same_kind * m.same_col * m.act_r, axis=1, keepdims=True)
    cwas_r = jnp.max(m.after * same_kind * m.same_col * m.act_c, axis=0, keepdims=True)
    big = f32(4 * N)
    lanes_f = m.lane.astype(f32)
    gates_r = m.act_r * (m.kind_r == 0).astype(f32)
    cidx_c = jnp.min(jnp.where(m.same_col * gates_r > 0, lanes_f, big), axis=1, keepdims=True)
    oidx_c = jnp.min(jnp.where(m.same_out * m.act_r > 0, lanes_f, big), axis=1, keepdims=True)
    rank_r = jnp.sum(m.after * same_kind * m.act_c, axis=0, keepdims=True)
    turn_c = ratio(rank_c, GROUP) * 3 + m.kind_c
    turn_r = ratio(rank_r, GROUP) * 3 + m.kind_r
    ahead = ((turn_r < turn_c) | ((turn_r == turn_c) & (rank_r < rank_c))).astype(f32)
    owas_c = jnp.max(m.same_out * ahead * m.act_r, axis=1, keepdims=True)
    part_c = jnp.where(pos_c < sz.keep, base_c * sz.keep + pos_c, f32(sz.blocks))
    fields = [(part_c, sz.blocks), (m.row_c, 0), (cidx_c, S), (cwas_c, 0), (oidx_c, N), (owas_c, 0)]
    rows = []
    head = []
    for k in range(3):
        lo, hi = k * S, (k + 1) * S
        n_k = total(m.act_c[lo:hi])
        head.append((k, n_k))
        for value, spare in fields:
            row = m.listed(m.act_c, rank_c, value, lo, hi)
            rows.append(jnp.where(lane_r < n_k, row, f32(spare)))
    leader_c = m.act_c * (1.0 - cwas_c) * (m.kind_c == 0).astype(f32)
    leader_r = m.act_r * (1.0 - cwas_r) * (m.kind_r == 0).astype(f32)
    n_cols = total(leader_c)
    cols = m.listed(leader_c, m.ranks(leader_r), sub_c, 0, S)
    rows.append(jnp.where(lane_r < n_cols, cols, f32(S)))
    head.append((HEAD_COLS, n_cols))
    lists, sent = [], []
    over = (m.most_on_chip() > sz.keep).astype(f32)
    for s in range(sz.n_tensor):
        chosen_c = m.lead_c * (m.shift_c == s).astype(f32)
        chosen_r = m.lead_r * (m.shift_r == s).astype(f32)
        rank = m.ranks(chosen_r)
        lists.append(m.listed(chosen_c, rank, sub_c))
        lists.append(m.listed(chosen_c, rank, m.local_c))
        n = total(chosen_c)
        head.append((HEAD_LISTS + s, n))
        sent.append(n)
        over = jnp.maximum(over, (n > sz.first).astype(f32))
    head += [(HEAD_OVER, over), (HEAD_CORE, core)]
    for s in range(1, sz.n_tensor):
        note = jnp.where(lane_r == sz.note_n, sent[s], lists[2 * s + 1])
        notes[s - 1][...] = jnp.where(lane_r == sz.note_over, over, note).astype(jnp.int32)
    rows.append(head_row(sz, head))
    rows.append(at_r)
    rows += lists
    for i, row in enumerate(rows):
        plan[i:i + 1, :] = row.astype(jnp.int32)
    for fits, copy in copies:
        pl.when(fits)(copy.wait)


def dot(a, b, ca, cb):
    return lax.dot_general(a, b, (((ca,), (cb,)), ((), ())), preferred_element_type=jnp.float32)


def field(sz, plan, k, j, e):
    return plan[k * FIELDS + j, e]


def walk(plan, body):
    most = jnp.maximum(jnp.maximum(plan[HEAD_ROW, 0], plan[HEAD_ROW, 1]), plan[HEAD_ROW, 2])
    lax.fori_loop(0, (most + (GROUP - 1)) // GROUP, lambda p, _: body(p * GROUP), None)


def each(plan, k, body):
    lax.fori_loop(0, plan[HEAD_ROW, k], lambda e, _: body(e), None)


def compute_kernel(sz, plan, tokens, cot, *refs):
    n_chunks, T = 2 * sz.ring, sz.n_tensor
    chunks, refs = refs[:n_chunks], refs[n_chunks:]
    same, far, near = refs[:3]
    firsts, refs = refs[3:3 + T], refs[3 + T:]
    xs, wbuf, parts, gate_acc, up_acc, hg_acc, acts, out_acc, stage, strip_sems, sems = refs
    A = sz.slots + 1
    get = functools.partial(field, sz, plan)

    def strip_copy(k, e):
        src = cot if k == 2 else tokens
        cols = pl.ds(pl.multiple_of(get(k, STRIP, e) * BLK, BLK), BLK)
        return pltpu.make_async_copy(src.at[:, cols], xs.at[k * sz.room + e], strip_sems.at[k * sz.room + e])

    core = plan[HEAD_ROW, HEAD_CORE]
    sides = [pl.ds(pl.multiple_of(c * ROWS, ROWS), ROWS) for c in (core, 1 - core)]
    loads = []
    for side, place in enumerate((sz.place, sz.place_across)):
        for d in sz.order:
            i = len(loads)
            there = wbuf.at[pl.ds(place(d), sz.keep), sides[side]]
            loads.append(pltpu.make_async_copy(chunks[i], there, sems.at[i]))
    for k in range(3):
        each(plan, k, lambda e, k=k: strip_copy(k, e).start())
    for c in loads:
        c.start()
    for k in range(3):
        each(plan, k, lambda e, k=k: strip_copy(k, e).wait())
    for c in loads:
        c.wait()

    group = [(k, u) for k in range(3) for u in range(GROUP)]

    def forward(e0):
        for k, u in group:
            e, acc = e0 + u, (gate_acc, up_acc, hg_acc)[k]
            prod = dot(xs[k * sz.room + e], wbuf[get(k, PART, e)], 1, 1 if k == 2 else 0)
            c = get(k, CIDX, e)
            acc[c] = prod + jnp.where(get(k, CWAS, e) == 0, 0.0, acc[c])

    walk(plan, forward)

    def columns(i, _):
        for j in range(COLUMNS):
            c = plan[COLS_ROW, i * COLUMNS + j]
            g, u, h = gate_acc[c], up_acc[c], hg_acc[c]
            s = lax.logistic(g)
            silu = g * s
            acts[c] = (h * u * s * (1.0 + g * (1.0 - s))).astype(jnp.bfloat16)
            acts[A + c] = (h * silu).astype(jnp.bfloat16)
            acts[2 * A + c] = (silu * u).astype(jnp.bfloat16)

    lax.fori_loop(0, (plan[HEAD_ROW, HEAD_COLS] + (COLUMNS - 1)) // COLUMNS, columns, None)

    def gradients(e0):
        for k, u in group:
            e = e0 + u
            a, x = acts[k * A + get(k, CIDX, e)], xs[k * sz.room + e]
            grad = dot(a, x, 0, 0) if k == 2 else dot(x, a, 0, 0)
            parts[get(k, PART, e)] = grad.astype(jnp.bfloat16)

    walk(plan, gradients)
    outs = []
    for j, d in enumerate(sz.order):
        ref, at = (far, j) if j < sz.far else (near, j - sz.far)
        outs.append(pltpu.make_async_copy(
            parts.at[pl.ds(sz.place_across(d), sz.keep), sides[1]], ref.at[pl.ds(at * sz.keep, sz.keep)], sems.at[j]))
    outs.append(pltpu.make_async_copy(parts.at[pl.ds(0, sz.blocks), sides[0]], same, sems.at[sz.ring]))
    for c in outs:
        c.start()

    def terms(e0):
        for k, u in group:
            e = e0 + u
            prod = dot(acts[k * A + get(k, CIDX, e)], wbuf[get(k, PART, e)], 1, 0 if k == 2 else 1)
            at = get(k, OIDX, e)
            out_acc[at] = prod + jnp.where(get(k, OWAS, e) == 0, 0.0, out_acc[at])

    walk(plan, terms)

    for s in reversed(range(T)):
        def staged(i, _, s=s):
            stage[s * sz.first + i] = out_acc[plan[LISTS_ROW + 2 * s, i]].astype(jnp.bfloat16)

        lax.fori_loop(0, jnp.minimum(plan[HEAD_ROW, HEAD_LISTS + s], sz.first), staged, None)
        copy = pltpu.make_async_copy(stage.at[pl.ds(s * sz.first, sz.first)], firsts[s], sems.at[sz.ring + 1 + s])
        copy.start()
        outs.append(copy)
    for c in outs:
        c.wait()


def strip_of(sz, at):
    w = jnp.where(at < sz.rbt, at, at - sz.rbt)
    return at < sz.rbt, pl.ds(pl.multiple_of(w * BLK, BLK), BLK)


def prepare_kernel(sz, plan, note, first, outputs, input_grads, strips):
    outputs[...] = jnp.zeros_like(outputs)
    input_grads[...] = jnp.zeros_like(input_grads)

    def step(i, _):
        is_out, cols = strip_of(sz, plan[LISTS_ROW + 1, i])

        @pl.when(is_out)
        def _():
            outputs[:, cols] = first[i]

        @pl.when(jnp.logical_not(is_out))
        def _():
            input_grads[:, cols] = first[i]

    lax.fori_loop(0, jnp.minimum(plan[HEAD_ROW, HEAD_LISTS], sz.first), step, None)

    def pick(i, _):
        is_out, cols = strip_of(sz, note[0, i])

        @pl.when(is_out)
        def _():
            strips[i] = outputs[:, cols]

        @pl.when(jnp.logical_not(is_out))
        def _():
            strips[i] = input_grads[:, cols]

    lax.fori_loop(0, jnp.minimum(note[0, sz.note_n], sz.first), pick, None)


def add_kernel(sz, plan, *refs):
    T = sz.n_tensor
    notes, refs = refs[:T - 1], refs[T - 1:]
    firsts, held_strips, refs = refs[:T - 1], refs[T - 1], refs[T + 2:]
    outputs, input_grads, flag, strips, read_sems, write_sems = refs
    over = plan[HEAD_ROW, HEAD_OVER]
    for note in notes:
        over = jnp.maximum(over, note[0, sz.note_over])
    flag[0] = over

    def move(s, i, back, act):
        is_out, cols = strip_of(sz, notes[s][0, i])
        for ref, here in ((outputs, is_out), (input_grads, jnp.logical_not(is_out))):
            @pl.when(here)
            def _(ref=ref):
                there = ref.at[:, cols]
                if back:
                    act(pltpu.make_async_copy(strips.at[i], there, write_sems.at[i]))
                else:
                    act(pltpu.make_async_copy(there, strips.at[i], read_sems.at[i]))

    def loop(s, body):
        lax.fori_loop(0, jnp.minimum(notes[s][0, sz.note_n], sz.first), lambda i, _: body(i), None)

    for s in range(T - 1):
        if s:
            loop(s, lambda i: move(s, i, False, lambda c: c.start()))

        def step(i):
            if s:
                move(s, i, False, lambda c: c.wait())
            held = strips[i] if s else held_strips[i]
            value = held.astype(jnp.float32) + firsts[s][i].astype(jnp.float32)
            strips[i] = value.astype(jnp.bfloat16)
            move(s, i, True, lambda c: c.start())

        loop(s, step)
        loop(s, lambda i: move(s, i, True, lambda c: c.wait()))


def last_kernel(sz, plan, *refs):
    mine, theirs, grads = refs[:3], refs[3:6], refs[6:]
    core = plan[HEAD_ROW, HEAD_CORE]
    for k in range(3):
        for a in range(sz.nb):
            at = plan[MINE_ROW, k * sz.nb + a]
            p = jnp.minimum(jnp.maximum(at - 1, 0), sz.keep - 1)
            for terms, c in ((mine, core), (theirs, 1 - core)):
                value = sum(t[p].astype(jnp.float32) for t in terms)
                rows = pl.ds(pl.multiple_of(c * ROWS, ROWS), ROWS)
                grads[k][0, a, rows] = jnp.where(at > 0, value, 0.0).astype(jnp.bfloat16)


def spec(space):
    return pl.BlockSpec(memory_space=space)


ANY, HBM, VMEM, SMEM = pl.ANY, pltpu.HBM, pltpu.VMEM, pltpu.SMEM


def cost(flops, moved):
    return pl.CostEstimate(flops=flops, bytes_accessed=moved, transcendentals=0)


def call_plan(sz, own, mine, theirs):
    return pl.pallas_call(
        functools.partial(plan_kernel, sz),
        out_shape=[
            jax.ShapeDtypeStruct((sz.plan_rows, sz.lanes), jnp.int32),
            halves(sz.keep),
        ] + [jax.ShapeDtypeStruct((1, sz.lanes), jnp.int32)] * (sz.n_tensor - 1),
        in_specs=[spec(VMEM)] + [spec(ANY)] * 6,
        out_specs=[spec(VMEM), spec(ANY)] + [spec(VMEM)] * (sz.n_tensor - 1),
        scratch_shapes=[pltpu.SemaphoreType.DMA((2 * sz.owned,))],
        compiler_params=pltpu.CompilerParams(vmem_limit_bytes=SMALL),
        cost_estimate=cost(1_000_000, 4_000_000),
        name="plan",
    )(own, *mine, *theirs)


def call_turn(handed, arrived):
    return pl.pallas_call(
        lambda *_: None,
        out_shape=[jax.ShapeDtypeStruct(x.shape, x.dtype) for x in handed],
        in_specs=[spec(ANY)] * (len(handed) + len(arrived)),
        out_specs=[spec(ANY)] * len(handed),
        input_output_aliases={i: i for i in range(len(handed))},
        compiler_params=pltpu.CompilerParams(vmem_limit_bytes=SMALL),
        cost_estimate=cost(1000, 1000),
        name="turn",
    )(*handed, *arrived)


def blocks(n):
    return jax.ShapeDtypeStruct((n, BLK, BLK), jnp.bfloat16)


def halves(n):
    return jax.ShapeDtypeStruct((n, ROWS, BLK), jnp.bfloat16)


def held(scratch):
    return sum(s[0] * s[1] * s[2] * jnp.dtype(t).itemsize for s, t in scratch) + 2 * 1024 * 1024


def call_compute(sz, plan, tokens, cot, chunks):
    bf, f32 = jnp.bfloat16, jnp.float32
    T, A = sz.n_tensor, sz.slots + 1
    out_shape = [halves(sz.ring * sz.keep), halves(sz.far * sz.keep), halves((sz.ring - sz.far) * sz.keep)]
    out_shape += [blocks(sz.first)] * T
    scratch = [
        ((3 * sz.room, sz.tok, BLK), bf),
        ((sz.blocks + 1, BLK, BLK), bf),
        ((sz.blocks + 1, BLK, BLK), bf),
        ((A, sz.tok, BLK), f32),
        ((A, sz.tok, BLK), f32),
        ((A, sz.tok, BLK), f32),
        ((3 * A, sz.tok, BLK), bf),
        ((sz.all + 1, sz.tok, BLK), f32),
        ((T * sz.first, sz.tok, BLK), bf),
    ]
    return pl.pallas_call(
        functools.partial(compute_kernel, sz),
        out_shape=out_shape,
        in_specs=[spec(SMEM)] + [spec(HBM)] * 2 + [spec(ANY)] * len(chunks),
        out_specs=[spec(ANY)] * len(out_shape),
        scratch_shapes=[pltpu.VMEM(s, t) for s, t in scratch] + [
            pltpu.SemaphoreType.DMA((3 * sz.room,)),
            pltpu.SemaphoreType.DMA((max(len(chunks), sz.ring + 1 + T),)),
        ],
        compiler_params=pltpu.CompilerParams(vmem_limit_bytes=held(scratch)),
        cost_estimate=cost(1_000_000_000, 20_000_000),
        name="compute",
    )(plan, pltpu.with_memory_space_constraint(tokens, HBM), pltpu.with_memory_space_constraint(cot, HBM), *chunks)


def call_prepare(sz, plan, note, first):
    half = jax.ShapeDtypeStruct((sz.tok, sz.width // sz.n_tensor), jnp.bfloat16)
    return pl.pallas_call(
        functools.partial(prepare_kernel, sz),
        out_shape=[half, half, blocks(sz.first)],
        in_specs=[spec(SMEM), spec(SMEM), spec(VMEM)],
        out_specs=[spec(VMEM)] * 3,
        compiler_params=pltpu.CompilerParams(vmem_limit_bytes=12 * 1024 * 1024),
        cost_estimate=cost(1_000_000, 6_000_000),
        name="prepare",
    )(plan, note, first)


def call_add(sz, plan, notes, firsts, strips, partial):
    n = 2 + len(notes) + len(firsts)
    return pl.pallas_call(
        functools.partial(add_kernel, sz),
        out_shape=[jax.ShapeDtypeStruct(p.shape, p.dtype) for p in partial] + [jax.ShapeDtypeStruct((1,), jnp.int32)],
        in_specs=[spec(SMEM)] * (1 + len(notes)) + [spec(VMEM)] * (len(firsts) + 1) + [spec(ANY)] * 2,
        out_specs=[spec(ANY)] * 2 + [spec(SMEM)],
        input_output_aliases={n: 0, n + 1: 1},
        scratch_shapes=[
            pltpu.VMEM((sz.first, sz.tok, BLK), jnp.bfloat16),
            pltpu.SemaphoreType.DMA((sz.first,)),
            pltpu.SemaphoreType.DMA((sz.first,)),
        ],
        compiler_params=pltpu.CompilerParams(vmem_limit_bytes=12 * 1024 * 1024),
        cost_estimate=cost(1_000_000, 3_000_000),
        name="add",
    )(plan, *notes, *firsts, strips, *partial)


def call_last(sz, plan, terms):
    out = jax.ShapeDtypeStruct((1, sz.nb, BLK, BLK), jnp.bfloat16)
    return pl.pallas_call(
        functools.partial(last_kernel, sz),
        out_shape=[out] * 3,
        in_specs=[spec(SMEM)] + [spec(VMEM)] * len(terms),
        out_specs=[spec(VMEM)] * 3,
        compiler_params=pltpu.CompilerParams(vmem_limit_bytes=SMALL),
        cost_estimate=cost(1_000_000, 1_000_000),
        name="last",
    )(plan, *terms)


def across(pairs):
    return [(i, j ^ 1) for i, j in pairs]


def gather_chunks(sz, chunk):
    ahead, behind, swap = permutations(sz)
    same = {0: chunk}
    a = b = chunk
    for s in range(1, sz.top):
        a, b = lax.ppermute(a, "fsdp", ahead), lax.ppermute(b, "fsdp", behind)
        same[sz.ring - s], same[s] = a, b
    other = {d: lax.ppermute(same[d], "fsdp", swap) for d in same}
    same[sz.top] = lax.ppermute(a, "fsdp", ahead)
    other[sz.top] = lax.ppermute(a, "fsdp", across(ahead))
    return [side[d] for side in (same, other) for d in sz.order]


def reduce_parts(sz, same, far, near, notes, prepare, sent):
    ahead, behind, swap = permutations(sz)
    keep = sz.keep
    far = lax.ppermute(far, "fsdp", swap)
    near = lax.ppermute(call_turn([near], [far])[0], "fsdp", swap)

    def term(d, *more):
        j = sz.order.index(d)
        pair = far[j * keep:(j + 1) * keep] if j < sz.far else near[(j - sz.far) * keep:][:keep]
        out = same[j * keep:(j + 1) * keep].astype(jnp.float32) + pair.astype(jnp.float32)
        for m in more:
            out = out + m.astype(jnp.float32)
        return out.astype(jnp.bfloat16)

    a, b = lax.optimization_barrier((term(sz.top), term(sz.top + 1)))
    here = term(0)
    here_across = lax.ppermute(here, "fsdp", swap)
    prepared = prepare(here_across)
    for s in range(1, sz.top):
        last_b = b
        a, b = lax.ppermute(a, "fsdp", ahead), lax.ppermute(b, "fsdp", behind)
        if s == 1:
            a, b = call_turn([a, b], notes)
        else:
            a = call_turn([a], [last_b] + (list(prepared[2:]) if s == 2 else sent))[0]
        a = term(sz.top - s, a)
        if s + 1 < sz.top:
            b = term(sz.top + 1 + s, call_turn([b], [a])[0])
    mine = [here, lax.ppermute(a, "fsdp", ahead), b]
    theirs = [
        here_across,
        lax.ppermute(a, "fsdp", across(ahead)),
        lax.ppermute(last_b, "fsdp", across(behind)),
    ]
    return mine + theirs, prepared


def program(sz, own, tokens, cotangent, mine):
    T = sz.n_tensor
    swap = permutations(sz)[-1]
    theirs = [lax.ppermute(b, "fsdp", swap) for b in mine]
    plan, chunk, *notes = call_plan(sz, own, mine, theirs)

    def exchange(array, s):
        return lax.ppermute(array, "tensor", [(i, (i + s) % T) for i in range(T)])

    notes = [exchange(note, s) for s, note in enumerate(notes, 1)]
    chunks = gather_chunks(sz, chunk)
    same, far, near, *firsts = call_compute(sz, plan, tokens, cotangent, chunks)

    def prepare(after):
        return call_prepare(sz, plan, notes[0], call_turn([firsts[0]], [after])[0])

    sent = [exchange(firsts[s], s) for s in range(1, T)]
    terms, (*partial, strips) = reduce_parts(sz, same, far, near, notes, prepare, sent)
    sent = call_turn(sent, [terms[2], terms[5]])
    outputs, input_grads, flag = call_add(sz, plan, notes, sent, strips, partial)
    return (outputs, input_grads, *call_last(sz, plan, terms)), flag


def shards(
    tokens,
    cotangent,
    gate_blocks,
    up_blocks,
    down_blocks,
    gate_where,
    up_where,
    down_where,
    block_counts,
):
    n_fsdp, n_tensor = lax.axis_size("fsdp"), lax.axis_size("tensor")
    f, rank = lax.axis_index("fsdp"), lax.axis_index("tensor")
    slots = gate_where.shape[1]
    full = Sizes(tokens, gate_blocks, slots, n_fsdp, n_tensor, False)
    own = jnp.concatenate([
        gate_where[0], up_where[0], down_where[0], block_counts[:, 0],
        f.astype(jnp.int32)[None], rank.astype(jnp.int32)[None]])
    own = jnp.pad(own, (0, full.lanes - own.shape[0]))[None]
    blocks_in = (gate_blocks, up_blocks, down_blocks)
    if slots >= full.cb:
        return program(full, own, tokens, cotangent, blocks_in)[0]
    lean = Sizes(tokens, gate_blocks, slots, n_fsdp, n_tensor, True)
    outs, flag = program(lean, own, tokens, cotangent, blocks_in)
    return lax.cond(
        flag[0] > 0,
        lambda outs, *args: program(full, *args)[0],
        lambda outs, *args: outs,
        outs, own, tokens, cotangent, blocks_in)


def solution(mesh):
    placed = (
        P("fsdp", None),
        P("fsdp", None),
        P("tensor", "fsdp", None, None),
        P("tensor", "fsdp", None, None),
        P("tensor", "fsdp", None, None),
        P("tensor", None),
        P("tensor", None),
        P("tensor", None),
        P(None, "tensor"),
    )
    return jax.shard_map(
        shards,
        mesh=mesh,
        in_specs=placed,
        out_specs=(
            P("fsdp", "tensor"),
            P("fsdp", "tensor"),
            P("tensor", "fsdp", None, None),
            P("tensor", "fsdp", None, None),
            P("tensor", "fsdp", None, None),
        ),
        check_vma=False,
    )
```

```python
import functools

import jax
import jax.numpy as jnp
from jax import lax
from jax.experimental import pallas as pl
from jax.experimental.pallas import tpu as pltpu
from jax.sharding import PartitionSpec as P

FF = 14336
BLK = 128
GROUP = 8
COLUMNS = 4
FIRST_SEND = 18
LEAN_SLOTS = 7
ROWS = BLK // 2
SMALL = 4 * 1024 * 1024
PART, STRIP, CIDX, CWAS, OIDX, OWAS = range(6)
FIELDS = 6
COLS_ROW = 3 * FIELDS
HEAD_ROW = COLS_ROW + 1
MINE_ROW = COLS_ROW + 2
LISTS_ROW = COLS_ROW + 3
HEAD_COLS, HEAD_OVER, HEAD_CORE, HEAD_LISTS = 3, 4, 5, 8


class Sizes:
    def __init__(self, tokens, gate_blocks, slots, n_fsdp, n_tensor, lean):
        self.tok, self.width = tokens.shape
        self.n_fsdp, self.n_tensor = n_fsdp, n_tensor
        self.rb = self.width // BLK
        self.cb = FF // (BLK * n_tensor)
        self.slots = slots
        self.all = 3 * slots
        self.lanes = -(-(self.all + GROUP) // 128) * 128
        self.nb = gate_blocks.shape[1]
        self.owned = 3 * self.nb
        self.ring = n_fsdp // 2
        self.top = self.ring // 2
        self.rbt = self.rb // n_tensor
        self.order = [self.top]
        for d in range(1, self.top):
            self.order += [self.top + d, self.top - d]
        self.order.append(0)
        self.far = min(2, self.ring - 1)
        self.keep = min(LEAN_SLOTS, 2 * self.owned) if lean else 2 * self.owned
        self.send_all = 2 * self.rbt
        self.first = min(FIRST_SEND, self.send_all) if lean else self.send_all
        self.blocks = self.ring * self.keep
        self.plan_rows = -(-(LISTS_ROW + 2 * n_tensor) // 8) * 8
        self.note_n, self.note_over = self.lanes - 1, self.lanes - 2
        self.room = slots + GROUP

    def place(self, d):
        return self.order.index(d) * self.keep

    def place_across(self, d):
        return self.place((self.ring - d) % self.ring)


def permutations(sz):
    seq = list(range(0, sz.ring, 2)) + list(range(sz.ring - 1, 0, -2))
    ahead, behind, swap = [], [], []
    for i, q in enumerate(seq):
        up, down = seq[(i + 1) % sz.ring], seq[i - 1]
        ahead += [(q * 2, up * 2), (q * 2 + 1, down * 2 + 1)]
        behind += [(q * 2, down * 2), (q * 2 + 1, up * 2 + 1)]
        swap += [(q * 2, q * 2 + 1), (q * 2 + 1, q * 2)]
    return ahead, behind, swap


def ratio(x, d):
    return jnp.floor((x + 0.5) * (1.0 / d))


def rest_of(x, d):
    return x - d * ratio(x, d)


def ring_position(sz, chip):
    return jnp.where(rest_of(chip, 2) == 0, ratio(chip, 2), sz.ring - 1 - ratio(chip, 2))


class Marks:
    def __init__(self, sz, own):
        N, L, S = sz.all, sz.lanes, sz.slots
        f32 = jnp.float32
        self.sz = sz
        self.sub = lax.broadcasted_iota(jnp.int32, (N, L), 0)
        self.lane = lax.broadcasted_iota(jnp.int32, (N, L), 1)
        self.same = self.sub == self.lane
        sub_c = self.sub[:, :1].astype(f32)
        lane_r = lax.broadcasted_iota(jnp.int32, (1, L), 1).astype(f32)
        self.sub_c, self.lane_r = sub_c, lane_r
        raw_r = own[...].astype(f32)

        def single(row, at):
            return jnp.sum(jnp.where(lane_r == at, row, 0.0), axis=1, keepdims=True)

        self.f, self.rank = single(raw_r, N + 3), single(raw_r, N + 4)

        def kind(x):
            return (x >= S).astype(f32) + (x >= 2 * S).astype(f32)

        self.kind_c, self.kind_r = kind(sub_c), kind(lane_r)
        self.n_r = lane_r - S * self.kind_r
        self.n_c = sub_c - S * self.kind_c
        limit = jnp.zeros((1, L), f32)
        for k in range(3):
            limit = limit + jnp.where(self.kind_r == k, single(raw_r, N + k), 0.0)
        live_r = jnp.where((lane_r < N) & (self.n_r < limit), 1.0, 0.0)
        w_c = self.col(raw_r)
        live_c = self.col(live_r)

        def place(w, k):
            gate, down = ratio(w, sz.cb), ratio(w, sz.rb)
            is_down = k == 2
            return jnp.where(is_down, w - down * sz.rb, gate), jnp.where(is_down, down, w - gate * sz.cb)

        self.row_c, col_c = place(w_c, self.kind_c)
        self.row_r, col_r = place(raw_r, self.kind_r)
        self.chip_c, chip_r = ratio(self.n_c, 2 * sz.nb), ratio(self.n_r, 2 * sz.nb)
        self.same_chip = (self.chip_c == chip_r).astype(f32)
        self.same_col = (col_c == col_r).astype(f32)
        act_c, act_r = live_c, live_r
        for k in range(3):
            lanes = self.same_col * (live_r * (self.kind_r == k).astype(f32))
            act_c = act_c * jnp.max(lanes, axis=1, keepdims=True)
            subs = self.same_col * (live_c * (self.kind_c == k).astype(f32))
            act_r = act_r * jnp.max(subs, axis=0, keepdims=True)
        self.act_c, self.act_r = act_c, act_r
        out_c = jnp.where(self.kind_c == 2, 0.0, f32(sz.rb)) + self.row_c
        out_r = jnp.where(self.kind_r == 2, 0.0, f32(sz.rb)) + self.row_r
        self.same_out = (out_c == out_r).astype(f32)
        self.before = (self.lane < self.sub).astype(f32)
        self.after = (self.sub < self.lane).astype(f32)
        self.owas_c = jnp.max(self.same_out * self.before * act_r, axis=1, keepdims=True)
        self.owas_r = jnp.max(self.same_out * self.after * act_c, axis=0, keepdims=True)
        self.lead_c = act_c * (1.0 - self.owas_c)
        self.lead_r = act_r * (1.0 - self.owas_r)

        def shift(row):
            away = ratio(row, sz.rbt) - self.rank
            return jnp.where(away < 0, away + sz.n_tensor, away)

        self.shift_c, self.shift_r = shift(self.row_c), shift(self.row_r)
        self.local_c = jnp.where(self.kind_c == 2, 0.0, f32(sz.rbt)) + rest_of(self.row_c, sz.rbt)

    def col(self, row):
        return jnp.sum(jnp.where(self.same, row, 0.0), axis=1, keepdims=True)

    def carried(self):
        sz = self.sz
        rank = jnp.sum(self.before * self.same_chip * self.act_r, axis=1, keepdims=True)
        away = ring_position(sz, self.chip_c) - ring_position(sz, ratio(self.f, 2))
        away = jnp.where(rest_of(self.f, 2) == 0, away, -away)
        rel = jnp.where(away < 0, away + sz.ring, away)
        j = jnp.where(rel > sz.top, 2 * (rel - sz.top) - 1, 2 * (sz.top - rel))
        return rank, jnp.where(rel == 0, sz.ring - 1.0, j)

    def ranks(self, chosen_r):
        return jnp.sum(self.before * chosen_r, axis=1, keepdims=True)

    def listed(self, chosen_c, rank_c, value_c, lo=0, hi=None):
        at = rank_c[lo:hi] == self.lane[lo:hi].astype(jnp.float32)
        return jnp.sum(jnp.where(at, chosen_c[lo:hi] * value_c[lo:hi], 0.0), axis=0, keepdims=True)

    def most_on_chip(self):
        return jnp.max(jnp.sum(self.same_chip * self.act_r, axis=1, keepdims=True), axis=0, keepdims=True)


def total(x):
    return jnp.sum(x, axis=0, keepdims=True)


def head_row(sz, entries):
    lane = lax.broadcasted_iota(jnp.int32, (1, sz.lanes), 1)
    row = jnp.zeros((1, sz.lanes), jnp.float32)
    for i, value in entries:
        row = jnp.where(lane == i, value, row)
    return row


def plan_kernel(sz, own, *refs):
    mine, theirs, (plan, chunk, *notes, sems) = refs[:3], refs[3:6], refs[6:]
    S, N = sz.slots, sz.all
    m = Marks(sz, own)
    f32 = jnp.float32
    lane_r, sub_c = m.lane_r, m.sub_c
    pos_c, base_c = m.carried()
    core = rest_of(m.f, 2)
    half = pl.ds(pl.multiple_of(jnp.max(core).astype(jnp.int32) * ROWS, ROWS), ROWS)

    pair = jnp.where(core == 0, m.f + 1, m.f - 1)
    i_r = rest_of(lane_r, sz.owned)
    owner_r = jnp.where(lane_r < sz.owned, m.f, pair)
    slot_r = ratio(i_r, sz.nb) * S + owner_r * sz.nb + rest_of(i_r, sz.nb)
    at_r = jnp.sum(jnp.where(sub_c == slot_r, m.act_c * (pos_c + 1.0), 0.0), axis=0, keepdims=True)
    copies = []
    for i in range(2 * sz.owned):
        side, k, a = i // sz.owned, i % sz.owned // sz.nb, i % sz.nb
        at = jnp.max(jnp.where(lane_r == i, at_r, 0.0)).astype(jnp.int32)
        fits = (at > 0) & (at <= sz.keep)
        place = jnp.minimum(jnp.maximum(at - 1, 0), sz.keep - 1)
        copy = pltpu.make_async_copy((mine, theirs)[side][k].at[0, a, half], chunk.at[place], sems.at[i])
        copies.append((fits, copy))
    for fits, copy in copies:
        pl.when(fits)(copy.start)

    same_kind = (m.kind_c == m.kind_r).astype(f32)
    rank_c = jnp.sum(m.before * same_kind * m.act_r, axis=1, keepdims=True)
    cwas_c = jnp.max(m.before * same_kind * m.same_col * m.act_r, axis=1, keepdims=True)
    cwas_r = jnp.max(m.after * same_kind * m.same_col * m.act_c, axis=0, keepdims=True)
    big = f32(4 * N)
    lanes_f = m.lane.astype(f32)
    gates_r = m.act_r * (m.kind_r == 0).astype(f32)
    cidx_c = jnp.min(jnp.where(m.same_col * gates_r > 0, lanes_f, big), axis=1, keepdims=True)
    oidx_c = jnp.min(jnp.where(m.same_out * m.act_r > 0, lanes_f, big), axis=1, keepdims=True)
    rank_r = jnp.sum(m.after * same_kind * m.act_c, axis=0, keepdims=True)
    turn_c = ratio(rank_c, GROUP) * 3 + m.kind_c
    turn_r = ratio(rank_r, GROUP) * 3 + m.kind_r
    ahead = ((turn_r < turn_c) | ((turn_r == turn_c) & (rank_r < rank_c))).astype(f32)
    owas_c = jnp.max(m.same_out * ahead * m.act_r, axis=1, keepdims=True)
    part_c = jnp.where(pos_c < sz.keep, base_c * sz.keep + pos_c, f32(sz.blocks))
    fields = [(part_c, sz.blocks), (m.row_c, 0), (cidx_c, S), (cwas_c, 0), (oidx_c, N), (owas_c, 0)]
    rows = []
    head = []
    for k in range(3):
        lo, hi = k * S, (k + 1) * S
        n_k = total(m.act_c[lo:hi])
        head.append((k, n_k))
        for value, spare in fields:
            row = m.listed(m.act_c, rank_c, value, lo, hi)
            rows.append(jnp.where(lane_r < n_k, row, f32(spare)))
    leader_c = m.act_c * (1.0 - cwas_c) * (m.kind_c == 0).astype(f32)
    leader_r = m.act_r * (1.0 - cwas_r) * (m.kind_r == 0).astype(f32)
    n_cols = total(leader_c)
    cols = m.listed(leader_c, m.ranks(leader_r), sub_c, 0, S)
    rows.append(jnp.where(lane_r < n_cols, cols, f32(S)))
    head.append((HEAD_COLS, n_cols))
    lists, sent = [], []
    over = (m.most_on_chip() > sz.keep).astype(f32)
    for s in range(sz.n_tensor):
        chosen_c = m.lead_c * (m.shift_c == s).astype(f32)
        chosen_r = m.lead_r * (m.shift_r == s).astype(f32)
        rank = m.ranks(chosen_r)
        lists.append(m.listed(chosen_c, rank, sub_c))
        lists.append(m.listed(chosen_c, rank, m.local_c))
        n = total(chosen_c)
        head.append((HEAD_LISTS + s, n))
        sent.append(n)
        over = jnp.maximum(over, (n > sz.first).astype(f32))
    head += [(HEAD_OVER, over), (HEAD_CORE, core)]
    for s in range(1, sz.n_tensor):
        note = jnp.where(lane_r == sz.note_n, sent[s], lists[2 * s + 1])
        notes[s - 1][...] = jnp.where(lane_r == sz.note_over, over, note).astype(jnp.int32)
    rows.append(head_row(sz, head))
    rows.append(at_r)
    rows += lists
    for i, row in enumerate(rows):
        plan[i:i + 1, :] = row.astype(jnp.int32)
    for fits, copy in copies:
        pl.when(fits)(copy.wait)


def dot(a, b, ca, cb):
    return lax.dot_general(a, b, (((ca,), (cb,)), ((), ())), preferred_element_type=jnp.float32)


def field(sz, plan, k, j, e):
    return plan[k * FIELDS + j, e]


def walk(plan, body):
    most = jnp.maximum(jnp.maximum(plan[HEAD_ROW, 0], plan[HEAD_ROW, 1]), plan[HEAD_ROW, 2])
    lax.fori_loop(0, (most + (GROUP - 1)) // GROUP, lambda p, _: body(p * GROUP), None)


def each(plan, k, body):
    lax.fori_loop(0, plan[HEAD_ROW, k], lambda e, _: body(e), None)


def compute_kernel(sz, plan, tokens, cot, *refs):
    n_chunks, T = 2 * sz.ring, sz.n_tensor
    chunks, refs = refs[:n_chunks], refs[n_chunks:]
    same, far, near = refs[:3]
    firsts, refs = refs[3:3 + T], refs[3 + T:]
    xs, wbuf, parts, gate_acc, up_acc, hg_acc, acts, out_acc, stage, strip_sems, sems = refs
    A = sz.slots + 1
    get = functools.partial(field, sz, plan)

    def strip_copy(k, e):
        src = cot if k == 2 else tokens
        cols = pl.ds(pl.multiple_of(get(k, STRIP, e) * BLK, BLK), BLK)
        return pltpu.make_async_copy(src.at[:, cols], xs.at[k * sz.room + e], strip_sems.at[k * sz.room + e])

    core = plan[HEAD_ROW, HEAD_CORE]
    sides = [pl.ds(pl.multiple_of(c * ROWS, ROWS), ROWS) for c in (core, 1 - core)]
    loads = []
    for side, place in enumerate((sz.place, sz.place_across)):
        for d in sz.order:
            i = len(loads)
            there = wbuf.at[pl.ds(place(d), sz.keep), sides[side]]
            loads.append(pltpu.make_async_copy(chunks[i], there, sems.at[i]))
    for k in range(3):
        each(plan, k, lambda e, k=k: strip_copy(k, e).start())
    for c in loads:
        c.start()
    for k in range(3):
        each(plan, k, lambda e, k=k: strip_copy(k, e).wait())
    for c in loads:
        c.wait()

    group = [(k, u) for k in range(3) for u in range(GROUP)]

    def forward(e0):
        for k, u in group:
            e, acc = e0 + u, (gate_acc, up_acc, hg_acc)[k]
            prod = dot(xs[k * sz.room + e], wbuf[get(k, PART, e)], 1, 1 if k == 2 else 0)
            c = get(k, CIDX, e)
            acc[c] = prod + jnp.where(get(k, CWAS, e) == 0, 0.0, acc[c])

    walk(plan, forward)

    def columns(i, _):
        for j in range(COLUMNS):
            c = plan[COLS_ROW, i * COLUMNS + j]
            g, u, h = gate_acc[c], up_acc[c], hg_acc[c]
            s = lax.logistic(g)
            silu = g * s
            acts[c] = (h * u * s * (1.0 + g * (1.0 - s))).astype(jnp.bfloat16)
            acts[A + c] = (h * silu).astype(jnp.bfloat16)
            acts[2 * A + c] = (silu * u).astype(jnp.bfloat16)

    lax.fori_loop(0, (plan[HEAD_ROW, HEAD_COLS] + (COLUMNS - 1)) // COLUMNS, columns, None)

    def gradients(e0):
        for k, u in group:
            e = e0 + u
            a, x = acts[k * A + get(k, CIDX, e)], xs[k * sz.room + e]
            grad = dot(a, x, 0, 0) if k == 2 else dot(x, a, 0, 0)
            parts[get(k, PART, e)] = grad.astype(jnp.bfloat16)

    walk(plan, gradients)
    outs = []
    for j, d in enumerate(sz.order):
        ref, at = (far, j) if j < sz.far else (near, j - sz.far)
        outs.append(pltpu.make_async_copy(
            parts.at[pl.ds(sz.place_across(d), sz.keep), sides[1]], ref.at[pl.ds(at * sz.keep, sz.keep)], sems.at[j]))
    outs.append(pltpu.make_async_copy(parts.at[pl.ds(0, sz.blocks), sides[0]], same, sems.at[sz.ring]))
    for c in outs:
        c.start()

    def terms(e0):
        for k, u in group:
            e = e0 + u
            prod = dot(acts[k * A + get(k, CIDX, e)], wbuf[get(k, PART, e)], 1, 0 if k == 2 else 1)
            at = get(k, OIDX, e)
            out_acc[at] = prod + jnp.where(get(k, OWAS, e) == 0, 0.0, out_acc[at])

    walk(plan, terms)

    for s in reversed(range(T)):
        def staged(i, _, s=s):
            stage[s * sz.first + i] = out_acc[plan[LISTS_ROW + 2 * s, i]].astype(jnp.bfloat16)

        lax.fori_loop(0, jnp.minimum(plan[HEAD_ROW, HEAD_LISTS + s], sz.first), staged, None)
        copy = pltpu.make_async_copy(stage.at[pl.ds(s * sz.first, sz.first)], firsts[s], sems.at[sz.ring + 1 + s])
        copy.start()
        outs.append(copy)
    for c in outs:
        c.wait()


def strip_of(sz, at):
    w = jnp.where(at < sz.rbt, at, at - sz.rbt)
    return at < sz.rbt, pl.ds(pl.multiple_of(w * BLK, BLK), BLK)


def prepare_kernel(sz, plan, note, first, outputs, input_grads, strips):
    outputs[...] = jnp.zeros_like(outputs)
    input_grads[...] = jnp.zeros_like(input_grads)

    def step(i, _):
        is_out, cols = strip_of(sz, plan[LISTS_ROW + 1, i])

        @pl.when(is_out)
        def _():
            outputs[:, cols] = first[i]

        @pl.when(jnp.logical_not(is_out))
        def _():
            input_grads[:, cols] = first[i]

    lax.fori_loop(0, jnp.minimum(plan[HEAD_ROW, HEAD_LISTS], sz.first), step, None)

    def pick(i, _):
        is_out, cols = strip_of(sz, note[0, i])

        @pl.when(is_out)
        def _():
            strips[i] = outputs[:, cols]

        @pl.when(jnp.logical_not(is_out))
        def _():
            strips[i] = input_grads[:, cols]

    lax.fori_loop(0, jnp.minimum(note[0, sz.note_n], sz.first), pick, None)


def add_kernel(sz, plan, *refs):
    T = sz.n_tensor
    notes, refs = refs[:T - 1], refs[T - 1:]
    firsts, held_strips, refs = refs[:T - 1], refs[T - 1], refs[T + 2:]
    outputs, input_grads, flag, strips, read_sems, write_sems = refs
    over = plan[HEAD_ROW, HEAD_OVER]
    for note in notes:
        over = jnp.maximum(over, note[0, sz.note_over])
    flag[0] = over

    def move(s, i, back, act):
        is_out, cols = strip_of(sz, notes[s][0, i])
        for ref, here in ((outputs, is_out), (input_grads, jnp.logical_not(is_out))):
            @pl.when(here)
            def _(ref=ref):
                there = ref.at[:, cols]
                if back:
                    act(pltpu.make_async_copy(strips.at[i], there, write_sems.at[i]))
                else:
                    act(pltpu.make_async_copy(there, strips.at[i], read_sems.at[i]))

    def loop(s, body):
        lax.fori_loop(0, jnp.minimum(notes[s][0, sz.note_n], sz.first), lambda i, _: body(i), None)

    for s in range(T - 1):
        if s:
            loop(s, lambda i: move(s, i, False, lambda c: c.start()))

        def step(i):
            if s:
                move(s, i, False, lambda c: c.wait())
            held = strips[i] if s else held_strips[i]
            value = held.astype(jnp.float32) + firsts[s][i].astype(jnp.float32)
            strips[i] = value.astype(jnp.bfloat16)
            move(s, i, True, lambda c: c.start())

        loop(s, step)
        loop(s, lambda i: move(s, i, True, lambda c: c.wait()))


def last_kernel(sz, plan, *refs):
    mine, theirs, grads = refs[:3], refs[3:6], refs[6:]
    core = plan[HEAD_ROW, HEAD_CORE]
    for k in range(3):
        for a in range(sz.nb):
            at = plan[MINE_ROW, k * sz.nb + a]
            p = jnp.minimum(jnp.maximum(at - 1, 0), sz.keep - 1)
            for terms, c in ((mine, core), (theirs, 1 - core)):
                value = sum(t[p].astype(jnp.float32) for t in terms)
                rows = pl.ds(pl.multiple_of(c * ROWS, ROWS), ROWS)
                grads[k][0, a, rows] = jnp.where(at > 0, value, 0.0).astype(jnp.bfloat16)


def spec(space):
    return pl.BlockSpec(memory_space=space)


ANY, HBM, VMEM, SMEM = pl.ANY, pltpu.HBM, pltpu.VMEM, pltpu.SMEM


def cost(flops, moved):
    return pl.CostEstimate(flops=flops, bytes_accessed=moved, transcendentals=0)


def call_plan(sz, own, mine, theirs):
    return pl.pallas_call(
        functools.partial(plan_kernel, sz),
        out_shape=[
            jax.ShapeDtypeStruct((sz.plan_rows, sz.lanes), jnp.int32),
            halves(sz.keep),
        ] + [jax.ShapeDtypeStruct((1, sz.lanes), jnp.int32)] * (sz.n_tensor - 1),
        in_specs=[spec(VMEM)] + [spec(ANY)] * 6,
        out_specs=[spec(VMEM), spec(ANY)] + [spec(VMEM)] * (sz.n_tensor - 1),
        scratch_shapes=[pltpu.SemaphoreType.DMA((2 * sz.owned,))],
        compiler_params=pltpu.CompilerParams(vmem_limit_bytes=SMALL),
        cost_estimate=cost(1_000_000, 4_000_000),
        name="plan",
    )(own, *mine, *theirs)


def call_turn(handed, arrived):
    return pl.pallas_call(
        lambda *_: None,
        out_shape=[jax.ShapeDtypeStruct(x.shape, x.dtype) for x in handed],
        in_specs=[spec(ANY)] * (len(handed) + len(arrived)),
        out_specs=[spec(ANY)] * len(handed),
        input_output_aliases={i: i for i in range(len(handed))},
        compiler_params=pltpu.CompilerParams(vmem_limit_bytes=SMALL),
        cost_estimate=cost(1000, 1000),
        name="turn",
    )(*handed, *arrived)


def blocks(n):
    return jax.ShapeDtypeStruct((n, BLK, BLK), jnp.bfloat16)


def halves(n):
    return jax.ShapeDtypeStruct((n, ROWS, BLK), jnp.bfloat16)


def held(scratch):
    return sum(s[0] * s[1] * s[2] * jnp.dtype(t).itemsize for s, t in scratch) + 2 * 1024 * 1024


def call_compute(sz, plan, tokens, cot, chunks):
    bf, f32 = jnp.bfloat16, jnp.float32
    T, A = sz.n_tensor, sz.slots + 1
    out_shape = [halves(sz.ring * sz.keep), halves(sz.far * sz.keep), halves((sz.ring - sz.far) * sz.keep)]
    out_shape += [blocks(sz.first)] * T
    scratch = [
        ((3 * sz.room, sz.tok, BLK), bf),
        ((sz.blocks + 1, BLK, BLK), bf),
        ((sz.blocks + 1, BLK, BLK), bf),
        ((A, sz.tok, BLK), f32),
        ((A, sz.tok, BLK), f32),
        ((A, sz.tok, BLK), f32),
        ((3 * A, sz.tok, BLK), bf),
        ((sz.all + 1, sz.tok, BLK), f32),
        ((T * sz.first, sz.tok, BLK), bf),
    ]
    return pl.pallas_call(
        functools.partial(compute_kernel, sz),
        out_shape=out_shape,
        in_specs=[spec(SMEM)] + [spec(HBM)] * 2 + [spec(ANY)] * len(chunks),
        out_specs=[spec(ANY)] * len(out_shape),
        scratch_shapes=[pltpu.VMEM(s, t) for s, t in scratch] + [
            pltpu.SemaphoreType.DMA((3 * sz.room,)),
            pltpu.SemaphoreType.DMA((max(len(chunks), sz.ring + 1 + T),)),
        ],
        compiler_params=pltpu.CompilerParams(vmem_limit_bytes=held(scratch)),
        cost_estimate=cost(1_000_000_000, 20_000_000),
        name="compute",
    )(plan, pltpu.with_memory_space_constraint(tokens, HBM), pltpu.with_memory_space_constraint(cot, HBM), *chunks)


def call_prepare(sz, plan, note, first):
    half = jax.ShapeDtypeStruct((sz.tok, sz.width // sz.n_tensor), jnp.bfloat16)
    return pl.pallas_call(
        functools.partial(prepare_kernel, sz),
        out_shape=[half, half, blocks(sz.first)],
        in_specs=[spec(SMEM), spec(SMEM), spec(VMEM)],
        out_specs=[spec(VMEM)] * 3,
        compiler_params=pltpu.CompilerParams(vmem_limit_bytes=12 * 1024 * 1024),
        cost_estimate=cost(1_000_000, 6_000_000),
        name="prepare",
    )(plan, note, first)


def call_add(sz, plan, notes, firsts, strips, partial):
    n = 2 + len(notes) + len(firsts)
    return pl.pallas_call(
        functools.partial(add_kernel, sz),
        out_shape=[jax.ShapeDtypeStruct(p.shape, p.dtype) for p in partial] + [jax.ShapeDtypeStruct((1,), jnp.int32)],
        in_specs=[spec(SMEM)] * (1 + len(notes)) + [spec(VMEM)] * (len(firsts) + 1) + [spec(ANY)] * 2,
        out_specs=[spec(ANY)] * 2 + [spec(SMEM)],
        input_output_aliases={n: 0, n + 1: 1},
        scratch_shapes=[
            pltpu.VMEM((sz.first, sz.tok, BLK), jnp.bfloat16),
            pltpu.SemaphoreType.DMA((sz.first,)),
            pltpu.SemaphoreType.DMA((sz.first,)),
        ],
        compiler_params=pltpu.CompilerParams(vmem_limit_bytes=12 * 1024 * 1024),
        cost_estimate=cost(1_000_000, 3_000_000),
        name="add",
    )(plan, *notes, *firsts, strips, *partial)


def call_last(sz, plan, terms):
    out = jax.ShapeDtypeStruct((1, sz.nb, BLK, BLK), jnp.bfloat16)
    return pl.pallas_call(
        functools.partial(last_kernel, sz),
        out_shape=[out] * 3,
        in_specs=[spec(SMEM)] + [spec(VMEM)] * len(terms),
        out_specs=[spec(VMEM)] * 3,
        compiler_params=pltpu.CompilerParams(vmem_limit_bytes=SMALL),
        cost_estimate=cost(1_000_000, 1_000_000),
        name="last",
    )(plan, *terms)


def across(pairs):
    return [(i, j ^ 1) for i, j in pairs]


def gather_chunks(sz, chunk):
    ahead, behind, swap = permutations(sz)
    same = {0: chunk}
    a = b = chunk
    for s in range(1, sz.top):
        a, b = lax.ppermute(a, "fsdp", ahead), lax.ppermute(b, "fsdp", behind)
        same[sz.ring - s], same[s] = a, b
    other = {d: lax.ppermute(same[d], "fsdp", swap) for d in same}
    same[sz.top] = lax.ppermute(a, "fsdp", ahead)
    other[sz.top] = lax.ppermute(a, "fsdp", across(ahead))
    return [side[d] for side in (same, other) for d in sz.order]


def reduce_parts(sz, same, far, near, exchange_notes, prepare, sent):
    ahead, behind, swap = permutations(sz)
    keep = sz.keep
    far = lax.ppermute(far, "fsdp", swap)
    near = lax.ppermute(call_turn([near], [far])[0], "fsdp", swap)

    def term(d, *more):
        j = sz.order.index(d)
        pair = far[j * keep:(j + 1) * keep] if j < sz.far else near[(j - sz.far) * keep:][:keep]
        out = same[j * keep:(j + 1) * keep].astype(jnp.float32) + pair.astype(jnp.float32)
        for m in more:
            out = out + m.astype(jnp.float32)
        return out.astype(jnp.bfloat16)

    a, b = lax.optimization_barrier((term(sz.top), term(sz.top + 1)))
    here = term(0)
    here_across = lax.ppermute(here, "fsdp", swap)
    for s in range(1, sz.top):
        last_b = b
        a, b = lax.ppermute(a, "fsdp", ahead), lax.ppermute(b, "fsdp", behind)
        if s == 1:
            a, b = call_turn([a, b], [])
        else:
            a = call_turn([a], [last_b] + (notes if s == 2 else sent + list(prepared[2:])))[0]
        a = term(sz.top - s, a)
        if s + 1 < sz.top:
            b = term(sz.top + 1 + s, call_turn([b], [a])[0])
        if s == 1:
            notes = exchange_notes(b)
            prepared = prepare(here_across, notes)
    mine = [here, lax.ppermute(a, "fsdp", ahead), b]
    theirs = [
        here_across,
        lax.ppermute(a, "fsdp", across(ahead)),
        lax.ppermute(last_b, "fsdp", across(behind)),
    ]
    return mine + theirs, notes, prepared


def program(sz, own, tokens, cotangent, mine):
    T = sz.n_tensor
    swap = permutations(sz)[-1]
    theirs = [lax.ppermute(b, "fsdp", swap) for b in mine]
    plan, chunk, *notes = call_plan(sz, own, mine, theirs)

    def exchange(array, s):
        return lax.ppermute(array, "tensor", [(i, (i + s) % T) for i in range(T)])

    chunks = gather_chunks(sz, chunk)
    same, far, near, *firsts = call_compute(sz, plan, tokens, cotangent, chunks)

    def exchange_notes(after):
        return [exchange(note, s) for s, note in enumerate(call_turn(notes, [after]), 1)]

    def prepare(after, notes):
        return call_prepare(sz, plan, notes[0], call_turn([firsts[0]], [after])[0])

    sent = [exchange(firsts[s], s) for s in range(1, T)]
    terms, notes, (*partial, strips) = reduce_parts(sz, same, far, near, exchange_notes, prepare, sent)
    sent = call_turn(sent, [terms[2], terms[5]])
    outputs, input_grads, flag = call_add(sz, plan, notes, sent, strips, partial)
    return (outputs, input_grads, *call_last(sz, plan, terms)), flag


def shards(
    tokens,
    cotangent,
    gate_blocks,
    up_blocks,
    down_blocks,
    gate_where,
    up_where,
    down_where,
    block_counts,
):
    n_fsdp, n_tensor = lax.axis_size("fsdp"), lax.axis_size("tensor")
    f, rank = lax.axis_index("fsdp"), lax.axis_index("tensor")
    slots = gate_where.shape[1]
    full = Sizes(tokens, gate_blocks, slots, n_fsdp, n_tensor, False)
    own = jnp.concatenate([
        gate_where[0], up_where[0], down_where[0], block_counts[:, 0],
        f.astype(jnp.int32)[None], rank.astype(jnp.int32)[None]])
    own = jnp.pad(own, (0, full.lanes - own.shape[0]))[None]
    blocks_in = (gate_blocks, up_blocks, down_blocks)
    if slots >= full.cb:
        return program(full, own, tokens, cotangent, blocks_in)[0]
    lean = Sizes(tokens, gate_blocks, slots, n_fsdp, n_tensor, True)
    outs, flag = program(lean, own, tokens, cotangent, blocks_in)
    return lax.cond(
        flag[0] > 0,
        lambda outs, *args: program(full, *args)[0],
        lambda outs, *args: outs,
        outs, own, tokens, cotangent, blocks_in)


def solution(mesh):
    placed = (
        P("fsdp", None),
        P("fsdp", None),
        P("tensor", "fsdp", None, None),
        P("tensor", "fsdp", None, None),
        P("tensor", "fsdp", None, None),
        P("tensor", None),
        P("tensor", None),
        P("tensor", None),
        P(None, "tensor"),
    )
    return jax.shard_map(
        shards,
        mesh=mesh,
        in_specs=placed,
        out_specs=(
            P("fsdp", "tensor"),
            P("fsdp", "tensor"),
            P("tensor", "fsdp", None, None),
            P("tensor", "fsdp", None, None),
            P("tensor", "fsdp", None, None),
        ),
        check_vma=False,
    )
```

```python
import functools

import jax
import jax.numpy as jnp
from jax import lax
from jax.experimental import pallas as pl
from jax.experimental.pallas import tpu as pltpu
from jax.sharding import PartitionSpec as P

FF = 14336
BLK = 128
GROUP = 8
COLUMNS = 4
FIRST_SEND = 17
LEAN_SLOTS = 7
ROWS = BLK // 2
SMALL = 4 * 1024 * 1024
PART, STRIP, CIDX, CWAS, OIDX, OWAS = range(6)
FIELDS = 6
COLS_ROW = 3 * FIELDS
HEAD_ROW = COLS_ROW + 1
MINE_ROW = COLS_ROW + 2
LISTS_ROW = COLS_ROW + 3
HEAD_COLS, HEAD_OVER, HEAD_CORE, HEAD_LISTS = 3, 4, 5, 8


class Sizes:
    def __init__(self, tokens, gate_blocks, slots, n_fsdp, n_tensor, lean):
        self.tok, self.width = tokens.shape
        self.n_fsdp, self.n_tensor = n_fsdp, n_tensor
        self.rb = self.width // BLK
        self.cb = FF // (BLK * n_tensor)
        self.slots = slots
        self.all = 3 * slots
        self.lanes = -(-(self.all + GROUP) // 128) * 128
        self.nb = gate_blocks.shape[1]
        self.owned = 3 * self.nb
        self.ring = n_fsdp // 2
        self.top = self.ring // 2
        self.rbt = self.rb // n_tensor
        self.order = [self.top]
        for d in range(1, self.top):
            self.order += [self.top + d, self.top - d]
        self.order.append(0)
        self.far = min(2, self.ring - 1)
        self.keep = min(LEAN_SLOTS, 2 * self.owned) if lean else 2 * self.owned
        self.send_all = 2 * self.rbt
        self.first = min(FIRST_SEND, self.send_all) if lean else self.send_all
        self.blocks = self.ring * self.keep
        self.plan_rows = -(-(LISTS_ROW + 2 * n_tensor) // 8) * 8
        self.note_n, self.note_over = self.lanes - 1, self.lanes - 2
        self.room = slots + GROUP

    def place(self, d):
        return self.order.index(d) * self.keep

    def place_across(self, d):
        return self.place((self.ring - d) % self.ring)


def permutations(sz):
    seq = list(range(0, sz.ring, 2)) + list(range(sz.ring - 1, 0, -2))
    ahead, behind, swap = [], [], []
    for i, q in enumerate(seq):
        up, down = seq[(i + 1) % sz.ring], seq[i - 1]
        ahead += [(q * 2, up * 2), (q * 2 + 1, down * 2 + 1)]
        behind += [(q * 2, down * 2), (q * 2 + 1, up * 2 + 1)]
        swap += [(q * 2, q * 2 + 1), (q * 2 + 1, q * 2)]
    return ahead, behind, swap


def ratio(x, d):
    return jnp.floor((x + 0.5) * (1.0 / d))


def rest_of(x, d):
    return x - d * ratio(x, d)


def ring_position(sz, chip):
    return jnp.where(rest_of(chip, 2) == 0, ratio(chip, 2), sz.ring - 1 - ratio(chip, 2))


class Marks:
    def __init__(self, sz, own):
        N, L, S = sz.all, sz.lanes, sz.slots
        f32 = jnp.float32
        self.sz = sz
        self.sub = lax.broadcasted_iota(jnp.int32, (N, L), 0)
        self.lane = lax.broadcasted_iota(jnp.int32, (N, L), 1)
        self.same = self.sub == self.lane
        sub_c = self.sub[:, :1].astype(f32)
        lane_r = lax.broadcasted_iota(jnp.int32, (1, L), 1).astype(f32)
        self.sub_c, self.lane_r = sub_c, lane_r
        raw_r = own[...].astype(f32)

        def single(row, at):
            return jnp.sum(jnp.where(lane_r == at, row, 0.0), axis=1, keepdims=True)

        self.f, self.rank = single(raw_r, N + 3), single(raw_r, N + 4)

        def kind(x):
            return (x >= S).astype(f32) + (x >= 2 * S).astype(f32)

        self.kind_c, self.kind_r = kind(sub_c), kind(lane_r)
        self.n_r = lane_r - S * self.kind_r
        self.n_c = sub_c - S * self.kind_c
        limit = jnp.zeros((1, L), f32)
        for k in range(3):
            limit = limit + jnp.where(self.kind_r == k, single(raw_r, N + k), 0.0)
        live_r = jnp.where((lane_r < N) & (self.n_r < limit), 1.0, 0.0)
        w_c = self.col(raw_r)
        live_c = self.col(live_r)

        def place(w, k):
            gate, down = ratio(w, sz.cb), ratio(w, sz.rb)
            is_down = k == 2
            return jnp.where(is_down, w - down * sz.rb, gate), jnp.where(is_down, down, w - gate * sz.cb)

        self.row_c, col_c = place(w_c, self.kind_c)
        self.row_r, col_r = place(raw_r, self.kind_r)
        self.chip_c, chip_r = ratio(self.n_c, 2 * sz.nb), ratio(self.n_r, 2 * sz.nb)
        self.same_chip = (self.chip_c == chip_r).astype(f32)
        self.same_col = (col_c == col_r).astype(f32)
        act_c, act_r = live_c, live_r
        for k in range(3):
            lanes = self.same_col * (live_r * (self.kind_r == k).astype(f32))
            act_c = act_c * jnp.max(lanes, axis=1, keepdims=True)
            subs = self.same_col * (live_c * (self.kind_c == k).astype(f32))
            act_r = act_r * jnp.max(subs, axis=0, keepdims=True)
        self.act_c, self.act_r = act_c, act_r
        out_c = jnp.where(self.kind_c == 2, 0.0, f32(sz.rb)) + self.row_c
        out_r = jnp.where(self.kind_r == 2, 0.0, f32(sz.rb)) + self.row_r
        self.same_out = (out_c == out_r).astype(f32)
        self.before = (self.lane < self.sub).astype(f32)
        self.after = (self.sub < self.lane).astype(f32)
        self.owas_c = jnp.max(self.same_out * self.before * act_r, axis=1, keepdims=True)
        self.owas_r = jnp.max(self.same_out * self.after * act_c, axis=0, keepdims=True)
        self.lead_c = act_c * (1.0 - self.owas_c)
        self.lead_r = act_r * (1.0 - self.owas_r)

        def shift(row):
            away = ratio(row, sz.rbt) - self.rank
            return jnp.where(away < 0, away + sz.n_tensor, away)

        self.shift_c, self.shift_r = shift(self.row_c), shift(self.row_r)
        self.local_c = jnp.where(self.kind_c == 2, 0.0, f32(sz.rbt)) + rest_of(self.row_c, sz.rbt)

    def col(self, row):
        return jnp.sum(jnp.where(self.same, row, 0.0), axis=1, keepdims=True)

    def carried(self):
        sz = self.sz
        rank = jnp.sum(self.before * self.same_chip * self.act_r, axis=1, keepdims=True)
        away = ring_position(sz, self.chip_c) - ring_position(sz, ratio(self.f, 2))
        away = jnp.where(rest_of(self.f, 2) == 0, away, -away)
        rel = jnp.where(away < 0, away + sz.ring, away)
        j = jnp.where(rel > sz.top, 2 * (rel - sz.top) - 1, 2 * (sz.top - rel))
        return rank, jnp.where(rel == 0, sz.ring - 1.0, j)

    def ranks(self, chosen_r):
        return jnp.sum(self.before * chosen_r, axis=1, keepdims=True)

    def listed(self, chosen_c, rank_c, value_c, lo=0, hi=None):
        at = rank_c[lo:hi] == self.lane[lo:hi].astype(jnp.float32)
        return jnp.sum(jnp.where(at, chosen_c[lo:hi] * value_c[lo:hi], 0.0), axis=0, keepdims=True)

    def most_on_chip(self):
        return jnp.max(jnp.sum(self.same_chip * self.act_r, axis=1, keepdims=True), axis=0, keepdims=True)


def total(x):
    return jnp.sum(x, axis=0, keepdims=True)


def head_row(sz, entries):
    lane = lax.broadcasted_iota(jnp.int32, (1, sz.lanes), 1)
    row = jnp.zeros((1, sz.lanes), jnp.float32)
    for i, value in entries:
        row = jnp.where(lane == i, value, row)
    return row


def plan_kernel(sz, own, *refs):
    mine, theirs, (plan, chunk, *notes, sems) = refs[:3], refs[3:6], refs[6:]
    S, N = sz.slots, sz.all
    m = Marks(sz, own)
    f32 = jnp.float32
    lane_r, sub_c = m.lane_r, m.sub_c
    pos_c, base_c = m.carried()
    core = rest_of(m.f, 2)
    half = pl.ds(pl.multiple_of(jnp.max(core).astype(jnp.int32) * ROWS, ROWS), ROWS)

    pair = jnp.where(core == 0, m.f + 1, m.f - 1)
    i_r = rest_of(lane_r, sz.owned)
    owner_r = jnp.where(lane_r < sz.owned, m.f, pair)
    slot_r = ratio(i_r, sz.nb) * S + owner_r * sz.nb + rest_of(i_r, sz.nb)
    at_r = jnp.sum(jnp.where(sub_c == slot_r, m.act_c * (pos_c + 1.0), 0.0), axis=0, keepdims=True)
    copies = []
    for i in range(2 * sz.owned):
        side, k, a = i // sz.owned, i % sz.owned // sz.nb, i % sz.nb
        at = jnp.max(jnp.where(lane_r == i, at_r, 0.0)).astype(jnp.int32)
        fits = (at > 0) & (at <= sz.keep)
        place = jnp.minimum(jnp.maximum(at - 1, 0), sz.keep - 1)
        copy = pltpu.make_async_copy((mine, theirs)[side][k].at[0, a, half], chunk.at[place], sems.at[i])
        copies.append((fits, copy))
    for fits, copy in copies:
        pl.when(fits)(copy.start)

    same_kind = (m.kind_c == m.kind_r).astype(f32)
    rank_c = jnp.sum(m.before * same_kind * m.act_r, axis=1, keepdims=True)
    cwas_c = jnp.max(m.before * same_kind * m.same_col * m.act_r, axis=1, keepdims=True)
    cwas_r = jnp.max(m.after * same_kind * m.same_col * m.act_c, axis=0, keepdims=True)
    big = f32(4 * N)
    lanes_f = m.lane.astype(f32)
    gates_r = m.act_r * (m.kind_r == 0).astype(f32)
    cidx_c = jnp.min(jnp.where(m.same_col * gates_r > 0, lanes_f, big), axis=1, keepdims=True)
    oidx_c = jnp.min(jnp.where(m.same_out * m.act_r > 0, lanes_f, big), axis=1, keepdims=True)
    rank_r = jnp.sum(m.after * same_kind * m.act_c, axis=0, keepdims=True)
    turn_c = ratio(rank_c, GROUP) * 3 + m.kind_c
    turn_r = ratio(rank_r, GROUP) * 3 + m.kind_r
    ahead = ((turn_r < turn_c) | ((turn_r == turn_c) & (rank_r < rank_c))).astype(f32)
    owas_c = jnp.max(m.same_out * ahead * m.act_r, axis=1, keepdims=True)
    part_c = jnp.where(pos_c < sz.keep, base_c * sz.keep + pos_c, f32(sz.blocks))
    fields = [(part_c, sz.blocks), (m.row_c, 0), (cidx_c, S), (cwas_c, 0), (oidx_c, N), (owas_c, 0)]
    rows = []
    head = []
    for k in range(3):
        lo, hi = k * S, (k + 1) * S
        n_k = total(m.act_c[lo:hi])
        head.append((k, n_k))
        for value, spare in fields:
            row = m.listed(m.act_c, rank_c, value, lo, hi)
            rows.append(jnp.where(lane_r < n_k, row, f32(spare)))
    leader_c = m.act_c * (1.0 - cwas_c) * (m.kind_c == 0).astype(f32)
    leader_r = m.act_r * (1.0 - cwas_r) * (m.kind_r == 0).astype(f32)
    n_cols = total(leader_c)
    cols = m.listed(leader_c, m.ranks(leader_r), sub_c, 0, S)
    rows.append(jnp.where(lane_r < n_cols, cols, f32(S)))
    head.append((HEAD_COLS, n_cols))
    lists, sent = [], []
    over = (m.most_on_chip() > sz.keep).astype(f32)
    for s in range(sz.n_tensor):
        chosen_c = m.lead_c * (m.shift_c == s).astype(f32)
        chosen_r = m.lead_r * (m.shift_r == s).astype(f32)
        rank = m.ranks(chosen_r)
        lists.append(m.listed(chosen_c, rank, sub_c))
        lists.append(m.listed(chosen_c, rank, m.local_c))
        n = total(chosen_c)
        head.append((HEAD_LISTS + s, n))
        sent.append(n)
        over = jnp.maximum(over, (n > sz.first).astype(f32))
    head += [(HEAD_OVER, over), (HEAD_CORE, core)]
    for s in range(1, sz.n_tensor):
        note = jnp.where(lane_r == sz.note_n, sent[s], lists[2 * s + 1])
        notes[s - 1][...] = jnp.where(lane_r == sz.note_over, over, note).astype(jnp.int32)
    rows.append(head_row(sz, head))
    rows.append(at_r)
    rows += lists
    for i, row in enumerate(rows):
        plan[i:i + 1, :] = row.astype(jnp.int32)
    for fits, copy in copies:
        pl.when(fits)(copy.wait)


def dot(a, b, ca, cb):
    return lax.dot_general(a, b, (((ca,), (cb,)), ((), ())), preferred_element_type=jnp.float32)


def field(sz, plan, k, j, e):
    return plan[k * FIELDS + j, e]


def walk(plan, body):
    most = jnp.maximum(jnp.maximum(plan[HEAD_ROW, 0], plan[HEAD_ROW, 1]), plan[HEAD_ROW, 2])
    lax.fori_loop(0, (most + (GROUP - 1)) // GROUP, lambda p, _: body(p * GROUP), None)


def each(plan, k, body):
    lax.fori_loop(0, plan[HEAD_ROW, k], lambda e, _: body(e), None)


def compute_kernel(sz, plan, tokens, cot, *refs):
    n_chunks, T = 2 * sz.ring, sz.n_tensor
    chunks, refs = refs[:n_chunks], refs[n_chunks:]
    same, far, near = refs[:3]
    firsts, refs = refs[3:3 + T], refs[3 + T:]
    xs, wbuf, parts, gate_acc, up_acc, hg_acc, acts, out_acc, stage, strip_sems, sems = refs
    A = sz.slots + 1
    get = functools.partial(field, sz, plan)

    def strip_copy(k, e):
        src = cot if k == 2 else tokens
        cols = pl.ds(pl.multiple_of(get(k, STRIP, e) * BLK, BLK), BLK)
        return pltpu.make_async_copy(src.at[:, cols], xs.at[k * sz.room + e], strip_sems.at[k * sz.room + e])

    core = plan[HEAD_ROW, HEAD_CORE]
    sides = [pl.ds(pl.multiple_of(c * ROWS, ROWS), ROWS) for c in (core, 1 - core)]
    loads = []
    for side, place in enumerate((sz.place, sz.place_across)):
        for d in sz.order:
            i = len(loads)
            there = wbuf.at[pl.ds(place(d), sz.keep), sides[side]]
            loads.append(pltpu.make_async_copy(chunks[i], there, sems.at[i]))
    for k in range(3):
        each(plan, k, lambda e, k=k: strip_copy(k, e).start())
    for c in loads:
        c.start()
    for k in range(3):
        each(plan, k, lambda e, k=k: strip_copy(k, e).wait())
    for c in loads:
        c.wait()

    group = [(k, u) for k in range(3) for u in range(GROUP)]

    def forward(e0):
        for k, u in group:
            e, acc = e0 + u, (gate_acc, up_acc, hg_acc)[k]
            prod = dot(xs[k * sz.room + e], wbuf[get(k, PART, e)], 1, 1 if k == 2 else 0)
            c = get(k, CIDX, e)
            acc[c] = prod + jnp.where(get(k, CWAS, e) == 0, 0.0, acc[c])

    walk(plan, forward)

    def columns(i, _):
        for j in range(COLUMNS):
            c = plan[COLS_ROW, i * COLUMNS + j]
            g, u, h = gate_acc[c], up_acc[c], hg_acc[c]
            s = lax.logistic(g)
            silu = g * s
            acts[c] = (h * u * s * (1.0 + g * (1.0 - s))).astype(jnp.bfloat16)
            acts[A + c] = (h * silu).astype(jnp.bfloat16)
            acts[2 * A + c] = (silu * u).astype(jnp.bfloat16)

    lax.fori_loop(0, (plan[HEAD_ROW, HEAD_COLS] + (COLUMNS - 1)) // COLUMNS, columns, None)

    def gradients(e0):
        for k, u in group:
            e = e0 + u
            a, x = acts[k * A + get(k, CIDX, e)], xs[k * sz.room + e]
            grad = dot(a, x, 0, 0) if k == 2 else dot(x, a, 0, 0)
            parts[get(k, PART, e)] = grad.astype(jnp.bfloat16)

    walk(plan, gradients)
    outs = []
    for j, d in enumerate(sz.order):
        ref, at = (far, j) if j < sz.far else (near, j - sz.far)
        outs.append(pltpu.make_async_copy(
            parts.at[pl.ds(sz.place_across(d), sz.keep), sides[1]], ref.at[pl.ds(at * sz.keep, sz.keep)], sems.at[j]))
    outs.append(pltpu.make_async_copy(parts.at[pl.ds(0, sz.blocks), sides[0]], same, sems.at[sz.ring]))
    for c in outs:
        c.start()

    def terms(e0):
        for k, u in group:
            e = e0 + u
            prod = dot(acts[k * A + get(k, CIDX, e)], wbuf[get(k, PART, e)], 1, 0 if k == 2 else 1)
            at = get(k, OIDX, e)
            out_acc[at] = prod + jnp.where(get(k, OWAS, e) == 0, 0.0, out_acc[at])

    walk(plan, terms)

    for s in reversed(range(T)):
        def staged(i, _, s=s):
            stage[s * sz.first + i] = out_acc[plan[LISTS_ROW + 2 * s, i]].astype(jnp.bfloat16)

        lax.fori_loop(0, jnp.minimum(plan[HEAD_ROW, HEAD_LISTS + s], sz.first), staged, None)
        copy = pltpu.make_async_copy(stage.at[pl.ds(s * sz.first, sz.first)], firsts[s], sems.at[sz.ring + 1 + s])
        copy.start()
        outs.append(copy)
    for c in outs:
        c.wait()


def strip_of(sz, at):
    w = jnp.where(at < sz.rbt, at, at - sz.rbt)
    return at < sz.rbt, pl.ds(pl.multiple_of(w * BLK, BLK), BLK)


def prepare_kernel(sz, plan, note, first, outputs, input_grads, strips):
    outputs[...] = jnp.zeros_like(outputs)
    input_grads[...] = jnp.zeros_like(input_grads)

    def step(i, _):
        is_out, cols = strip_of(sz, plan[LISTS_ROW + 1, i])

        @pl.when(is_out)
        def _():
            outputs[:, cols] = first[i]

        @pl.when(jnp.logical_not(is_out))
        def _():
            input_grads[:, cols] = first[i]

    lax.fori_loop(0, jnp.minimum(plan[HEAD_ROW, HEAD_LISTS], sz.first), step, None)

    def pick(i, _):
        is_out, cols = strip_of(sz, note[0, i])

        @pl.when(is_out)
        def _():
            strips[i] = outputs[:, cols]

        @pl.when(jnp.logical_not(is_out))
        def _():
            strips[i] = input_grads[:, cols]

    lax.fori_loop(0, jnp.minimum(note[0, sz.note_n], sz.first), pick, None)


def add_kernel(sz, plan, *refs):
    T = sz.n_tensor
    notes, refs = refs[:T - 1], refs[T - 1:]
    firsts, held_strips, refs = refs[:T - 1], refs[T - 1], refs[T + 2:]
    outputs, input_grads, flag, strips, read_sems, write_sems = refs
    over = plan[HEAD_ROW, HEAD_OVER]
    for note in notes:
        over = jnp.maximum(over, note[0, sz.note_over])
    flag[0] = over

    def move(s, i, back, act):
        is_out, cols = strip_of(sz, notes[s][0, i])
        for ref, here in ((outputs, is_out), (input_grads, jnp.logical_not(is_out))):
            @pl.when(here)
            def _(ref=ref):
                there = ref.at[:, cols]
                if back:
                    act(pltpu.make_async_copy(strips.at[i], there, write_sems.at[i]))
                else:
                    act(pltpu.make_async_copy(there, strips.at[i], read_sems.at[i]))

    def loop(s, body):
        lax.fori_loop(0, jnp.minimum(notes[s][0, sz.note_n], sz.first), lambda i, _: body(i), None)

    for s in range(T - 1):
        if s:
            loop(s, lambda i: move(s, i, False, lambda c: c.start()))

        def step(i):
            if s:
                move(s, i, False, lambda c: c.wait())
            held = strips[i] if s else held_strips[i]
            value = held.astype(jnp.float32) + firsts[s][i].astype(jnp.float32)
            strips[i] = value.astype(jnp.bfloat16)
            move(s, i, True, lambda c: c.start())

        loop(s, step)
        loop(s, lambda i: move(s, i, True, lambda c: c.wait()))


def last_kernel(sz, plan, *refs):
    mine, theirs, grads = refs[:3], refs[3:6], refs[6:]
    core = plan[HEAD_ROW, HEAD_CORE]
    for k in range(3):
        for a in range(sz.nb):
            at = plan[MINE_ROW, k * sz.nb + a]
            p = jnp.minimum(jnp.maximum(at - 1, 0), sz.keep - 1)
            for terms, c in ((mine, core), (theirs, 1 - core)):
                value = sum(t[p].astype(jnp.float32) for t in terms)
                rows = pl.ds(pl.multiple_of(c * ROWS, ROWS), ROWS)
                grads[k][0, a, rows] = jnp.where(at > 0, value, 0.0).astype(jnp.bfloat16)


def spec(space):
    return pl.BlockSpec(memory_space=space)


ANY, HBM, VMEM, SMEM = pl.ANY, pltpu.HBM, pltpu.VMEM, pltpu.SMEM


def cost(flops, moved):
    return pl.CostEstimate(flops=flops, bytes_accessed=moved, transcendentals=0)


def call_plan(sz, own, mine, theirs):
    return pl.pallas_call(
        functools.partial(plan_kernel, sz),
        out_shape=[
            jax.ShapeDtypeStruct((sz.plan_rows, sz.lanes), jnp.int32),
            halves(sz.keep),
        ] + [jax.ShapeDtypeStruct((1, sz.lanes), jnp.int32)] * (sz.n_tensor - 1),
        in_specs=[spec(VMEM)] + [spec(ANY)] * 6,
        out_specs=[spec(VMEM), spec(ANY)] + [spec(VMEM)] * (sz.n_tensor - 1),
        scratch_shapes=[pltpu.SemaphoreType.DMA((2 * sz.owned,))],
        compiler_params=pltpu.CompilerParams(vmem_limit_bytes=SMALL),
        cost_estimate=cost(1_000_000, 4_000_000),
        name="plan",
    )(own, *mine, *theirs)


def call_turn(handed, arrived):
    return pl.pallas_call(
        lambda *_: None,
        out_shape=[jax.ShapeDtypeStruct(x.shape, x.dtype) for x in handed],
        in_specs=[spec(ANY)] * (len(handed) + len(arrived)),
        out_specs=[spec(ANY)] * len(handed),
        input_output_aliases={i: i for i in range(len(handed))},
        compiler_params=pltpu.CompilerParams(vmem_limit_bytes=SMALL),
        cost_estimate=cost(1000, 1000),
        name="turn",
    )(*handed, *arrived)


def blocks(n):
    return jax.ShapeDtypeStruct((n, BLK, BLK), jnp.bfloat16)


def halves(n):
    return jax.ShapeDtypeStruct((n, ROWS, BLK), jnp.bfloat16)


def held(scratch):
    return sum(s[0] * s[1] * s[2] * jnp.dtype(t).itemsize for s, t in scratch) + 2 * 1024 * 1024


def call_compute(sz, plan, tokens, cot, chunks):
    bf, f32 = jnp.bfloat16, jnp.float32
    T, A = sz.n_tensor, sz.slots + 1
    out_shape = [halves(sz.ring * sz.keep), halves(sz.far * sz.keep), halves((sz.ring - sz.far) * sz.keep)]
    out_shape += [blocks(sz.first)] * T
    scratch = [
        ((3 * sz.room, sz.tok, BLK), bf),
        ((sz.blocks + 1, BLK, BLK), bf),
        ((sz.blocks + 1, BLK, BLK), bf),
        ((A, sz.tok, BLK), f32),
        ((A, sz.tok, BLK), f32),
        ((A, sz.tok, BLK), f32),
        ((3 * A, sz.tok, BLK), bf),
        ((sz.all + 1, sz.tok, BLK), f32),
        ((T * sz.first, sz.tok, BLK), bf),
    ]
    return pl.pallas_call(
        functools.partial(compute_kernel, sz),
        out_shape=out_shape,
        in_specs=[spec(SMEM)] + [spec(HBM)] * 2 + [spec(ANY)] * len(chunks),
        out_specs=[spec(ANY)] * len(out_shape),
        scratch_shapes=[pltpu.VMEM(s, t) for s, t in scratch] + [
            pltpu.SemaphoreType.DMA((3 * sz.room,)),
            pltpu.SemaphoreType.DMA((max(len(chunks), sz.ring + 1 + T),)),
        ],
        compiler_params=pltpu.CompilerParams(vmem_limit_bytes=held(scratch)),
        cost_estimate=cost(1_000_000_000, 20_000_000),
        name="compute",
    )(plan, pltpu.with_memory_space_constraint(tokens, HBM), pltpu.with_memory_space_constraint(cot, HBM), *chunks)


def call_prepare(sz, plan, note, first):
    half = jax.ShapeDtypeStruct((sz.tok, sz.width // sz.n_tensor), jnp.bfloat16)
    return pl.pallas_call(
        functools.partial(prepare_kernel, sz),
        out_shape=[half, half, blocks(sz.first)],
        in_specs=[spec(SMEM), spec(SMEM), spec(VMEM)],
        out_specs=[spec(VMEM)] * 3,
        compiler_params=pltpu.CompilerParams(vmem_limit_bytes=12 * 1024 * 1024),
        cost_estimate=cost(1_000_000, 6_000_000),
        name="prepare",
    )(plan, note, first)


def call_add(sz, plan, notes, firsts, strips, partial):
    n = 2 + len(notes) + len(firsts)
    return pl.pallas_call(
        functools.partial(add_kernel, sz),
        out_shape=[jax.ShapeDtypeStruct(p.shape, p.dtype) for p in partial] + [jax.ShapeDtypeStruct((1,), jnp.int32)],
        in_specs=[spec(SMEM)] * (1 + len(notes)) + [spec(VMEM)] * (len(firsts) + 1) + [spec(ANY)] * 2,
        out_specs=[spec(ANY)] * 2 + [spec(SMEM)],
        input_output_aliases={n: 0, n + 1: 1},
        scratch_shapes=[
            pltpu.VMEM((sz.first, sz.tok, BLK), jnp.bfloat16),
            pltpu.SemaphoreType.DMA((sz.first,)),
            pltpu.SemaphoreType.DMA((sz.first,)),
        ],
        compiler_params=pltpu.CompilerParams(vmem_limit_bytes=12 * 1024 * 1024),
        cost_estimate=cost(1_000_000, 3_000_000),
        name="add",
    )(plan, *notes, *firsts, strips, *partial)


def call_last(sz, plan, terms):
    out = jax.ShapeDtypeStruct((1, sz.nb, BLK, BLK), jnp.bfloat16)
    return pl.pallas_call(
        functools.partial(last_kernel, sz),
        out_shape=[out] * 3,
        in_specs=[spec(SMEM)] + [spec(VMEM)] * len(terms),
        out_specs=[spec(VMEM)] * 3,
        compiler_params=pltpu.CompilerParams(vmem_limit_bytes=SMALL),
        cost_estimate=cost(1_000_000, 1_000_000),
        name="last",
    )(plan, *terms)


def across(pairs):
    return [(i, j ^ 1) for i, j in pairs]


def gather_chunks(sz, chunk):
    ahead, behind, swap = permutations(sz)
    same = {0: chunk}
    a = b = chunk
    for s in range(1, sz.top):
        a, b = lax.ppermute(a, "fsdp", ahead), lax.ppermute(b, "fsdp", behind)
        same[sz.ring - s], same[s] = a, b
    other = {d: lax.ppermute(same[d], "fsdp", swap) for d in same}
    same[sz.top] = lax.ppermute(a, "fsdp", ahead)
    other[sz.top] = lax.ppermute(a, "fsdp", across(ahead))
    return [side[d] for side in (same, other) for d in sz.order]


def reduce_parts(sz, same, far, near, notes, prepare, sent):
    ahead, behind, swap = permutations(sz)
    keep = sz.keep
    far = lax.ppermute(far, "fsdp", swap)
    near = lax.ppermute(call_turn([near], [far])[0], "fsdp", swap)

    def term(d, *more):
        j = sz.order.index(d)
        pair = far[j * keep:(j + 1) * keep] if j < sz.far else near[(j - sz.far) * keep:][:keep]
        out = same[j * keep:(j + 1) * keep].astype(jnp.float32) + pair.astype(jnp.float32)
        for m in more:
            out = out + m.astype(jnp.float32)
        return out.astype(jnp.bfloat16)

    a, b = lax.optimization_barrier((term(sz.top), term(sz.top + 1)))
    here = term(0)
    here_across = lax.ppermute(here, "fsdp", swap)
    prepared = prepare(here_across)
    for s in range(1, sz.top):
        last_b = b
        a, b = lax.ppermute(a, "fsdp", ahead), lax.ppermute(b, "fsdp", behind)
        if s == 1:
            a, b = call_turn([a, b], [])
        else:
            a = call_turn([a], [last_b] + (notes if s == 2 else sent + list(prepared[2:])))[0]
        a = term(sz.top - s, a)
        if s + 1 < sz.top:
            b = term(sz.top + 1 + s, call_turn([b], [a])[0])
    mine = [here, lax.ppermute(a, "fsdp", ahead), b]
    theirs = [
        here_across,
        lax.ppermute(a, "fsdp", across(ahead)),
        lax.ppermute(last_b, "fsdp", across(behind)),
    ]
    return mine + theirs, prepared


def program(sz, own, tokens, cotangent, mine):
    T = sz.n_tensor
    swap = permutations(sz)[-1]
    theirs = [lax.ppermute(b, "fsdp", swap) for b in mine]
    plan, chunk, *notes = call_plan(sz, own, mine, theirs)

    def exchange(array, s):
        return lax.ppermute(array, "tensor", [(i, (i + s) % T) for i in range(T)])

    notes = [exchange(note, s) for s, note in enumerate(notes, 1)]
    chunks = gather_chunks(sz, chunk)
    same, far, near, *firsts = call_compute(sz, plan, tokens, cotangent, chunks)

    def prepare(after):
        return call_prepare(sz, plan, notes[0], call_turn([firsts[0]], [after])[0])

    sent = [exchange(firsts[s], s) for s in range(1, T)]
    terms, (*partial, strips) = reduce_parts(sz, same, far, near, notes, prepare, sent)
    sent = call_turn(sent, [terms[2], terms[5]])
    outputs, input_grads, flag = call_add(sz, plan, notes, sent, strips, partial)
    return (outputs, input_grads, *call_last(sz, plan, terms)), flag


def shards(
    tokens,
    cotangent,
    gate_blocks,
    up_blocks,
    down_blocks,
    gate_where,
    up_where,
    down_where,
    block_counts,
):
    n_fsdp, n_tensor = lax.axis_size("fsdp"), lax.axis_size("tensor")
    f, rank = lax.axis_index("fsdp"), lax.axis_index("tensor")
    slots = gate_where.shape[1]
    full = Sizes(tokens, gate_blocks, slots, n_fsdp, n_tensor, False)
    own = jnp.concatenate([
        gate_where[0], up_where[0], down_where[0], block_counts[:, 0],
        f.astype(jnp.int32)[None], rank.astype(jnp.int32)[None]])
    own = jnp.pad(own, (0, full.lanes - own.shape[0]))[None]
    blocks_in = (gate_blocks, up_blocks, down_blocks)
    if slots >= full.cb:
        return program(full, own, tokens, cotangent, blocks_in)[0]
    lean = Sizes(tokens, gate_blocks, slots, n_fsdp, n_tensor, True)
    outs, flag = program(lean, own, tokens, cotangent, blocks_in)
    return lax.cond(
        flag[0] > 0,
        lambda outs, *args: program(full, *args)[0],
        lambda outs, *args: outs,
        outs, own, tokens, cotangent, blocks_in)


def solution(mesh):
    placed = (
        P("fsdp", None),
        P("fsdp", None),
        P("tensor", "fsdp", None, None),
        P("tensor", "fsdp", None, None),
        P("tensor", "fsdp", None, None),
        P("tensor", None),
        P("tensor", None),
        P("tensor", None),
        P(None, "tensor"),
    )
    return jax.shard_map(
        shards,
        mesh=mesh,
        in_specs=placed,
        out_specs=(
            P("fsdp", "tensor"),
            P("fsdp", "tensor"),
            P("tensor", "fsdp", None, None),
            P("tensor", "fsdp", None, None),
            P("tensor", "fsdp", None, None),
        ),
        check_vma=False,
    )
```

```python
import functools

import jax
import jax.numpy as jnp
from jax import lax
from jax.experimental import pallas as pl
from jax.experimental.pallas import tpu as pltpu
from jax.sharding import PartitionSpec as P

FF = 14336
BLK = 128
GROUP = 8
COLUMNS = 4
FIRST_SEND = 16
LEAN_SLOTS = 7
ROWS = BLK // 2
SMALL = 4 * 1024 * 1024
PART, STRIP, CIDX, CWAS, OIDX, OWAS = range(6)
FIELDS = 6
COLS_ROW = 3 * FIELDS
HEAD_ROW = COLS_ROW + 1
MINE_ROW = COLS_ROW + 2
LISTS_ROW = COLS_ROW + 3
HEAD_COLS, HEAD_OVER, HEAD_CORE, HEAD_LISTS = 3, 4, 5, 8


class Sizes:
    def __init__(self, tokens, gate_blocks, slots, n_fsdp, n_tensor, lean):
        self.tok, self.width = tokens.shape
        self.n_fsdp, self.n_tensor = n_fsdp, n_tensor
        self.rb = self.width // BLK
        self.cb = FF // (BLK * n_tensor)
        self.slots = slots
        self.all = 3 * slots
        self.lanes = -(-(self.all + GROUP) // 128) * 128
        self.nb = gate_blocks.shape[1]
        self.owned = 3 * self.nb
        self.ring = n_fsdp // 2
        self.top = self.ring // 2
        self.rbt = self.rb // n_tensor
        self.order = [self.top]
        for d in range(1, self.top):
            self.order += [self.top + d, self.top - d]
        self.order.append(0)
        self.far = min(2, self.ring - 1)
        self.keep = min(LEAN_SLOTS, 2 * self.owned) if lean else 2 * self.owned
        self.send_all = 2 * self.rbt
        self.first = min(FIRST_SEND, self.send_all) if lean else self.send_all
        self.blocks = self.ring * self.keep
        self.plan_rows = -(-(LISTS_ROW + 2 * n_tensor) // 8) * 8
        self.note_n, self.note_over = self.lanes - 1, self.lanes - 2
        self.room = slots + GROUP

    def place(self, d):
        return self.order.index(d) * self.keep

    def place_across(self, d):
        return self.place((self.ring - d) % self.ring)


def permutations(sz):
    seq = list(range(0, sz.ring, 2)) + list(range(sz.ring - 1, 0, -2))
    ahead, behind, swap = [], [], []
    for i, q in enumerate(seq):
        up, down = seq[(i + 1) % sz.ring], seq[i - 1]
        ahead += [(q * 2, up * 2), (q * 2 + 1, down * 2 + 1)]
        behind += [(q * 2, down * 2), (q * 2 + 1, up * 2 + 1)]
        swap += [(q * 2, q * 2 + 1), (q * 2 + 1, q * 2)]
    return ahead, behind, swap


def ratio(x, d):
    return jnp.floor((x + 0.5) * (1.0 / d))


def rest_of(x, d):
    return x - d * ratio(x, d)


def ring_position(sz, chip):
    return jnp.where(rest_of(chip, 2) == 0, ratio(chip, 2), sz.ring - 1 - ratio(chip, 2))


class Marks:
    def __init__(self, sz, own):
        N, L, S = sz.all, sz.lanes, sz.slots
        f32 = jnp.float32
        self.sz = sz
        self.sub = lax.broadcasted_iota(jnp.int32, (N, L), 0)
        self.lane = lax.broadcasted_iota(jnp.int32, (N, L), 1)
        self.same = self.sub == self.lane
        sub_c = self.sub[:, :1].astype(f32)
        lane_r = lax.broadcasted_iota(jnp.int32, (1, L), 1).astype(f32)
        self.sub_c, self.lane_r = sub_c, lane_r
        raw_r = own[...].astype(f32)

        def single(row, at):
            return jnp.sum(jnp.where(lane_r == at, row, 0.0), axis=1, keepdims=True)

        self.f, self.rank = single(raw_r, N + 3), single(raw_r, N + 4)

        def kind(x):
            return (x >= S).astype(f32) + (x >= 2 * S).astype(f32)

        self.kind_c, self.kind_r = kind(sub_c), kind(lane_r)
        self.n_r = lane_r - S * self.kind_r
        self.n_c = sub_c - S * self.kind_c
        limit = jnp.zeros((1, L), f32)
        for k in range(3):
            limit = limit + jnp.where(self.kind_r == k, single(raw_r, N + k), 0.0)
        live_r = jnp.where((lane_r < N) & (self.n_r < limit), 1.0, 0.0)
        w_c = self.col(raw_r)
        live_c = self.col(live_r)

        def place(w, k):
            gate, down = ratio(w, sz.cb), ratio(w, sz.rb)
            is_down = k == 2
            return jnp.where(is_down, w - down * sz.rb, gate), jnp.where(is_down, down, w - gate * sz.cb)

        self.row_c, col_c = place(w_c, self.kind_c)
        self.row_r, col_r = place(raw_r, self.kind_r)
        self.chip_c, chip_r = ratio(self.n_c, 2 * sz.nb), ratio(self.n_r, 2 * sz.nb)
        self.same_chip = (self.chip_c == chip_r).astype(f32)
        self.same_col = (col_c == col_r).astype(f32)
        act_c, act_r = live_c, live_r
        for k in range(3):
            lanes = self.same_col * (live_r * (self.kind_r == k).astype(f32))
            act_c = act_c * jnp.max(lanes, axis=1, keepdims=True)
            subs = self.same_col * (live_c * (self.kind_c == k).astype(f32))
            act_r = act_r * jnp.max(subs, axis=0, keepdims=True)
        self.act_c, self.act_r = act_c, act_r
        out_c = jnp.where(self.kind_c == 2, 0.0, f32(sz.rb)) + self.row_c
        out_r = jnp.where(self.kind_r == 2, 0.0, f32(sz.rb)) + self.row_r
        self.same_out = (out_c == out_r).astype(f32)
        self.before = (self.lane < self.sub).astype(f32)
        self.after = (self.sub < self.lane).astype(f32)
        self.owas_c = jnp.max(self.same_out * self.before * act_r, axis=1, keepdims=True)
        self.owas_r = jnp.max(self.same_out * self.after * act_c, axis=0, keepdims=True)
        self.lead_c = act_c * (1.0 - self.owas_c)
        self.lead_r = act_r * (1.0 - self.owas_r)

        def shift(row):
            away = ratio(row, sz.rbt) - self.rank
            return jnp.where(away < 0, away + sz.n_tensor, away)

        self.shift_c, self.shift_r = shift(self.row_c), shift(self.row_r)
        self.local_c = jnp.where(self.kind_c == 2, 0.0, f32(sz.rbt)) + rest_of(self.row_c, sz.rbt)

    def col(self, row):
        return jnp.sum(jnp.where(self.same, row, 0.0), axis=1, keepdims=True)

    def carried(self):
        sz = self.sz
        rank = jnp.sum(self.before * self.same_chip * self.act_r, axis=1, keepdims=True)
        away = ring_position(sz, self.chip_c) - ring_position(sz, ratio(self.f, 2))
        away = jnp.where(rest_of(self.f, 2) == 0, away, -away)
        rel = jnp.where(away < 0, away + sz.ring, away)
        j = jnp.where(rel > sz.top, 2 * (rel - sz.top) - 1, 2 * (sz.top - rel))
        return rank, jnp.where(rel == 0, sz.ring - 1.0, j)

    def ranks(self, chosen_r):
        return jnp.sum(self.before * chosen_r, axis=1, keepdims=True)

    def listed(self, chosen_c, rank_c, value_c, lo=0, hi=None):
        at = rank_c[lo:hi] == self.lane[lo:hi].astype(jnp.float32)
        return jnp.sum(jnp.where(at, chosen_c[lo:hi] * value_c[lo:hi], 0.0), axis=0, keepdims=True)

    def most_on_chip(self):
        return jnp.max(jnp.sum(self.same_chip * self.act_r, axis=1, keepdims=True), axis=0, keepdims=True)


def total(x):
    return jnp.sum(x, axis=0, keepdims=True)


def head_row(sz, entries):
    lane = lax.broadcasted_iota(jnp.int32, (1, sz.lanes), 1)
    row = jnp.zeros((1, sz.lanes), jnp.float32)
    for i, value in entries:
        row = jnp.where(lane == i, value, row)
    return row


def plan_kernel(sz, own, *refs):
    mine, theirs, (plan, chunk, *notes, sems) = refs[:3], refs[3:6], refs[6:]
    S, N = sz.slots, sz.all
    m = Marks(sz, own)
    f32 = jnp.float32
    lane_r, sub_c = m.lane_r, m.sub_c
    pos_c, base_c = m.carried()
    core = rest_of(m.f, 2)
    half = pl.ds(pl.multiple_of(jnp.max(core).astype(jnp.int32) * ROWS, ROWS), ROWS)

    pair = jnp.where(core == 0, m.f + 1, m.f - 1)
    i_r = rest_of(lane_r, sz.owned)
    owner_r = jnp.where(lane_r < sz.owned, m.f, pair)
    slot_r = ratio(i_r, sz.nb) * S + owner_r * sz.nb + rest_of(i_r, sz.nb)
    at_r = jnp.sum(jnp.where(sub_c == slot_r, m.act_c * (pos_c + 1.0), 0.0), axis=0, keepdims=True)
    copies = []
    for i in range(2 * sz.owned):
        side, k, a = i // sz.owned, i % sz.owned // sz.nb, i % sz.nb
        at = jnp.max(jnp.where(lane_r == i, at_r, 0.0)).astype(jnp.int32)
        fits = (at > 0) & (at <= sz.keep)
        place = jnp.minimum(jnp.maximum(at - 1, 0), sz.keep - 1)
        copy = pltpu.make_async_copy((mine, theirs)[side][k].at[0, a, half], chunk.at[place], sems.at[i])
        copies.append((fits, copy))
    for fits, copy in copies:
        pl.when(fits)(copy.start)

    same_kind = (m.kind_c == m.kind_r).astype(f32)
    rank_c = jnp.sum(m.before * same_kind * m.act_r, axis=1, keepdims=True)
    cwas_c = jnp.max(m.before * same_kind * m.same_col * m.act_r, axis=1, keepdims=True)
    cwas_r = jnp.max(m.after * same_kind * m.same_col * m.act_c, axis=0, keepdims=True)
    big = f32(4 * N)
    lanes_f = m.lane.astype(f32)
    gates_r = m.act_r * (m.kind_r == 0).astype(f32)
    cidx_c = jnp.min(jnp.where(m.same_col * gates_r > 0, lanes_f, big), axis=1, keepdims=True)
    oidx_c = jnp.min(jnp.where(m.same_out * m.act_r > 0, lanes_f, big), axis=1, keepdims=True)
    rank_r = jnp.sum(m.after * same_kind * m.act_c, axis=0, keepdims=True)
    turn_c = ratio(rank_c, GROUP) * 3 + m.kind_c
    turn_r = ratio(rank_r, GROUP) * 3 + m.kind_r
    ahead = ((turn_r < turn_c) | ((turn_r == turn_c) & (rank_r < rank_c))).astype(f32)
    owas_c = jnp.max(m.same_out * ahead * m.act_r, axis=1, keepdims=True)
    part_c = jnp.where(pos_c < sz.keep, base_c * sz.keep + pos_c, f32(sz.blocks))
    fields = [(part_c, sz.blocks), (m.row_c, 0), (cidx_c, S), (cwas_c, 0), (oidx_c, N), (owas_c, 0)]
    rows = []
    head = []
    for k in range(3):
        lo, hi = k * S, (k + 1) * S
        n_k = total(m.act_c[lo:hi])
        head.append((k, n_k))
        for value, spare in fields:
            row = m.listed(m.act_c, rank_c, value, lo, hi)
            rows.append(jnp.where(lane_r < n_k, row, f32(spare)))
    leader_c = m.act_c * (1.0 - cwas_c) * (m.kind_c == 0).astype(f32)
    leader_r = m.act_r * (1.0 - cwas_r) * (m.kind_r == 0).astype(f32)
    n_cols = total(leader_c)
    cols = m.listed(leader_c, m.ranks(leader_r), sub_c, 0, S)
    rows.append(jnp.where(lane_r < n_cols, cols, f32(S)))
    head.append((HEAD_COLS, n_cols))
    lists, sent = [], []
    over = (m.most_on_chip() > sz.keep).astype(f32)
    for s in range(sz.n_tensor):
        chosen_c = m.lead_c * (m.shift_c == s).astype(f32)
        chosen_r = m.lead_r * (m.shift_r == s).astype(f32)
        rank = m.ranks(chosen_r)
        lists.append(m.listed(chosen_c, rank, sub_c))
        lists.append(m.listed(chosen_c, rank, m.local_c))
        n = total(chosen_c)
        head.append((HEAD_LISTS + s, n))
        sent.append(n)
        over = jnp.maximum(over, (n > sz.first).astype(f32))
    head += [(HEAD_OVER, over), (HEAD_CORE, core)]
    for s in range(1, sz.n_tensor):
        note = jnp.where(lane_r == sz.note_n, sent[s], lists[2 * s + 1])
        notes[s - 1][...] = jnp.where(lane_r == sz.note_over, over, note).astype(jnp.int32)
    rows.append(head_row(sz, head))
    rows.append(at_r)
    rows += lists
    for i, row in enumerate(rows):
        plan[i:i + 1, :] = row.astype(jnp.int32)
    for fits, copy in copies:
        pl.when(fits)(copy.wait)


def dot(a, b, ca, cb):
    return lax.dot_general(a, b, (((ca,), (cb,)), ((), ())), preferred_element_type=jnp.float32)


def field(sz, plan, k, j, e):
    return plan[k * FIELDS + j, e]


def walk(plan, body):
    most = jnp.maximum(jnp.maximum(plan[HEAD_ROW, 0], plan[HEAD_ROW, 1]), plan[HEAD_ROW, 2])
    lax.fori_loop(0, (most + (GROUP - 1)) // GROUP, lambda p, _: body(p * GROUP), None)


def each(plan, k, body):
    lax.fori_loop(0, plan[HEAD_ROW, k], lambda e, _: body(e), None)


def compute_kernel(sz, plan, tokens, cot, *refs):
    n_chunks, T = 2 * sz.ring, sz.n_tensor
    chunks, refs = refs[:n_chunks], refs[n_chunks:]
    same, far, near = refs[:3]
    firsts, refs = refs[3:3 + T], refs[3 + T:]
    xs, wbuf, parts, gate_acc, up_acc, hg_acc, acts, out_acc, stage, strip_sems, sems = refs
    A = sz.slots + 1
    get = functools.partial(field, sz, plan)

    def strip_copy(k, e):
        src = cot if k == 2 else tokens
        cols = pl.ds(pl.multiple_of(get(k, STRIP, e) * BLK, BLK), BLK)
        return pltpu.make_async_copy(src.at[:, cols], xs.at[k * sz.room + e], strip_sems.at[k * sz.room + e])

    core = plan[HEAD_ROW, HEAD_CORE]
    sides = [pl.ds(pl.multiple_of(c * ROWS, ROWS), ROWS) for c in (core, 1 - core)]
    loads = []
    for side, place in enumerate((sz.place, sz.place_across)):
        for d in sz.order:
            i = len(loads)
            there = wbuf.at[pl.ds(place(d), sz.keep), sides[side]]
            loads.append(pltpu.make_async_copy(chunks[i], there, sems.at[i]))
    for k in range(3):
        each(plan, k, lambda e, k=k: strip_copy(k, e).start())
    for c in loads:
        c.start()
    for k in range(3):
        each(plan, k, lambda e, k=k: strip_copy(k, e).wait())
    for c in loads:
        c.wait()

    group = [(k, u) for k in range(3) for u in range(GROUP)]

    def forward(e0):
        for k, u in group:
            e, acc = e0 + u, (gate_acc, up_acc, hg_acc)[k]
            prod = dot(xs[k * sz.room + e], wbuf[get(k, PART, e)], 1, 1 if k == 2 else 0)
            c = get(k, CIDX, e)
            acc[c] = prod + jnp.where(get(k, CWAS, e) == 0, 0.0, acc[c])

    walk(plan, forward)

    def columns(i, _):
        for j in range(COLUMNS):
            c = plan[COLS_ROW, i * COLUMNS + j]
            g, u, h = gate_acc[c], up_acc[c], hg_acc[c]
            s = lax.logistic(g)
            silu = g * s
            acts[c] = (h * u * s * (1.0 + g * (1.0 - s))).astype(jnp.bfloat16)
            acts[A + c] = (h * silu).astype(jnp.bfloat16)
            acts[2 * A + c] = (silu * u).astype(jnp.bfloat16)

    lax.fori_loop(0, (plan[HEAD_ROW, HEAD_COLS] + (COLUMNS - 1)) // COLUMNS, columns, None)

    def gradients(e0):
        for k, u in group:
            e = e0 + u
            a, x = acts[k * A + get(k, CIDX, e)], xs[k * sz.room + e]
            grad = dot(a, x, 0, 0) if k == 2 else dot(x, a, 0, 0)
            parts[get(k, PART, e)] = grad.astype(jnp.bfloat16)

    walk(plan, gradients)
    outs = []
    for j, d in enumerate(sz.order):
        ref, at = (far, j) if j < sz.far else (near, j - sz.far)
        outs.append(pltpu.make_async_copy(
            parts.at[pl.ds(sz.place_across(d), sz.keep), sides[1]], ref.at[pl.ds(at * sz.keep, sz.keep)], sems.at[j]))
    outs.append(pltpu.make_async_copy(parts.at[pl.ds(0, sz.blocks), sides[0]], same, sems.at[sz.ring]))
    for c in outs:
        c.start()

    def terms(e0):
        for k, u in group:
            e = e0 + u
            prod = dot(acts[k * A + get(k, CIDX, e)], wbuf[get(k, PART, e)], 1, 0 if k == 2 else 1)
            at = get(k, OIDX, e)
            out_acc[at] = prod + jnp.where(get(k, OWAS, e) == 0, 0.0, out_acc[at])

    walk(plan, terms)

    for s in reversed(range(T)):
        def staged(i, _, s=s):
            stage[s * sz.first + i] = out_acc[plan[LISTS_ROW + 2 * s, i]].astype(jnp.bfloat16)

        lax.fori_loop(0, jnp.minimum(plan[HEAD_ROW, HEAD_LISTS + s], sz.first), staged, None)
        copy = pltpu.make_async_copy(stage.at[pl.ds(s * sz.first, sz.first)], firsts[s], sems.at[sz.ring + 1 + s])
        copy.start()
        outs.append(copy)
    for c in outs:
        c.wait()


def strip_of(sz, at):
    w = jnp.where(at < sz.rbt, at, at - sz.rbt)
    return at < sz.rbt, pl.ds(pl.multiple_of(w * BLK, BLK), BLK)


def prepare_kernel(sz, plan, note, first, outputs, input_grads, strips):
    outputs[...] = jnp.zeros_like(outputs)
    input_grads[...] = jnp.zeros_like(input_grads)

    def step(i, _):
        is_out, cols = strip_of(sz, plan[LISTS_ROW + 1, i])

        @pl.when(is_out)
        def _():
            outputs[:, cols] = first[i]

        @pl.when(jnp.logical_not(is_out))
        def _():
            input_grads[:, cols] = first[i]

    lax.fori_loop(0, jnp.minimum(plan[HEAD_ROW, HEAD_LISTS], sz.first), step, None)

    def pick(i, _):
        is_out, cols = strip_of(sz, note[0, i])

        @pl.when(is_out)
        def _():
            strips[i] = outputs[:, cols]

        @pl.when(jnp.logical_not(is_out))
        def _():
            strips[i] = input_grads[:, cols]

    lax.fori_loop(0, jnp.minimum(note[0, sz.note_n], sz.first), pick, None)


def add_kernel(sz, plan, *refs):
    T = sz.n_tensor
    notes, refs = refs[:T - 1], refs[T - 1:]
    firsts, held_strips, refs = refs[:T - 1], refs[T - 1], refs[T + 2:]
    outputs, input_grads, flag, strips, read_sems, write_sems = refs
    over = plan[HEAD_ROW, HEAD_OVER]
    for note in notes:
        over = jnp.maximum(over, note[0, sz.note_over])
    flag[0] = over

    def move(s, i, back, act):
        is_out, cols = strip_of(sz, notes[s][0, i])
        for ref, here in ((outputs, is_out), (input_grads, jnp.logical_not(is_out))):
            @pl.when(here)
            def _(ref=ref):
                there = ref.at[:, cols]
                if back:
                    act(pltpu.make_async_copy(strips.at[i], there, write_sems.at[i]))
                else:
                    act(pltpu.make_async_copy(there, strips.at[i], read_sems.at[i]))

    def loop(s, body):
        lax.fori_loop(0, jnp.minimum(notes[s][0, sz.note_n], sz.first), lambda i, _: body(i), None)

    for s in range(T - 1):
        if s:
            loop(s, lambda i: move(s, i, False, lambda c: c.start()))

        def step(i):
            if s:
                move(s, i, False, lambda c: c.wait())
            held = strips[i] if s else held_strips[i]
            value = held.astype(jnp.float32) + firsts[s][i].astype(jnp.float32)
            strips[i] = value.astype(jnp.bfloat16)
            move(s, i, True, lambda c: c.start())

        loop(s, step)
        loop(s, lambda i: move(s, i, True, lambda c: c.wait()))


def last_kernel(sz, plan, *refs):
    mine, theirs, grads = refs[:3], refs[3:6], refs[6:]
    core = plan[HEAD_ROW, HEAD_CORE]
    for k in range(3):
        for a in range(sz.nb):
            at = plan[MINE_ROW, k * sz.nb + a]
            p = jnp.minimum(jnp.maximum(at - 1, 0), sz.keep - 1)
            for terms, c in ((mine, core), (theirs, 1 - core)):
                value = sum(t[p].astype(jnp.float32) for t in terms)
                rows = pl.ds(pl.multiple_of(c * ROWS, ROWS), ROWS)
                grads[k][0, a, rows] = jnp.where(at > 0, value, 0.0).astype(jnp.bfloat16)


def spec(space):
    return pl.BlockSpec(memory_space=space)


ANY, HBM, VMEM, SMEM = pl.ANY, pltpu.HBM, pltpu.VMEM, pltpu.SMEM


def cost(flops, moved):
    return pl.CostEstimate(flops=flops, bytes_accessed=moved, transcendentals=0)


def call_plan(sz, own, mine, theirs):
    return pl.pallas_call(
        functools.partial(plan_kernel, sz),
        out_shape=[
            jax.ShapeDtypeStruct((sz.plan_rows, sz.lanes), jnp.int32),
            halves(sz.keep),
        ] + [jax.ShapeDtypeStruct((1, sz.lanes), jnp.int32)] * (sz.n_tensor - 1),
        in_specs=[spec(VMEM)] + [spec(ANY)] * 6,
        out_specs=[spec(VMEM), spec(ANY)] + [spec(VMEM)] * (sz.n_tensor - 1),
        scratch_shapes=[pltpu.SemaphoreType.DMA((2 * sz.owned,))],
        compiler_params=pltpu.CompilerParams(vmem_limit_bytes=SMALL),
        cost_estimate=cost(1_000_000, 4_000_000),
        name="plan",
    )(own, *mine, *theirs)


def call_turn(handed, arrived):
    return pl.pallas_call(
        lambda *_: None,
        out_shape=[jax.ShapeDtypeStruct(x.shape, x.dtype) for x in handed],
        in_specs=[spec(ANY)] * (len(handed) + len(arrived)),
        out_specs=[spec(ANY)] * len(handed),
        input_output_aliases={i: i for i in range(len(handed))},
        compiler_params=pltpu.CompilerParams(vmem_limit_bytes=SMALL),
        cost_estimate=cost(1000, 1000),
        name="turn",
    )(*handed, *arrived)


def blocks(n):
    return jax.ShapeDtypeStruct((n, BLK, BLK), jnp.bfloat16)


def halves(n):
    return jax.ShapeDtypeStruct((n, ROWS, BLK), jnp.bfloat16)


def held(scratch):
    return sum(s[0] * s[1] * s[2] * jnp.dtype(t).itemsize for s, t in scratch) + 2 * 1024 * 1024


def call_compute(sz, plan, tokens, cot, chunks):
    bf, f32 = jnp.bfloat16, jnp.float32
    T, A = sz.n_tensor, sz.slots + 1
    out_shape = [halves(sz.ring * sz.keep), halves(sz.far * sz.keep), halves((sz.ring - sz.far) * sz.keep)]
    out_shape += [blocks(sz.first)] * T
    scratch = [
        ((3 * sz.room, sz.tok, BLK), bf),
        ((sz.blocks + 1, BLK, BLK), bf),
        ((sz.blocks + 1, BLK, BLK), bf),
        ((A, sz.tok, BLK), f32),
        ((A, sz.tok, BLK), f32),
        ((A, sz.tok, BLK), f32),
        ((3 * A, sz.tok, BLK), bf),
        ((sz.all + 1, sz.tok, BLK), f32),
        ((T * sz.first, sz.tok, BLK), bf),
    ]
    return pl.pallas_call(
        functools.partial(compute_kernel, sz),
        out_shape=out_shape,
        in_specs=[spec(SMEM)] + [spec(HBM)] * 2 + [spec(ANY)] * len(chunks),
        out_specs=[spec(ANY)] * len(out_shape),
        scratch_shapes=[pltpu.VMEM(s, t) for s, t in scratch] + [
            pltpu.SemaphoreType.DMA((3 * sz.room,)),
            pltpu.SemaphoreType.DMA((max(len(chunks), sz.ring + 1 + T),)),
        ],
        compiler_params=pltpu.CompilerParams(vmem_limit_bytes=held(scratch)),
        cost_estimate=cost(1_000_000_000, 20_000_000),
        name="compute",
    )(plan, pltpu.with_memory_space_constraint(tokens, HBM), pltpu.with_memory_space_constraint(cot, HBM), *chunks)


def call_prepare(sz, plan, note, first):
    half = jax.ShapeDtypeStruct((sz.tok, sz.width // sz.n_tensor), jnp.bfloat16)
    return pl.pallas_call(
        functools.partial(prepare_kernel, sz),
        out_shape=[half, half, blocks(sz.first)],
        in_specs=[spec(SMEM), spec(SMEM), spec(VMEM)],
        out_specs=[spec(VMEM)] * 3,
        compiler_params=pltpu.CompilerParams(vmem_limit_bytes=12 * 1024 * 1024),
        cost_estimate=cost(1_000_000, 6_000_000),
        name="prepare",
    )(plan, note, first)


def call_add(sz, plan, notes, firsts, strips, partial):
    n = 2 + len(notes) + len(firsts)
    return pl.pallas_call(
        functools.partial(add_kernel, sz),
        out_shape=[jax.ShapeDtypeStruct(p.shape, p.dtype) for p in partial] + [jax.ShapeDtypeStruct((1,), jnp.int32)],
        in_specs=[spec(SMEM)] * (1 + len(notes)) + [spec(VMEM)] * (len(firsts) + 1) + [spec(ANY)] * 2,
        out_specs=[spec(ANY)] * 2 + [spec(SMEM)],
        input_output_aliases={n: 0, n + 1: 1},
        scratch_shapes=[
            pltpu.VMEM((sz.first, sz.tok, BLK), jnp.bfloat16),
            pltpu.SemaphoreType.DMA((sz.first,)),
            pltpu.SemaphoreType.DMA((sz.first,)),
        ],
        compiler_params=pltpu.CompilerParams(vmem_limit_bytes=12 * 1024 * 1024),
        cost_estimate=cost(1_000_000, 3_000_000),
        name="add",
    )(plan, *notes, *firsts, strips, *partial)


def call_last(sz, plan, terms):
    out = jax.ShapeDtypeStruct((1, sz.nb, BLK, BLK), jnp.bfloat16)
    return pl.pallas_call(
        functools.partial(last_kernel, sz),
        out_shape=[out] * 3,
        in_specs=[spec(SMEM)] + [spec(VMEM)] * len(terms),
        out_specs=[spec(VMEM)] * 3,
        compiler_params=pltpu.CompilerParams(vmem_limit_bytes=SMALL),
        cost_estimate=cost(1_000_000, 1_000_000),
        name="last",
    )(plan, *terms)


def across(pairs):
    return [(i, j ^ 1) for i, j in pairs]


def gather_chunks(sz, chunk):
    ahead, behind, swap = permutations(sz)
    same = {0: chunk}
    a = b = chunk
    for s in range(1, sz.top):
        a, b = lax.ppermute(a, "fsdp", ahead), lax.ppermute(b, "fsdp", behind)
        same[sz.ring - s], same[s] = a, b
    other = {d: lax.ppermute(same[d], "fsdp", swap) for d in same}
    same[sz.top] = lax.ppermute(a, "fsdp", ahead)
    other[sz.top] = lax.ppermute(a, "fsdp", across(ahead))
    return [side[d] for side in (same, other) for d in sz.order]


def reduce_parts(sz, same, far, near, notes, prepare, sent):
    ahead, behind, swap = permutations(sz)
    keep = sz.keep
    far = lax.ppermute(far, "fsdp", swap)
    near = lax.ppermute(call_turn([near], [far])[0], "fsdp", swap)

    def term(d, *more):
        j = sz.order.index(d)
        pair = far[j * keep:(j + 1) * keep] if j < sz.far else near[(j - sz.far) * keep:][:keep]
        out = same[j * keep:(j + 1) * keep].astype(jnp.float32) + pair.astype(jnp.float32)
        for m in more:
            out = out + m.astype(jnp.float32)
        return out.astype(jnp.bfloat16)

    a, b = lax.optimization_barrier((term(sz.top), term(sz.top + 1)))
    here = term(0)
    here_across = lax.ppermute(here, "fsdp", swap)
    prepared = prepare(here_across)
    for s in range(1, sz.top):
        last_b = b
        a, b = lax.ppermute(a, "fsdp", ahead), lax.ppermute(b, "fsdp", behind)
        if s == 1:
            a, b = call_turn([a, b], [])
        else:
            a = call_turn([a], [last_b] + (notes + list(prepared[2:]) if s == 2 else sent))[0]
        a = term(sz.top - s, a)
        if s + 1 < sz.top:
            b = term(sz.top + 1 + s, call_turn([b], [a])[0])
    mine = [here, lax.ppermute(a, "fsdp", ahead), b]
    theirs = [
        here_across,
        lax.ppermute(a, "fsdp", across(ahead)),
        lax.ppermute(last_b, "fsdp", across(behind)),
    ]
    return mine + theirs, prepared


def program(sz, own, tokens, cotangent, mine):
    T = sz.n_tensor
    swap = permutations(sz)[-1]
    theirs = [lax.ppermute(b, "fsdp", swap) for b in mine]
    plan, chunk, *notes = call_plan(sz, own, mine, theirs)

    def exchange(array, s):
        return lax.ppermute(array, "tensor", [(i, (i + s) % T) for i in range(T)])

    notes = [exchange(note, s) for s, note in enumerate(notes, 1)]
    chunks = gather_chunks(sz, chunk)
    same, far, near, *firsts = call_compute(sz, plan, tokens, cotangent, chunks)

    def prepare(after):
        return call_prepare(sz, plan, notes[0], call_turn([firsts[0]], [after])[0])

    sent = [exchange(firsts[s], s) for s in range(1, T)]
    terms, (*partial, strips) = reduce_parts(sz, same, far, near, notes, prepare, sent)
    sent = call_turn(sent, [terms[2], terms[5]])
    outputs, input_grads, flag = call_add(sz, plan, notes, sent, strips, partial)
    return (outputs, input_grads, *call_last(sz, plan, terms)), flag


def shards(
    tokens,
    cotangent,
    gate_blocks,
    up_blocks,
    down_blocks,
    gate_where,
    up_where,
    down_where,
    block_counts,
):
    n_fsdp, n_tensor = lax.axis_size("fsdp"), lax.axis_size("tensor")
    f, rank = lax.axis_index("fsdp"), lax.axis_index("tensor")
    slots = gate_where.shape[1]
    full = Sizes(tokens, gate_blocks, slots, n_fsdp, n_tensor, False)
    own = jnp.concatenate([
        gate_where[0], up_where[0], down_where[0], block_counts[:, 0],
        f.astype(jnp.int32)[None], rank.astype(jnp.int32)[None]])
    own = jnp.pad(own, (0, full.lanes - own.shape[0]))[None]
    blocks_in = (gate_blocks, up_blocks, down_blocks)
    if slots >= full.cb:
        return program(full, own, tokens, cotangent, blocks_in)[0]
    lean = Sizes(tokens, gate_blocks, slots, n_fsdp, n_tensor, True)
    outs, flag = program(lean, own, tokens, cotangent, blocks_in)
    return lax.cond(
        flag[0] > 0,
        lambda outs, *args: program(full, *args)[0],
        lambda outs, *args: outs,
        outs, own, tokens, cotangent, blocks_in)


def solution(mesh):
    placed = (
        P("fsdp", None),
        P("fsdp", None),
        P("tensor", "fsdp", None, None),
        P("tensor", "fsdp", None, None),
        P("tensor", "fsdp", None, None),
        P("tensor", None),
        P("tensor", None),
        P("tensor", None),
        P(None, "tensor"),
    )
    return jax.shard_map(
        shards,
        mesh=mesh,
        in_specs=placed,
        out_specs=(
            P("fsdp", "tensor"),
            P("fsdp", "tensor"),
            P("tensor", "fsdp", None, None),
            P("tensor", "fsdp", None, None),
            P("tensor", "fsdp", None, None),
        ),
        check_vma=False,
    )
```

```python
import functools

import jax
import jax.numpy as jnp
from jax import lax
from jax.experimental import pallas as pl
from jax.experimental.pallas import tpu as pltpu
from jax.sharding import PartitionSpec as P

FF = 14336
BLK = 128
GROUP = 8
COLUMNS = 4
FIRST_SEND = 17
LEAN_SLOTS = 7
ROWS = BLK // 2
SMALL = 4 * 1024 * 1024
PART, STRIP, CIDX, CWAS, OIDX, OWAS = range(6)
FIELDS = 6
COLS_ROW = 3 * FIELDS
HEAD_ROW = COLS_ROW + 1
MINE_ROW = COLS_ROW + 2
LISTS_ROW = COLS_ROW + 3
HEAD_COLS, HEAD_OVER, HEAD_CORE, HEAD_LISTS = 3, 4, 5, 8


class Sizes:
    def __init__(self, tokens, gate_blocks, slots, n_fsdp, n_tensor, lean):
        self.tok, self.width = tokens.shape
        self.n_fsdp, self.n_tensor = n_fsdp, n_tensor
        self.rb = self.width // BLK
        self.cb = FF // (BLK * n_tensor)
        self.slots = slots
        self.all = 3 * slots
        self.lanes = -(-(self.all + GROUP) // 128) * 128
        self.nb = gate_blocks.shape[1]
        self.owned = 3 * self.nb
        self.ring = n_fsdp // 2
        self.top = self.ring // 2
        self.rbt = self.rb // n_tensor
        self.order = [self.top]
        for d in range(1, self.top):
            self.order += [self.top + d, self.top - d]
        self.order.append(0)
        self.far = min(2, self.ring - 1)
        self.keep = min(LEAN_SLOTS, 2 * self.owned) if lean else 2 * self.owned
        self.send_all = 2 * self.rbt
        self.first = min(FIRST_SEND, self.send_all) if lean else self.send_all
        self.blocks = self.ring * self.keep
        self.plan_rows = -(-(LISTS_ROW + 2 * n_tensor) // 8) * 8
        self.note_n, self.note_over = self.lanes - 1, self.lanes - 2
        self.room = slots + GROUP

    def place(self, d):
        return self.order.index(d) * self.keep

    def place_across(self, d):
        return self.place((self.ring - d) % self.ring)


def permutations(sz):
    seq = list(range(0, sz.ring, 2)) + list(range(sz.ring - 1, 0, -2))
    ahead, behind, swap = [], [], []
    for i, q in enumerate(seq):
        up, down = seq[(i + 1) % sz.ring], seq[i - 1]
        ahead += [(q * 2, up * 2), (q * 2 + 1, down * 2 + 1)]
        behind += [(q * 2, down * 2), (q * 2 + 1, up * 2 + 1)]
        swap += [(q * 2, q * 2 + 1), (q * 2 + 1, q * 2)]
    return ahead, behind, swap


def ratio(x, d):
    return jnp.floor((x + 0.5) * (1.0 / d))


def rest_of(x, d):
    return x - d * ratio(x, d)


def ring_position(sz, chip):
    return jnp.where(rest_of(chip, 2) == 0, ratio(chip, 2), sz.ring - 1 - ratio(chip, 2))


class Marks:
    def __init__(self, sz, own):
        N, L, S = sz.all, sz.lanes, sz.slots
        f32 = jnp.float32
        self.sz = sz
        self.sub = lax.broadcasted_iota(jnp.int32, (N, L), 0)
        self.lane = lax.broadcasted_iota(jnp.int32, (N, L), 1)
        self.same = self.sub == self.lane
        sub_c = self.sub[:, :1].astype(f32)
        lane_r = lax.broadcasted_iota(jnp.int32, (1, L), 1).astype(f32)
        self.sub_c, self.lane_r = sub_c, lane_r
        raw_r = own[...].astype(f32)

        def single(row, at):
            return jnp.sum(jnp.where(lane_r == at, row, 0.0), axis=1, keepdims=True)

        self.f, self.rank = single(raw_r, N + 3), single(raw_r, N + 4)

        def kind(x):
            return (x >= S).astype(f32) + (x >= 2 * S).astype(f32)

        self.kind_c, self.kind_r = kind(sub_c), kind(lane_r)
        self.n_r = lane_r - S * self.kind_r
        self.n_c = sub_c - S * self.kind_c
        limit = jnp.zeros((1, L), f32)
        for k in range(3):
            limit = limit + jnp.where(self.kind_r == k, single(raw_r, N + k), 0.0)
        live_r = jnp.where((lane_r < N) & (self.n_r < limit), 1.0, 0.0)
        w_c = self.col(raw_r)
        live_c = self.col(live_r)

        def place(w, k):
            gate, down = ratio(w, sz.cb), ratio(w, sz.rb)
            is_down = k == 2
            return jnp.where(is_down, w - down * sz.rb, gate), jnp.where(is_down, down, w - gate * sz.cb)

        self.row_c, col_c = place(w_c, self.kind_c)
        self.row_r, col_r = place(raw_r, self.kind_r)
        self.chip_c, chip_r = ratio(self.n_c, 2 * sz.nb), ratio(self.n_r, 2 * sz.nb)
        self.same_chip = (self.chip_c == chip_r).astype(f32)
        self.same_col = (col_c == col_r).astype(f32)
        act_c, act_r = live_c, live_r
        for k in range(3):
            lanes = self.same_col * (live_r * (self.kind_r == k).astype(f32))
            act_c = act_c * jnp.max(lanes, axis=1, keepdims=True)
            subs = self.same_col * (live_c * (self.kind_c == k).astype(f32))
            act_r = act_r * jnp.max(subs, axis=0, keepdims=True)
        self.act_c, self.act_r = act_c, act_r
        out_c = jnp.where(self.kind_c == 2, 0.0, f32(sz.rb)) + self.row_c
        out_r = jnp.where(self.kind_r == 2, 0.0, f32(sz.rb)) + self.row_r
        self.same_out = (out_c == out_r).astype(f32)
        self.before = (self.lane < self.sub).astype(f32)
        self.after = (self.sub < self.lane).astype(f32)
        self.owas_c = jnp.max(self.same_out * self.before * act_r, axis=1, keepdims=True)
        self.owas_r = jnp.max(self.same_out * self.after * act_c, axis=0, keepdims=True)
        self.lead_c = act_c * (1.0 - self.owas_c)
        self.lead_r = act_r * (1.0 - self.owas_r)

        def shift(row):
            away = ratio(row, sz.rbt) - self.rank
            return jnp.where(away < 0, away + sz.n_tensor, away)

        self.shift_c, self.shift_r = shift(self.row_c), shift(self.row_r)
        self.local_c = jnp.where(self.kind_c == 2, 0.0, f32(sz.rbt)) + rest_of(self.row_c, sz.rbt)

    def col(self, row):
        return jnp.sum(jnp.where(self.same, row, 0.0), axis=1, keepdims=True)

    def carried(self):
        sz = self.sz
        rank = jnp.sum(self.before * self.same_chip * self.act_r, axis=1, keepdims=True)
        away = ring_position(sz, self.chip_c) - ring_position(sz, ratio(self.f, 2))
        away = jnp.where(rest_of(self.f, 2) == 0, away, -away)
        rel = jnp.where(away < 0, away + sz.ring, away)
        j = jnp.where(rel > sz.top, 2 * (rel - sz.top) - 1, 2 * (sz.top - rel))
        return rank, jnp.where(rel == 0, sz.ring - 1.0, j)

    def ranks(self, chosen_r):
        return jnp.sum(self.before * chosen_r, axis=1, keepdims=True)

    def listed(self, chosen_c, rank_c, value_c, lo=0, hi=None):
        at = rank_c[lo:hi] == self.lane[lo:hi].astype(jnp.float32)
        return jnp.sum(jnp.where(at, chosen_c[lo:hi] * value_c[lo:hi], 0.0), axis=0, keepdims=True)

    def most_on_chip(self):
        return jnp.max(jnp.sum(self.same_chip * self.act_r, axis=1, keepdims=True), axis=0, keepdims=True)


def total(x):
    return jnp.sum(x, axis=0, keepdims=True)


def head_row(sz, entries):
    lane = lax.broadcasted_iota(jnp.int32, (1, sz.lanes), 1)
    row = jnp.zeros((1, sz.lanes), jnp.float32)
    for i, value in entries:
        row = jnp.where(lane == i, value, row)
    return row


def plan_kernel(sz, own, *refs):
    mine, theirs, (plan, chunk, *notes, sems) = refs[:3], refs[3:6], refs[6:]
    S, N = sz.slots, sz.all
    m = Marks(sz, own)
    f32 = jnp.float32
    lane_r, sub_c = m.lane_r, m.sub_c
    pos_c, base_c = m.carried()
    core = rest_of(m.f, 2)
    half = pl.ds(pl.multiple_of(jnp.max(core).astype(jnp.int32) * ROWS, ROWS), ROWS)

    pair = jnp.where(core == 0, m.f + 1, m.f - 1)
    i_r = rest_of(lane_r, sz.owned)
    owner_r = jnp.where(lane_r < sz.owned, m.f, pair)
    slot_r = ratio(i_r, sz.nb) * S + owner_r * sz.nb + rest_of(i_r, sz.nb)
    at_r = jnp.sum(jnp.where(sub_c == slot_r, m.act_c * (pos_c + 1.0), 0.0), axis=0, keepdims=True)
    copies = []
    for i in range(2 * sz.owned):
        side, k, a = i // sz.owned, i % sz.owned // sz.nb, i % sz.nb
        at = jnp.max(jnp.where(lane_r == i, at_r, 0.0)).astype(jnp.int32)
        fits = (at > 0) & (at <= sz.keep)
        place = jnp.minimum(jnp.maximum(at - 1, 0), sz.keep - 1)
        copy = pltpu.make_async_copy((mine, theirs)[side][k].at[0, a, half], chunk.at[place], sems.at[i])
        copies.append((fits, copy))
    for fits, copy in copies:
        pl.when(fits)(copy.start)

    same_kind = (m.kind_c == m.kind_r).astype(f32)
    rank_c = jnp.sum(m.before * same_kind * m.act_r, axis=1, keepdims=True)
    cwas_c = jnp.max(m.before * same_kind * m.same_col * m.act_r, axis=1, keepdims=True)
    cwas_r = jnp.max(m.after * same_kind * m.same_col * m.act_c, axis=0, keepdims=True)
    big = f32(4 * N)
    lanes_f = m.lane.astype(f32)
    gates_r = m.act_r * (m.kind_r == 0).astype(f32)
    cidx_c = jnp.min(jnp.where(m.same_col * gates_r > 0, lanes_f, big), axis=1, keepdims=True)
    oidx_c = jnp.min(jnp.where(m.same_out * m.act_r > 0, lanes_f, big), axis=1, keepdims=True)
    rank_r = jnp.sum(m.after * same_kind * m.act_c, axis=0, keepdims=True)
    turn_c = ratio(rank_c, GROUP) * 3 + m.kind_c
    turn_r = ratio(rank_r, GROUP) * 3 + m.kind_r
    ahead = ((turn_r < turn_c) | ((turn_r == turn_c) & (rank_r < rank_c))).astype(f32)
    owas_c = jnp.max(m.same_out * ahead * m.act_r, axis=1, keepdims=True)
    part_c = jnp.where(pos_c < sz.keep, base_c * sz.keep + pos_c, f32(sz.blocks))
    fields = [(part_c, sz.blocks), (m.row_c, 0), (cidx_c, S), (cwas_c, 0), (oidx_c, N), (owas_c, 0)]
    rows = []
    head = []
    for k in range(3):
        lo, hi = k * S, (k + 1) * S
        n_k = total(m.act_c[lo:hi])
        head.append((k, n_k))
        for value, spare in fields:
            row = m.listed(m.act_c, rank_c, value, lo, hi)
            rows.append(jnp.where(lane_r < n_k, row, f32(spare)))
    leader_c = m.act_c * (1.0 - cwas_c) * (m.kind_c == 0).astype(f32)
    leader_r = m.act_r * (1.0 - cwas_r) * (m.kind_r == 0).astype(f32)
    n_cols = total(leader_c)
    cols = m.listed(leader_c, m.ranks(leader_r), sub_c, 0, S)
    rows.append(jnp.where(lane_r < n_cols, cols, f32(S)))
    head.append((HEAD_COLS, n_cols))
    lists, sent = [], []
    over = (m.most_on_chip() > sz.keep).astype(f32)
    for s in range(sz.n_tensor):
        chosen_c = m.lead_c * (m.shift_c == s).astype(f32)
        chosen_r = m.lead_r * (m.shift_r == s).astype(f32)
        rank = m.ranks(chosen_r)
        lists.append(m.listed(chosen_c, rank, sub_c))
        lists.append(m.listed(chosen_c, rank, m.local_c))
        n = total(chosen_c)
        head.append((HEAD_LISTS + s, n))
        sent.append(n)
        over = jnp.maximum(over, (n > sz.first).astype(f32))
    head += [(HEAD_OVER, over), (HEAD_CORE, core)]
    for s in range(1, sz.n_tensor):
        note = jnp.where(lane_r == sz.note_n, sent[s], lists[2 * s + 1])
        notes[s - 1][...] = jnp.where(lane_r == sz.note_over, over, note).astype(jnp.int32)
    rows.append(head_row(sz, head))
    rows.append(at_r)
    rows += lists
    for i, row in enumerate(rows):
        plan[i:i + 1, :] = row.astype(jnp.int32)
    for fits, copy in copies:
        pl.when(fits)(copy.wait)


def dot(a, b, ca, cb):
    return lax.dot_general(a, b, (((ca,), (cb,)), ((), ())), preferred_element_type=jnp.float32)


def field(sz, plan, k, j, e):
    return plan[k * FIELDS + j, e]


def walk(plan, body):
    most = jnp.maximum(jnp.maximum(plan[HEAD_ROW, 0], plan[HEAD_ROW, 1]), plan[HEAD_ROW, 2])
    lax.fori_loop(0, (most + (GROUP - 1)) // GROUP, lambda p, _: body(p * GROUP), None)


def each(plan, k, body):
    lax.fori_loop(0, plan[HEAD_ROW, k], lambda e, _: body(e), None)


def compute_kernel(sz, plan, tokens, cot, *refs):
    n_chunks, T = 2 * sz.ring, sz.n_tensor
    chunks, refs = refs[:n_chunks], refs[n_chunks:]
    same, far, near = refs[:3]
    firsts, refs = refs[3:3 + T], refs[3 + T:]
    xs, wbuf, parts, gate_acc, up_acc, hg_acc, acts, out_acc, stage, strip_sems, sems = refs
    A = sz.slots + 1
    get = functools.partial(field, sz, plan)

    def strip_copy(k, e):
        src = cot if k == 2 else tokens
        cols = pl.ds(pl.multiple_of(get(k, STRIP, e) * BLK, BLK), BLK)
        return pltpu.make_async_copy(src.at[:, cols], xs.at[k * sz.room + e], strip_sems.at[k * sz.room + e])

    core = plan[HEAD_ROW, HEAD_CORE]
    sides = [pl.ds(pl.multiple_of(c * ROWS, ROWS), ROWS) for c in (core, 1 - core)]
    loads = []
    for side, place in enumerate((sz.place, sz.place_across)):
        for d in sz.order:
            i = len(loads)
            there = wbuf.at[pl.ds(place(d), sz.keep), sides[side]]
            loads.append(pltpu.make_async_copy(chunks[i], there, sems.at[i]))
    for k in range(3):
        each(plan, k, lambda e, k=k: strip_copy(k, e).start())
    for c in loads:
        c.start()
    for k in range(3):
        each(plan, k, lambda e, k=k: strip_copy(k, e).wait())
    for c in loads:
        c.wait()

    group = [(k, u) for k in range(3) for u in range(GROUP)]

    def forward(e0):
        for k, u in group:
            e, acc = e0 + u, (gate_acc, up_acc, hg_acc)[k]
            prod = dot(xs[k * sz.room + e], wbuf[get(k, PART, e)], 1, 1 if k == 2 else 0)
            c = get(k, CIDX, e)
            acc[c] = prod + jnp.where(get(k, CWAS, e) == 0, 0.0, acc[c])

    walk(plan, forward)

    def columns(i, _):
        for j in range(COLUMNS):
            c = plan[COLS_ROW, i * COLUMNS + j]
            g, u, h = gate_acc[c], up_acc[c], hg_acc[c]
            s = lax.logistic(g)
            silu = g * s
            acts[c] = (h * u * s * (1.0 + g * (1.0 - s))).astype(jnp.bfloat16)
            acts[A + c] = (h * silu).astype(jnp.bfloat16)
            acts[2 * A + c] = (silu * u).astype(jnp.bfloat16)

    lax.fori_loop(0, (plan[HEAD_ROW, HEAD_COLS] + (COLUMNS - 1)) // COLUMNS, columns, None)

    def gradients(e0):
        for k, u in group:
            e = e0 + u
            a, x = acts[k * A + get(k, CIDX, e)], xs[k * sz.room + e]
            grad = dot(a, x, 0, 0) if k == 2 else dot(x, a, 0, 0)
            parts[get(k, PART, e)] = grad.astype(jnp.bfloat16)

    walk(plan, gradients)
    outs = []
    for j, d in enumerate(sz.order):
        ref, at = (far, j) if j < sz.far else (near, j - sz.far)
        outs.append(pltpu.make_async_copy(
            parts.at[pl.ds(sz.place_across(d), sz.keep), sides[1]], ref.at[pl.ds(at * sz.keep, sz.keep)], sems.at[j]))
    outs.append(pltpu.make_async_copy(parts.at[pl.ds(0, sz.blocks), sides[0]], same, sems.at[sz.ring]))
    for c in outs:
        c.start()

    def terms(e0):
        for k, u in group:
            e = e0 + u
            prod = dot(acts[k * A + get(k, CIDX, e)], wbuf[get(k, PART, e)], 1, 0 if k == 2 else 1)
            at = get(k, OIDX, e)
            out_acc[at] = prod + jnp.where(get(k, OWAS, e) == 0, 0.0, out_acc[at])

    walk(plan, terms)

    for s in reversed(range(T)):
        def staged(i, _, s=s):
            stage[s * sz.first + i] = out_acc[plan[LISTS_ROW + 2 * s, i]].astype(jnp.bfloat16)

        lax.fori_loop(0, jnp.minimum(plan[HEAD_ROW, HEAD_LISTS + s], sz.first), staged, None)
        copy = pltpu.make_async_copy(stage.at[pl.ds(s * sz.first, sz.first)], firsts[s], sems.at[sz.ring + 1 + s])
        copy.start()
        outs.append(copy)
    for c in outs:
        c.wait()


def strip_of(sz, at):
    w = jnp.where(at < sz.rbt, at, at - sz.rbt)
    return at < sz.rbt, pl.ds(pl.multiple_of(w * BLK, BLK), BLK)


def prepare_kernel(sz, plan, note, first, outputs, input_grads, strips):
    outputs[...] = jnp.zeros_like(outputs)
    input_grads[...] = jnp.zeros_like(input_grads)

    def step(i, _):
        is_out, cols = strip_of(sz, plan[LISTS_ROW + 1, i])

        @pl.when(is_out)
        def _():
            outputs[:, cols] = first[i]

        @pl.when(jnp.logical_not(is_out))
        def _():
            input_grads[:, cols] = first[i]

    lax.fori_loop(0, jnp.minimum(plan[HEAD_ROW, HEAD_LISTS], sz.first), step, None)

    def pick(i, _):
        is_out, cols = strip_of(sz, note[0, i])

        @pl.when(is_out)
        def _():
            strips[i] = outputs[:, cols]

        @pl.when(jnp.logical_not(is_out))
        def _():
            strips[i] = input_grads[:, cols]

    lax.fori_loop(0, jnp.minimum(note[0, sz.note_n], sz.first), pick, None)


def add_kernel(sz, plan, *refs):
    T = sz.n_tensor
    notes, refs = refs[:T - 1], refs[T - 1:]
    firsts, held_strips, refs = refs[:T - 1], refs[T - 1], refs[T + 2:]
    outputs, input_grads, flag, strips, read_sems, write_sems = refs
    over = plan[HEAD_ROW, HEAD_OVER]
    for note in notes:
        over = jnp.maximum(over, note[0, sz.note_over])
    flag[0] = over

    def move(s, i, back, act):
        is_out, cols = strip_of(sz, notes[s][0, i])
        for ref, here in ((outputs, is_out), (input_grads, jnp.logical_not(is_out))):
            @pl.when(here)
            def _(ref=ref):
                there = ref.at[:, cols]
                if back:
                    act(pltpu.make_async_copy(strips.at[i], there, write_sems.at[i]))
                else:
                    act(pltpu.make_async_copy(there, strips.at[i], read_sems.at[i]))

    def loop(s, body):
        lax.fori_loop(0, jnp.minimum(notes[s][0, sz.note_n], sz.first), lambda i, _: body(i), None)

    for s in range(T - 1):
        if s:
            loop(s, lambda i: move(s, i, False, lambda c: c.start()))

        def step(i):
            if s:
                move(s, i, False, lambda c: c.wait())
            held = strips[i] if s else held_strips[i]
            value = held.astype(jnp.float32) + firsts[s][i].astype(jnp.float32)
            strips[i] = value.astype(jnp.bfloat16)
            move(s, i, True, lambda c: c.start())

        loop(s, step)
        loop(s, lambda i: move(s, i, True, lambda c: c.wait()))


def last_kernel(sz, plan, *refs):
    mine, theirs, grads = refs[:2], refs[2:4], refs[4:]
    core = plan[HEAD_ROW, HEAD_CORE]
    for k in range(3):
        for a in range(sz.nb):
            at = plan[MINE_ROW, k * sz.nb + a]
            p = jnp.minimum(jnp.maximum(at - 1, 0), sz.keep - 1)
            for terms, c in ((mine, core), (theirs, 1 - core)):
                value = sum(t[p].astype(jnp.float32) for t in terms)
                rows = pl.ds(pl.multiple_of(c * ROWS, ROWS), ROWS)
                grads[k][0, a, rows] = jnp.where(at > 0, value, 0.0).astype(jnp.bfloat16)


def spec(space):
    return pl.BlockSpec(memory_space=space)


ANY, HBM, VMEM, SMEM = pl.ANY, pltpu.HBM, pltpu.VMEM, pltpu.SMEM


def cost(flops, moved):
    return pl.CostEstimate(flops=flops, bytes_accessed=moved, transcendentals=0)


def call_plan(sz, own, mine, theirs):
    return pl.pallas_call(
        functools.partial(plan_kernel, sz),
        out_shape=[
            jax.ShapeDtypeStruct((sz.plan_rows, sz.lanes), jnp.int32),
            halves(sz.keep),
        ] + [jax.ShapeDtypeStruct((1, sz.lanes), jnp.int32)] * (sz.n_tensor - 1),
        in_specs=[spec(VMEM)] + [spec(ANY)] * 6,
        out_specs=[spec(VMEM), spec(ANY)] + [spec(VMEM)] * (sz.n_tensor - 1),
        scratch_shapes=[pltpu.SemaphoreType.DMA((2 * sz.owned,))],
        compiler_params=pltpu.CompilerParams(vmem_limit_bytes=SMALL),
        cost_estimate=cost(1_000_000, 4_000_000),
        name="plan",
    )(own, *mine, *theirs)


def call_turn(handed, arrived):
    return pl.pallas_call(
        lambda *_: None,
        out_shape=[jax.ShapeDtypeStruct(x.shape, x.dtype) for x in handed],
        in_specs=[spec(ANY)] * (len(handed) + len(arrived)),
        out_specs=[spec(ANY)] * len(handed),
        input_output_aliases={i: i for i in range(len(handed))},
        compiler_params=pltpu.CompilerParams(vmem_limit_bytes=SMALL),
        cost_estimate=cost(1000, 1000),
        name="turn",
    )(*handed, *arrived)


def blocks(n):
    return jax.ShapeDtypeStruct((n, BLK, BLK), jnp.bfloat16)


def halves(n):
    return jax.ShapeDtypeStruct((n, ROWS, BLK), jnp.bfloat16)


def held(scratch):
    return sum(s[0] * s[1] * s[2] * jnp.dtype(t).itemsize for s, t in scratch) + 2 * 1024 * 1024


def call_compute(sz, plan, tokens, cot, chunks):
    bf, f32 = jnp.bfloat16, jnp.float32
    T, A = sz.n_tensor, sz.slots + 1
    out_shape = [halves(sz.ring * sz.keep), halves(sz.far * sz.keep), halves((sz.ring - sz.far) * sz.keep)]
    out_shape += [blocks(sz.first)] * T
    scratch = [
        ((3 * sz.room, sz.tok, BLK), bf),
        ((sz.blocks + 1, BLK, BLK), bf),
        ((sz.blocks + 1, BLK, BLK), bf),
        ((A, sz.tok, BLK), f32),
        ((A, sz.tok, BLK), f32),
        ((A, sz.tok, BLK), f32),
        ((3 * A, sz.tok, BLK), bf),
        ((sz.all + 1, sz.tok, BLK), f32),
        ((T * sz.first, sz.tok, BLK), bf),
    ]
    return pl.pallas_call(
        functools.partial(compute_kernel, sz),
        out_shape=out_shape,
        in_specs=[spec(SMEM)] + [spec(HBM)] * 2 + [spec(ANY)] * len(chunks),
        out_specs=[spec(ANY)] * len(out_shape),
        scratch_shapes=[pltpu.VMEM(s, t) for s, t in scratch] + [
            pltpu.SemaphoreType.DMA((3 * sz.room,)),
            pltpu.SemaphoreType.DMA((max(len(chunks), sz.ring + 1 + T),)),
        ],
        compiler_params=pltpu.CompilerParams(vmem_limit_bytes=held(scratch)),
        cost_estimate=cost(1_000_000_000, 20_000_000),
        name="compute",
    )(plan, pltpu.with_memory_space_constraint(tokens, HBM), pltpu.with_memory_space_constraint(cot, HBM), *chunks)


def call_prepare(sz, plan, note, first):
    half = jax.ShapeDtypeStruct((sz.tok, sz.width // sz.n_tensor), jnp.bfloat16)
    return pl.pallas_call(
        functools.partial(prepare_kernel, sz),
        out_shape=[half, half, blocks(sz.first)],
        in_specs=[spec(SMEM), spec(SMEM), spec(VMEM)],
        out_specs=[spec(VMEM)] * 3,
        compiler_params=pltpu.CompilerParams(vmem_limit_bytes=12 * 1024 * 1024),
        cost_estimate=cost(1_000_000, 6_000_000),
        name="prepare",
    )(plan, note, first)


def call_add(sz, plan, notes, firsts, strips, partial):
    n = 2 + len(notes) + len(firsts)
    return pl.pallas_call(
        functools.partial(add_kernel, sz),
        out_shape=[jax.ShapeDtypeStruct(p.shape, p.dtype) for p in partial] + [jax.ShapeDtypeStruct((1,), jnp.int32)],
        in_specs=[spec(SMEM)] * (1 + len(notes)) + [spec(VMEM)] * (len(firsts) + 1) + [spec(ANY)] * 2,
        out_specs=[spec(ANY)] * 2 + [spec(SMEM)],
        input_output_aliases={n: 0, n + 1: 1},
        scratch_shapes=[
            pltpu.VMEM((sz.first, sz.tok, BLK), jnp.bfloat16),
            pltpu.SemaphoreType.DMA((sz.first,)),
            pltpu.SemaphoreType.DMA((sz.first,)),
        ],
        compiler_params=pltpu.CompilerParams(vmem_limit_bytes=12 * 1024 * 1024),
        cost_estimate=cost(1_000_000, 3_000_000),
        name="add",
    )(plan, *notes, *firsts, strips, *partial)


def call_last(sz, plan, terms):
    out = jax.ShapeDtypeStruct((1, sz.nb, BLK, BLK), jnp.bfloat16)
    return pl.pallas_call(
        functools.partial(last_kernel, sz),
        out_shape=[out] * 3,
        in_specs=[spec(SMEM)] + [spec(VMEM)] * len(terms),
        out_specs=[spec(VMEM)] * 3,
        compiler_params=pltpu.CompilerParams(vmem_limit_bytes=SMALL),
        cost_estimate=cost(1_000_000, 1_000_000),
        name="last",
    )(plan, *terms)


def across(pairs):
    return [(i, j ^ 1) for i, j in pairs]


def gather_chunks(sz, chunk):
    ahead, behind, swap = permutations(sz)
    same = {0: chunk}
    a = b = chunk
    for s in range(1, sz.top):
        a, b = lax.ppermute(a, "fsdp", ahead), lax.ppermute(b, "fsdp", behind)
        same[sz.ring - s], same[s] = a, b
    other = {d: lax.ppermute(same[d], "fsdp", swap) for d in same}
    same[sz.top] = lax.ppermute(a, "fsdp", ahead)
    other[sz.top] = lax.ppermute(a, "fsdp", across(ahead))
    return [side[d] for side in (same, other) for d in sz.order]


def reduce_parts(sz, same, far, near, notes, prepare, sent):
    ahead, behind, swap = permutations(sz)
    keep = sz.keep
    far = lax.ppermute(far, "fsdp", swap)
    near = lax.ppermute(call_turn([near], [far])[0], "fsdp", swap)

    def term(d, *more):
        j = sz.order.index(d)
        pair = far[j * keep:(j + 1) * keep] if j < sz.far else near[(j - sz.far) * keep:][:keep]
        out = same[j * keep:(j + 1) * keep].astype(jnp.float32) + pair.astype(jnp.float32)
        for m in more:
            out = out + m.astype(jnp.float32)
        return out.astype(jnp.bfloat16)

    a, b = lax.optimization_barrier((term(sz.top), term(sz.top + 1)))
    here = term(0)
    here_across = lax.ppermute(here, "fsdp", swap)
    prepared = prepare(here_across)
    for s in range(1, sz.top):
        last_b = b
        a, b = lax.ppermute(a, "fsdp", ahead), lax.ppermute(b, "fsdp", behind)
        if s == 1:
            a, b = call_turn([a, b], [])
        else:
            a = call_turn([a], [last_b] + (notes if s == 2 else sent + list(prepared[2:])))[0]
        a = term(sz.top - s, a)
        if s + 1 < sz.top:
            b = term(sz.top + 1 + s, call_turn([b], [a])[0])
    def joined(x, y):
        return (x.astype(jnp.float32) + y.astype(jnp.float32)).astype(jnp.bfloat16)

    b_across = lax.ppermute(last_b, "fsdp", across(behind))
    mine = [joined(here, b), lax.ppermute(a, "fsdp", ahead)]
    theirs = [joined(here_across, b_across), lax.ppermute(a, "fsdp", across(ahead))]
    return mine + theirs, prepared


def program(sz, own, tokens, cotangent, mine):
    T = sz.n_tensor
    swap = permutations(sz)[-1]
    theirs = [lax.ppermute(b, "fsdp", swap) for b in mine]
    plan, chunk, *notes = call_plan(sz, own, mine, theirs)

    def exchange(array, s):
        return lax.ppermute(array, "tensor", [(i, (i + s) % T) for i in range(T)])

    notes = [exchange(note, s) for s, note in enumerate(notes, 1)]
    chunks = gather_chunks(sz, chunk)
    same, far, near, *firsts = call_compute(sz, plan, tokens, cotangent, chunks)

    def prepare(after):
        return call_prepare(sz, plan, notes[0], call_turn([firsts[0]], [after])[0])

    sent = [exchange(firsts[s], s) for s in range(1, T)]
    terms, (*partial, strips) = reduce_parts(sz, same, far, near, notes, prepare, sent)
    sent = call_turn(sent, [terms[0], terms[2]])
    outputs, input_grads, flag = call_add(sz, plan, notes, sent, strips, partial)
    return (outputs, input_grads, *call_last(sz, plan, terms)), flag


def shards(
    tokens,
    cotangent,
    gate_blocks,
    up_blocks,
    down_blocks,
    gate_where,
    up_where,
    down_where,
    block_counts,
):
    n_fsdp, n_tensor = lax.axis_size("fsdp"), lax.axis_size("tensor")
    f, rank = lax.axis_index("fsdp"), lax.axis_index("tensor")
    slots = gate_where.shape[1]
    full = Sizes(tokens, gate_blocks, slots, n_fsdp, n_tensor, False)
    own = jnp.concatenate([
        gate_where[0], up_where[0], down_where[0], block_counts[:, 0],
        f.astype(jnp.int32)[None], rank.astype(jnp.int32)[None]])
    own = jnp.pad(own, (0, full.lanes - own.shape[0]))[None]
    blocks_in = (gate_blocks, up_blocks, down_blocks)
    if slots >= full.cb:
        return program(full, own, tokens, cotangent, blocks_in)[0]
    lean = Sizes(tokens, gate_blocks, slots, n_fsdp, n_tensor, True)
    outs, flag = program(lean, own, tokens, cotangent, blocks_in)
    return lax.cond(
        flag[0] > 0,
        lambda outs, *args: program(full, *args)[0],
        lambda outs, *args: outs,
        outs, own, tokens, cotangent, blocks_in)


def solution(mesh):
    placed = (
        P("fsdp", None),
        P("fsdp", None),
        P("tensor", "fsdp", None, None),
        P("tensor", "fsdp", None, None),
        P("tensor", "fsdp", None, None),
        P("tensor", None),
        P("tensor", None),
        P("tensor", None),
        P(None, "tensor"),
    )
    return jax.shard_map(
        shards,
        mesh=mesh,
        in_specs=placed,
        out_specs=(
            P("fsdp", "tensor"),
            P("fsdp", "tensor"),
            P("tensor", "fsdp", None, None),
            P("tensor", "fsdp", None, None),
            P("tensor", "fsdp", None, None),
        ),
        check_vma=False,
    )
```
